32 devices in a mesh: dp: 8 (over z, x), tensor: 4 (over y, core).
Axes of the slice: x: 2, y: 2, z: 4, core: 2. Of those that a mesh axis runs over, the one named last changes fastest.
Arguments:
- x_first: bfloat16 [64, 8192], P('dp', 'tensor'), may hold values from -64 to 64
- x_second: bfloat16 [64, 8192], P('dp', 'tensor'), may hold values from -64 to 64
- cache_keys: bfloat16 [64, 32, 1024], P('dp', 'tensor'), may hold values from -512 to 512
- cache_values: bfloat16 [64, 32, 1024], P('dp', 'tensor'), may hold values from -6 to 6
- ancestors: int32 [64], replicated, may hold values from 0 to 63, as said below
- attn_gain: float32 [8192], P('tensor'), may hold values from 0.1 to 1.9
- ffn_gain: float32 [8192], P('tensor'), may hold values from 0.1 to 1.9
- w_query: bfloat16 [8192, 8192], P('tensor', 'dp'), may hold values from -0.0625 to 0.0625
- w_keyval: bfloat16 [8192, 2048], P('tensor', 'dp'), may hold values from -0.0625 to 0.0625
- w_out: bfloat16 [8192, 8192], P('dp', 'tensor'), may hold values from -0.5 to 0.5
- w_gate: bfloat16 [8192, 14336], P('tensor', 'dp'), may hold values from -0.0625 to 0.0625
- w_up: bfloat16 [8192, 14336], P('tensor', 'dp'), may hold values from -0.0625 to 0.0625
- w_down: bfloat16 [14336, 8192], P('dp', 'tensor'), may hold values from -0.046875 to 0.046875
Outputs:
- attn_update: bfloat16 [2, 64, 8192], P(None, 'dp', 'tensor')
- ffn_update: bfloat16 [2, 64, 8192], P(None, 'dp', 'tensor')
The draws below stay inside these ranges and needn't reach their ends.
Inputs may be any that keep to these rules, and one draw needn't show every extreme that they name: Particle p continues the cache of particle ancestors[p]. Among the 8 particles of one index of dp, at most 2 have ancestors in any one aligned block of 8 particles, and for every index of dp some block is named exactly 2 times.
All inputs are finite; a program needn't handle non-finite values.
Results may differ from the reference program's by a relative error of at most 0.04.
Values may be sent and summed in bfloat16 or wider, within the bound.
No kernel may reach another device: no remote copies, remote signals or barrier semaphores. Data moves between devices by JAX's collectives and lax.ppermute only.
A program may use at most 64 MiB of HBM per device.

```python
import math
import jax
import jax.numpy as jnp
from jax import lax

D = 8192
HEADS = 64
KVH = 8
HD = 128
GROUP = 8
FF = 14336
PART_DEV = 8
PARTICLES = 64
CTX = 32
CAP = 2
N_DP = 8


def residual_rows(key):
    first, second, third = jax.random.split(key, 3)
    row_scale = jnp.exp(jax.random.uniform(first, (PARTICLES, 1), minval=math.log(0.5), maxval=math.log(5.0)))
    column = jnp.arange(D, dtype=jnp.float32) / D
    column_scale = jnp.power(3.0, column)[None, :] * jnp.exp(jax.random.uniform(second, (1, D), minval=0.0, maxval=math.log(2.0))) * 0.5
    base = jnp.clip(jax.random.normal(third, (PARTICLES, D)), -4.0, 4.0)
    return base * row_scale * column_scale


def draw_x_first(key, part):
    return residual_rows(jax.random.fold_in(key, 11)).astype(jnp.bfloat16)


def draw_x_second(key, part):
    return residual_rows(jax.random.fold_in(key, 12)).astype(jnp.bfloat16)


def draw_cache_keys(key, part):
    first = jax.random.fold_in(jax.random.fold_in(key, 21), 0)
    shape = (PARTICLES, CTX, KVH * HD)
    base = jnp.clip(jax.random.normal(first, shape), -5.0, 5.0)
    return base.astype(jnp.bfloat16)


def draw_ancestors(key, part):
    first, second, third, fourth, fifth = jax.random.split(jax.random.fold_in(key, 31), 5)
    slot_count = N_DP * CAP
    forced = jax.random.randint(first, (N_DP, 1), 0, N_DP)
    orders = jax.vmap(lambda subkey: jax.random.permutation(subkey, slot_count))(jax.random.split(second, N_DP))
    owners = jnp.arange(slot_count, dtype=jnp.int32) // CAP
    scores = orders.astype(jnp.int32) + slot_count * (owners[None, :] == forced).astype(jnp.int32)
    ranked = jnp.argsort(scores, axis=1)
    picked = owners[ranked[:, :PART_DEV - 2]]
    sources = jnp.concatenate([forced, forced, picked], axis=1)
    shuffle = jax.vmap(lambda subkey: jax.random.permutation(subkey, PART_DEV))(jax.random.split(third, N_DP))
    sources = jnp.take_along_axis(sources, shuffle, axis=1)
    local_index = jnp.minimum(jax.random.randint(fourth, (N_DP, PART_DEV), 0, PART_DEV), jax.random.randint(fifth, (N_DP, PART_DEV), 0, PART_DEV))
    return (sources * PART_DEV + local_index).reshape(PARTICLES).astype(jnp.int32)


def levels(own_key, shape, shards, smallest, top_value):
    def one(dim, shards_of):
        draws = jax.random.uniform(jax.random.fold_in(jax.random.fold_in(own_key, 6), dim), (shards_of,), jnp.float32, smallest / len(shards), top_value / len(shards))
        return jnp.repeat(jnp.exp(draws), shape[dim] // shards_of).reshape((-1,) + (1,) * (len(shape) - dim - 1))

    factor_of = one(*shards[0])
    for cut in shards[1:]:
        factor_of = factor_of * one(*cut)
    return factor_of


def noise(stream_key, extent, width, reach, shards=(), held_as=jnp.bfloat16):
    loudness = levels(stream_key, extent, shards, -0.22, 0.18) if shards else 1.0
    values = jax.random.normal(stream_key, extent, jnp.float32) * width * loudness
    return jnp.minimum(jnp.maximum(values, -reach), reach).astype(held_as)


def setup_inputs(seed: int = 0) -> dict:
    key_list = jax.random.split(jax.random.key(seed), 14)
    x_first = draw_x_first(jax.random.fold_in(key_list[13], 71), 0)
    x_second = draw_x_second(jax.random.fold_in(key_list[13], 71), 0)
    cache_keys = draw_cache_keys(jax.random.fold_in(key_list[13], 71), 0)
    cache_values = noise(key_list[3], (PARTICLES, CTX, KVH * HD), 1.0, 6.0, ((0, 8), (1, 4)))
    ancestors = draw_ancestors(jax.random.fold_in(key_list[13], 71), 0)
    attn_gain = jnp.clip(1.0 + 0.18 * jax.random.normal(key_list[5], (D,), jnp.float32), 0.1, 1.9)
    ffn_gain = jnp.clip(1.0 + 0.18 * jax.random.normal(key_list[6], (D,), jnp.float32), 0.1, 1.9)
    w_query = noise(key_list[7], (D, HEADS * HD), D ** -0.5, 0.0625, ((0, 4), (1, 8)))
    w_keyval = noise(key_list[8], (D, 2 * KVH * HD), D ** -0.5, 0.0625, ((0, 4), (1, 8)))
    w_out = noise(key_list[9], (HEADS * HD, D), (HEADS * HD // 64) ** -0.5, 0.5, ((0, 8), (1, 4)))
    w_gate = noise(key_list[10], (D, FF), D ** -0.5, 0.0625, ((0, 4), (1, 8)))
    w_up = noise(key_list[11], (D, FF), D ** -0.5, 0.0625, ((0, 4), (1, 8)))
    w_down = noise(key_list[12], (FF, D), FF ** -0.5, 0.046875, ((0, 8), (1, 4)))
    return {"x_first": x_first, "x_second": x_second, "cache_keys": cache_keys, "cache_values": cache_values, "ancestors": ancestors, "attn_gain": attn_gain, "ffn_gain": ffn_gain, "w_query": w_query, "w_keyval": w_keyval, "w_out": w_out, "w_gate": w_gate, "w_up": w_up, "w_down": w_down}


EPS = 1e-05
ROPE_BASE = 500000.0

def rounded_sum(left, right):
    return jnp.dot(left, right, preferred_element_type=jnp.float32)

def normalize(residual_in, gain):
    wide = residual_in.astype(jnp.float32)
    mean_square = lax.optimization_barrier(jnp.mean(wide * wide, axis=1, keepdims=True))
    return (wide * lax.rsqrt(mean_square + EPS) * gain[None, :]).astype(jnp.bfloat16)

def rotate(tensor, position):
    half_width = tensor.shape[-1] // 2
    freq = jnp.power(jnp.float32(ROPE_BASE), -2.0 * jnp.arange(half_width, dtype=jnp.float32) / tensor.shape[-1])
    angle = jnp.float32(position) * freq
    cosine = jnp.cos(angle)
    sine = jnp.sin(angle)
    first_half = tensor[..., :half_width]
    second_half = tensor[..., half_width:]
    return jnp.concatenate([first_half * cosine - second_half * sine, second_half * cosine + first_half * sine], axis=-1)

def project(residual_in, gain, w_query, w_keyval, position):
    normed = normalize(residual_in, gain)
    queries = rounded_sum(normed, w_query).astype(jnp.bfloat16)
    keyvals = rounded_sum(normed, w_keyval).astype(jnp.bfloat16)
    count = residual_in.shape[0]
    queries = rotate(queries.astype(jnp.float32).reshape(count, KVH, GROUP, HD), position).astype(jnp.bfloat16)
    keyvals = keyvals.reshape(count, 2, KVH, HD)
    new_keys = rotate(keyvals[:, 0].astype(jnp.float32), position).astype(jnp.bfloat16)
    return (queries, new_keys, keyvals[:, 1])

def attend(queries, keys, values):
    scale = 1.0 / math.sqrt(HD)
    scores = jnp.einsum('kgd,lkd->kgl', queries.astype(jnp.float32), keys.astype(jnp.float32), precision=lax.Precision.HIGHEST) * scale
    highest = lax.optimization_barrier(jnp.max(scores, axis=-1, keepdims=True))
    weights = jnp.exp(scores - highest)
    totals = lax.optimization_barrier(jnp.sum(weights, axis=-1))
    mixed = jnp.einsum('kgl,lkd->kgd', weights, values.astype(jnp.float32), precision=lax.Precision.HIGHEST)
    return (mixed / totals[..., None]).reshape(-1).astype(jnp.bfloat16)

def attention_all(queries, cache_keys, cache_values, sources, extra_keys, extra_values):

    def one_particle(item):
        source_row, query_one, key_more, value_more = item
        keys = jnp.concatenate([cache_keys[source_row].reshape(CTX, KVH, HD), key_more], axis=0)
        values = jnp.concatenate([cache_values[source_row].reshape(CTX, KVH, HD), value_more], axis=0)
        return attend(query_one, keys, values)
    return lax.map(one_particle, (sources, queries, extra_keys, extra_values))

def updates(residual_in, mixed, ffn_gain, w_out, w_gate, w_up, w_down):
    attn_part = rounded_sum(mixed, w_out).astype(jnp.bfloat16)
    hidden_in = (residual_in.astype(jnp.float32) + attn_part.astype(jnp.float32)).astype(jnp.bfloat16)
    normed = normalize(hidden_in, ffn_gain)
    gate = rounded_sum(normed, w_gate)
    upward = rounded_sum(normed, w_up)
    hidden = (jax.nn.silu(gate) * upward).astype(jnp.bfloat16)
    ffn_part = rounded_sum(hidden, w_down).astype(jnp.bfloat16)
    return (attn_part, ffn_part)

def reference(x_first, x_second, cache_keys, cache_values, ancestors, attn_gain, ffn_gain, w_query, w_keyval, w_out, w_gate, w_up, w_down):
    count = x_first.shape[0]
    queries_one, keys_one, values_one = project(x_first, attn_gain, w_query, w_keyval, CTX)
    queries_two, keys_two, values_two = project(x_second, attn_gain, w_query, w_keyval, CTX + 1)
    own_rows = jnp.arange(count, dtype=jnp.int32)
    mixed_one = attention_all(queries_one, cache_keys, cache_values, own_rows, keys_one[:, None], values_one[:, None])
    ancestor_rows = ancestors.astype(jnp.int32)
    extra_keys = jnp.stack([jnp.take(keys_one, ancestor_rows, axis=0), keys_two], axis=1)
    extra_values = jnp.stack([jnp.take(values_one, ancestor_rows, axis=0), values_two], axis=1)
    mixed_two = attention_all(queries_two, cache_keys, cache_values, ancestor_rows, extra_keys, extra_values)
    attn_one, ffn_one = updates(x_first, mixed_one, ffn_gain, w_out, w_gate, w_up, w_down)
    attn_two, ffn_two = updates(x_second, mixed_two, ffn_gain, w_out, w_gate, w_up, w_down)
    return (jnp.stack([attn_one, attn_two]), jnp.stack([ffn_one, ffn_two]))
```

```python
import functools
import math

import jax
import jax.numpy as jnp
import numpy as np
from jax import lax
from jax.experimental import pallas as pl
from jax.experimental.pallas import tpu as pltpu
from jax.sharding import PartitionSpec as P

KVH = 8
HD = 128
EPS = 1e-05
ROPE_BASE = 500000.0
MASKED = -1e30
BF16 = jnp.bfloat16
F32 = jnp.float32


def swap(x, axis, bits):
    size = lax.axis_size(axis)
    return lax.ppermute(x, axis, [(i, i ^ bits) for i in range(size)])


def rope_tables(position):
    half = HD // 2
    freq = np.power(np.float32(ROPE_BASE), -2.0 * np.arange(half, dtype=np.float32) / HD)
    angle = (np.float32(position) * freq.astype(np.float32)).astype(np.float32)
    cosine, sine = np.cos(angle), np.sin(angle)
    return (
        np.concatenate([cosine, cosine]).astype(np.float32),
        np.concatenate([-sine, sine]).astype(np.float32),
    )


def gather_rows(rows):
    groups = lax.axis_size("dp")
    return jnp.stack([rows] + [swap(rows, "dp", k) for k in range(1, groups)])


def split_ss(x):
    high = x.astype(BF16)
    low = (x - high.astype(F32)).astype(BF16)
    return jnp.pad(jnp.stack([high, low], axis=-1), ((0, 0), (0, 126)))


def scale_of(summed, width):
    return lax.rsqrt((summed[..., 0] + summed[..., 1]) / width + EPS)[..., None]


def attention_kernel(
    sizes, own_ref, anc_ref, q_ref, scale_ref, kv_ref, nk_ref, nv_ref, target_ref, rope_ref, out_ref, keys_ref, values_ref
):
    parts, part_dev, heads, tensor, span = sizes
    ctx = tensor * span
    scale = 1.0 / math.sqrt(HD)
    queries = q_ref[...] * scale_ref[...]
    blocks = parts // part_dev
    rows = heads * parts
    pieces = []
    cos_key = jnp.concatenate([jnp.broadcast_to(rope_ref[2 * s : 2 * s + 1, :], (part_dev, HD)) for s in range(2)])
    sin_key = jnp.concatenate([jnp.broadcast_to(rope_ref[2 * s + 1 : 2 * s + 2, :], (part_dev, HD)) for s in range(2)])
    groups = nk_ref.shape[0] // (2 * part_dev)
    new_keys = nk_ref[...].astype(F32).reshape(groups, 2 * part_dev, HD)
    turned = pltpu.roll(nk_ref[...].astype(F32), HD // 2, 1).reshape(groups, 2 * part_dev, HD)
    new_keys = (new_keys * cos_key[None] + turned * sin_key[None]).reshape(-1, HD).astype(BF16)
    new_values = nv_ref[...]
    for step in range(2):
        source = own_ref if step == 0 else anc_ref

        def bring(i, _, source=source):
            particle = source[i]
            for t in range(tensor):
                both = kv_ref[t, particle].astype(F32)
                start = pl.multiple_of(i * ctx + t * span, 8)
                keys_ref[pl.ds(start, span), :] = both[:span]
                values_ref[pl.ds(start, span), :] = both[span:]
            return 0

        lax.fori_loop(0, parts, bring, 0)
        keys = keys_ref[...].astype(BF16)
        values = values_ref[...].astype(BF16)
        cosine = rope_ref[2 * step : 2 * step + 1, :]
        sine = rope_ref[2 * step + 1 : 2 * step + 2, :]
        per_head = []
        for h in range(heads):
            for b in range(blocks):
                first = b * 2 * part_dev + step * part_dev
                per_head.append(queries[first : first + part_dev, h * HD : (h + 1) * HD])
        query = jnp.concatenate(per_head, axis=0)
        query = query.astype(BF16).astype(F32)
        query = (query * cosine + pltpu.roll(query, HD // 2, 1) * sine).astype(BF16)
        contract = (((1,), (1,)), ((), ()))
        cached = lax.dot_general(query, keys, contract, preferred_element_type=F32) * scale
        fresh = lax.dot_general(query, new_keys, contract, preferred_element_type=F32) * scale
        row_part = lax.rem(lax.broadcasted_iota(jnp.int32, (rows, 1), 0), parts)
        col_part = lax.div(lax.broadcasted_iota(jnp.int32, (1, parts * ctx), 1), ctx)
        cached = jnp.where(row_part == col_part, cached, MASKED)
        col = lax.broadcasted_iota(jnp.int32, (1, new_keys.shape[0]), 1)
        wanted = col == target_ref[:, step : step + 1]
        if step == 1:
            wanted = wanted | (col == target_ref[:, 2:3])
        fresh = jnp.where(wanted, fresh, MASKED)
        highest = jnp.maximum(jnp.max(cached, axis=1, keepdims=True), jnp.max(fresh, axis=1, keepdims=True))
        cached = jnp.exp(cached - highest)
        fresh = jnp.exp(fresh - highest)
        total = jnp.sum(cached, axis=1, keepdims=True) + jnp.sum(fresh, axis=1, keepdims=True)
        mixed = jnp.dot(cached.astype(BF16), values, preferred_element_type=F32)
        mixed += jnp.dot(fresh.astype(BF16), new_values, preferred_element_type=F32)
        pieces.append(mixed / total)
    for h in range(heads):
        for b in range(blocks):
            first = h * parts + b * part_dev
            both = jnp.concatenate([piece[first : first + part_dev] for piece in pieces], axis=0)
            out_ref[b * 2 * part_dev : (b + 1) * 2 * part_dev, h * HD : (h + 1) * HD] = both.astype(BF16)


def attention(own, anc, q, scale, kv, nk, nv, targets, rope, part_dev):
    parts = own.shape[0]
    heads = q.shape[1] // HD
    tensor, _, span2, _ = kv.shape
    span = span2 // 2
    ctx = tensor * span
    smem = pl.BlockSpec(memory_space=pltpu.SMEM)
    vmem = pl.BlockSpec(memory_space=pltpu.VMEM)
    return pl.pallas_call(
        functools.partial(attention_kernel, (parts, part_dev, heads, tensor, span)),
        out_shape=jax.ShapeDtypeStruct((q.shape[0], q.shape[1]), BF16),
        in_specs=[smem, smem] + [vmem] * 7,
        out_specs=vmem,
        scratch_shapes=[pltpu.VMEM((parts * ctx, HD), F32), pltpu.VMEM((parts * ctx, HD), F32)],
        compiler_params=pltpu.CompilerParams(vmem_limit_bytes=40 << 20),
        cost_estimate=pl.CostEstimate(flops=100 << 20, bytes_accessed=2 << 20, transcendentals=1 << 18),
    )(own, anc, q, scale, kv, nk, nv, targets, rope)


def local(
    x_first,
    x_second,
    cache_keys,
    cache_values,
    ancestors,
    attn_gain,
    ffn_gain,
    w_query,
    w_keyval,
    w_out,
    w_gate,
    w_up,
    w_down,
):
    groups = lax.axis_size("dp")
    tensor = lax.axis_size("tensor")
    part_dev, features = x_first.shape
    span = cache_keys.shape[1]
    width = features * tensor
    context = span * tensor
    d = lax.axis_index("dp")
    t = lax.axis_index("tensor")
    pair = 2 * part_dev
    near = groups // tensor

    heads_of = np.arange(groups) * KVH // groups
    both = jnp.concatenate(
        [
            cache_keys.reshape(part_dev, span, KVH, HD),
            cache_values.reshape(part_dev, span, KVH, HD),
        ],
        axis=1,
    )
    sent = jnp.stack([both[:, :, h] for h in heads_of])
    cache = lax.all_to_all(sent, "dp", split_axis=0, concat_axis=0, tiled=True)
    cache = lax.all_gather(cache.reshape(groups * part_dev, 2 * span, HD), "tensor", axis=0)

    x = jnp.concatenate([x_first, x_second], axis=0)
    rows = gather_rows(x).reshape(groups * pair, features)
    wide = rows.astype(F32)
    squares = split_ss(jnp.sum(wide * wide, axis=1))
    lifted = (wide * attn_gain[None, :]).astype(BF16)
    kv_part = jnp.dot(lifted, w_keyval, preferred_element_type=F32).astype(BF16)
    kv_part = jnp.concatenate([kv_part, squares], axis=1)
    q_part = jnp.dot(lifted, w_query, preferred_element_type=F32).astype(BF16)
    q_part = q_part.reshape(tensor, near * pair, -1)
    kv_sum = kv_part.astype(F32)
    for k in range(1, tensor):
        kv_sum = kv_sum + swap(kv_part, "tensor", k).astype(F32)
    kv_cols = w_keyval.shape[1]
    scale = scale_of(kv_sum[:, kv_cols:], width)
    keyvals = (kv_sum[:, :kv_cols] * scale).astype(BF16).reshape(groups, pair, kv_cols)
    keyvals = jnp.take(keyvals, jnp.arange(groups) ^ d, axis=0).reshape(groups * pair, kv_cols)
    if groups == KVH:
        halves = (keyvals[:, :HD], keyvals[:, HD:])
        half = groups // 2
        lower = d < half
        one = lax.ppermute(
            jnp.where(lower, halves[0], halves[1]),
            "dp",
            [(i, 2 * i) for i in range(half)] + [(half + i, 2 * i + 1) for i in range(half)],
        )
        two = lax.ppermute(
            jnp.where(lower, halves[1], halves[0]),
            "dp",
            [(i, 2 * i + 1) for i in range(half)] + [(half + i, 2 * i) for i in range(half)],
        )
        even = d % 2 == 0
        new_keys = jnp.where(even, one, two)
        new_values = jnp.where(even, two, one)
    else:
        every = lax.all_gather(keyvals, "dp", axis=1, tiled=True)
        start = (d * KVH // groups) * HD
        new_keys = lax.dynamic_slice_in_dim(every, start, HD, axis=1)
        new_values = lax.dynamic_slice_in_dim(every, KVH * HD + start, HD, axis=1)

    queries = lax.dynamic_index_in_dim(q_part, t, 0, keepdims=False).astype(F32)
    for k in range(1, tensor):
        piece = lax.dynamic_index_in_dim(q_part, t ^ k, 0, keepdims=False)
        queries = queries + swap(piece, "tensor", k).astype(F32)
    own_scale = lax.dynamic_slice_in_dim(scale, t * near * pair, near * pair, axis=0)

    own_blocks = (t * near + jnp.arange(near)) ^ d
    own = (own_blocks[:, None] * part_dev + jnp.arange(part_dev)[None, :]).reshape(-1).astype(jnp.int32)
    anc = jnp.take(ancestors, own, axis=0)
    heads = w_query.shape[1] // HD

    def row_of(particle, step):
        return (particle // part_dev) * pair + step * part_dev + particle % part_dev

    targets = jnp.stack([row_of(own, 0), row_of(anc, 0), row_of(own, 1)], axis=1)
    targets = jnp.tile(targets, (heads, 1)).astype(jnp.int32)
    rope = jnp.asarray(np.stack(rope_tables(context) + rope_tables(context + 1)))
    mixed = attention(own, anc, queries, own_scale, cache, new_keys, new_values, targets, rope, part_dev)

    def gather_near(block, order):
        blocks = jnp.stack([block] + [swap(block, "tensor", k) for k in range(1, tensor)])
        return jnp.take(blocks.reshape(groups, pair, -1), order, axis=0).reshape(groups * pair, -1)

    def stacked(k):
        return ((k // near) ^ t) * near + k % near

    relative = jnp.arange(groups)
    spread = gather_near(mixed, stacked(relative ^ d))
    out_part = jnp.dot(spread, w_out, preferred_element_type=F32).astype(BF16)
    arrived = lax.all_to_all(out_part.reshape(groups, pair, -1), "dp", split_axis=0, concat_axis=0, tiled=True)
    attn_part = jnp.sum(arrived.astype(F32), axis=0).astype(BF16)
    residual = (x.astype(F32) + attn_part.astype(F32)).astype(BF16)

    rows = gather_rows(residual).reshape(groups * pair, features)
    wide = rows.astype(F32)
    squares = split_ss(jnp.sum(wide * wide, axis=1))
    lifted = (wide * ffn_gain[None, :]).astype(BF16)
    gate = jnp.dot(lifted, w_gate, preferred_element_type=F32).astype(BF16)
    up = jnp.dot(lifted, w_up, preferred_element_type=F32).astype(BF16)
    hidden_cols = w_gate.shape[1]
    part = jnp.concatenate([gate, up, squares], axis=1).reshape(tensor, near * pair, -1)
    summed = lax.dynamic_index_in_dim(part, t, 0, keepdims=False).astype(F32)
    for k in range(1, tensor):
        piece = lax.dynamic_index_in_dim(part, t ^ k, 0, keepdims=False)
        summed = summed + swap(piece, "tensor", k).astype(F32)
    scale = scale_of(summed[:, 2 * hidden_cols :], width)
    hidden = jax.nn.silu(summed[:, :hidden_cols] * scale) * (summed[:, hidden_cols : 2 * hidden_cols] * scale)
    spread = gather_near(hidden.astype(BF16), stacked(relative))
    down = jnp.dot(spread, w_down, preferred_element_type=F32).astype(BF16).reshape(groups, pair, -1)
    total = down[0].astype(F32)
    for k in range(1, groups):
        total = total + swap(down[k], "dp", k).astype(F32)
    ffn_part = total.astype(BF16)
    return (attn_part.reshape(2, part_dev, features), ffn_part.reshape(2, part_dev, features))


def solution(mesh):
    return jax.shard_map(
        local,
        mesh=mesh,
        in_specs=(
            P("dp", "tensor"),
            P("dp", "tensor"),
            P("dp", "tensor", None),
            P("dp", "tensor", None),
            P(),
            P("tensor"),
            P("tensor"),
            P("tensor", "dp"),
            P("tensor", "dp"),
            P("dp", "tensor"),
            P("tensor", "dp"),
            P("tensor", "dp"),
            P("dp", "tensor"),
        ),
        out_specs=(P(None, "dp", "tensor"), P(None, "dp", "tensor")),
        check_vma=False,
    )
```

```python
import functools
import math

import jax
import jax.numpy as jnp
import numpy as np
from jax import lax
from jax.experimental import pallas as pl
from jax.experimental.pallas import tpu as pltpu
from jax.sharding import PartitionSpec as P

KVH = 8
HD = 128
EPS = 1e-05
ROPE_BASE = 500000.0
MASKED = -1e30
BF16 = jnp.bfloat16
F32 = jnp.float32


def swap(x, axis, bits):
    size = lax.axis_size(axis)
    return lax.ppermute(x, axis, [(i, i ^ bits) for i in range(size)])


def rope_tables(position):
    half = HD // 2
    freq = np.power(np.float32(ROPE_BASE), -2.0 * np.arange(half, dtype=np.float32) / HD)
    angle = (np.float32(position) * freq.astype(np.float32)).astype(np.float32)
    cosine, sine = np.cos(angle), np.sin(angle)
    return (
        np.concatenate([cosine, cosine]).astype(np.float32),
        np.concatenate([-sine, sine]).astype(np.float32),
    )


def gather_rows(rows):
    groups = lax.axis_size("dp")
    blocks = {0: rows}
    for k in range(groups - 2, 0, -2):
        blocks[k] = swap(rows, "dp", k)
    blocks[1] = swap(rows, "dp", 1)
    for k in range(groups - 2, 0, -2):
        blocks[k + 1] = swap(blocks[k], "dp", 1)
    return jnp.stack([blocks[k] for k in range(groups)])


def sum_rows(parts):
    groups = lax.axis_size("dp")
    paired = {}
    for k in list(range(groups - 2, 0, -2)) + [0]:
        paired[k] = parts[k].astype(F32) + swap(parts[k + 1], "dp", 1).astype(F32)
    total = paired[0]
    for k in range(groups - 2, 0, -2):
        total = total + swap(paired[k].astype(BF16), "dp", k).astype(F32)
    return total


def sum_blocks(blocks):
    tensor = lax.axis_size("tensor")
    t = lax.axis_index("tensor")

    def take(bits):
        return jnp.concatenate([lax.dynamic_index_in_dim(blocks, t ^ k, 0, keepdims=True) for k in bits])

    even = range(0, tensor, 2)
    paired = take(even).astype(F32) + swap(take([k + 1 for k in even]), "tensor", 1).astype(F32)
    total = paired[0]
    for i in range(1, tensor // 2):
        total = total + swap(paired[i].astype(BF16), "tensor", 2 * i).astype(F32)
    return total


def gather_blocks(block):
    tensor = lax.axis_size("tensor")
    blocks = {0: block}
    for k in range(2, tensor, 2):
        blocks[k] = swap(block, "tensor", k)
    blocks[1] = swap(block, "tensor", 1)
    for k in range(2, tensor, 2):
        blocks[k + 1] = swap(blocks[k], "tensor", 1)
    return jnp.stack([blocks[k] for k in range(tensor)])


def split_ss(x):
    high = x.astype(BF16)
    low = (x - high.astype(F32)).astype(BF16)
    return jnp.pad(jnp.stack([high, low], axis=-1), ((0, 0), (0, 126)))


def scale_of(summed, width):
    return lax.rsqrt((summed[..., 0] + summed[..., 1]) / width + EPS)[..., None]


def pack_kernel(heads_of, keys_ref, values_ref, out_ref):
    for g, h in enumerate(heads_of):
        out_ref[g, 0] = keys_ref[:, :, h * HD : (h + 1) * HD]
        out_ref[g, 1] = values_ref[:, :, h * HD : (h + 1) * HD]


def pack(cache_keys, cache_values, heads_of):
    part_dev, span, _ = cache_keys.shape
    vmem = pl.BlockSpec(memory_space=pltpu.VMEM)
    return pl.pallas_call(
        functools.partial(pack_kernel, heads_of),
        out_shape=jax.ShapeDtypeStruct((len(heads_of), 2, part_dev, span, HD), BF16),
        in_specs=[vmem] * 2,
        out_specs=vmem,
        compiler_params=pltpu.CompilerParams(vmem_limit_bytes=8 << 20),
    )(cache_keys, cache_values)


def attention_kernel(
    sizes, own_ref, anc_ref, q_ref, scale_ref, kv_ref, nk_ref, nv_ref, target_ref, rope_ref, out_ref, keys_ref, values_ref
):
    parts, part_dev, heads, tensor, span = sizes
    ctx = tensor * span
    scale = 1.0 / math.sqrt(HD)
    queries = q_ref[...] * scale_ref[...]
    blocks = parts // part_dev
    rows = heads * parts
    pieces = []
    cos_key = jnp.concatenate([jnp.broadcast_to(rope_ref[2 * s : 2 * s + 1, :], (part_dev, HD)) for s in range(2)])
    sin_key = jnp.concatenate([jnp.broadcast_to(rope_ref[2 * s + 1 : 2 * s + 2, :], (part_dev, HD)) for s in range(2)])
    groups = nk_ref.shape[0] // (2 * part_dev)
    new_keys = nk_ref[...].astype(F32).reshape(groups, 2 * part_dev, HD)
    turned = pltpu.roll(nk_ref[...].astype(F32), HD // 2, 1).reshape(groups, 2 * part_dev, HD)
    new_keys = (new_keys * cos_key[None] + turned * sin_key[None]).reshape(-1, HD).astype(BF16)
    new_values = nv_ref[...]
    for step in range(2):
        source = own_ref if step == 0 else anc_ref

        def bring(i, _, source=source):
            particle = source[i]
            place = (particle // part_dev) * 2 * part_dev + particle % part_dev
            for t in range(tensor):
                start = pl.multiple_of(i * ctx + t * span, 8)
                keys_ref[pl.ds(start, span), :] = kv_ref[t, place].astype(F32)
                values_ref[pl.ds(start, span), :] = kv_ref[t, place + part_dev].astype(F32)
            return 0

        lax.fori_loop(0, parts, bring, 0)
        keys = keys_ref[...].astype(BF16)
        values = values_ref[...].astype(BF16)
        cosine = rope_ref[2 * step : 2 * step + 1, :]
        sine = rope_ref[2 * step + 1 : 2 * step + 2, :]
        per_head = []
        for h in range(heads):
            for b in range(blocks):
                first = b * 2 * part_dev + step * part_dev
                per_head.append(queries[first : first + part_dev, h * HD : (h + 1) * HD])
        query = jnp.concatenate(per_head, axis=0)
        query = query.astype(BF16).astype(F32)
        query = (query * cosine + pltpu.roll(query, HD // 2, 1) * sine).astype(BF16)
        contract = (((1,), (1,)), ((), ()))
        cached = lax.dot_general(query, keys, contract, preferred_element_type=F32) * scale
        fresh = lax.dot_general(query, new_keys, contract, preferred_element_type=F32) * scale
        row_part = lax.rem(lax.broadcasted_iota(jnp.int32, (rows, 1), 0), parts)
        col_part = lax.div(lax.broadcasted_iota(jnp.int32, (1, parts * ctx), 1), ctx)
        cached = jnp.where(row_part == col_part, cached, MASKED)
        col = lax.broadcasted_iota(jnp.int32, (1, new_keys.shape[0]), 1)
        wanted = col == target_ref[:, step : step + 1]
        if step == 1:
            wanted = wanted | (col == target_ref[:, 2:3])
        fresh = jnp.where(wanted, fresh, MASKED)
        highest = jnp.maximum(jnp.max(cached, axis=1, keepdims=True), jnp.max(fresh, axis=1, keepdims=True))
        cached = jnp.exp(cached - highest)
        fresh = jnp.exp(fresh - highest)
        total = jnp.sum(cached, axis=1, keepdims=True) + jnp.sum(fresh, axis=1, keepdims=True)
        mixed = jnp.dot(cached.astype(BF16), values, preferred_element_type=F32)
        mixed += jnp.dot(fresh.astype(BF16), new_values, preferred_element_type=F32)
        pieces.append(mixed / total)
    for h in range(heads):
        for b in range(blocks):
            first = h * parts + b * part_dev
            both = jnp.concatenate([piece[first : first + part_dev] for piece in pieces], axis=0)
            out_ref[b * 2 * part_dev : (b + 1) * 2 * part_dev, h * HD : (h + 1) * HD] = both.astype(BF16)


def attention(own, anc, q, scale, kv, nk, nv, targets, rope, part_dev):
    parts = own.shape[0]
    heads = q.shape[1] // HD
    tensor, _, span, _ = kv.shape
    ctx = tensor * span
    smem = pl.BlockSpec(memory_space=pltpu.SMEM)
    vmem = pl.BlockSpec(memory_space=pltpu.VMEM)
    limit = (8 << 20) + 2 * kv.size * 2 + 4 * (2 * heads * parts * parts * ctx)
    return pl.pallas_call(
        functools.partial(attention_kernel, (parts, part_dev, heads, tensor, span)),
        out_shape=jax.ShapeDtypeStruct((q.shape[0], q.shape[1]), BF16),
        in_specs=[smem, smem] + [vmem] * 7,
        out_specs=vmem,
        scratch_shapes=[pltpu.VMEM((parts * ctx, HD), F32), pltpu.VMEM((parts * ctx, HD), F32)],
        compiler_params=pltpu.CompilerParams(vmem_limit_bytes=limit),
        cost_estimate=pl.CostEstimate(flops=100 << 20, bytes_accessed=2 << 20, transcendentals=1 << 18),
    )(own, anc, q, scale, kv, nk, nv, targets, rope)


def local(
    x_first,
    x_second,
    cache_keys,
    cache_values,
    ancestors,
    attn_gain,
    ffn_gain,
    w_query,
    w_keyval,
    w_out,
    w_gate,
    w_up,
    w_down,
):
    groups = lax.axis_size("dp")
    tensor = lax.axis_size("tensor")
    part_dev, features = x_first.shape
    span = cache_keys.shape[1]
    width = features * tensor
    context = span * tensor
    d = lax.axis_index("dp")
    t = lax.axis_index("tensor")
    pair = 2 * part_dev
    near = groups // tensor

    sent = pack(cache_keys, cache_values, [g * KVH // groups for g in range(groups)])
    cache = lax.all_to_all(sent, "dp", split_axis=0, concat_axis=0, tiled=True)
    cache = lax.all_gather(cache.reshape(groups * pair, span, HD), "tensor", axis=0)

    x = jnp.concatenate([x_first, x_second], axis=0)
    rows = gather_rows(x).reshape(groups * pair, features)
    wide = rows.astype(F32)
    lifted = (wide * attn_gain[None, :]).astype(BF16)
    kv_part = jnp.dot(lifted, w_keyval, preferred_element_type=F32).astype(BF16)
    q_part = jnp.dot(lifted, w_query, preferred_element_type=F32).astype(BF16)
    q_part = q_part.reshape(tensor, near * pair, -1)
    squares = jnp.sum(wide * wide, axis=1)
    relative = jnp.arange(groups)
    squares = jnp.take(squares.reshape(groups, pair), relative ^ d, axis=0).reshape(-1)
    kv_cols = w_keyval.shape[1]
    keyvals = jnp.take(kv_part.reshape(groups, pair, kv_cols), relative ^ d, axis=0).reshape(groups * pair, kv_cols)
    if groups == KVH:
        halves = (keyvals[:, :HD], keyvals[:, HD:])
        half = groups // 2
        lower = d < half
        one = lax.ppermute(
            jnp.where(lower, halves[0], halves[1]),
            "dp",
            [(i, 2 * i) for i in range(half)] + [(half + i, 2 * i + 1) for i in range(half)],
        )
        two = lax.ppermute(
            jnp.where(lower, halves[1], halves[0]),
            "dp",
            [(i, 2 * i + 1) for i in range(half)] + [(half + i, 2 * i) for i in range(half)],
        )
        even = d % 2 == 0
        new_kv = jnp.concatenate([jnp.where(even, one, two), jnp.where(even, two, one)], axis=1)
    else:
        every = lax.all_gather(keyvals, "dp", axis=1, tiled=True)
        start = (d * KVH // groups) * HD
        new_kv = jnp.concatenate(
            [lax.dynamic_slice_in_dim(every, first + start, HD, axis=1) for first in (0, KVH * HD)], axis=1
        )
    new_kv = new_kv.astype(F32)
    bits = 1
    while bits < tensor:
        message = jnp.concatenate([new_kv.astype(BF16), split_ss(squares)], axis=1)
        arrived = swap(message, "tensor", bits).astype(F32)
        new_kv = new_kv + arrived[:, : 2 * HD]
        squares = squares + (arrived[:, 2 * HD] + arrived[:, 2 * HD + 1])
        bits *= 2
    scale = lax.rsqrt(squares / width + EPS)[:, None]
    new_kv = (new_kv * scale).astype(BF16)
    new_keys, new_values = new_kv[:, :HD], new_kv[:, HD:]
    queries = sum_blocks(q_part)
    scale = jnp.take(scale.reshape(groups, pair), relative ^ d, axis=0).reshape(groups * pair, 1)
    own_scale = lax.dynamic_slice_in_dim(scale, t * near * pair, near * pair, axis=0)

    own_blocks = (t * near + jnp.arange(near)) ^ d
    own = (own_blocks[:, None] * part_dev + jnp.arange(part_dev)[None, :]).reshape(-1).astype(jnp.int32)
    anc = jnp.take(ancestors, own, axis=0)
    heads = w_query.shape[1] // HD

    def row_of(particle, step):
        return (particle // part_dev) * pair + step * part_dev + particle % part_dev

    targets = jnp.stack([row_of(own, 0), row_of(anc, 0), row_of(own, 1)], axis=1)
    targets = jnp.tile(targets, (heads, 1)).astype(jnp.int32)
    rope = jnp.asarray(np.stack(rope_tables(context) + rope_tables(context + 1)))
    mixed = attention(own, anc, queries, own_scale, cache, new_keys, new_values, targets, rope, part_dev)

    stacked = ((relative // near) ^ t) * near + relative % near

    def spread(block):
        blocks = gather_blocks(block).reshape(groups, pair, -1)
        return jnp.take(blocks, stacked, axis=0).reshape(groups * pair, -1)

    out_part = jnp.dot(spread(mixed), w_out, preferred_element_type=F32).astype(BF16)
    attn_part = sum_rows(out_part.reshape(groups, pair, -1)).astype(BF16)
    residual = (x.astype(F32) + attn_part.astype(F32)).astype(BF16)

    rows = gather_rows(residual).reshape(groups * pair, features)
    wide = rows.astype(F32)
    squares = split_ss(jnp.sum(wide * wide, axis=1))
    lifted = (wide * ffn_gain[None, :]).astype(BF16)
    hidden_cols = w_gate.shape[1]
    gate = jnp.dot(lifted, w_gate, preferred_element_type=F32).astype(BF16)
    gate = sum_blocks(jnp.concatenate([gate, squares], axis=1).reshape(tensor, near * pair, -1))
    up = jnp.dot(lifted, w_up, preferred_element_type=F32).astype(BF16)
    up = sum_blocks(up.reshape(tensor, near * pair, -1))
    scale = scale_of(gate[:, hidden_cols:], width)
    hidden = jax.nn.silu(gate[:, :hidden_cols] * scale) * (up * scale)
    down = jnp.dot(spread(hidden.astype(BF16)), w_down, preferred_element_type=F32).astype(BF16)
    ffn_part = sum_rows(down.reshape(groups, pair, -1)).astype(BF16)
    return (attn_part.reshape(2, part_dev, features), ffn_part.reshape(2, part_dev, features))


def solution(mesh):
    return jax.shard_map(
        local,
        mesh=mesh,
        in_specs=(
            P("dp", "tensor"),
            P("dp", "tensor"),
            P("dp", "tensor", None),
            P("dp", "tensor", None),
            P(),
            P("tensor"),
            P("tensor"),
            P("tensor", "dp"),
            P("tensor", "dp"),
            P("dp", "tensor"),
            P("tensor", "dp"),
            P("tensor", "dp"),
            P("dp", "tensor"),
        ),
        out_specs=(P(None, "dp", "tensor"), P(None, "dp", "tensor")),
        check_vma=False,
    )
```

```python
import functools
import math

import jax
import jax.numpy as jnp
import numpy as np
from jax import lax
from jax.experimental import pallas as pl
from jax.experimental.pallas import tpu as pltpu
from jax.sharding import PartitionSpec as P

KVH = 8
HD = 128
EPS = 1e-05
ROPE_BASE = 500000.0
MASKED = -1e30
BF16 = jnp.bfloat16
F32 = jnp.float32


def swap(x, axis, bits):
    size = lax.axis_size(axis)
    return lax.ppermute(x, axis, [(i, i ^ bits) for i in range(size)])


def rope_tables(position):
    half = HD // 2
    freq = np.power(np.float32(ROPE_BASE), -2.0 * np.arange(half, dtype=np.float32) / HD)
    angle = (np.float32(position) * freq.astype(np.float32)).astype(np.float32)
    cosine, sine = np.cos(angle), np.sin(angle)
    return (
        np.concatenate([cosine, cosine]).astype(np.float32),
        np.concatenate([-sine, sine]).astype(np.float32),
    )


SMEM = pl.BlockSpec(memory_space=pltpu.SMEM)
VMEM = pl.BlockSpec(memory_space=pltpu.VMEM)
ANY = pl.BlockSpec(memory_space=pl.ANY)


def call(body, outs, ins, specs, scratch=(), limit=16 << 20, flops=0, moved=0):
    return pl.pallas_call(
        body,
        out_shape=outs,
        in_specs=specs,
        out_specs=jax.tree.map(lambda _: VMEM, outs),
        scratch_shapes=scratch,
        compiler_params=pltpu.CompilerParams(vmem_limit_bytes=limit),
        cost_estimate=pl.CostEstimate(flops=flops, bytes_accessed=moved, transcendentals=0),
    )(*ins)


def shaped(shape, dtype=BF16):
    return jax.ShapeDtypeStruct(shape, dtype)


def gather_rows(rows):
    groups = lax.axis_size("dp")
    blocks = {0: rows}
    for k in range(groups - 2, 0, -2):
        blocks[k] = swap(rows, "dp", k)
    blocks[1] = swap(rows, "dp", 1)
    for k in range(groups - 2, 0, -2):
        blocks[k + 1] = swap(blocks[k], "dp", 1)
    return [blocks[k] for k in range(groups)]


def gather_blocks(block):
    tensor = lax.axis_size("tensor")
    blocks = {0: block}
    for k in range(2, tensor, 2):
        blocks[k] = swap(block, "tensor", k)
    blocks[1] = swap(block, "tensor", 1)
    for k in range(2, tensor, 2):
        blocks[k + 1] = swap(blocks[k], "tensor", 1)
    return [blocks[k] for k in range(tensor)]


def sum_blocks(keep, send):
    tensor = lax.axis_size("tensor")
    rows = keep.shape[0] // (tensor // 2)
    paired = (keep + swap(send, "tensor", 1).astype(F32)).reshape(tensor // 2, rows, -1)
    return paired[0], [swap(paired[i].astype(BF16), "tensor", 2 * i) for i in range(1, tensor // 2)]


def slot(relative, size):
    return lax.shift_right_logical(relative, 1) + (relative & 1) * (size // 2)


def tiles(columns):
    for tile in (256, 384, 128):
        if columns % tile == 0:
            return tile
    return columns


def multiply(left_ref, w_ref, write):
    columns = w_ref.shape[1]
    tile = tiles(columns)
    left = left_ref[...]

    def turn(i, _):
        first = pl.multiple_of(i * tile, tile)
        write(first, tile, jnp.dot(left, w_ref[:, pl.ds(first, tile)], preferred_element_type=F32))
        return 0

    if tile == columns:
        write(0, tile, jnp.dot(left, w_ref[...], preferred_element_type=F32))
    else:
        lax.fori_loop(0, columns // tile, turn, 0)


def hold(w, after):
    pieces = 4 if w.shape[0] % 64 == 0 else 1
    rows = w.shape[0] // pieces

    def body(w_ref, after_ref, out_ref, sems):
        copies = [
            pltpu.make_async_copy(w_ref.at[pl.ds(i * rows, rows)], out_ref.at[pl.ds(i * rows, rows)], sems.at[i])
            for i in range(pieces)
        ]
        for copy in copies:
            copy.start()
        for copy in copies:
            copy.wait()

    return call(
        body, shaped(w.shape), (w, after), [ANY, ANY], [pltpu.SemaphoreType.DMA((pieces,))], moved=2 * w.size
    )


def stack_tokens(x_first, x_second):
    part_dev, features = x_first.shape

    def body(first_ref, second_ref, out_ref, one, two, sems):
        copies = [pltpu.make_async_copy(first_ref, one, sems.at[0]), pltpu.make_async_copy(second_ref, two, sems.at[1])]
        for copy in copies:
            copy.start()
        for copy in copies:
            copy.wait()
        out_ref[...] = jnp.concatenate([one[...].astype(F32), two[...].astype(F32)], axis=0).astype(BF16)

    return call(
        body,
        shaped((2 * part_dev, features)),
        (x_first, x_second),
        [ANY, ANY],
        [pltpu.VMEM(x_first.shape, BF16), pltpu.VMEM(x_first.shape, BF16), pltpu.SemaphoreType.DMA((2,))],
        moved=4 * x_first.size * 2,
    )


def pack(cache_keys, cache_values, where, after):
    groups = lax.axis_size("dp")
    part_dev, span, _ = cache_keys.shape
    shape = (groups // 2, 2, part_dev, span, HD)

    def body(where_ref, keys_hbm, values_hbm, after_ref, keep_ref, send_ref, keys_ref, values_ref, sems):
        copies = [
            pltpu.make_async_copy(keys_hbm, keys_ref, sems.at[0]),
            pltpu.make_async_copy(values_hbm, values_ref, sems.at[1]),
        ]
        for copy in copies:
            copy.start()
        for copy in copies:
            copy.wait()
        for k in range(groups):
            head = lax.div((where_ref[0] ^ k) * KVH, groups)
            lanes = pl.ds(pl.multiple_of(head * HD, HD), HD)
            out_ref = send_ref if k % 2 else keep_ref
            out_ref[k // 2, 0] = keys_ref[:, :, lanes]
            out_ref[k // 2, 1] = values_ref[:, :, lanes]

    return call(
        body,
        (shaped(shape), shaped(shape)),
        (where, cache_keys, cache_values, after),
        [SMEM, ANY, ANY, ANY],
        [pltpu.VMEM(cache_keys.shape, BF16), pltpu.VMEM(cache_keys.shape, BF16), pltpu.SemaphoreType.DMA((2,))],
        moved=8 * cache_keys.size,
    )


def move_cache(keep, send):
    groups = lax.axis_size("dp")
    tensor = lax.axis_size("tensor")
    both = jnp.stack([keep, swap(send, "dp", 1)], axis=1)
    both = jnp.concatenate([both[:1]] + [swap(both[i : i + 1], "dp", 2 * i) for i in range(1, groups // 2)])
    both = both.reshape(groups * both.shape[2] * both.shape[3], *both.shape[4:])
    return gather_blocks(both)


def lift(where_ref, gain_ref, block_refs, h_ref, ss_ref, absolute):
    groups = len(block_refs)
    tensor = lax.axis_size("tensor")
    pair = block_refs[0].shape[0]
    near = groups // tensor
    d, t = where_ref[0], where_ref[1]
    gain = gain_ref[...]
    places = []
    for k in range(groups):
        g = d ^ k
        place = slot(lax.div(g, near) ^ t, tensor) * near + lax.rem(g, near)
        place = pl.multiple_of(place * pair, pair)
        wide = block_refs[k][...].astype(F32)
        squares = jnp.broadcast_to(jnp.sum(wide * wide, axis=1, keepdims=True), (pair, 128))
        ss_ref[pl.ds(pl.multiple_of(g * pair, pair) if absolute else place, pair), :] = squares
        h_ref[pl.ds(place, pair), :] = (wide * gain).astype(BF16)
        places.append((pl.multiple_of(g * pair, pair), place))
    return places


def project_keyval(where, blocks, gain, w):
    pair, features = blocks[0].shape
    rows = len(blocks) * pair
    columns = w.shape[1]

    def body(where_ref, gain_ref, *refs):
        block_refs, (w_ref, h_ref, ss_ref, kv_ref, product) = refs[: len(blocks)], refs[len(blocks) :]
        places = lift(where_ref, gain_ref, block_refs, h_ref, ss_ref, True)
        product[...] = jnp.dot(h_ref[...], w_ref[...], preferred_element_type=F32)
        for to, place in places:
            kv_ref[pl.ds(to, pair), :] = product[pl.ds(place, pair), :].astype(BF16)

    return call(
        body,
        (shaped((rows, features)), shaped((rows, 128), F32), shaped((rows, columns))),
        (where, gain[None], *blocks, w),
        [SMEM] + [VMEM] * (2 + len(blocks)),
        [pltpu.VMEM((rows, columns), F32)],
        flops=2 * rows * w.size,
        moved=4 * rows * features + 2 * w.size,
    )


def project(h, w):
    half = h.shape[0] // 2

    def body(h_ref, w_ref, keep_ref, send_ref):
        def write(first, tile, product):
            keep_ref[:, pl.ds(first, tile)] = product[:half]
            send_ref[:, pl.ds(first, tile)] = product[half:].astype(BF16)

        multiply(h_ref, w_ref, write)

    columns = w.shape[1]
    return call(
        body,
        (shaped((half, columns), F32), shaped((half, columns))),
        (h, w),
        [VMEM] * 2,
        flops=4 * half * w.size,
        moved=2 * w.size,
    )


def project_gate(where, blocks, gain, w):
    pair, features = blocks[0].shape
    rows = len(blocks) * pair
    half = rows // 2
    columns = w.shape[1]

    def body(where_ref, gain_ref, *refs):
        block_refs, (w_ref, h_ref, keep_ref, send_ref, ss_ref) = refs[: len(blocks)], refs[len(blocks) :]
        lift(where_ref, gain_ref, block_refs, h_ref, ss_ref, False)

        def write(first, tile, product):
            keep_ref[:, pl.ds(first, tile)] = product[:half]
            send_ref[:, pl.ds(first, tile)] = product[half:].astype(BF16)

        multiply(h_ref, w_ref, write)
        squares = ss_ref[...]
        high = squares.astype(BF16).astype(F32)
        lane = lax.broadcasted_iota(jnp.int32, squares.shape, 1)
        ends = jnp.where(lane == 0, high, jnp.where(lane == 1, squares - high, 0.0))
        keep_ref[:, columns:] = ends[:half]
        send_ref[:, columns:] = ends[half:].astype(BF16)

    return call(
        body,
        (shaped((rows, features)), shaped((half, columns + 128), F32), shaped((half, columns + 128))),
        (where, gain[None], *blocks, w),
        [SMEM] + [VMEM] * (2 + len(blocks)),
        [pltpu.VMEM((rows, 128), F32)],
        flops=2 * rows * w.size,
        moved=4 * rows * features + 2 * w.size,
    )


def project_back(where, blocks, w):
    groups = lax.axis_size("dp")
    rows, depth = blocks[0].shape
    near = groups // len(blocks)
    pair = rows // near
    total = len(blocks) * rows
    half = total // 2
    columns = w.shape[1]

    def body(where_ref, *refs):
        block_refs, (w_ref, keep_ref, far_ref, close_ref, left) = refs[: len(blocks)], refs[len(blocks) :]
        d, t = where_ref[0], where_ref[1]
        for k, block_ref in enumerate(block_refs):
            for i in range(near):
                place = slot(((t ^ k) * near + i) ^ d, groups)
                left[pl.ds(pl.multiple_of(place * pair, pair), pair), :] = block_ref[i * pair : (i + 1) * pair, :]

        def write(first, tile, product):
            keep_ref[:, pl.ds(first, tile)] = product[:half]
            middle = half + half // 2
            close_ref[:, pl.ds(first, tile)] = product[half:middle].astype(BF16)
            far_ref[:, pl.ds(first, tile)] = product[middle:].astype(BF16)

        multiply(left, w_ref, write)

    return call(
        body,
        (shaped((half, columns), F32), shaped((half // 2, columns)), shaped((half // 2, columns))),
        (where, *blocks, w),
        [SMEM] + [VMEM] * (1 + len(blocks)),
        [pltpu.VMEM((total, depth), BF16)],
        flops=2 * total * w.size,
        moved=2 * w.size,
    )


def add_pairs(keep, arrived, first, pair, own):
    count = arrived.shape[0] // pair
    columns = keep.shape[1]

    def body(keep_ref, arrived_ref, *out_refs):
        for i, out_ref in enumerate(out_refs):
            start = (first + i) * pair
            summed = keep_ref[start : start + pair, :] + arrived_ref[i * pair : (i + 1) * pair, :].astype(F32)
            out_ref[...] = summed.astype(out_ref.dtype)

    outs = tuple(shaped((pair, columns), F32 if own and i == 0 else BF16) for i in range(count))
    return call(body, outs, (keep, arrived), [VMEM] * 2, moved=8 * arrived.size)


def sum_rows(keep, far, close, pair):
    groups = lax.axis_size("dp")
    far = swap(far, "dp", 1)
    close = swap(close, "dp", 1)
    quarter = groups // 4
    sums = add_pairs(keep, far, quarter, pair, False)
    arrived = [swap(sums[i], "dp", 2 * (quarter + i)) for i in range(quarter)]
    own = add_pairs(keep, close, 0, pair, True)
    arrived += [swap(own[i], "dp", 2 * i) for i in range(1, quarter)]
    return own[0], arrived


def finish(own, arrived, x=None):
    rows, columns = own.shape

    def body(own_ref, *refs):
        total = own_ref[...]
        for ref in refs[: len(arrived)]:
            total = total + ref[...].astype(F32)
        rounded = total.astype(BF16)
        if x is None:
            refs[-1][...] = rounded
        else:
            refs[-2][...] = rounded
            refs[-1][...] = (refs[len(arrived)][...].astype(F32) + rounded.astype(F32)).astype(BF16)

    outs = (shaped(own.shape),) * (1 if x is None else 2)
    ins = (own, *arrived) + (() if x is None else (x,))
    return call(body, outs, ins, [VMEM] * len(ins), moved=8 * own.size)


def attention_kernel(sizes, where_ref, anc_ref, rope_ref, target_ref, *refs):
    tensor, groups, part_dev, span, n_q, n_kv = sizes
    q_refs, kv_refs = refs[:n_q], refs[n_q : n_q + n_kv]
    cache_refs, (out_ref, keys_ref, values_ref, scale_ref) = refs[n_q + n_kv : n_q + n_kv + tensor], refs[n_q + n_kv + tensor :]
    d, t = where_ref[0], where_ref[1]
    near = groups // tensor
    parts = near * part_dev
    pair = 2 * part_dev
    ctx = tensor * span
    scale = 1.0 / math.sqrt(HD)
    summed = kv_refs[0][...].astype(F32)
    squares = summed[:, 2 * HD : 2 * HD + 1] + summed[:, 2 * HD + 1 : 2 * HD + 2]
    new_kv = summed[:, : 2 * HD]
    for ref in kv_refs[1:]:
        more = ref[...].astype(F32)
        squares = squares + (more[:, 2 * HD : 2 * HD + 1] + more[:, 2 * HD + 1 : 2 * HD + 2])
        new_kv = new_kv + more[:, : 2 * HD]
    width = rope_ref[4:5, 0:1]
    norm = lax.rsqrt(squares / width + EPS)
    scale_ref[...] = jnp.broadcast_to(norm, (groups * pair, 128))
    new_kv = (new_kv * norm).astype(BF16)
    new_values = new_kv[:, HD:]
    plain = new_kv[:, :HD].astype(F32)
    cos_key = jnp.concatenate([jnp.broadcast_to(rope_ref[2 * s : 2 * s + 1, :], (part_dev, HD)) for s in range(2)])
    sin_key = jnp.concatenate([jnp.broadcast_to(rope_ref[2 * s + 1 : 2 * s + 2, :], (part_dev, HD)) for s in range(2)])
    turned = pltpu.roll(plain, HD // 2, 1).reshape(groups, pair, HD)
    new_keys = plain.reshape(groups, pair, HD) * cos_key[None] + turned * sin_key[None]
    new_keys = new_keys.reshape(groups * pair, HD).astype(BF16)
    queries = q_refs[0][...]
    for ref in q_refs[1:]:
        queries = queries + ref[...].astype(F32)
    heads = queries.shape[1] // HD
    rows = heads * parts
    queries = queries * scale_ref[pl.ds(pl.multiple_of(t * near * pair, pair), near * pair), 0:1]
    pieces = []
    for step in range(2):

        def bring(i, _, step=step):
            if step == 0:
                block, member = (t * near + lax.div(i, part_dev)) ^ d, lax.rem(i, part_dev)
            else:
                block, member = lax.div(anc_ref[i], part_dev) ^ d, lax.rem(anc_ref[i], part_dev)
            place = block * pair + member
            for k in range(tensor):
                start = pl.multiple_of(i * ctx + k * span, 8)
                keys_ref[pl.ds(start, span), :] = cache_refs[k][place].astype(F32)
                values_ref[pl.ds(start, span), :] = cache_refs[k][place + part_dev].astype(F32)
            return 0

        lax.fori_loop(0, parts, bring, 0)
        keys = keys_ref[...].astype(BF16)
        values = values_ref[...].astype(BF16)
        cosine = rope_ref[2 * step : 2 * step + 1, :]
        sine = rope_ref[2 * step + 1 : 2 * step + 2, :]
        per_head = []
        for h in range(heads):
            for b in range(near):
                first = b * pair + step * part_dev
                per_head.append(queries[first : first + part_dev, h * HD : (h + 1) * HD])
        query = jnp.concatenate(per_head, axis=0)
        query = query.astype(BF16).astype(F32)
        query = (query * cosine + pltpu.roll(query, HD // 2, 1) * sine).astype(BF16)
        contract = (((1,), (1,)), ((), ()))
        cached = lax.dot_general(query, keys, contract, preferred_element_type=F32) * scale
        fresh = lax.dot_general(query, new_keys, contract, preferred_element_type=F32) * scale
        row_part = lax.rem(lax.broadcasted_iota(jnp.int32, (rows, 1), 0), parts)
        col_part = lax.div(lax.broadcasted_iota(jnp.int32, (1, parts * ctx), 1), ctx)
        cached = jnp.where(row_part == col_part, cached, MASKED)
        col = lax.broadcasted_iota(jnp.int32, (1, groups * pair), 1)
        wanted = col == target_ref[:, step : step + 1]
        if step == 1:
            wanted = wanted | (col == target_ref[:, 2:3])
        fresh = jnp.where(wanted, fresh, MASKED)
        highest = jnp.maximum(jnp.max(cached, axis=1, keepdims=True), jnp.max(fresh, axis=1, keepdims=True))
        cached = jnp.exp(cached - highest)
        fresh = jnp.exp(fresh - highest)
        total = jnp.sum(cached, axis=1, keepdims=True) + jnp.sum(fresh, axis=1, keepdims=True)
        mixed = jnp.dot(cached.astype(BF16), values, preferred_element_type=F32)
        mixed += jnp.dot(fresh.astype(BF16), new_values, preferred_element_type=F32)
        pieces.append(mixed / total)
    for h in range(heads):
        for b in range(near):
            first = h * parts + b * part_dev
            both = jnp.concatenate([piece[first : first + part_dev] for piece in pieces], axis=0)
            out_ref[b * pair : (b + 1) * pair, h * HD : (h + 1) * HD] = both.astype(BF16)


def attention(where, anc, rope, targets, queries, new_kv, cache, part_dev):
    tensor = lax.axis_size("tensor")
    groups = lax.axis_size("dp")
    span = cache[0].shape[1]
    rows, columns = queries[0].shape
    parts = rows // 2
    heads = columns // HD
    limit = (16 << 20) + 4 * (3 * heads * parts * parts * tensor * span)
    ins = (where, anc, rope, targets, *queries, *new_kv, *cache)
    return call(
        functools.partial(attention_kernel, (tensor, groups, part_dev, span, len(queries), len(new_kv))),
        shaped((rows, columns)),
        ins,
        [SMEM] * 2 + [VMEM] * (len(ins) - 2),
        [
            pltpu.VMEM((parts * tensor * span, HD), F32),
            pltpu.VMEM((parts * tensor * span, HD), F32),
            pltpu.VMEM((groups * 2 * part_dev, 128), F32),
        ],
        limit=limit,
        flops=1 << 30,
        moved=4 << 20,
    )


def split_ss(x):
    high = x.astype(BF16)
    low = (x - high.astype(F32)).astype(BF16)
    return jnp.pad(jnp.stack([high, low], axis=-1), ((0, 0), (0, 126)))


def move_keyvals(kv):
    groups = lax.axis_size("dp")
    d = lax.axis_index("dp")
    if groups == KVH:
        halves = (kv[:, :HD], kv[:, HD:])
        half = groups // 2
        lower = d < half
        one = lax.ppermute(
            jnp.where(lower, halves[0], halves[1]),
            "dp",
            [(i, 2 * i) for i in range(half)] + [(half + i, 2 * i + 1) for i in range(half)],
        )
        two = lax.ppermute(
            jnp.where(lower, halves[1], halves[0]),
            "dp",
            [(i, 2 * i + 1) for i in range(half)] + [(half + i, 2 * i) for i in range(half)],
        )
        even = d % 2 == 0
        return jnp.concatenate([jnp.where(even, one, two), jnp.where(even, two, one)], axis=1)
    every = lax.all_gather(kv, "dp", axis=1, tiled=True)
    start = (d * KVH // groups) * HD
    return jnp.concatenate(
        [lax.dynamic_slice_in_dim(every, first + start, HD, axis=1) for first in (0, KVH * HD)], axis=1
    )


def local(
    x_first,
    x_second,
    cache_keys,
    cache_values,
    ancestors,
    attn_gain,
    ffn_gain,
    w_query,
    w_keyval,
    w_out,
    w_gate,
    w_up,
    w_down,
):
    groups = lax.axis_size("dp")
    tensor = lax.axis_size("tensor")
    part_dev, features = x_first.shape
    span = cache_keys.shape[1]
    width = features * tensor
    context = span * tensor
    d = lax.axis_index("dp")
    t = lax.axis_index("tensor")
    pair = 2 * part_dev
    near = groups // tensor
    parts = near * part_dev
    where = jnp.stack([d, t]).astype(jnp.int32)

    x = stack_tokens(x_first, x_second)
    blocks = gather_rows(x)
    held_keyval = hold(w_keyval, x)
    held_query = hold(w_query, x)
    cache = move_cache(*pack(cache_keys, cache_values, where, x))

    h, squares, keyvals = project_keyval(where, blocks, attn_gain, held_keyval)
    new_kv = move_keyvals(keyvals)
    queries, queries_arrived = sum_blocks(*project(h, held_query))
    held_out = hold(w_out, h)
    message = jnp.concatenate([new_kv, split_ss(squares[:, 0])], axis=1)
    bits = 1
    while bits < tensor:
        arrived = swap(message, "tensor", bits)
        bits *= 2
        if bits == tensor:
            break
        summed = message.astype(F32) + arrived.astype(F32)
        squares = summed[:, 2 * HD] + summed[:, 2 * HD + 1]
        message = jnp.concatenate([summed[:, : 2 * HD].astype(BF16), split_ss(squares)], axis=1)

    own = t * parts + jnp.arange(parts, dtype=jnp.int32)
    anc = lax.dynamic_slice_in_dim(ancestors, t * parts, parts).astype(jnp.int32)
    heads = w_query.shape[1] // HD

    def row_of(particle, step):
        return (particle // part_dev) * pair + step * part_dev + particle % part_dev

    targets = jnp.stack([row_of(own, 0), row_of(anc, 0), row_of(own, 1)], axis=1)
    targets = jnp.tile(targets, (heads, 1)).astype(jnp.int32)
    rope = rope_tables(context) + rope_tables(context + 1)
    rope = jnp.asarray(np.stack(rope + (np.full(HD, width, np.float32),) * 4))
    mixed = attention(where, anc, rope, targets, [queries] + queries_arrived, [message, arrived], cache, part_dev)

    keep, far, close = project_back(where, gather_blocks(mixed), held_out)
    held_gate = hold(w_gate, far)
    held_up = hold(w_up, far)
    attn_part, residual = finish(*sum_rows(keep, far, close, pair), x)

    hidden_cols = w_gate.shape[1]
    h, keep, send = project_gate(where, gather_rows(residual), ffn_gain, held_gate)
    gate, gate_arrived = sum_blocks(keep, send)
    up, up_arrived = sum_blocks(*project(h, held_up))
    held_down = hold(w_down, h)
    for piece in gate_arrived:
        gate = gate + piece.astype(F32)
    for piece in up_arrived:
        up = up + piece.astype(F32)
    scale = lax.rsqrt((gate[:, hidden_cols] + gate[:, hidden_cols + 1]) / width + EPS)[:, None]
    hidden = jax.nn.silu(gate[:, :hidden_cols] * scale) * (up * scale)
    keep, far, close = project_back(where, gather_blocks(hidden.astype(BF16)), held_down)
    (ffn_part,) = finish(*sum_rows(keep, far, close, pair))
    return (attn_part.reshape(2, part_dev, features), ffn_part.reshape(2, part_dev, features))


def solution(mesh):
    return jax.shard_map(
        local,
        mesh=mesh,
        in_specs=(
            P("dp", "tensor"),
            P("dp", "tensor"),
            P("dp", "tensor", None),
            P("dp", "tensor", None),
            P(),
            P("tensor"),
            P("tensor"),
            P("tensor", "dp"),
            P("tensor", "dp"),
            P("dp", "tensor"),
            P("tensor", "dp"),
            P("tensor", "dp"),
            P("dp", "tensor"),
        ),
        out_specs=(P(None, "dp", "tensor"), P(None, "dp", "tensor")),
        check_vma=False,
    )
```

```python
import functools
import math

import jax
import jax.numpy as jnp
import numpy as np
from jax import lax
from jax.experimental import pallas as pl
from jax.experimental.pallas import tpu as pltpu
from jax.sharding import PartitionSpec as P

KVH = 8
HD = 128
EPS = 1e-05
ROPE_BASE = 500000.0
MASKED = -1e30
BF16 = jnp.bfloat16
F32 = jnp.float32


def swap(x, axis, bits):
    size = lax.axis_size(axis)
    return lax.ppermute(x, axis, [(i, i ^ bits) for i in range(size)])


def rope_tables(position):
    half = HD // 2
    freq = np.power(np.float32(ROPE_BASE), -2.0 * np.arange(half, dtype=np.float32) / HD)
    angle = (np.float32(position) * freq.astype(np.float32)).astype(np.float32)
    cosine, sine = np.cos(angle), np.sin(angle)
    return (
        np.concatenate([cosine, cosine]).astype(np.float32),
        np.concatenate([-sine, sine]).astype(np.float32),
    )


SMEM = pl.BlockSpec(memory_space=pltpu.SMEM)
VMEM = pl.BlockSpec(memory_space=pltpu.VMEM)
ANY = pl.BlockSpec(memory_space=pl.ANY)
HBM = pl.BlockSpec(memory_space=pltpu.HBM)


def call(body, outs, ins, specs, scratch=(), limit=16 << 20, flops=0, moved=0):
    return pl.pallas_call(
        body,
        out_shape=outs,
        in_specs=specs,
        out_specs=jax.tree.map(lambda _: VMEM, outs),
        scratch_shapes=scratch,
        compiler_params=pltpu.CompilerParams(vmem_limit_bytes=limit),
        cost_estimate=pl.CostEstimate(flops=flops, bytes_accessed=moved, transcendentals=0),
    )(*ins)


def shaped(shape, dtype=BF16):
    return jax.ShapeDtypeStruct(shape, dtype)


def gather_rows(rows):
    groups = lax.axis_size("dp")
    blocks = {0: rows}
    for k in range(groups - 2, 0, -2):
        blocks[k] = swap(rows, "dp", k)
    blocks[1] = swap(rows, "dp", 1)
    for k in range(groups - 2, 0, -2):
        blocks[k + 1] = swap(blocks[k], "dp", 1)
    return [blocks[k] for k in range(groups)]


def gather_blocks(block):
    tensor = lax.axis_size("tensor")
    blocks = {0: block}
    for k in range(2, tensor, 2):
        blocks[k] = swap(block, "tensor", k)
    blocks[1] = swap(block, "tensor", 1)
    for k in range(2, tensor, 2):
        blocks[k + 1] = swap(blocks[k], "tensor", 1)
    return [blocks[k] for k in range(tensor)]


def sum_blocks(keep, send):
    tensor = lax.axis_size("tensor")
    rows = keep.shape[0] // (tensor // 2)
    paired = (keep + swap(send, "tensor", 1).astype(F32)).reshape(tensor // 2, rows, -1)
    return paired[0], [swap(paired[i].astype(BF16), "tensor", 2 * i) for i in range(1, tensor // 2)]


def slot(relative, size):
    return lax.shift_right_logical(relative, 1) + (relative & 1) * (size // 2)


def tiles(columns):
    for tile in (256, 384, 128):
        if columns % tile == 0:
            return tile
    return columns


def multiply(left, w_ref, write):
    columns = w_ref.shape[1]
    tile = tiles(columns)
    for first in range(0, columns, tile):
        write(first, tile, jnp.dot(left, w_ref[:, first : first + tile], preferred_element_type=F32))


def streamed(w_hbm, w_ref, sems):
    columns = w_ref.shape[1]
    tile = tiles(columns)
    copies = [
        pltpu.make_async_copy(w_hbm.at[:, pl.ds(first, tile)], w_ref.at[:, pl.ds(first, tile)], sems.at[i])
        for i, first in enumerate(range(0, columns, tile))
    ]
    for copy in copies:
        copy.start()

    def run(left, write):
        for i, first in enumerate(range(0, columns, tile)):
            copies[i].wait()
            write(first, tile, jnp.dot(left, w_ref[:, first : first + tile], preferred_element_type=F32))

    return run


def stream_scratch(w):
    return [pltpu.VMEM(w.shape, BF16), pltpu.SemaphoreType.DMA((w.shape[1] // tiles(w.shape[1]),))]


def stack_tokens(x_first, x_second):
    part_dev, features = x_first.shape

    def body(first_ref, second_ref, out_ref, one, two, sems):
        copies = [pltpu.make_async_copy(first_ref, one, sems.at[0]), pltpu.make_async_copy(second_ref, two, sems.at[1])]
        for copy in copies:
            copy.start()
        for copy in copies:
            copy.wait()
        out_ref[...] = jnp.concatenate([one[...].astype(F32), two[...].astype(F32)], axis=0).astype(BF16)

    return call(
        body,
        shaped((2 * part_dev, features)),
        (x_first, x_second),
        [HBM, HBM],
        [pltpu.VMEM(x_first.shape, BF16), pltpu.VMEM(x_first.shape, BF16), pltpu.SemaphoreType.DMA((2,))],
        moved=4 * x_first.size * 2,
    )


def pack(cache_keys, cache_values, after):
    groups = lax.axis_size("dp")
    part_dev, span, _ = cache_keys.shape

    def body(keys_hbm, values_hbm, after_ref, out_ref, keys_ref, values_ref, sems):
        copies = [
            pltpu.make_async_copy(keys_hbm, keys_ref, sems.at[0]),
            pltpu.make_async_copy(values_hbm, values_ref, sems.at[1]),
        ]
        for copy in copies:
            copy.start()
        for copy in copies:
            copy.wait()
        for g in range(groups):
            first = g * KVH // groups * HD
            out_ref[g, 0] = keys_ref[:, :, first : first + HD]
            out_ref[g, 1] = values_ref[:, :, first : first + HD]

    return call(
        body,
        shaped((groups, 2, part_dev, span, HD)),
        (cache_keys, cache_values, after),
        [HBM, HBM, ANY],
        [pltpu.VMEM(cache_keys.shape, BF16), pltpu.VMEM(cache_keys.shape, BF16), pltpu.SemaphoreType.DMA((2,))],
        moved=8 * cache_keys.size,
    )


def lift(where_ref, gain_ref, block_refs, h_ref, ss_ref, absolute):
    groups = len(block_refs)
    tensor = lax.axis_size("tensor")
    pair = block_refs[0].shape[0]
    near = groups // tensor
    d, t = where_ref[0], where_ref[1]
    gain = gain_ref[...]
    places = []
    for k in range(groups):
        g = d ^ k
        place = slot(lax.div(g, near) ^ t, tensor) * near + lax.rem(g, near)
        place = pl.multiple_of(place * pair, pair)
        wide = block_refs[k][...].astype(F32)
        squares = jnp.broadcast_to(jnp.sum(wide * wide, axis=1, keepdims=True), (pair, 128))
        ss_ref[pl.ds(pl.multiple_of(g * pair, pair) if absolute else place, pair), :] = squares
        h_ref[pl.ds(place, pair), :] = (wide * gain).astype(BF16)
        places.append((pl.multiple_of(g * pair, pair), place))
    return places


def project_keyval(where, blocks, gain, w):
    pair, features = blocks[0].shape
    rows = len(blocks) * pair
    columns = w.shape[1]

    def body(where_ref, gain_ref, *refs):
        block_refs, (w_ref, h_ref, ss_ref, kv_ref, product) = refs[: len(blocks)], refs[len(blocks) :]
        places = lift(where_ref, gain_ref, block_refs, h_ref, ss_ref, True)
        product[...] = jnp.dot(h_ref[...], w_ref[...], preferred_element_type=F32)
        for to, place in places:
            kv_ref[pl.ds(to, pair), :] = product[pl.ds(place, pair), :].astype(BF16)

    return call(
        body,
        (shaped((rows, features)), shaped((rows, 128), F32), shaped((rows, columns))),
        (where, gain[None], *blocks, w),
        [SMEM] + [VMEM] * (2 + len(blocks)),
        [pltpu.VMEM((rows, columns), F32)],
        flops=2 * rows * w.size,
        moved=4 * rows * features + 2 * w.size,
    )


def project(h, w, after=None):
    half = h.shape[0] // 2

    def body(h_ref, w_ref, *refs):
        run = None if after is None else streamed(w_ref, refs[-2], refs[-1])
        keep_ref, send_ref = refs[:2] if after is None else refs[1:3]
        left = h_ref[...]

        def write(first, tile, product):
            keep_ref[:, first : first + tile] = product[:half]
            send_ref[:, first : first + tile] = product[half:].astype(BF16)

        if run is None:
            multiply(left, w_ref, write)
        else:
            run(left, write)

    columns = w.shape[1]
    return call(
        body,
        (shaped((half, columns), F32), shaped((half, columns))),
        (h, w) if after is None else (h, w, after),
        [VMEM] * 2 if after is None else [VMEM, HBM, ANY],
        () if after is None else stream_scratch(w),
        flops=4 * half * w.size,
        moved=2 * w.size,
    )


def project_gate(where, blocks, gain, w):
    pair, features = blocks[0].shape
    rows = len(blocks) * pair
    half = rows // 2
    columns = w.shape[1]

    def body(where_ref, gain_ref, *refs):
        block_refs, (w_ref, h_ref, keep_ref, send_ref, ss_ref) = refs[: len(blocks)], refs[len(blocks) :]
        lift(where_ref, gain_ref, block_refs, h_ref, ss_ref, False)

        def write(first, tile, product):
            keep_ref[:, first : first + tile] = product[:half]
            send_ref[:, first : first + tile] = product[half:].astype(BF16)

        multiply(h_ref[...], w_ref, write)
        squares = ss_ref[...]
        high = squares.astype(BF16).astype(F32)
        lane = lax.broadcasted_iota(jnp.int32, squares.shape, 1)
        ends = jnp.where(lane == 0, high, jnp.where(lane == 1, squares - high, 0.0))
        keep_ref[:, columns:] = ends[:half]
        send_ref[:, columns:] = ends[half:].astype(BF16)

    return call(
        body,
        (shaped((rows, features)), shaped((half, columns + 128), F32), shaped((half, columns + 128))),
        (where, gain[None], *blocks, w),
        [SMEM] + [VMEM] * (2 + len(blocks)),
        [pltpu.VMEM((rows, 128), F32)],
        flops=2 * rows * w.size,
        moved=4 * rows * features + 2 * w.size,
    )


def project_back(where, blocks, w, stream):
    groups = lax.axis_size("dp")
    rows, depth = blocks[0].shape
    near = groups // len(blocks)
    pair = rows // near
    total = len(blocks) * rows
    half = total // 2
    columns = w.shape[1]

    def body(where_ref, *refs):
        block_refs, (w_ref, keep_ref, far_ref, close_ref, left) = refs[: len(blocks)], refs[len(blocks) :][:5]
        run = streamed(w_ref, refs[-2], refs[-1]) if stream else None
        d, t = where_ref[0], where_ref[1]
        for k, block_ref in enumerate(block_refs):
            for i in range(near):
                place = slot(((t ^ k) * near + i) ^ d, groups)
                left[pl.ds(pl.multiple_of(place * pair, pair), pair), :] = block_ref[i * pair : (i + 1) * pair, :]

        def write(first, tile, product):
            keep_ref[:, first : first + tile] = product[:half]
            middle = half + half // 2
            close_ref[:, first : first + tile] = product[half:middle].astype(BF16)
            far_ref[:, first : first + tile] = product[middle:].astype(BF16)

        if stream:
            run(left[...], write)
        else:
            multiply(left[...], w_ref, write)

    return call(
        body,
        (shaped((half, columns), F32), shaped((half // 2, columns)), shaped((half // 2, columns))),
        (where, *blocks, w),
        [SMEM] + [VMEM] * len(blocks) + [HBM if stream else VMEM],
        [pltpu.VMEM((total, depth), BF16)] + (stream_scratch(w) if stream else []),
        flops=2 * total * w.size,
        moved=2 * w.size,
    )


def add_pairs(keep, arrived, first, pair, own):
    count = arrived.shape[0] // pair
    columns = keep.shape[1]

    def body(keep_ref, arrived_ref, *out_refs):
        for i, out_ref in enumerate(out_refs):
            start = (first + i) * pair
            summed = keep_ref[start : start + pair, :] + arrived_ref[i * pair : (i + 1) * pair, :].astype(F32)
            out_ref[...] = summed.astype(out_ref.dtype)

    outs = tuple(shaped((pair, columns), F32 if own and i == 0 else BF16) for i in range(count))
    return call(body, outs, (keep, arrived), [VMEM] * 2, moved=8 * arrived.size)


def sum_rows(keep, far, close, pair):
    groups = lax.axis_size("dp")
    far = swap(far, "dp", 1)
    close = swap(close, "dp", 1)
    quarter = groups // 4
    sums = add_pairs(keep, far, quarter, pair, False)
    arrived = [swap(sums[i], "dp", 2 * (quarter + i)) for i in range(quarter)]
    own = add_pairs(keep, close, 0, pair, True)
    arrived += [swap(own[i], "dp", 2 * i) for i in range(1, quarter)]
    return own[0], arrived


def finish(own, arrived, x=None):
    rows, columns = own.shape

    def body(own_ref, *refs):
        total = own_ref[...]
        for ref in refs[: len(arrived)]:
            total = total + ref[...].astype(F32)
        rounded = total.astype(BF16)
        if x is None:
            refs[-1][...] = rounded
        else:
            refs[-2][...] = rounded
            refs[-1][...] = (refs[len(arrived)][...].astype(F32) + rounded.astype(F32)).astype(BF16)

    outs = (shaped(own.shape),) * (1 if x is None else 2)
    ins = (own, *arrived) + (() if x is None else (x,))
    return call(body, outs, ins, [VMEM] * len(ins), moved=8 * own.size)


def attention_kernel(sizes, where_ref, anc_ref, rope_ref, target_ref, *refs):
    tensor, groups, part_dev, span, n_q, n_kv = sizes
    q_refs, kv_refs = refs[:n_q], refs[n_q : n_q + n_kv]
    cache_refs, (out_ref, keys_ref, values_ref, scale_ref) = refs[n_q + n_kv : n_q + n_kv + tensor], refs[n_q + n_kv + tensor :]
    t = where_ref[1]
    near = groups // tensor
    parts = near * part_dev
    pair = 2 * part_dev
    ctx = tensor * span
    scale = 1.0 / math.sqrt(HD)
    summed = kv_refs[0][...].astype(F32)
    squares = summed[:, 2 * HD : 2 * HD + 1] + summed[:, 2 * HD + 1 : 2 * HD + 2]
    new_kv = summed[:, : 2 * HD]
    for ref in kv_refs[1:]:
        more = ref[...].astype(F32)
        squares = squares + (more[:, 2 * HD : 2 * HD + 1] + more[:, 2 * HD + 1 : 2 * HD + 2])
        new_kv = new_kv + more[:, : 2 * HD]
    width = rope_ref[4:5, 0:1]
    norm = lax.rsqrt(squares / width + EPS)
    scale_ref[...] = jnp.broadcast_to(norm, (groups * pair, 128))
    new_kv = (new_kv * norm).astype(BF16)
    new_values = new_kv[:, HD:]
    plain = new_kv[:, :HD].astype(F32)
    cos_key = jnp.concatenate([jnp.broadcast_to(rope_ref[2 * s : 2 * s + 1, :], (part_dev, HD)) for s in range(2)])
    sin_key = jnp.concatenate([jnp.broadcast_to(rope_ref[2 * s + 1 : 2 * s + 2, :], (part_dev, HD)) for s in range(2)])
    turned = pltpu.roll(plain, HD // 2, 1).reshape(groups, pair, HD)
    new_keys = plain.reshape(groups, pair, HD) * cos_key[None] + turned * sin_key[None]
    new_keys = new_keys.reshape(groups * pair, HD).astype(BF16)
    queries = q_refs[0][...]
    for ref in q_refs[1:]:
        queries = queries + ref[...].astype(F32)
    heads = queries.shape[1] // HD
    rows = heads * parts
    queries = queries * scale_ref[pl.ds(pl.multiple_of(t * near * pair, pair), near * pair), 0:1]
    pieces = []
    for step in range(2):

        def bring(i, _, step=step):
            if step == 0:
                block, member = t * near + lax.div(i, part_dev), lax.rem(i, part_dev)
            else:
                block, member = lax.div(anc_ref[i], part_dev), lax.rem(anc_ref[i], part_dev)
            place = block * pair + member
            for k in range(tensor):
                start = pl.multiple_of(i * ctx + k * span, 8)
                keys_ref[pl.ds(start, span), :] = cache_refs[k][place].astype(F32)
                values_ref[pl.ds(start, span), :] = cache_refs[k][place + part_dev].astype(F32)
            return 0

        lax.fori_loop(0, parts, bring, 0)
        keys = keys_ref[...].astype(BF16)
        values = values_ref[...].astype(BF16)
        cosine = rope_ref[2 * step : 2 * step + 1, :]
        sine = rope_ref[2 * step + 1 : 2 * step + 2, :]
        per_head = []
        for h in range(heads):
            for b in range(near):
                first = b * pair + step * part_dev
                per_head.append(queries[first : first + part_dev, h * HD : (h + 1) * HD])
        query = jnp.concatenate(per_head, axis=0)
        query = query.astype(BF16).astype(F32)
        query = (query * cosine + pltpu.roll(query, HD // 2, 1) * sine).astype(BF16)
        contract = (((1,), (1,)), ((), ()))
        cached = lax.dot_general(query, keys, contract, preferred_element_type=F32) * scale
        fresh = lax.dot_general(query, new_keys, contract, preferred_element_type=F32) * scale
        row_part = lax.rem(lax.broadcasted_iota(jnp.int32, (rows, 1), 0), parts)
        col_part = lax.div(lax.broadcasted_iota(jnp.int32, (1, parts * ctx), 1), ctx)
        cached = jnp.where(row_part == col_part, cached, MASKED)
        col = lax.broadcasted_iota(jnp.int32, (1, groups * pair), 1)
        wanted = col == target_ref[:, step : step + 1]
        if step == 1:
            wanted = wanted | (col == target_ref[:, 2:3])
        fresh = jnp.where(wanted, fresh, MASKED)
        highest = jnp.maximum(jnp.max(cached, axis=1, keepdims=True), jnp.max(fresh, axis=1, keepdims=True))
        cached = jnp.exp(cached - highest)
        fresh = jnp.exp(fresh - highest)
        total = jnp.sum(cached, axis=1, keepdims=True) + jnp.sum(fresh, axis=1, keepdims=True)
        mixed = jnp.dot(cached.astype(BF16), values, preferred_element_type=F32)
        mixed += jnp.dot(fresh.astype(BF16), new_values, preferred_element_type=F32)
        pieces.append(mixed / total)
    for h in range(heads):
        for b in range(near):
            first = h * parts + b * part_dev
            both = jnp.concatenate([piece[first : first + part_dev] for piece in pieces], axis=0)
            out_ref[b * pair : (b + 1) * pair, h * HD : (h + 1) * HD] = both.astype(BF16)


def attention(where, anc, rope, targets, queries, new_kv, cache, part_dev):
    tensor = lax.axis_size("tensor")
    groups = lax.axis_size("dp")
    span = cache[0].shape[1]
    rows, columns = queries[0].shape
    parts = rows // 2
    heads = columns // HD
    limit = (16 << 20) + 4 * (3 * heads * parts * parts * tensor * span)
    ins = (where, anc, rope, targets, *queries, *new_kv, *cache)
    return call(
        functools.partial(attention_kernel, (tensor, groups, part_dev, span, len(queries), len(new_kv))),
        shaped((rows, columns)),
        ins,
        [SMEM] * 2 + [VMEM] * (len(ins) - 2),
        [
            pltpu.VMEM((parts * tensor * span, HD), F32),
            pltpu.VMEM((parts * tensor * span, HD), F32),
            pltpu.VMEM((groups * 2 * part_dev, 128), F32),
        ],
        limit=limit,
        flops=1 << 30,
        moved=4 << 20,
    )


def split_ss(x):
    high = x.astype(BF16)
    low = (x - high.astype(F32)).astype(BF16)
    return jnp.pad(jnp.stack([high, low], axis=-1), ((0, 0), (0, 126)))


def move_keyvals(kv):
    groups = lax.axis_size("dp")
    d = lax.axis_index("dp")
    if groups == KVH:
        halves = (kv[:, :HD], kv[:, HD:])
        half = groups // 2
        lower = d < half
        one = lax.ppermute(
            jnp.where(lower, halves[0], halves[1]),
            "dp",
            [(i, 2 * i) for i in range(half)] + [(half + i, 2 * i + 1) for i in range(half)],
        )
        two = lax.ppermute(
            jnp.where(lower, halves[1], halves[0]),
            "dp",
            [(i, 2 * i + 1) for i in range(half)] + [(half + i, 2 * i) for i in range(half)],
        )
        even = d % 2 == 0
        return jnp.concatenate([jnp.where(even, one, two), jnp.where(even, two, one)], axis=1)
    every = lax.all_gather(kv, "dp", axis=1, tiled=True)
    start = (d * KVH // groups) * HD
    return jnp.concatenate(
        [lax.dynamic_slice_in_dim(every, first + start, HD, axis=1) for first in (0, KVH * HD)], axis=1
    )


def local(
    x_first,
    x_second,
    cache_keys,
    cache_values,
    ancestors,
    attn_gain,
    ffn_gain,
    w_query,
    w_keyval,
    w_out,
    w_gate,
    w_up,
    w_down,
):
    groups = lax.axis_size("dp")
    tensor = lax.axis_size("tensor")
    part_dev, features = x_first.shape
    span = cache_keys.shape[1]
    width = features * tensor
    context = span * tensor
    d = lax.axis_index("dp")
    t = lax.axis_index("tensor")
    pair = 2 * part_dev
    near = groups // tensor
    parts = near * part_dev
    where = jnp.stack([d, t]).astype(jnp.int32)

    x = stack_tokens(x_first, x_second)
    blocks = gather_rows(x)
    cache = lax.all_to_all(pack(cache_keys, cache_values, x), "dp", split_axis=0, concat_axis=0, tiled=True)
    cache = cache.reshape(groups * pair, span, HD)
    caches = gather_blocks(cache)

    h, squares, keyvals = project_keyval(where, blocks, attn_gain, w_keyval)
    new_kv = move_keyvals(keyvals)
    queries, queries_arrived = sum_blocks(*project(h, w_query, cache))
    message = jnp.concatenate([new_kv, split_ss(squares[:, 0])], axis=1)
    bits = 1
    while bits < tensor:
        arrived = swap(message, "tensor", bits)
        bits *= 2
        if bits == tensor:
            break
        summed = message.astype(F32) + arrived.astype(F32)
        squares = summed[:, 2 * HD] + summed[:, 2 * HD + 1]
        message = jnp.concatenate([summed[:, : 2 * HD].astype(BF16), split_ss(squares)], axis=1)

    own = t * parts + jnp.arange(parts, dtype=jnp.int32)
    anc = lax.dynamic_slice_in_dim(ancestors, t * parts, parts).astype(jnp.int32)
    heads = w_query.shape[1] // HD

    def row_of(particle, step):
        return (particle // part_dev) * pair + step * part_dev + particle % part_dev

    targets = jnp.stack([row_of(own, 0), row_of(anc, 0), row_of(own, 1)], axis=1)
    targets = jnp.tile(targets, (heads, 1)).astype(jnp.int32)
    rope = rope_tables(context) + rope_tables(context + 1)
    rope = jnp.asarray(np.stack(rope + (np.full(HD, width, np.float32),) * 4))
    mixed = attention(where, anc, rope, targets, [queries] + queries_arrived, [message, arrived], caches, part_dev)

    keep, far, close = project_back(where, gather_blocks(mixed), w_out, True)
    attn_part, residual = finish(*sum_rows(keep, far, close, pair), x)

    hidden_cols = w_gate.shape[1]
    h, keep, send = project_gate(where, gather_rows(residual), ffn_gain, w_gate)
    gate, gate_arrived = sum_blocks(keep, send)
    up, up_arrived = sum_blocks(*project(h, w_up))
    for piece in gate_arrived:
        gate = gate + piece.astype(F32)
    for piece in up_arrived:
        up = up + piece.astype(F32)
    scale = lax.rsqrt((gate[:, hidden_cols] + gate[:, hidden_cols + 1]) / width + EPS)[:, None]
    hidden = jax.nn.silu(gate[:, :hidden_cols] * scale) * (up * scale)
    keep, far, close = project_back(where, gather_blocks(hidden.astype(BF16)), w_down, False)
    (ffn_part,) = finish(*sum_rows(keep, far, close, pair))
    return (attn_part.reshape(2, part_dev, features), ffn_part.reshape(2, part_dev, features))


def solution(mesh):
    return jax.shard_map(
        local,
        mesh=mesh,
        in_specs=(
            P("dp", "tensor"),
            P("dp", "tensor"),
            P("dp", "tensor", None),
            P("dp", "tensor", None),
            P(),
            P("tensor"),
            P("tensor"),
            P("tensor", "dp"),
            P("tensor", "dp"),
            P("dp", "tensor"),
            P("tensor", "dp"),
            P("tensor", "dp"),
            P("dp", "tensor"),
        ),
        out_specs=(P(None, "dp", "tensor"), P(None, "dp", "tensor")),
        check_vma=False,
    )
```

```python
import functools
import math

import jax
import jax.numpy as jnp
import numpy as np
from jax import lax
from jax.experimental import pallas as pl
from jax.experimental.pallas import tpu as pltpu
from jax.sharding import PartitionSpec as P

KVH = 8
HD = 128
EPS = 1e-05
ROPE_BASE = 500000.0
MASKED = -1e30
BF16 = jnp.bfloat16
F32 = jnp.float32


def swap(x, axis, bits):
    size = lax.axis_size(axis)
    return lax.ppermute(x, axis, [(i, i ^ bits) for i in range(size)])


def rope_tables(position):
    half = HD // 2
    freq = np.power(np.float32(ROPE_BASE), -2.0 * np.arange(half, dtype=np.float32) / HD)
    angle = (np.float32(position) * freq.astype(np.float32)).astype(np.float32)
    cosine, sine = np.cos(angle), np.sin(angle)
    return (
        np.concatenate([cosine, cosine]).astype(np.float32),
        np.concatenate([-sine, sine]).astype(np.float32),
    )


SMEM = pl.BlockSpec(memory_space=pltpu.SMEM)
VMEM = pl.BlockSpec(memory_space=pltpu.VMEM)
ANY = pl.BlockSpec(memory_space=pl.ANY)
HBM = pl.BlockSpec(memory_space=pltpu.HBM)


def call(body, outs, ins, specs, scratch=(), limit=8 << 20, flops=0, moved=0):
    return pl.pallas_call(
        body,
        out_shape=outs,
        in_specs=specs,
        out_specs=jax.tree.map(lambda _: VMEM, outs),
        scratch_shapes=scratch,
        compiler_params=pltpu.CompilerParams(vmem_limit_bytes=limit),
        cost_estimate=pl.CostEstimate(flops=flops, bytes_accessed=moved, transcendentals=0),
    )(*ins)


def shaped(shape, dtype=BF16):
    return jax.ShapeDtypeStruct(shape, dtype)


def gather_rows(rows):
    groups = lax.axis_size("dp")
    blocks = {0: rows}
    for k in range(groups - 2, 0, -2):
        blocks[k] = swap(rows, "dp", k)
    blocks[1] = swap(rows, "dp", 1)
    for k in range(groups - 2, 0, -2):
        blocks[k + 1] = swap(blocks[k], "dp", 1)
    return [blocks[k] for k in range(groups)]


def gather_blocks(block):
    tensor = lax.axis_size("tensor")
    blocks = {0: block}
    for k in range(2, tensor, 2):
        blocks[k] = swap(block, "tensor", k)
    blocks[1] = swap(block, "tensor", 1)
    for k in range(2, tensor, 2):
        blocks[k + 1] = swap(blocks[k], "tensor", 1)
    return [blocks[k] for k in range(tensor)]


def sum_blocks(keep, send):
    tensor = lax.axis_size("tensor")
    rows = keep.shape[0] // (tensor // 2)
    paired = (keep + swap(send, "tensor", 1).astype(F32)).reshape(tensor // 2, rows, -1)
    return paired[0], [swap(paired[i].astype(BF16), "tensor", 2 * i) for i in range(1, tensor // 2)]


def slot(relative, size):
    return lax.shift_right_logical(relative, 1) + (relative & 1) * (size // 2)


def tiles(columns):
    for tile in (256, 384, 128):
        if columns % tile == 0:
            return tile
    return columns


def multiply(left, w_ref, write):
    columns = w_ref.shape[1]
    tile = tiles(columns)
    for first in range(0, columns, tile):
        write(first, tile, jnp.dot(left, w_ref[:, first : first + tile], preferred_element_type=F32))


def streamed(w_hbm, w_ref, sems):
    columns = w_ref.shape[1]
    tile = tiles(columns)
    copies = [
        pltpu.make_async_copy(w_hbm.at[:, pl.ds(first, tile)], w_ref.at[:, pl.ds(first, tile)], sems.at[i])
        for i, first in enumerate(range(0, columns, tile))
    ]
    for copy in copies:
        copy.start()

    def run(left, write):
        for i, first in enumerate(range(0, columns, tile)):
            copies[i].wait()
            write(first, tile, jnp.dot(left, w_ref[:, first : first + tile], preferred_element_type=F32))

    return run


def stream_scratch(w):
    return [pltpu.VMEM(w.shape, BF16), pltpu.SemaphoreType.DMA((w.shape[1] // tiles(w.shape[1]),))]


def stack_tokens(x_first, x_second):
    part_dev, features = x_first.shape

    def body(first_ref, second_ref, out_ref, one, two, sems):
        copies = [pltpu.make_async_copy(first_ref, one, sems.at[0]), pltpu.make_async_copy(second_ref, two, sems.at[1])]
        for copy in copies:
            copy.start()
        for copy in copies:
            copy.wait()
        out_ref[...] = jnp.concatenate([one[...].astype(F32), two[...].astype(F32)], axis=0).astype(BF16)

    return call(
        body,
        shaped((2 * part_dev, features)),
        (x_first, x_second),
        [HBM, HBM],
        [pltpu.VMEM(x_first.shape, BF16), pltpu.VMEM(x_first.shape, BF16), pltpu.SemaphoreType.DMA((2,))],
        limit=None,
        moved=4 * x_first.size * 2,
    )


def pack(cache_keys, cache_values, afters):
    groups = lax.axis_size("dp")
    part_dev, span, _ = cache_keys.shape

    def body(keys_hbm, values_hbm, *refs):
        out_ref, keys_ref, values_ref, sems = refs[len(afters) :]
        copies = [
            pltpu.make_async_copy(keys_hbm, keys_ref, sems.at[0]),
            pltpu.make_async_copy(values_hbm, values_ref, sems.at[1]),
        ]
        for copy in copies:
            copy.start()
        for copy in copies:
            copy.wait()
        for g in range(groups):
            first = g * KVH // groups * HD
            out_ref[g, 0] = keys_ref[:, :, first : first + HD]
            out_ref[g, 1] = values_ref[:, :, first : first + HD]

    return call(
        body,
        shaped((groups, 2, part_dev, span, HD)),
        (cache_keys, cache_values, *afters),
        [HBM, HBM] + [ANY] * len(afters),
        [pltpu.VMEM(cache_keys.shape, BF16), pltpu.VMEM(cache_keys.shape, BF16), pltpu.SemaphoreType.DMA((2,))],
        limit=None,
        moved=8 * cache_keys.size,
    )


def lift(where_ref, gain_ref, block_refs, h_ref, ss_ref, absolute):
    groups = len(block_refs)
    tensor = lax.axis_size("tensor")
    pair = block_refs[0].shape[0]
    near = groups // tensor
    d, t = where_ref[0], where_ref[1]
    gain = gain_ref[...]
    places = []
    for k in range(groups):
        g = d ^ k
        place = slot(lax.div(g, near) ^ t, tensor) * near + lax.rem(g, near)
        place = pl.multiple_of(place * pair, pair)
        wide = block_refs[k][...].astype(F32)
        squares = jnp.broadcast_to(jnp.sum(wide * wide, axis=1, keepdims=True), (pair, 128))
        ss_ref[pl.ds(pl.multiple_of(g * pair, pair) if absolute else place, pair), :] = squares
        h_ref[pl.ds(place, pair), :] = (wide * gain).astype(BF16)
        places.append((pl.multiple_of(g * pair, pair), place))
    return places


def project_keyval(where, blocks, gain, w):
    pair, features = blocks[0].shape
    rows = len(blocks) * pair
    columns = w.shape[1]

    def body(where_ref, gain_ref, *refs):
        block_refs, (w_hbm, h_ref, ss_ref, kv_ref, product, w_ref, sem) = refs[: len(blocks)], refs[len(blocks) :]
        copy = pltpu.make_async_copy(w_hbm, w_ref, sem)
        copy.start()
        places = lift(where_ref, gain_ref, block_refs, h_ref, ss_ref, True)
        copy.wait()
        product[...] = jnp.dot(h_ref[...], w_ref[...], preferred_element_type=F32)
        for to, place in places:
            kv_ref[pl.ds(to, pair), :] = product[pl.ds(place, pair), :].astype(BF16)

    return call(
        body,
        (shaped((rows, features)), shaped((rows, 128), F32), shaped((rows, columns))),
        (where, gain[None], *blocks, w),
        [SMEM] + [VMEM] * (1 + len(blocks)) + [HBM],
        [pltpu.VMEM((rows, columns), F32), pltpu.VMEM(w.shape, BF16), pltpu.SemaphoreType.DMA],
        limit=None,
        flops=2 * rows * w.size,
        moved=4 * rows * features + 2 * w.size,
    )


def project(h, w, after=None):
    half = h.shape[0] // 2

    def body(h_ref, w_ref, *refs):
        run = None if after is None else streamed(w_ref, refs[-2], refs[-1])
        keep_ref, send_ref = refs[:2] if after is None else refs[1:3]
        left = h_ref[...]

        def write(first, tile, product):
            keep_ref[:, first : first + tile] = product[:half]
            send_ref[:, first : first + tile] = product[half:].astype(BF16)

        if run is None:
            multiply(left, w_ref, write)
        else:
            run(left, write)

    columns = w.shape[1]
    return call(
        body,
        (shaped((half, columns), F32), shaped((half, columns))),
        (h, w) if after is None else (h, w, after),
        [VMEM] * 2 if after is None else [VMEM, HBM, ANY],
        () if after is None else stream_scratch(w),
        limit=None if after is not None else 8 << 20,
        flops=4 * half * w.size,
        moved=2 * w.size,
    )


def project_gate(where, blocks, gain, w):
    pair, features = blocks[0].shape
    rows = len(blocks) * pair
    half = rows // 2
    columns = w.shape[1]

    def body(where_ref, gain_ref, *refs):
        block_refs, (w_ref, h_ref, keep_ref, send_ref, ss_ref) = refs[: len(blocks)], refs[len(blocks) :]
        lift(where_ref, gain_ref, block_refs, h_ref, ss_ref, False)

        def write(first, tile, product):
            keep_ref[:, first : first + tile] = product[:half]
            send_ref[:, first : first + tile] = product[half:].astype(BF16)

        multiply(h_ref[...], w_ref, write)
        squares = ss_ref[...]
        high = squares.astype(BF16).astype(F32)
        lane = lax.broadcasted_iota(jnp.int32, squares.shape, 1)
        ends = jnp.where(lane == 0, high, jnp.where(lane == 1, squares - high, 0.0))
        keep_ref[:, columns:] = ends[:half]
        send_ref[:, columns:] = ends[half:].astype(BF16)

    return call(
        body,
        (shaped((rows, features)), shaped((half, columns + 128), F32), shaped((half, columns + 128))),
        (where, gain[None], *blocks, w),
        [SMEM] + [VMEM] * (2 + len(blocks)),
        [pltpu.VMEM((rows, 128), F32)],
        flops=2 * rows * w.size,
        moved=4 * rows * features + 2 * w.size,
    )


def project_back(where, blocks, w, stream):
    groups = lax.axis_size("dp")
    rows, depth = blocks[0].shape
    near = groups // len(blocks)
    pair = rows // near
    total = len(blocks) * rows
    columns = w.shape[1]
    close = min(groups, 4)
    far = (groups - close) // 2

    def body(where_ref, *refs):
        block_refs, (w_ref, *out_refs) = refs[: len(blocks)], refs[len(blocks) :]
        left = out_refs[close + 2]
        run = streamed(w_ref, refs[-2], refs[-1]) if stream else None
        d, t = where_ref[0], where_ref[1]
        for k, block_ref in enumerate(block_refs):
            for i in range(near):
                relative = ((t ^ k) * near + i) ^ d
                beyond = close + lax.shift_right_logical(relative - close, 1) + (relative & 1) * far
                place = jnp.where(relative < close, relative, beyond)
                left[pl.ds(pl.multiple_of(place * pair, pair), pair), :] = block_ref[i * pair : (i + 1) * pair, :]

        def write(first, tile, product):
            lanes = slice(first, first + tile)
            for i in range(close):
                out_refs[i][:, lanes] = product[i * pair : (i + 1) * pair].astype(out_refs[i].dtype)
            middle = (close + far) * pair
            out_refs[close][:, lanes] = product[close * pair : middle]
            out_refs[close + 1][:, lanes] = product[middle:].astype(BF16)

        if stream:
            run(left[...], write)
        else:
            multiply(left[...], w_ref, write)

    outs = [shaped((pair, columns), F32)] + [shaped((pair, columns))] * (close - 1)
    outs += [shaped((far * pair, columns), F32), shaped((far * pair, columns))]
    return call(
        body,
        tuple(outs),
        (where, *blocks, w),
        [SMEM] + [VMEM] * len(blocks) + [HBM if stream else VMEM],
        [pltpu.VMEM((total, depth), BF16)] + (stream_scratch(w) if stream else []),
        limit=None if stream else 8 << 20,
        flops=2 * total * w.size,
        moved=2 * w.size,
    )


def add_pairs(keep, arrived, pair):
    def body(keep_ref, arrived_ref, *out_refs):
        for i, out_ref in enumerate(out_refs):
            rows = slice(i * pair, (i + 1) * pair)
            out_ref[...] = (keep_ref[rows, :] + arrived_ref[rows, :].astype(F32)).astype(BF16)

    outs = (shaped((pair, keep.shape[1])),) * (keep.shape[0] // pair)
    return call(body, outs, (keep, arrived), [VMEM] * 2, moved=8 * arrived.size)


def sum_rows(parts, pair):
    own, *near, keep, send = parts
    sums = add_pairs(keep, swap(send, "dp", 1), pair)
    arrived = [swap(piece, "dp", len(near) + 1 + 2 * i) for i, piece in enumerate(sums)]
    arrived += [swap(piece, "dp", k + 1) for k, piece in enumerate(near)]
    return own, arrived


def finish(own, arrived, x=None):
    def body(own_ref, *refs):
        total = own_ref[...]
        for ref in refs[: len(arrived)]:
            total = total + ref[...].astype(F32)
        rounded = total.astype(BF16)
        if x is None:
            refs[-1][...] = rounded
        else:
            refs[-2][...] = rounded
            refs[-1][...] = (refs[len(arrived)][...].astype(F32) + rounded.astype(F32)).astype(BF16)

    outs = (shaped(own.shape),) * (1 if x is None else 2)
    ins = (own, *arrived) + (() if x is None else (x,))
    return call(body, outs, ins, [VMEM] * len(ins), moved=8 * own.size)


def attention_kernel(sizes, where_ref, anc_ref, rope_ref, target_ref, scale_ref, *refs):
    tensor, groups, part_dev, span, n_q, n_kv = sizes
    q_refs, kv_refs = refs[:n_q], refs[n_q : n_q + 2 * n_kv]
    first_cache = n_q + 2 * n_kv
    cache_refs, (out_ref, keys_ref, values_ref) = refs[first_cache : first_cache + tensor], refs[first_cache + tensor :]
    d, t = where_ref[0], where_ref[1]
    near = groups // tensor
    parts = near * part_dev
    pair = 2 * part_dev
    ctx = tensor * span
    scale = 1.0 / math.sqrt(HD)
    new = []
    for which in range(2):
        summed = kv_refs[which * n_kv][...].astype(F32)
        for ref in kv_refs[which * n_kv + 1 : (which + 1) * n_kv]:
            summed = summed + ref[...].astype(F32)
        new.append(summed * scale_ref[...])
    even = d % 2 == 0 if groups == KVH else True
    plain = jnp.where(even, new[0], new[1]).astype(BF16).astype(F32)
    new_values = jnp.where(even, new[1], new[0]).astype(BF16)
    cos_key = jnp.concatenate([jnp.broadcast_to(rope_ref[2 * s : 2 * s + 1, :], (part_dev, HD)) for s in range(2)])
    sin_key = jnp.concatenate([jnp.broadcast_to(rope_ref[2 * s + 1 : 2 * s + 2, :], (part_dev, HD)) for s in range(2)])
    turned = pltpu.roll(plain, HD // 2, 1).reshape(groups, pair, HD)
    new_keys = plain.reshape(groups, pair, HD) * cos_key[None] + turned * sin_key[None]
    new_keys = new_keys.reshape(groups * pair, HD).astype(BF16)
    queries = q_refs[0][...]
    for ref in q_refs[1:]:
        queries = queries + ref[...].astype(F32)
    heads = queries.shape[1] // HD
    rows = heads * parts
    queries = queries * scale_ref[pl.ds(pl.multiple_of(t * near * pair, pair), near * pair), :]
    pieces = []
    for step in range(2):

        def bring(i, _, step=step):
            if step == 0:
                block, member = t * near + lax.div(i, part_dev), lax.rem(i, part_dev)
            else:
                block, member = lax.div(anc_ref[i], part_dev), lax.rem(anc_ref[i], part_dev)
            place = block * pair + member
            for k in range(tensor):
                start = pl.multiple_of(i * ctx + k * span, 8)
                keys_ref[pl.ds(start, span), :] = cache_refs[k][place].astype(F32)
                values_ref[pl.ds(start, span), :] = cache_refs[k][place + part_dev].astype(F32)
            return 0

        lax.fori_loop(0, parts, bring, 0)
        keys = keys_ref[...].astype(BF16)
        values = values_ref[...].astype(BF16)
        cosine = rope_ref[2 * step : 2 * step + 1, :]
        sine = rope_ref[2 * step + 1 : 2 * step + 2, :]
        per_head = []
        for h in range(heads):
            for b in range(near):
                first = b * pair + step * part_dev
                per_head.append(queries[first : first + part_dev, h * HD : (h + 1) * HD])
        query = jnp.concatenate(per_head, axis=0)
        query = query.astype(BF16).astype(F32)
        query = (query * cosine + pltpu.roll(query, HD // 2, 1) * sine).astype(BF16)
        contract = (((1,), (1,)), ((), ()))
        cached = lax.dot_general(query, keys, contract, preferred_element_type=F32) * scale
        fresh = lax.dot_general(query, new_keys, contract, preferred_element_type=F32) * scale
        row_part = lax.rem(lax.broadcasted_iota(jnp.int32, (rows, 1), 0), parts)
        col_part = lax.div(lax.broadcasted_iota(jnp.int32, (1, parts * ctx), 1), ctx)
        cached = jnp.where(row_part == col_part, cached, MASKED)
        col = lax.broadcasted_iota(jnp.int32, (1, groups * pair), 1)
        wanted = col == target_ref[:, step : step + 1]
        if step == 1:
            wanted = wanted | (col == target_ref[:, 2:3])
        fresh = jnp.where(wanted, fresh, MASKED)
        highest = jnp.maximum(jnp.max(cached, axis=1, keepdims=True), jnp.max(fresh, axis=1, keepdims=True))
        cached = jnp.exp(cached - highest)
        fresh = jnp.exp(fresh - highest)
        total = jnp.sum(cached, axis=1, keepdims=True) + jnp.sum(fresh, axis=1, keepdims=True)
        mixed = jnp.dot(cached.astype(BF16), values, preferred_element_type=F32)
        mixed += jnp.dot(fresh.astype(BF16), new_values, preferred_element_type=F32)
        pieces.append(mixed / total)
    for h in range(heads):
        for b in range(near):
            first = h * parts + b * part_dev
            both = jnp.concatenate([piece[first : first + part_dev] for piece in pieces], axis=0)
            out_ref[b * pair : (b + 1) * pair, h * HD : (h + 1) * HD] = both.astype(BF16)


def attention(where, anc, rope, targets, scale, queries, new_kv, cache, part_dev):
    tensor = lax.axis_size("tensor")
    groups = lax.axis_size("dp")
    span = cache[0].shape[1]
    rows, columns = queries[0].shape
    parts = rows // 2
    heads = columns // HD
    limit = (8 << 20) + 4 * (3 * heads * parts * parts * tensor * span)
    ins = (where, anc, rope, targets, scale, *queries, *new_kv, *cache)
    return call(
        functools.partial(attention_kernel, (tensor, groups, part_dev, span, len(queries), len(new_kv) // 2)),
        shaped((rows, columns)),
        ins,
        [SMEM] * 2 + [VMEM] * (len(ins) - 2),
        [pltpu.VMEM((parts * tensor * span, HD), F32), pltpu.VMEM((parts * tensor * span, HD), F32)],
        limit=limit,
        flops=1 << 30,
        moved=4 << 20,
    )


def move_keyvals(kv):
    groups = lax.axis_size("dp")
    tensor = lax.axis_size("tensor")
    d = lax.axis_index("dp")
    kv = (kv.astype(F32) + swap(kv, "tensor", 1).astype(F32)).astype(BF16)
    if groups == KVH:
        half = groups // 2
        lower = d < half
        one = jnp.where(lower, kv[:, :HD], kv[:, HD:])
        two = jnp.where(lower, kv[:, HD:], kv[:, :HD])

        def move(x, flip, k):
            to = [2 * i + flip for i in range(half)] + [2 * i + 1 - flip for i in range(half)]
            pairs = [(i * tensor + t, to[i] * tensor + (t ^ k)) for i in range(groups) for t in range(tensor)]
            return lax.ppermute(x, ("dp", "tensor"), pairs)

        return [move(x, flip, k) for flip, x in enumerate((one, two)) for k in range(0, tensor, 2)]
    every = lax.all_gather(kv, "dp", axis=1, tiled=True)
    start = (d * KVH // groups) * HD
    mine = [lax.dynamic_slice_in_dim(every, first + start, HD, axis=1) for first in (0, KVH * HD)]
    return [x if k == 0 else swap(x, "tensor", k) for x in mine for k in range(0, tensor, 2)]


def local(
    x_first,
    x_second,
    cache_keys,
    cache_values,
    ancestors,
    attn_gain,
    ffn_gain,
    w_query,
    w_keyval,
    w_out,
    w_gate,
    w_up,
    w_down,
):
    groups = lax.axis_size("dp")
    tensor = lax.axis_size("tensor")
    part_dev, features = x_first.shape
    span = cache_keys.shape[1]
    width = features * tensor
    context = span * tensor
    d = lax.axis_index("dp")
    t = lax.axis_index("tensor")
    pair = 2 * part_dev
    near = groups // tensor
    parts = near * part_dev
    where = jnp.stack([d, t]).astype(jnp.int32)

    x = stack_tokens(x_first, x_second)
    blocks = gather_rows(x)
    cache = pack(cache_keys, cache_values, blocks[2::2])
    cache = lax.all_to_all(cache, "dp", split_axis=0, concat_axis=0, tiled=True)
    cache = cache.reshape(groups * pair, span, HD)
    caches = gather_blocks(cache)

    h, squares, keyvals = project_keyval(where, blocks, attn_gain, w_keyval)
    new_kv = move_keyvals(keyvals)
    queries, queries_arrived = sum_blocks(*project(h, w_query, cache))
    squares = squares[:, 0]
    for bits in [1 << i for i in range(tensor.bit_length() - 1)]:
        squares = squares + swap(squares, "tensor", bits)
    scale = lax.rsqrt(squares / width + EPS)[:, None]

    own = t * parts + jnp.arange(parts, dtype=jnp.int32)
    anc = lax.dynamic_slice_in_dim(ancestors, t * parts, parts).astype(jnp.int32)
    heads = w_query.shape[1] // HD

    def row_of(particle, step):
        return (particle // part_dev) * pair + step * part_dev + particle % part_dev

    targets = jnp.stack([row_of(own, 0), row_of(anc, 0), row_of(own, 1)], axis=1)
    targets = jnp.tile(targets, (heads, 1)).astype(jnp.int32)
    rope = rope_tables(context) + rope_tables(context + 1)
    rope = jnp.asarray(np.stack(rope))
    mixed = attention(where, anc, rope, targets, scale, [queries] + queries_arrived, new_kv, caches, part_dev)

    parts = project_back(where, gather_blocks(mixed), w_out, True)
    attn_part, residual = finish(*sum_rows(parts, pair), x)

    hidden_cols = w_gate.shape[1]
    h, keep, send = project_gate(where, gather_rows(residual), ffn_gain, w_gate)
    gate, gate_arrived = sum_blocks(keep, send)
    up, up_arrived = sum_blocks(*project(h, w_up))
    for piece in gate_arrived:
        gate = gate + piece.astype(F32)
    for piece in up_arrived:
        up = up + piece.astype(F32)
    scale = lax.rsqrt((gate[:, hidden_cols] + gate[:, hidden_cols + 1]) / width + EPS)[:, None]
    hidden = jax.nn.silu(gate[:, :hidden_cols] * scale) * (up * scale)
    parts = project_back(where, gather_blocks(hidden.astype(BF16)), w_down, False)
    (ffn_part,) = finish(*sum_rows(parts, pair))
    return (attn_part.reshape(2, part_dev, features), ffn_part.reshape(2, part_dev, features))


def solution(mesh):
    return jax.shard_map(
        local,
        mesh=mesh,
        in_specs=(
            P("dp", "tensor"),
            P("dp", "tensor"),
            P("dp", "tensor", None),
            P("dp", "tensor", None),
            P(),
            P("tensor"),
            P("tensor"),
            P("tensor", "dp"),
            P("tensor", "dp"),
            P("dp", "tensor"),
            P("tensor", "dp"),
            P("tensor", "dp"),
            P("dp", "tensor"),
        ),
        out_specs=(P(None, "dp", "tensor"), P(None, "dp", "tensor")),
        check_vma=False,
    )
```

```python
import functools
import math

import jax
import jax.numpy as jnp
import numpy as np
from jax import lax
from jax.experimental import pallas as pl
from jax.experimental.pallas import tpu as pltpu
from jax.sharding import PartitionSpec as P

KVH = 8
HD = 128
EPS = 1e-05
ROPE_BASE = 500000.0
MASKED = -1e30
AROUND = 5 << 30
BF16 = jnp.bfloat16
F32 = jnp.float32


def swap(x, axis, bits):
    size = lax.axis_size(axis)
    return lax.ppermute(x, axis, [(i, i ^ bits) for i in range(size)])


def rope_tables(position):
    half = HD // 2
    freq = np.power(np.float32(ROPE_BASE), -2.0 * np.arange(half, dtype=np.float32) / HD)
    angle = (np.float32(position) * freq.astype(np.float32)).astype(np.float32)
    cosine, sine = np.cos(angle), np.sin(angle)
    return (
        np.concatenate([cosine, cosine]).astype(np.float32),
        np.concatenate([-sine, sine]).astype(np.float32),
    )


SMEM = pl.BlockSpec(memory_space=pltpu.SMEM)
VMEM = pl.BlockSpec(memory_space=pltpu.VMEM)
ANY = pl.BlockSpec(memory_space=pl.ANY)
HBM = pl.BlockSpec(memory_space=pltpu.HBM)


def call(body, outs, ins, specs, scratch=(), flops=0, moved=0, limit=8 << 20):
    return pl.pallas_call(
        body,
        out_shape=outs,
        in_specs=specs,
        out_specs=jax.tree.map(lambda _: VMEM, outs),
        scratch_shapes=scratch,
        compiler_params=pltpu.CompilerParams(vmem_limit_bytes=limit),
        cost_estimate=pl.CostEstimate(flops=flops + AROUND, bytes_accessed=moved, transcendentals=0),
    )(*ins)


def shaped(shape, dtype=BF16):
    return jax.ShapeDtypeStruct(shape, dtype)


def gather_rows(rows):
    groups = lax.axis_size("dp")
    blocks = {0: rows}
    for k in range(groups - 2, 0, -2):
        blocks[k] = swap(rows, "dp", k)
    blocks[1] = swap(rows, "dp", 1)
    for k in range(groups - 2, 0, -2):
        blocks[k + 1] = swap(blocks[k], "dp", 1)
    return [blocks[k] for k in range(groups)]


def gather_blocks(block):
    tensor = lax.axis_size("tensor")
    blocks = {0: block}
    for k in range(2, tensor, 2):
        blocks[k] = swap(block, "tensor", k)
    blocks[1] = swap(block, "tensor", 1)
    for k in range(2, tensor, 2):
        blocks[k + 1] = swap(blocks[k], "tensor", 1)
    return [blocks[k] for k in range(tensor)]


def sum_blocks(keep, send):
    tensor = lax.axis_size("tensor")
    rows = keep.shape[0] // (tensor // 2)
    paired = (keep + swap(send, "tensor", 1).astype(F32)).reshape(tensor // 2, rows, -1)
    return paired[0], [swap(paired[i].astype(BF16), "tensor", 2 * i) for i in range(1, tensor // 2)]


def slot(relative, size):
    return lax.shift_right_logical(relative, 1) + (relative & 1) * (size // 2)


def tiles(columns):
    for tile in (256, 384, 128):
        if columns % tile == 0:
            return tile
    return columns


def multiply(left, w_ref, write):
    columns = w_ref.shape[1]
    tile = tiles(columns)
    for first in range(0, columns, tile):
        write(first, tile, jnp.dot(left, w_ref[:, first : first + tile], preferred_element_type=F32))


def stack_tokens(x_first, x_second):
    part_dev, features = x_first.shape

    def body(first_ref, second_ref, out_ref, one, two, sems):
        copies = [pltpu.make_async_copy(first_ref, one, sems.at[0]), pltpu.make_async_copy(second_ref, two, sems.at[1])]
        for copy in copies:
            copy.start()
        for copy in copies:
            copy.wait()
        out_ref[...] = jnp.concatenate([one[...].astype(F32), two[...].astype(F32)], axis=0).astype(BF16)

    return call(
        body,
        shaped((2 * part_dev, features)),
        (x_first, x_second),
        [HBM, HBM],
        [pltpu.VMEM(x_first.shape, BF16), pltpu.VMEM(x_first.shape, BF16), pltpu.SemaphoreType.DMA((2,))],
        moved=4 * x_first.size * 2,
    )


def pack(cache_keys, cache_values, afters):
    groups = lax.axis_size("dp")
    part_dev, span, _ = cache_keys.shape

    def body(keys_hbm, values_hbm, *refs):
        out_ref, keys_ref, values_ref, sems = refs[len(afters) :]
        copies = [
            pltpu.make_async_copy(keys_hbm, keys_ref, sems.at[0]),
            pltpu.make_async_copy(values_hbm, values_ref, sems.at[1]),
        ]
        for copy in copies:
            copy.start()
        for copy in copies:
            copy.wait()
        for g in range(groups):
            first = g * KVH // groups * HD
            out_ref[g, 0] = keys_ref[:, :, first : first + HD]
            out_ref[g, 1] = values_ref[:, :, first : first + HD]

    return call(
        body,
        shaped((groups, 2, part_dev, span, HD)),
        (cache_keys, cache_values, *afters),
        [HBM, HBM] + [ANY] * len(afters),
        [pltpu.VMEM(cache_keys.shape, BF16), pltpu.VMEM(cache_keys.shape, BF16), pltpu.SemaphoreType.DMA((2,))],
        moved=8 * cache_keys.size,
    )


def lift(where_ref, gain_ref, block_refs, h_ref, ss_ref, absolute):
    groups = len(block_refs)
    tensor = lax.axis_size("tensor")
    pair = block_refs[0].shape[0]
    near = groups // tensor
    d, t = where_ref[0], where_ref[1]
    gain = gain_ref[...]
    places = []
    for k in range(groups):
        g = d ^ k
        place = slot(lax.div(g, near) ^ t, tensor) * near + lax.rem(g, near)
        place = pl.multiple_of(place * pair, pair)
        wide = block_refs[k][...].astype(F32)
        squares = jnp.broadcast_to(jnp.sum(wide * wide, axis=1, keepdims=True), (pair, 128))
        ss_ref[pl.ds(pl.multiple_of(g * pair, pair) if absolute else place, pair), :] = squares
        h_ref[pl.ds(place, pair), :] = (wide * gain).astype(BF16)
        places.append((pl.multiple_of(g * pair, pair), place))
    return places


def project_keyval(where, blocks, gain, w):
    pair, features = blocks[0].shape
    rows = len(blocks) * pair
    columns = w.shape[1]

    def body(where_ref, gain_ref, *refs):
        block_refs, (w_ref, h_ref, ss_ref, kv_ref, product) = refs[: len(blocks)], refs[len(blocks) :]
        places = lift(where_ref, gain_ref, block_refs, h_ref, ss_ref, True)
        product[...] = jnp.dot(h_ref[...], w_ref[...], preferred_element_type=F32)
        for to, place in places:
            kv_ref[pl.ds(to, pair), :] = product[pl.ds(place, pair), :].astype(BF16)

    return call(
        body,
        (shaped((rows, features)), shaped((rows, 128), F32), shaped((rows, columns))),
        (where, gain[None], *blocks, w),
        [SMEM] + [VMEM] * (2 + len(blocks)),
        [pltpu.VMEM((rows, columns), F32)],
        flops=2 * rows * w.size,
        moved=4 * rows * features + 2 * w.size,
    )


def project(h, w, after=None):
    half = h.shape[0] // 2

    def body(h_ref, w_ref, *refs):
        keep_ref, send_ref = refs[-2:]

        def write(first, tile, product):
            keep_ref[:, first : first + tile] = product[:half]
            send_ref[:, first : first + tile] = product[half:].astype(BF16)

        multiply(h_ref[...], w_ref, write)

    columns = w.shape[1]
    return call(
        body,
        (shaped((half, columns), F32), shaped((half, columns))),
        (h, w) if after is None else (h, w, after),
        [VMEM] * 2 + [ANY] * (after is not None),
        flops=4 * half * w.size,
        moved=2 * w.size,
    )


def project_gate(where, blocks, gain, w):
    pair, features = blocks[0].shape
    rows = len(blocks) * pair
    half = rows // 2
    columns = w.shape[1]

    def body(where_ref, gain_ref, *refs):
        block_refs, (w_ref, h_ref, keep_ref, send_ref, ss_ref) = refs[: len(blocks)], refs[len(blocks) :]
        lift(where_ref, gain_ref, block_refs, h_ref, ss_ref, False)

        def write(first, tile, product):
            keep_ref[:, first : first + tile] = product[:half]
            send_ref[:, first : first + tile] = product[half:].astype(BF16)

        multiply(h_ref[...], w_ref, write)
        squares = ss_ref[...]
        high = squares.astype(BF16).astype(F32)
        lane = lax.broadcasted_iota(jnp.int32, squares.shape, 1)
        ends = jnp.where(lane == 0, high, jnp.where(lane == 1, squares - high, 0.0))
        keep_ref[:, columns:] = ends[:half]
        send_ref[:, columns:] = ends[half:].astype(BF16)

    return call(
        body,
        (shaped((rows, features)), shaped((half, columns + 128), F32), shaped((half, columns + 128))),
        (where, gain[None], *blocks, w),
        [SMEM] + [VMEM] * (2 + len(blocks)),
        [pltpu.VMEM((rows, 128), F32)],
        flops=2 * rows * w.size,
        moved=4 * rows * features + 2 * w.size,
    )


def project_back(where, blocks, w):
    groups = lax.axis_size("dp")
    rows, depth = blocks[0].shape
    near = groups // len(blocks)
    pair = rows // near
    total = len(blocks) * rows
    columns = w.shape[1]
    close = min(groups, 4)
    far = (groups - close) // 2

    def body(where_ref, *refs):
        block_refs, (w_ref, *out_refs) = refs[: len(blocks)], refs[len(blocks) :]
        left = out_refs[-1]
        d, t = where_ref[0], where_ref[1]
        for k, block_ref in enumerate(block_refs):
            for i in range(near):
                relative = ((t ^ k) * near + i) ^ d
                beyond = close + lax.shift_right_logical(relative - close, 1) + (relative & 1) * far
                place = jnp.where(relative < close, relative, beyond)
                left[pl.ds(pl.multiple_of(place * pair, pair), pair), :] = block_ref[i * pair : (i + 1) * pair, :]

        def write(first, tile, product):
            lanes = slice(first, first + tile)
            for i in range(close):
                out_refs[i][:, lanes] = product[i * pair : (i + 1) * pair].astype(out_refs[i].dtype)
            middle = (close + far) * pair
            out_refs[close][:, lanes] = product[close * pair : middle]
            out_refs[close + 1][:, lanes] = product[middle:].astype(BF16)

        multiply(left[...], w_ref, write)

    outs = [shaped((pair, columns), F32)] + [shaped((pair, columns))] * (close - 1)
    outs += [shaped((far * pair, columns), F32), shaped((far * pair, columns))]
    return call(
        body,
        tuple(outs),
        (where, *blocks, w),
        [SMEM] + [VMEM] * (1 + len(blocks)),
        [pltpu.VMEM((total, depth), BF16)],
        flops=2 * total * w.size,
        moved=2 * w.size,
    )


def add_pairs(keep, arrived, pair):
    def body(keep_ref, arrived_ref, *out_refs):
        for i, out_ref in enumerate(out_refs):
            rows = slice(i * pair, (i + 1) * pair)
            out_ref[...] = (keep_ref[rows, :] + arrived_ref[rows, :].astype(F32)).astype(BF16)

    outs = (shaped((pair, keep.shape[1])),) * (keep.shape[0] // pair)
    return call(body, outs, (keep, arrived), [VMEM] * 2, moved=8 * arrived.size)


def sum_rows(parts, pair):
    own, *near, keep, send = parts
    sums = add_pairs(keep, swap(send, "dp", 1), pair)
    arrived = [swap(piece, "dp", len(near) + 1 + 2 * i) for i, piece in enumerate(sums)]
    arrived += [swap(piece, "dp", k + 1) for k, piece in enumerate(near)]
    return own, arrived


def finish(own, arrived, x=None):
    def body(own_ref, *refs):
        total = own_ref[...]
        for ref in refs[: len(arrived)]:
            total = total + ref[...].astype(F32)
        rounded = total.astype(BF16)
        if x is None:
            refs[-1][...] = rounded
        else:
            refs[-2][...] = rounded
            refs[-1][...] = (refs[len(arrived)][...].astype(F32) + rounded.astype(F32)).astype(BF16)

    outs = (shaped(own.shape),) * (1 if x is None else 2)
    ins = (own, *arrived) + (() if x is None else (x,))
    return call(body, outs, ins, [VMEM] * len(ins), moved=8 * own.size)


def attention_kernel(sizes, where_ref, anc_ref, rope_ref, target_ref, scale_ref, *refs):
    tensor, groups, part_dev, span, n_q, n_kv = sizes
    q_refs, kv_refs = refs[:n_q], refs[n_q : n_q + 2 * n_kv]
    first_cache = n_q + 2 * n_kv
    cache_refs, (out_ref, keys_ref, values_ref) = refs[first_cache : first_cache + tensor], refs[first_cache + tensor :]
    d, t = where_ref[0], where_ref[1]
    near = groups // tensor
    parts = near * part_dev
    pair = 2 * part_dev
    ctx = tensor * span
    scale = 1.0 / math.sqrt(HD)
    new = []
    for which in range(2):
        summed = kv_refs[which * n_kv][...].astype(F32)
        for ref in kv_refs[which * n_kv + 1 : (which + 1) * n_kv]:
            summed = summed + ref[...].astype(F32)
        new.append(summed * scale_ref[...])
    even = d % 2 == 0 if groups == KVH else True
    plain = jnp.where(even, new[0], new[1]).astype(BF16).astype(F32)
    new_values = jnp.where(even, new[1], new[0]).astype(BF16)
    cos_key = jnp.concatenate([jnp.broadcast_to(rope_ref[2 * s : 2 * s + 1, :], (part_dev, HD)) for s in range(2)])
    sin_key = jnp.concatenate([jnp.broadcast_to(rope_ref[2 * s + 1 : 2 * s + 2, :], (part_dev, HD)) for s in range(2)])
    turned = pltpu.roll(plain, HD // 2, 1).reshape(groups, pair, HD)
    new_keys = plain.reshape(groups, pair, HD) * cos_key[None] + turned * sin_key[None]
    new_keys = new_keys.reshape(groups * pair, HD).astype(BF16)
    queries = q_refs[0][...]
    for ref in q_refs[1:]:
        queries = queries + ref[...].astype(F32)
    heads = queries.shape[1] // HD
    rows = heads * parts
    queries = queries * scale_ref[pl.ds(pl.multiple_of(t * near * pair, pair), near * pair), :]
    pieces = []
    for step in range(2):

        def bring(i, _, step=step):
            if step == 0:
                block, member = t * near + lax.div(i, part_dev), lax.rem(i, part_dev)
            else:
                block, member = lax.div(anc_ref[i], part_dev), lax.rem(anc_ref[i], part_dev)
            place = block * pair + member
            for k in range(tensor):
                start = pl.multiple_of(i * ctx + k * span, 8)
                keys_ref[pl.ds(start, span), :] = cache_refs[k][place].astype(F32)
                values_ref[pl.ds(start, span), :] = cache_refs[k][place + part_dev].astype(F32)
            return 0

        lax.fori_loop(0, parts, bring, 0)
        keys = keys_ref[...].astype(BF16)
        values = values_ref[...].astype(BF16)
        cosine = rope_ref[2 * step : 2 * step + 1, :]
        sine = rope_ref[2 * step + 1 : 2 * step + 2, :]
        per_head = []
        for h in range(heads):
            for b in range(near):
                first = b * pair + step * part_dev
                per_head.append(queries[first : first + part_dev, h * HD : (h + 1) * HD])
        query = jnp.concatenate(per_head, axis=0)
        query = query.astype(BF16).astype(F32)
        query = (query * cosine + pltpu.roll(query, HD // 2, 1) * sine).astype(BF16)
        contract = (((1,), (1,)), ((), ()))
        cached = lax.dot_general(query, keys, contract, preferred_element_type=F32) * scale
        fresh = lax.dot_general(query, new_keys, contract, preferred_element_type=F32) * scale
        row_part = lax.rem(lax.broadcasted_iota(jnp.int32, (rows, 1), 0), parts)
        col_part = lax.div(lax.broadcasted_iota(jnp.int32, (1, parts * ctx), 1), ctx)
        cached = jnp.where(row_part == col_part, cached, MASKED)
        col = lax.broadcasted_iota(jnp.int32, (1, groups * pair), 1)
        wanted = col == target_ref[:, step : step + 1]
        if step == 1:
            wanted = wanted | (col == target_ref[:, 2:3])
        fresh = jnp.where(wanted, fresh, MASKED)
        highest = jnp.maximum(jnp.max(cached, axis=1, keepdims=True), jnp.max(fresh, axis=1, keepdims=True))
        cached = jnp.exp(cached - highest)
        fresh = jnp.exp(fresh - highest)
        total = jnp.sum(cached, axis=1, keepdims=True) + jnp.sum(fresh, axis=1, keepdims=True)
        mixed = jnp.dot(cached.astype(BF16), values, preferred_element_type=F32)
        mixed += jnp.dot(fresh.astype(BF16), new_values, preferred_element_type=F32)
        pieces.append(mixed / total)
    for h in range(heads):
        for b in range(near):
            first = h * parts + b * part_dev
            both = jnp.concatenate([piece[first : first + part_dev] for piece in pieces], axis=0)
            out_ref[b * pair : (b + 1) * pair, h * HD : (h + 1) * HD] = both.astype(BF16)


def attention(where, anc, rope, targets, scale, queries, new_kv, cache, part_dev):
    tensor = lax.axis_size("tensor")
    groups = lax.axis_size("dp")
    span = cache[0].shape[1]
    rows, columns = queries[0].shape
    parts = rows // 2
    heads = columns // HD
    limit = (4 << 20) + 4 * (3 * heads * parts * parts * tensor * span)
    ins = (where, anc, rope, targets, scale, *queries, *new_kv, *cache)
    return call(
        functools.partial(attention_kernel, (tensor, groups, part_dev, span, len(queries), len(new_kv) // 2)),
        shaped((rows, columns)),
        ins,
        [SMEM] * 2 + [VMEM] * (len(ins) - 2),
        [pltpu.VMEM((parts * tensor * span, HD), F32), pltpu.VMEM((parts * tensor * span, HD), F32)],
        limit=limit,
        flops=1 << 30,
        moved=4 << 20,
    )


def move_keyvals(kv):
    groups = lax.axis_size("dp")
    tensor = lax.axis_size("tensor")
    d = lax.axis_index("dp")
    kv = (kv.astype(F32) + swap(kv, "tensor", 1).astype(F32)).astype(BF16)
    if groups == KVH:
        half = groups // 2
        lower = d < half
        one = jnp.where(lower, kv[:, :HD], kv[:, HD:])
        two = jnp.where(lower, kv[:, HD:], kv[:, :HD])

        def move(x, flip, k):
            to = [2 * i + flip for i in range(half)] + [2 * i + 1 - flip for i in range(half)]
            pairs = [(i * tensor + t, to[i] * tensor + (t ^ k)) for i in range(groups) for t in range(tensor)]
            return lax.ppermute(x, ("dp", "tensor"), pairs)

        return [move(x, flip, k) for flip, x in enumerate((one, two)) for k in range(0, tensor, 2)]
    every = lax.all_gather(kv, "dp", axis=1, tiled=True)
    start = (d * KVH // groups) * HD
    mine = [lax.dynamic_slice_in_dim(every, first + start, HD, axis=1) for first in (0, KVH * HD)]
    return [x if k == 0 else swap(x, "tensor", k) for x in mine for k in range(0, tensor, 2)]


def local(
    x_first,
    x_second,
    cache_keys,
    cache_values,
    ancestors,
    attn_gain,
    ffn_gain,
    w_query,
    w_keyval,
    w_out,
    w_gate,
    w_up,
    w_down,
):
    groups = lax.axis_size("dp")
    tensor = lax.axis_size("tensor")
    part_dev, features = x_first.shape
    span = cache_keys.shape[1]
    width = features * tensor
    context = span * tensor
    d = lax.axis_index("dp")
    t = lax.axis_index("tensor")
    pair = 2 * part_dev
    near = groups // tensor
    parts = near * part_dev
    where = jnp.stack([d, t]).astype(jnp.int32)

    x = stack_tokens(x_first, x_second)
    blocks = gather_rows(x)
    cache = pack(cache_keys, cache_values, blocks[2::2])
    cache = lax.all_to_all(cache, "dp", split_axis=0, concat_axis=0, tiled=True)
    cache = cache.reshape(groups * pair, span, HD)
    caches = gather_blocks(cache)

    h, squares, keyvals = project_keyval(where, blocks, attn_gain, w_keyval)
    new_kv = move_keyvals(keyvals)
    queries, queries_arrived = sum_blocks(*project(h, w_query, cache))
    squares = squares[:, 0]
    for bits in [1 << i for i in range(tensor.bit_length() - 1)]:
        squares = squares + swap(squares, "tensor", bits)
    scale = lax.rsqrt(squares / width + EPS)[:, None]

    own = t * parts + jnp.arange(parts, dtype=jnp.int32)
    anc = lax.dynamic_slice_in_dim(ancestors, t * parts, parts).astype(jnp.int32)
    heads = w_query.shape[1] // HD

    def row_of(particle, step):
        return (particle // part_dev) * pair + step * part_dev + particle % part_dev

    targets = jnp.stack([row_of(own, 0), row_of(anc, 0), row_of(own, 1)], axis=1)
    targets = jnp.tile(targets, (heads, 1)).astype(jnp.int32)
    rope = rope_tables(context) + rope_tables(context + 1)
    rope = jnp.asarray(np.stack(rope))
    mixed = attention(where, anc, rope, targets, scale, [queries] + queries_arrived, new_kv, caches, part_dev)

    parts = project_back(where, gather_blocks(mixed), w_out)
    attn_part, residual = finish(*sum_rows(parts, pair), x)

    hidden_cols = w_gate.shape[1]
    h, keep, send = project_gate(where, gather_rows(residual), ffn_gain, w_gate)
    gate, gate_arrived = sum_blocks(keep, send)
    up, up_arrived = sum_blocks(*project(h, w_up))
    for piece in gate_arrived:
        gate = gate + piece.astype(F32)
    for piece in up_arrived:
        up = up + piece.astype(F32)
    scale = lax.rsqrt((gate[:, hidden_cols] + gate[:, hidden_cols + 1]) / width + EPS)[:, None]
    hidden = jax.nn.silu(gate[:, :hidden_cols] * scale) * (up * scale)
    parts = project_back(where, gather_blocks(hidden.astype(BF16)), w_down)
    (ffn_part,) = finish(*sum_rows(parts, pair))
    return (attn_part.reshape(2, part_dev, features), ffn_part.reshape(2, part_dev, features))


def solution(mesh):
    return jax.shard_map(
        local,
        mesh=mesh,
        in_specs=(
            P("dp", "tensor"),
            P("dp", "tensor"),
            P("dp", "tensor", None),
            P("dp", "tensor", None),
            P(),
            P("tensor"),
            P("tensor"),
            P("tensor", "dp"),
            P("tensor", "dp"),
            P("dp", "tensor"),
            P("tensor", "dp"),
            P("tensor", "dp"),
            P("dp", "tensor"),
        ),
        out_specs=(P(None, "dp", "tensor"), P(None, "dp", "tensor")),
        check_vma=False,
    )
```

```python
import functools
import math

import jax
import jax.numpy as jnp
import numpy as np
from jax import lax
from jax.experimental import pallas as pl
from jax.experimental.pallas import tpu as pltpu
from jax.sharding import PartitionSpec as P

KVH = 8
HD = 128
EPS = 1e-05
ROPE_BASE = 500000.0
MASKED = -1e30
AROUND = 5 << 30
BF16 = jnp.bfloat16
F32 = jnp.float32


def swap(x, axis, bits):
    size = lax.axis_size(axis)
    return lax.ppermute(x, axis, [(i, i ^ bits) for i in range(size)])


def rope_tables(position):
    half = HD // 2
    freq = np.power(np.float32(ROPE_BASE), -2.0 * np.arange(half, dtype=np.float32) / HD)
    angle = (np.float32(position) * freq.astype(np.float32)).astype(np.float32)
    cosine, sine = np.cos(angle), np.sin(angle)
    return (
        np.concatenate([cosine, cosine]).astype(np.float32),
        np.concatenate([-sine, sine]).astype(np.float32),
    )


SMEM = pl.BlockSpec(memory_space=pltpu.SMEM)
VMEM = pl.BlockSpec(memory_space=pltpu.VMEM)
ANY = pl.BlockSpec(memory_space=pl.ANY)
HBM = pl.BlockSpec(memory_space=pltpu.HBM)


def call(body, outs, ins, specs, scratch=(), flops=0, moved=0, limit=8 << 20):
    return pl.pallas_call(
        body,
        out_shape=outs,
        in_specs=specs,
        out_specs=jax.tree.map(lambda _: VMEM, outs),
        scratch_shapes=scratch,
        compiler_params=pltpu.CompilerParams(vmem_limit_bytes=limit),
        cost_estimate=pl.CostEstimate(flops=flops + AROUND, bytes_accessed=moved, transcendentals=0),
    )(*ins)


def shaped(shape, dtype=BF16):
    return jax.ShapeDtypeStruct(shape, dtype)


def gather_rows(rows):
    groups = lax.axis_size("dp")
    close = min(groups, 4)
    blocks = {0: rows}
    for k in range(groups - 2, close - 1, -2):
        blocks[k] = swap(rows, "dp", k)
    for k in range(close - 1, 0, -1):
        blocks[k] = swap(rows, "dp", k)
    for k in range(groups - 2, close - 1, -2):
        blocks[k + 1] = swap(blocks[k], "dp", 1)
    return [blocks[k] for k in range(groups)]


def gather_blocks(block):
    tensor = lax.axis_size("tensor")
    blocks = {0: block}
    for k in range(2, tensor, 2):
        blocks[k] = swap(block, "tensor", k)
    blocks[1] = swap(block, "tensor", 1)
    for k in range(2, tensor, 2):
        blocks[k + 1] = swap(blocks[k], "tensor", 1)
    return [blocks[k] for k in range(tensor)]


def sum_blocks(keep, send):
    tensor = lax.axis_size("tensor")
    rows = keep.shape[0] // (tensor // 2)
    paired = (keep + swap(send, "tensor", 1).astype(F32)).reshape(tensor // 2, rows, -1)
    return paired[0], [swap(paired[i].astype(BF16), "tensor", 2 * i) for i in range(1, tensor // 2)]


def slot(relative, size):
    return lax.shift_right_logical(relative, 1) + (relative & 1) * (size // 2)


def tiles(columns):
    for tile in (256, 384, 128):
        if columns % tile == 0:
            return tile
    return columns


def multiply(left, w_ref, write):
    columns = w_ref.shape[1]
    tile = tiles(columns)
    for first in range(0, columns, tile):
        write(first, tile, jnp.dot(left, w_ref[:, first : first + tile], preferred_element_type=F32))


def prologue(where, x_first, x_second, cache_keys, cache_values):
    groups = lax.axis_size("dp")
    part_dev, features = x_first.shape
    span = cache_keys.shape[1]
    shape = (groups // 2, 2, part_dev, span, HD)

    def body(where_ref, first_hbm, second_hbm, keys_hbm, values_hbm, x_ref, keep_ref, send_ref, *refs):
        one, two, keys_ref, values_ref, sems = refs
        pairs = ((first_hbm, one), (second_hbm, two), (keys_hbm, keys_ref), (values_hbm, values_ref))
        copies = [pltpu.make_async_copy(src, dst, sems.at[i]) for i, (src, dst) in enumerate(pairs)]
        for copy in copies:
            copy.start()
        for copy in copies[:2]:
            copy.wait()
        x_ref[...] = jnp.concatenate([one[...].astype(F32), two[...].astype(F32)], axis=0).astype(BF16)
        for copy in copies[2:]:
            copy.wait()
        for k in range(groups):
            head = lax.div((where_ref[0] ^ k) * KVH, groups)
            lanes = pl.ds(pl.multiple_of(head * HD, HD), HD)
            out_ref = send_ref if k % 2 else keep_ref
            out_ref[k // 2, 0] = keys_ref[:, :, lanes]
            out_ref[k // 2, 1] = values_ref[:, :, lanes]

    return call(
        body,
        (shaped((2 * part_dev, features)), shaped(shape), shaped(shape)),
        (where, x_first, x_second, cache_keys, cache_values),
        [SMEM] + [HBM] * 4,
        [pltpu.VMEM(a.shape, BF16) for a in (x_first, x_second, cache_keys, cache_values)]
        + [pltpu.SemaphoreType.DMA((4,))],
        limit=None,
        moved=8 * cache_keys.size,
    )


def move_cache(keep, send):
    groups = lax.axis_size("dp")
    both = jnp.stack([keep, swap(send, "dp", 1)], axis=1)
    moved = [both[:1]] + [swap(both[i : i + 1], "dp", 2 * i) for i in range(groups // 2 - 1, 0, -1)][::-1]
    both = jnp.concatenate(moved)
    return gather_blocks(both.reshape(groups * 2 * both.shape[3], *both.shape[4:]))


def lift(where_ref, gain_ref, block_refs, h_ref, ss_ref, absolute):
    groups = len(block_refs)
    tensor = lax.axis_size("tensor")
    pair = block_refs[0].shape[0]
    near = groups // tensor
    d, t = where_ref[0], where_ref[1]
    gain = gain_ref[...]
    places = []
    for k in range(groups):
        g = d ^ k
        place = slot(lax.div(g, near) ^ t, tensor) * near + lax.rem(g, near)
        place = pl.multiple_of(place * pair, pair)
        wide = block_refs[k][...].astype(F32)
        squares = jnp.broadcast_to(jnp.sum(wide * wide, axis=1, keepdims=True), (pair, 128))
        ss_ref[pl.ds(pl.multiple_of(g * pair, pair) if absolute else place, pair), :] = squares
        h_ref[pl.ds(place, pair), :] = (wide * gain).astype(BF16)
        places.append((pl.multiple_of(g * pair, pair), place))
    return places


def split(total, base, lane):
    high = total.astype(BF16).astype(F32)
    return jnp.where(lane == 0, high, jnp.where(lane == 1, total - high, base))


def project_attention(where, blocks, gain, w_keyval, w_query):
    pair, features = blocks[0].shape
    rows = len(blocks) * pair
    half = rows // 2
    columns = w_keyval.shape[1]
    wide = w_query.shape[1]

    def body(where_ref, gain_ref, *refs):
        block_refs, refs = refs[: len(blocks)], refs[len(blocks) :]
        w_kv_ref, w_q_ref, kv_ref, keep_ref, send_ref, h_ref, ss_ref, product = refs
        places = lift(where_ref, gain_ref, block_refs, h_ref, ss_ref, True)
        h = h_ref[...]
        product[...] = jnp.dot(h, w_kv_ref[...], preferred_element_type=F32)
        for to, place in places:
            kv_ref[pl.ds(to, pair), :columns] = product[pl.ds(place, pair), :].astype(BF16)
        squares = ss_ref[...]
        lane = lax.broadcasted_iota(jnp.int32, squares.shape, 1)
        kv_ref[:, columns:] = split(squares, 0.0, lane).astype(BF16)

        def write(first, tile, product):
            keep_ref[:, first : first + tile] = product[:half]
            send_ref[:, first : first + tile] = product[half:].astype(BF16)

        multiply(h, w_q_ref, write)

    return call(
        body,
        (shaped((rows, columns + 128)), shaped((half, wide), F32), shaped((half, wide))),
        (where, gain[None], *blocks, w_keyval, w_query),
        [SMEM] + [VMEM] * (3 + len(blocks)),
        [pltpu.VMEM((rows, features), BF16), pltpu.VMEM((rows, 128), F32), pltpu.VMEM((rows, columns), F32)],
        flops=2 * rows * (w_keyval.size + w_query.size),
        moved=4 * rows * features + 2 * (w_keyval.size + w_query.size),
    )


def add_keyvals(own, arrived):
    rows, columns = own.shape

    def body(own_ref, arrived_ref, out_ref):
        summed = own_ref[...].astype(F32) + arrived_ref[...].astype(F32)
        ends = summed[:, columns - 128 :]
        lane = lax.broadcasted_iota(jnp.int32, ends.shape, 1)
        out_ref[:, : columns - 128] = summed[:, : columns - 128].astype(BF16)
        out_ref[:, columns - 128 :] = split(ends[:, 0:1] + ends[:, 1:2], ends, lane).astype(BF16)

    return call(body, shaped(own.shape), (own, arrived), [VMEM] * 2, moved=6 * own.size)


def finish_keyvals(where, own, arrived, width):
    groups = lax.axis_size("dp")
    rows, columns = own.shape
    columns -= 128

    def body(where_ref, own_ref, arrived_ref, scale_ref, *out_refs):
        summed = own_ref[...].astype(F32) + arrived_ref[...].astype(F32)
        squares = summed[:, columns : columns + 1] + summed[:, columns + 1 : columns + 2]
        scale = lax.rsqrt(squares / width + EPS)
        scale_ref[...] = jnp.broadcast_to(scale, (rows, 128))
        scaled = summed[:, :columns] * scale
        if groups == KVH:
            lower = where_ref[0] < groups // 2
            out_refs[0][...] = jnp.where(lower, scaled[:, :HD], scaled[:, HD:]).astype(BF16)
            out_refs[1][...] = jnp.where(lower, scaled[:, HD:], scaled[:, :HD]).astype(BF16)
        else:
            out_refs[0][...] = scaled.astype(BF16)

    outs = [shaped((rows, 128), F32)]
    outs += [shaped((rows, HD))] * 2 if groups == KVH else [shaped((rows, columns))]
    return call(body, tuple(outs), (where, own, arrived), [SMEM, VMEM, VMEM], moved=8 * own.size)


def project(h, w):
    half = h.shape[0] // 2

    def body(h_ref, w_ref, keep_ref, send_ref):
        def write(first, tile, product):
            keep_ref[:, first : first + tile] = product[:half]
            send_ref[:, first : first + tile] = product[half:].astype(BF16)

        multiply(h_ref[...], w_ref, write)

    columns = w.shape[1]
    return call(
        body,
        (shaped((half, columns), F32), shaped((half, columns))),
        (h, w),
        [VMEM] * 2,
        flops=4 * half * w.size,
        moved=2 * w.size,
    )


def project_gate(where, blocks, gain, w):
    pair, features = blocks[0].shape
    rows = len(blocks) * pair
    half = rows // 2
    columns = w.shape[1]

    def body(where_ref, gain_ref, *refs):
        block_refs, (w_ref, h_ref, keep_ref, send_ref, ss_ref) = refs[: len(blocks)], refs[len(blocks) :]
        lift(where_ref, gain_ref, block_refs, h_ref, ss_ref, False)

        def write(first, tile, product):
            keep_ref[:, first : first + tile] = product[:half]
            send_ref[:, first : first + tile] = product[half:].astype(BF16)

        multiply(h_ref[...], w_ref, write)
        squares = ss_ref[...]
        high = squares.astype(BF16).astype(F32)
        lane = lax.broadcasted_iota(jnp.int32, squares.shape, 1)
        ends = jnp.where(lane == 0, high, jnp.where(lane == 1, squares - high, 0.0))
        keep_ref[:, columns:] = ends[:half]
        send_ref[:, columns:] = ends[half:].astype(BF16)

    return call(
        body,
        (shaped((rows, features)), shaped((half, columns + 128), F32), shaped((half, columns + 128))),
        (where, gain[None], *blocks, w),
        [SMEM] + [VMEM] * (2 + len(blocks)),
        [pltpu.VMEM((rows, 128), F32)],
        flops=2 * rows * w.size,
        moved=4 * rows * features + 2 * w.size,
    )


def project_back(where, blocks, w):
    groups = lax.axis_size("dp")
    rows, depth = blocks[0].shape
    near = groups // len(blocks)
    pair = rows // near
    total = len(blocks) * rows
    columns = w.shape[1]
    close = min(groups, 4)
    far = (groups - close) // 2

    def body(where_ref, *refs):
        block_refs, (w_ref, *out_refs) = refs[: len(blocks)], refs[len(blocks) :]
        left = out_refs[-1]
        d, t = where_ref[0], where_ref[1]
        for k, block_ref in enumerate(block_refs):
            for i in range(near):
                relative = ((t ^ k) * near + i) ^ d
                beyond = close + lax.shift_right_logical(relative - close, 1) + (relative & 1) * far
                place = jnp.where(relative < close, relative, beyond)
                left[pl.ds(pl.multiple_of(place * pair, pair), pair), :] = block_ref[i * pair : (i + 1) * pair, :]

        def write(first, tile, product):
            lanes = slice(first, first + tile)
            for i in range(close):
                out_refs[i][:, lanes] = product[i * pair : (i + 1) * pair].astype(out_refs[i].dtype)
            middle = (close + far) * pair
            cut = middle + far // 2 * pair
            out_refs[close][:, lanes] = product[close * pair : middle]
            out_refs[close + 1][:, lanes] = product[middle:cut].astype(BF16)
            out_refs[close + 2][:, lanes] = product[cut:].astype(BF16)

        multiply(left[...], w_ref, write)

    outs = [shaped((pair, columns), F32)] + [shaped((pair, columns))] * (close - 1)
    outs += [shaped((far * pair, columns), F32)] + [shaped((far // 2 * pair, columns))] * 2
    return call(
        body,
        tuple(outs),
        (where, *blocks, w),
        [SMEM] + [VMEM] * (1 + len(blocks)),
        [pltpu.VMEM((total, depth), BF16)],
        flops=2 * total * w.size,
        moved=2 * w.size,
    )


def add_pairs(keep, arrived, first, pair):
    def body(keep_ref, arrived_ref, *out_refs):
        for i, out_ref in enumerate(out_refs):
            own = keep_ref[first + i * pair : first + (i + 1) * pair, :]
            out_ref[...] = (own + arrived_ref[i * pair : (i + 1) * pair, :].astype(F32)).astype(BF16)

    outs = (shaped((pair, keep.shape[1])),) * (arrived.shape[0] // pair)
    return call(body, outs, (keep, arrived), [VMEM] * 2, moved=8 * arrived.size)


def sum_rows(parts, pair):
    own, *near, keep, one, two = parts
    sums = add_pairs(keep, swap(one, "dp", 1), 0, pair)
    sums += add_pairs(keep, swap(two, "dp", 1), one.shape[0], pair)
    arrived = [swap(piece, "dp", len(near) + 1 + 2 * i) for i, piece in enumerate(sums)]
    arrived += [swap(piece, "dp", k + 1) for k, piece in enumerate(near)]
    return own, arrived


def finish(own, arrived, x=None):
    def body(own_ref, *refs):
        total = own_ref[...]
        for ref in refs[: len(arrived)]:
            total = total + ref[...].astype(F32)
        rounded = total.astype(BF16)
        if x is None:
            refs[-1][...] = rounded
        else:
            refs[-2][...] = rounded
            refs[-1][...] = (refs[len(arrived)][...].astype(F32) + rounded.astype(F32)).astype(BF16)

    outs = (shaped(own.shape),) * (1 if x is None else 2)
    ins = (own, *arrived) + (() if x is None else (x,))
    return call(body, outs, ins, [VMEM] * len(ins), moved=8 * own.size)


def attend_cached(where, anc, rope, scale, queries, cache, part_dev):
    tensor = lax.axis_size("tensor")
    groups = lax.axis_size("dp")
    near = groups // tensor
    pair = 2 * part_dev
    span = cache[0].shape[1]
    ctx = tensor * span
    columns = queries[0].shape[1]
    heads = columns // HD
    parts = near * part_dev
    rows = heads * parts

    def body(where_ref, anc_ref, rope_ref, scale_ref, *refs):
        q_refs, refs = refs[: len(queries)], refs[len(queries) :]
        cache_refs, (query_ref, mixed_ref, highest_ref, total_ref, keys_ref, values_ref) = refs[:tensor], refs[tensor:]
        d, t = where_ref[0], where_ref[1]
        query_sum = q_refs[0][...]
        for ref in q_refs[1:]:
            query_sum = query_sum + ref[...].astype(F32)
        query_sum = query_sum * scale_ref[pl.ds(pl.multiple_of(t * near * pair, pair), near * pair), 0:1]
        for step in range(2):

            def bring(i, _, step=step):
                if step == 0:
                    block, member = (t * near + lax.div(i, part_dev)) ^ d, lax.rem(i, part_dev)
                else:
                    block, member = lax.div(anc_ref[i], part_dev) ^ d, lax.rem(anc_ref[i], part_dev)
                place = block * pair + member
                for k in range(tensor):
                    start = pl.multiple_of(i * ctx + k * span, 8)
                    keys_ref[pl.ds(start, span), :] = cache_refs[k][place].astype(F32)
                    values_ref[pl.ds(start, span), :] = cache_refs[k][place + part_dev].astype(F32)
                return 0

            lax.fori_loop(0, parts, bring, 0)
            keys = keys_ref[...].astype(BF16)
            values = values_ref[...].astype(BF16)
            per_head = []
            for h in range(heads):
                for b in range(near):
                    first = b * pair + step * part_dev
                    per_head.append(query_sum[first : first + part_dev, h * HD : (h + 1) * HD])
            query = jnp.concatenate(per_head, axis=0).astype(BF16).astype(F32)
            cosine = rope_ref[2 * step : 2 * step + 1, :]
            sine = rope_ref[2 * step + 1 : 2 * step + 2, :]
            query = (query * cosine + pltpu.roll(query, HD // 2, 1) * sine).astype(BF16)
            scores = lax.dot_general(query, keys, (((1,), (1,)), ((), ())), preferred_element_type=F32)
            scores = scores * (1.0 / math.sqrt(HD))
            row_part = lax.rem(lax.broadcasted_iota(jnp.int32, (rows, 1), 0), parts)
            col_part = lax.div(lax.broadcasted_iota(jnp.int32, (1, parts * ctx), 1), ctx)
            scores = jnp.where(row_part == col_part, scores, MASKED)
            highest = jnp.max(scores, axis=1, keepdims=True)
            weights = jnp.exp(scores - highest)
            here = slice(step * rows, (step + 1) * rows)
            query_ref[here, :] = query
            mixed_ref[here, :] = jnp.dot(weights.astype(BF16), values, preferred_element_type=F32)
            highest_ref[here, :] = jnp.broadcast_to(highest, (rows, 128))
            total_ref[here, :] = jnp.broadcast_to(jnp.sum(weights, axis=1, keepdims=True), (rows, 128))

    ins = (where, anc, rope, scale, *queries, *cache)
    return call(
        body,
        (shaped((2 * rows, HD)), shaped((2 * rows, HD), F32), shaped((2 * rows, 128), F32), shaped((2 * rows, 128), F32)),
        ins,
        [SMEM] * 2 + [VMEM] * (len(ins) - 2),
        [pltpu.VMEM((parts * ctx, HD), F32), pltpu.VMEM((parts * ctx, HD), F32)],
        limit=(4 << 20) + 12 * rows * parts * ctx,
        moved=4 << 20,
    )


def attend_new(where, rope, targets, pieces, state, shape, part_dev):
    groups = lax.axis_size("dp")
    tensor = lax.axis_size("tensor")
    near = groups // tensor
    pair = 2 * part_dev
    parts = near * part_dev
    heads = shape[1] // HD
    rows = heads * parts

    def body(where_ref, rope_ref, target_ref, one_ref, two_ref, query_ref, mixed_ref, highest_ref, total_ref, out_ref):
        even = where_ref[0] % 2 == 0 if groups == KVH else True
        one, two = one_ref[...].astype(F32), two_ref[...].astype(F32)
        plain = jnp.where(even, one, two)
        values = jnp.where(even, two, one).astype(BF16)
        cosine = jnp.concatenate([jnp.broadcast_to(rope_ref[2 * s : 2 * s + 1, :], (part_dev, HD)) for s in range(2)])
        sine = jnp.concatenate([jnp.broadcast_to(rope_ref[2 * s + 1 : 2 * s + 2, :], (part_dev, HD)) for s in range(2)])
        turned = pltpu.roll(plain, HD // 2, 1).reshape(groups, pair, HD)
        keys = plain.reshape(groups, pair, HD) * cosine[None] + turned * sine[None]
        keys = keys.reshape(groups * pair, HD).astype(BF16)
        scores = lax.dot_general(query_ref[...], keys, (((1,), (1,)), ((), ())), preferred_element_type=F32)
        scores = scores * (1.0 / math.sqrt(HD))
        col = lax.broadcasted_iota(jnp.int32, (1, groups * pair), 1)
        wanted = (col == target_ref[:, 0:1]) | (col == target_ref[:, 1:2])
        scores = jnp.where(wanted, scores, MASKED)
        before = highest_ref[:, 0:1]
        highest = jnp.maximum(before, jnp.max(scores, axis=1, keepdims=True))
        weights = jnp.exp(scores - highest)
        keep = jnp.exp(before - highest)
        total = total_ref[:, 0:1] * keep + jnp.sum(weights, axis=1, keepdims=True)
        mixed = mixed_ref[...] * keep + jnp.dot(weights.astype(BF16), values, preferred_element_type=F32)
        mixed = mixed / total
        for h in range(heads):
            for b in range(near):
                first = h * parts + b * part_dev
                both = [mixed[s * rows + first : s * rows + first + part_dev] for s in range(2)]
                here = slice(b * pair, (b + 1) * pair)
                out_ref[here, h * HD : (h + 1) * HD] = jnp.concatenate(both, axis=0).astype(BF16)

    ins = (where, rope, targets, *pieces, *state)
    return call(body, shaped(shape), ins, [SMEM] + [VMEM] * (len(ins) - 1), moved=1 << 20)


def move_keyvals(pieces):
    groups = lax.axis_size("dp")
    d = lax.axis_index("dp")
    if groups == KVH:
        half = groups // 2
        one = [(i, 2 * i) for i in range(half)] + [(half + i, 2 * i + 1) for i in range(half)]
        two = [(i, 2 * i + 1) for i in range(half)] + [(half + i, 2 * i) for i in range(half)]
        return [lax.ppermute(x, "dp", to) for x, to in zip(pieces, (one, two))]
    every = lax.all_gather(pieces[0], "dp", axis=1, tiled=True)
    start = (d * KVH // groups) * HD
    return [lax.dynamic_slice_in_dim(every, first + start, HD, axis=1) for first in (0, KVH * HD)]


def local(
    x_first,
    x_second,
    cache_keys,
    cache_values,
    ancestors,
    attn_gain,
    ffn_gain,
    w_query,
    w_keyval,
    w_out,
    w_gate,
    w_up,
    w_down,
):
    groups = lax.axis_size("dp")
    tensor = lax.axis_size("tensor")
    part_dev, features = x_first.shape
    span = cache_keys.shape[1]
    width = features * tensor
    context = span * tensor
    d = lax.axis_index("dp")
    t = lax.axis_index("tensor")
    pair = 2 * part_dev
    near = groups // tensor
    parts = near * part_dev
    where = jnp.stack([d, t]).astype(jnp.int32)

    x, keep, send = prologue(where, x_first, x_second, cache_keys, cache_values)
    blocks = gather_rows(x)
    caches = move_cache(keep, send)

    message, *queries = project_attention(where, blocks, attn_gain, w_keyval, w_query)
    bits = 1
    while 2 * bits < tensor:
        message = add_keyvals(message, swap(message, "tensor", bits))
        bits *= 2
    scale, *pieces = finish_keyvals(where, message, swap(message, "tensor", bits), width)
    pieces = move_keyvals(pieces)
    queries, queries_arrived = sum_blocks(*queries)

    own = t * parts + jnp.arange(parts, dtype=jnp.int32)
    anc = lax.dynamic_slice_in_dim(ancestors, t * parts, parts).astype(jnp.int32)
    heads = w_query.shape[1] // HD

    def row_of(particle, step):
        return (particle // part_dev) * pair + step * part_dev + particle % part_dev

    first = jnp.stack([row_of(own, 0)] * 2, axis=1)
    second = jnp.stack([row_of(anc, 0), row_of(own, 1)], axis=1)
    targets = jnp.concatenate([jnp.tile(first, (heads, 1)), jnp.tile(second, (heads, 1))]).astype(jnp.int32)
    rope = jnp.asarray(np.stack(rope_tables(context) + rope_tables(context + 1)))
    state = attend_cached(where, anc, rope, scale, [queries] + queries_arrived, caches, part_dev)
    mixed = attend_new(where, rope, targets, pieces, state, queries.shape, part_dev)

    parts = project_back(where, gather_blocks(mixed), w_out)
    attn_part, residual = finish(*sum_rows(parts, pair), x)

    hidden_cols = w_gate.shape[1]
    h, keep, send = project_gate(where, gather_rows(residual), ffn_gain, w_gate)
    gate, gate_arrived = sum_blocks(keep, send)
    up, up_arrived = sum_blocks(*project(h, w_up))
    for piece in gate_arrived:
        gate = gate + piece.astype(F32)
    for piece in up_arrived:
        up = up + piece.astype(F32)
    scale = lax.rsqrt((gate[:, hidden_cols] + gate[:, hidden_cols + 1]) / width + EPS)[:, None]
    hidden = jax.nn.silu(gate[:, :hidden_cols] * scale) * (up * scale)
    parts = project_back(where, gather_blocks(hidden.astype(BF16)), w_down)
    (ffn_part,) = finish(*sum_rows(parts, pair))
    return (attn_part.reshape(2, part_dev, features), ffn_part.reshape(2, part_dev, features))


def solution(mesh):
    return jax.shard_map(
        local,
        mesh=mesh,
        in_specs=(
            P("dp", "tensor"),
            P("dp", "tensor"),
            P("dp", "tensor", None),
            P("dp", "tensor", None),
            P(),
            P("tensor"),
            P("tensor"),
            P("tensor", "dp"),
            P("tensor", "dp"),
            P("dp", "tensor"),
            P("tensor", "dp"),
            P("tensor", "dp"),
            P("dp", "tensor"),
        ),
        out_specs=(P(None, "dp", "tensor"), P(None, "dp", "tensor")),
        check_vma=False,
    )
```

```python
import functools
import math

import jax
import jax.numpy as jnp
import numpy as np
from jax import lax
from jax.experimental import pallas as pl
from jax.experimental.pallas import tpu as pltpu
from jax.sharding import PartitionSpec as P

KVH = 8
HD = 128
EPS = 1e-05
ROPE_BASE = 500000.0
MASKED = -1e30
AROUND = 5 << 30
BF16 = jnp.bfloat16
F32 = jnp.float32


def swap(x, axis, bits):
    size = lax.axis_size(axis)
    return lax.ppermute(x, axis, [(i, i ^ bits) for i in range(size)])


def rope_tables(position):
    half = HD // 2
    freq = np.power(np.float32(ROPE_BASE), -2.0 * np.arange(half, dtype=np.float32) / HD)
    angle = (np.float32(position) * freq.astype(np.float32)).astype(np.float32)
    cosine, sine = np.cos(angle), np.sin(angle)
    return (
        np.concatenate([cosine, cosine]).astype(np.float32),
        np.concatenate([-sine, sine]).astype(np.float32),
    )


SMEM = pl.BlockSpec(memory_space=pltpu.SMEM)
VMEM = pl.BlockSpec(memory_space=pltpu.VMEM)
ANY = pl.BlockSpec(memory_space=pl.ANY)
HBM = pl.BlockSpec(memory_space=pltpu.HBM)


def call(body, outs, ins, specs, scratch=(), flops=0, moved=0, limit=8 << 20):
    return pl.pallas_call(
        body,
        out_shape=outs,
        in_specs=specs,
        out_specs=jax.tree.map(lambda _: VMEM, outs),
        scratch_shapes=scratch,
        compiler_params=pltpu.CompilerParams(vmem_limit_bytes=limit),
        cost_estimate=pl.CostEstimate(flops=flops + AROUND, bytes_accessed=moved, transcendentals=0),
    )(*ins)


def shaped(shape, dtype=BF16):
    return jax.ShapeDtypeStruct(shape, dtype)


def gather_rows(rows):
    groups = lax.axis_size("dp")
    close = min(groups, 4)
    blocks = {0: rows}
    for k in range(groups - 2, close - 1, -2):
        blocks[k] = swap(rows, "dp", k)
    for k in range(close - 1, 0, -1):
        blocks[k] = swap(rows, "dp", k)
    for k in range(groups - 2, close - 1, -2):
        blocks[k + 1] = swap(blocks[k], "dp", 1)
    return [blocks[k] for k in range(groups)]


def gather_blocks(block):
    tensor = lax.axis_size("tensor")
    blocks = {0: block}
    for k in range(2, tensor, 2):
        blocks[k] = swap(block, "tensor", k)
    blocks[1] = swap(block, "tensor", 1)
    for k in range(2, tensor, 2):
        blocks[k + 1] = swap(blocks[k], "tensor", 1)
    return [blocks[k] for k in range(tensor)]


def sum_blocks(keep, send):
    tensor = lax.axis_size("tensor")
    rows = keep.shape[0] // (tensor // 2)
    paired = (keep + swap(send, "tensor", 1).astype(F32)).reshape(tensor // 2, rows, -1)
    return paired[0], [swap(paired[i].astype(BF16), "tensor", 2 * i) for i in range(1, tensor // 2)]


def slot(relative, size):
    return lax.shift_right_logical(relative, 1) + (relative & 1) * (size // 2)


def tiles(columns):
    for tile in (256, 384, 128):
        if columns % tile == 0:
            return tile
    return columns


def multiply(left, w_ref, write):
    columns = w_ref.shape[1]
    tile = tiles(columns)
    for first in range(0, columns, tile):
        write(first, tile, jnp.dot(left, w_ref[:, first : first + tile], preferred_element_type=F32))


def stack_tokens(x_first, x_second):
    part_dev, features = x_first.shape

    def body(first_ref, second_ref, out_ref, one, two, sems):
        copies = [pltpu.make_async_copy(first_ref, one, sems.at[0]), pltpu.make_async_copy(second_ref, two, sems.at[1])]
        for copy in copies:
            copy.start()
        for copy in copies:
            copy.wait()
        out_ref[...] = jnp.concatenate([one[...].astype(F32), two[...].astype(F32)], axis=0).astype(BF16)

    return call(
        body,
        shaped((2 * part_dev, features)),
        (x_first, x_second),
        [HBM, HBM],
        [pltpu.VMEM(x_first.shape, BF16), pltpu.VMEM(x_first.shape, BF16), pltpu.SemaphoreType.DMA((2,))],
        limit=None,
    )


def pack(cache_keys, cache_values, after):
    groups = lax.axis_size("dp")
    part_dev, span, _ = cache_keys.shape

    def body(keys_ref, values_ref, after_ref, out_ref):
        for g in range(groups):
            first = g * KVH // groups * HD
            out_ref[g, 0] = keys_ref[:, :, first : first + HD]
            out_ref[g, 1] = values_ref[:, :, first : first + HD]

    return call(
        body,
        shaped((groups, 2, part_dev, span, HD)),
        (cache_keys, cache_values, after),
        [VMEM, VMEM, ANY],
        flops=4 * AROUND,
    )


def lift(where_ref, gain_ref, block_refs, h_ref, ss_ref, absolute):
    groups = len(block_refs)
    tensor = lax.axis_size("tensor")
    pair = block_refs[0].shape[0]
    near = groups // tensor
    d, t = where_ref[0], where_ref[1]
    gain = gain_ref[...]
    places = []
    for k in range(groups):
        g = d ^ k
        place = slot(lax.div(g, near) ^ t, tensor) * near + lax.rem(g, near)
        place = pl.multiple_of(place * pair, pair)
        wide = block_refs[k][...].astype(F32)
        squares = jnp.broadcast_to(jnp.sum(wide * wide, axis=1, keepdims=True), (pair, 128))
        ss_ref[pl.ds(pl.multiple_of(g * pair, pair) if absolute else place, pair), :] = squares
        h_ref[pl.ds(place, pair), :] = (wide * gain).astype(BF16)
        places.append((pl.multiple_of(g * pair, pair), place))
    return places


def split(total, base, lane):
    high = total.astype(BF16).astype(F32)
    return jnp.where(lane == 0, high, jnp.where(lane == 1, total - high, base))


def project_attention(where, blocks, gain, w_keyval, w_query):
    pair, features = blocks[0].shape
    rows = len(blocks) * pair
    half = rows // 2
    columns = w_keyval.shape[1]
    wide = w_query.shape[1]

    def body(where_ref, gain_ref, *refs):
        block_refs, refs = refs[: len(blocks)], refs[len(blocks) :]
        w_kv_ref, w_q_ref, kv_ref, keep_ref, send_ref, h_ref, ss_ref, product = refs
        places = lift(where_ref, gain_ref, block_refs, h_ref, ss_ref, True)
        h = h_ref[...]
        product[...] = jnp.dot(h, w_kv_ref[...], preferred_element_type=F32)
        for to, place in places:
            kv_ref[pl.ds(to, pair), :columns] = product[pl.ds(place, pair), :].astype(BF16)
        squares = ss_ref[...]
        lane = lax.broadcasted_iota(jnp.int32, squares.shape, 1)
        kv_ref[:, columns:] = split(squares, 0.0, lane).astype(BF16)

        def write(first, tile, product):
            keep_ref[:, first : first + tile] = product[:half]
            send_ref[:, first : first + tile] = product[half:].astype(BF16)

        multiply(h, w_q_ref, write)

    return call(
        body,
        (shaped((rows, columns + 128)), shaped((half, wide), F32), shaped((half, wide))),
        (where, gain[None], *blocks, w_keyval, w_query),
        [SMEM] + [VMEM] * (3 + len(blocks)),
        [pltpu.VMEM((rows, features), BF16), pltpu.VMEM((rows, 128), F32), pltpu.VMEM((rows, columns), F32)],
        flops=2 * rows * (w_keyval.size + w_query.size),
        moved=4 * rows * features + 2 * (w_keyval.size + w_query.size),
    )


def add_keyvals(own, arrived):
    rows, columns = own.shape

    def body(own_ref, arrived_ref, out_ref):
        summed = own_ref[...].astype(F32) + arrived_ref[...].astype(F32)
        ends = summed[:, columns - 128 :]
        lane = lax.broadcasted_iota(jnp.int32, ends.shape, 1)
        out_ref[:, : columns - 128] = summed[:, : columns - 128].astype(BF16)
        out_ref[:, columns - 128 :] = split(ends[:, 0:1] + ends[:, 1:2], ends, lane).astype(BF16)

    return call(body, shaped(own.shape), (own, arrived), [VMEM] * 2, moved=6 * own.size)


def finish_keyvals(where, own, arrived, width):
    groups = lax.axis_size("dp")
    rows, columns = own.shape
    columns -= 128

    def body(where_ref, own_ref, arrived_ref, scale_ref, *out_refs):
        summed = own_ref[...].astype(F32) + arrived_ref[...].astype(F32)
        squares = summed[:, columns : columns + 1] + summed[:, columns + 1 : columns + 2]
        scale = lax.rsqrt(squares / width + EPS)
        scale_ref[...] = jnp.broadcast_to(scale, (rows, 128))
        scaled = summed[:, :columns] * scale
        if groups == KVH:
            lower = where_ref[0] < groups // 2
            out_refs[0][...] = jnp.where(lower, scaled[:, :HD], scaled[:, HD:]).astype(BF16)
            out_refs[1][...] = jnp.where(lower, scaled[:, HD:], scaled[:, :HD]).astype(BF16)
        else:
            out_refs[0][...] = scaled.astype(BF16)

    outs = [shaped((rows, 128), F32)]
    outs += [shaped((rows, HD))] * 2 if groups == KVH else [shaped((rows, columns))]
    return call(body, tuple(outs), (where, own, arrived), [SMEM, VMEM, VMEM], moved=8 * own.size)


def project(h, w):
    half = h.shape[0] // 2

    def body(h_ref, w_ref, keep_ref, send_ref):
        def write(first, tile, product):
            keep_ref[:, first : first + tile] = product[:half]
            send_ref[:, first : first + tile] = product[half:].astype(BF16)

        multiply(h_ref[...], w_ref, write)

    columns = w.shape[1]
    return call(
        body,
        (shaped((half, columns), F32), shaped((half, columns))),
        (h, w),
        [VMEM] * 2,
        flops=4 * half * w.size,
        moved=2 * w.size,
    )


def project_gate(where, blocks, gain, w):
    pair, features = blocks[0].shape
    rows = len(blocks) * pair
    half = rows // 2
    columns = w.shape[1]

    def body(where_ref, gain_ref, *refs):
        block_refs, (w_ref, h_ref, keep_ref, send_ref, ss_ref) = refs[: len(blocks)], refs[len(blocks) :]
        lift(where_ref, gain_ref, block_refs, h_ref, ss_ref, False)

        def write(first, tile, product):
            keep_ref[:, first : first + tile] = product[:half]
            send_ref[:, first : first + tile] = product[half:].astype(BF16)

        multiply(h_ref[...], w_ref, write)
        squares = ss_ref[...]
        high = squares.astype(BF16).astype(F32)
        lane = lax.broadcasted_iota(jnp.int32, squares.shape, 1)
        ends = jnp.where(lane == 0, high, jnp.where(lane == 1, squares - high, 0.0))
        keep_ref[:, columns:] = ends[:half]
        send_ref[:, columns:] = ends[half:].astype(BF16)

    return call(
        body,
        (shaped((rows, features)), shaped((half, columns + 128), F32), shaped((half, columns + 128))),
        (where, gain[None], *blocks, w),
        [SMEM] + [VMEM] * (2 + len(blocks)),
        [pltpu.VMEM((rows, 128), F32)],
        flops=2 * rows * w.size,
        moved=4 * rows * features + 2 * w.size,
    )


def project_back(where, blocks, w):
    groups = lax.axis_size("dp")
    rows, depth = blocks[0].shape
    near = groups // len(blocks)
    pair = rows // near
    total = len(blocks) * rows
    columns = w.shape[1]
    close = min(groups, 4)
    far = (groups - close) // 2

    def body(where_ref, *refs):
        block_refs, (w_ref, *out_refs) = refs[: len(blocks)], refs[len(blocks) :]
        left = out_refs[-1]
        d, t = where_ref[0], where_ref[1]
        for k, block_ref in enumerate(block_refs):
            for i in range(near):
                relative = ((t ^ k) * near + i) ^ d
                beyond = close + lax.shift_right_logical(relative - close, 1) + (relative & 1) * far
                place = jnp.where(relative < close, relative, beyond)
                left[pl.ds(pl.multiple_of(place * pair, pair), pair), :] = block_ref[i * pair : (i + 1) * pair, :]

        def write(first, tile, product):
            lanes = slice(first, first + tile)
            for i in range(close):
                out_refs[i][:, lanes] = product[i * pair : (i + 1) * pair].astype(out_refs[i].dtype)
            middle = (close + far) * pair
            cut = middle + far // 2 * pair
            out_refs[close][:, lanes] = product[close * pair : middle]
            out_refs[close + 1][:, lanes] = product[middle:cut].astype(BF16)
            out_refs[close + 2][:, lanes] = product[cut:].astype(BF16)

        multiply(left[...], w_ref, write)

    outs = [shaped((pair, columns), F32)] + [shaped((pair, columns))] * (close - 1)
    outs += [shaped((far * pair, columns), F32)] + [shaped((far // 2 * pair, columns))] * 2
    return call(
        body,
        tuple(outs),
        (where, *blocks, w),
        [SMEM] + [VMEM] * (1 + len(blocks)),
        [pltpu.VMEM((total, depth), BF16)],
        flops=2 * total * w.size,
        moved=2 * w.size,
    )


def add_pairs(keep, arrived, first, pair):
    def body(keep_ref, arrived_ref, *out_refs):
        for i, out_ref in enumerate(out_refs):
            own = keep_ref[first + i * pair : first + (i + 1) * pair, :]
            out_ref[...] = (own + arrived_ref[i * pair : (i + 1) * pair, :].astype(F32)).astype(BF16)

    outs = (shaped((pair, keep.shape[1])),) * (arrived.shape[0] // pair)
    return call(body, outs, (keep, arrived), [VMEM] * 2, moved=8 * arrived.size)


def sum_rows(parts, pair):
    own, *near, keep, one, two = parts
    sums = add_pairs(keep, swap(one, "dp", 1), 0, pair)
    sums += add_pairs(keep, swap(two, "dp", 1), one.shape[0], pair)
    arrived = [swap(piece, "dp", len(near) + 1 + 2 * i) for i, piece in enumerate(sums)]
    arrived += [swap(piece, "dp", k + 1) for k, piece in enumerate(near)]
    return own, arrived


def finish(own, arrived, x=None):
    def body(own_ref, *refs):
        total = own_ref[...]
        for ref in refs[: len(arrived)]:
            total = total + ref[...].astype(F32)
        rounded = total.astype(BF16)
        if x is None:
            refs[-1][...] = rounded
        else:
            refs[-2][...] = rounded
            refs[-1][...] = (refs[len(arrived)][...].astype(F32) + rounded.astype(F32)).astype(BF16)

    outs = (shaped(own.shape),) * (1 if x is None else 2)
    ins = (own, *arrived) + (() if x is None else (x,))
    return call(body, outs, ins, [VMEM] * len(ins), moved=8 * own.size)


def attend_cached(where, anc, rope, scale, queries, cache, part_dev):
    tensor = lax.axis_size("tensor")
    groups = lax.axis_size("dp")
    near = groups // tensor
    pair = 2 * part_dev
    span = cache[0].shape[1]
    ctx = tensor * span
    columns = queries[0].shape[1]
    heads = columns // HD
    parts = near * part_dev
    rows = heads * parts

    def body(where_ref, anc_ref, rope_ref, scale_ref, *refs):
        q_refs, refs = refs[: len(queries)], refs[len(queries) :]
        cache_refs, (query_ref, mixed_ref, highest_ref, total_ref, keys_ref, values_ref) = refs[:tensor], refs[tensor:]
        t = where_ref[1]
        query_sum = q_refs[0][...]
        for ref in q_refs[1:]:
            query_sum = query_sum + ref[...].astype(F32)
        query_sum = query_sum * scale_ref[pl.ds(pl.multiple_of(t * near * pair, pair), near * pair), 0:1]
        for step in range(2):

            def bring(i, _, step=step):
                if step == 0:
                    block, member = t * near + lax.div(i, part_dev), lax.rem(i, part_dev)
                else:
                    block, member = lax.div(anc_ref[i], part_dev), lax.rem(anc_ref[i], part_dev)
                place = block * pair + member
                for k in range(tensor):
                    start = pl.multiple_of(i * ctx + k * span, 8)
                    keys_ref[pl.ds(start, span), :] = cache_refs[k][place].astype(F32)
                    values_ref[pl.ds(start, span), :] = cache_refs[k][place + part_dev].astype(F32)
                return 0

            lax.fori_loop(0, parts, bring, 0)
            keys = keys_ref[...].astype(BF16)
            values = values_ref[...].astype(BF16)
            per_head = []
            for h in range(heads):
                for b in range(near):
                    first = b * pair + step * part_dev
                    per_head.append(query_sum[first : first + part_dev, h * HD : (h + 1) * HD])
            query = jnp.concatenate(per_head, axis=0).astype(BF16).astype(F32)
            cosine = rope_ref[2 * step : 2 * step + 1, :]
            sine = rope_ref[2 * step + 1 : 2 * step + 2, :]
            query = (query * cosine + pltpu.roll(query, HD // 2, 1) * sine).astype(BF16)
            scores = lax.dot_general(query, keys, (((1,), (1,)), ((), ())), preferred_element_type=F32)
            scores = scores * (1.0 / math.sqrt(HD))
            row_part = lax.rem(lax.broadcasted_iota(jnp.int32, (rows, 1), 0), parts)
            col_part = lax.div(lax.broadcasted_iota(jnp.int32, (1, parts * ctx), 1), ctx)
            scores = jnp.where(row_part == col_part, scores, MASKED)
            highest = jnp.max(scores, axis=1, keepdims=True)
            weights = jnp.exp(scores - highest)
            here = slice(step * rows, (step + 1) * rows)
            query_ref[here, :] = query
            mixed_ref[here, :] = jnp.dot(weights.astype(BF16), values, preferred_element_type=F32)
            highest_ref[here, :] = jnp.broadcast_to(highest, (rows, 128))
            total_ref[here, :] = jnp.broadcast_to(jnp.sum(weights, axis=1, keepdims=True), (rows, 128))

    ins = (where, anc, rope, scale, *queries, *cache)
    return call(
        body,
        (shaped((2 * rows, HD)), shaped((2 * rows, HD), F32), shaped((2 * rows, 128), F32), shaped((2 * rows, 128), F32)),
        ins,
        [SMEM] * 2 + [VMEM] * (len(ins) - 2),
        [pltpu.VMEM((parts * ctx, HD), F32), pltpu.VMEM((parts * ctx, HD), F32)],
        limit=(4 << 20) + 12 * rows * parts * ctx,
        moved=4 << 20,
    )


def attend_new(where, rope, targets, pieces, state, shape, part_dev):
    groups = lax.axis_size("dp")
    tensor = lax.axis_size("tensor")
    near = groups // tensor
    pair = 2 * part_dev
    parts = near * part_dev
    heads = shape[1] // HD
    rows = heads * parts

    def body(where_ref, rope_ref, target_ref, one_ref, two_ref, query_ref, mixed_ref, highest_ref, total_ref, out_ref):
        even = where_ref[0] % 2 == 0 if groups == KVH else True
        one, two = one_ref[...].astype(F32), two_ref[...].astype(F32)
        plain = jnp.where(even, one, two)
        values = jnp.where(even, two, one).astype(BF16)
        cosine = jnp.concatenate([jnp.broadcast_to(rope_ref[2 * s : 2 * s + 1, :], (part_dev, HD)) for s in range(2)])
        sine = jnp.concatenate([jnp.broadcast_to(rope_ref[2 * s + 1 : 2 * s + 2, :], (part_dev, HD)) for s in range(2)])
        turned = pltpu.roll(plain, HD // 2, 1).reshape(groups, pair, HD)
        keys = plain.reshape(groups, pair, HD) * cosine[None] + turned * sine[None]
        keys = keys.reshape(groups * pair, HD).astype(BF16)
        scores = lax.dot_general(query_ref[...], keys, (((1,), (1,)), ((), ())), preferred_element_type=F32)
        scores = scores * (1.0 / math.sqrt(HD))
        col = lax.broadcasted_iota(jnp.int32, (1, groups * pair), 1)
        wanted = (col == target_ref[:, 0:1]) | (col == target_ref[:, 1:2])
        scores = jnp.where(wanted, scores, MASKED)
        before = highest_ref[:, 0:1]
        highest = jnp.maximum(before, jnp.max(scores, axis=1, keepdims=True))
        weights = jnp.exp(scores - highest)
        keep = jnp.exp(before - highest)
        total = total_ref[:, 0:1] * keep + jnp.sum(weights, axis=1, keepdims=True)
        mixed = mixed_ref[...] * keep + jnp.dot(weights.astype(BF16), values, preferred_element_type=F32)
        mixed = mixed / total
        for h in range(heads):
            for b in range(near):
                first = h * parts + b * part_dev
                both = [mixed[s * rows + first : s * rows + first + part_dev] for s in range(2)]
                here = slice(b * pair, (b + 1) * pair)
                out_ref[here, h * HD : (h + 1) * HD] = jnp.concatenate(both, axis=0).astype(BF16)

    ins = (where, rope, targets, *pieces, *state)
    return call(body, shaped(shape), ins, [SMEM] + [VMEM] * (len(ins) - 1), moved=1 << 20)


def move_keyvals(pieces):
    groups = lax.axis_size("dp")
    d = lax.axis_index("dp")
    if groups == KVH:
        half = groups // 2
        one = [(i, 2 * i) for i in range(half)] + [(half + i, 2 * i + 1) for i in range(half)]
        two = [(i, 2 * i + 1) for i in range(half)] + [(half + i, 2 * i) for i in range(half)]
        return [lax.ppermute(x, "dp", to) for x, to in zip(pieces, (one, two))]
    every = lax.all_gather(pieces[0], "dp", axis=1, tiled=True)
    start = (d * KVH // groups) * HD
    return [lax.dynamic_slice_in_dim(every, first + start, HD, axis=1) for first in (0, KVH * HD)]


def local(
    x_first,
    x_second,
    cache_keys,
    cache_values,
    ancestors,
    attn_gain,
    ffn_gain,
    w_query,
    w_keyval,
    w_out,
    w_gate,
    w_up,
    w_down,
):
    groups = lax.axis_size("dp")
    tensor = lax.axis_size("tensor")
    part_dev, features = x_first.shape
    span = cache_keys.shape[1]
    width = features * tensor
    context = span * tensor
    d = lax.axis_index("dp")
    t = lax.axis_index("tensor")
    pair = 2 * part_dev
    near = groups // tensor
    parts = near * part_dev
    where = jnp.stack([d, t]).astype(jnp.int32)

    x = stack_tokens(x_first, x_second)
    blocks = gather_rows(x)
    cache = lax.all_to_all(pack(cache_keys, cache_values, x), "dp", split_axis=0, concat_axis=0, tiled=True)
    caches = gather_blocks(cache.reshape(groups * pair, span, HD))

    message, *queries = project_attention(where, blocks, attn_gain, w_keyval, w_query)
    bits = 1
    while 2 * bits < tensor:
        message = add_keyvals(message, swap(message, "tensor", bits))
        bits *= 2
    scale, *pieces = finish_keyvals(where, message, swap(message, "tensor", bits), width)
    pieces = move_keyvals(pieces)
    queries, queries_arrived = sum_blocks(*queries)

    own = t * parts + jnp.arange(parts, dtype=jnp.int32)
    anc = lax.dynamic_slice_in_dim(ancestors, t * parts, parts).astype(jnp.int32)
    heads = w_query.shape[1] // HD

    def row_of(particle, step):
        return (particle // part_dev) * pair + step * part_dev + particle % part_dev

    first = jnp.stack([row_of(own, 0)] * 2, axis=1)
    second = jnp.stack([row_of(anc, 0), row_of(own, 1)], axis=1)
    targets = jnp.concatenate([jnp.tile(first, (heads, 1)), jnp.tile(second, (heads, 1))]).astype(jnp.int32)
    rope = jnp.asarray(np.stack(rope_tables(context) + rope_tables(context + 1)))
    state = attend_cached(where, anc, rope, scale, [queries] + queries_arrived, caches, part_dev)
    mixed = attend_new(where, rope, targets, pieces, state, queries.shape, part_dev)

    parts = project_back(where, gather_blocks(mixed), w_out)
    attn_part, residual = finish(*sum_rows(parts, pair), x)

    hidden_cols = w_gate.shape[1]
    h, keep, send = project_gate(where, gather_rows(residual), ffn_gain, w_gate)
    gate, gate_arrived = sum_blocks(keep, send)
    up, up_arrived = sum_blocks(*project(h, w_up))
    for piece in gate_arrived:
        gate = gate + piece.astype(F32)
    for piece in up_arrived:
        up = up + piece.astype(F32)
    scale = lax.rsqrt((gate[:, hidden_cols] + gate[:, hidden_cols + 1]) / width + EPS)[:, None]
    hidden = jax.nn.silu(gate[:, :hidden_cols] * scale) * (up * scale)
    parts = project_back(where, gather_blocks(hidden.astype(BF16)), w_down)
    (ffn_part,) = finish(*sum_rows(parts, pair))
    return (attn_part.reshape(2, part_dev, features), ffn_part.reshape(2, part_dev, features))


def solution(mesh):
    return jax.shard_map(
        local,
        mesh=mesh,
        in_specs=(
            P("dp", "tensor"),
            P("dp", "tensor"),
            P("dp", "tensor", None),
            P("dp", "tensor", None),
            P(),
            P("tensor"),
            P("tensor"),
            P("tensor", "dp"),
            P("tensor", "dp"),
            P("dp", "tensor"),
            P("tensor", "dp"),
            P("tensor", "dp"),
            P("dp", "tensor"),
        ),
        out_specs=(P(None, "dp", "tensor"), P(None, "dp", "tensor")),
        check_vma=False,
    )
```

```python
import functools
import math

import jax
import jax.numpy as jnp
import numpy as np
from jax import lax
from jax.experimental import pallas as pl
from jax.experimental.pallas import tpu as pltpu
from jax.sharding import PartitionSpec as P

KVH = 8
HD = 128
EPS = 1e-05
ROPE_BASE = 500000.0
MASKED = -1e30
AROUND = 5 << 30
BF16 = jnp.bfloat16
F32 = jnp.float32


def swap(x, axis, bits):
    size = lax.axis_size(axis)
    return lax.ppermute(x, axis, [(i, i ^ bits) for i in range(size)])


def rope_tables(position):
    half = HD // 2
    freq = np.power(np.float32(ROPE_BASE), -2.0 * np.arange(half, dtype=np.float32) / HD)
    angle = (np.float32(position) * freq.astype(np.float32)).astype(np.float32)
    cosine, sine = np.cos(angle), np.sin(angle)
    return (
        np.concatenate([cosine, cosine]).astype(np.float32),
        np.concatenate([-sine, sine]).astype(np.float32),
    )


SMEM = pl.BlockSpec(memory_space=pltpu.SMEM)
VMEM = pl.BlockSpec(memory_space=pltpu.VMEM)
ANY = pl.BlockSpec(memory_space=pl.ANY)
HBM = pl.BlockSpec(memory_space=pltpu.HBM)


def call(body, outs, ins, specs, scratch=(), flops=0, moved=0, limit=8 << 20):
    return pl.pallas_call(
        body,
        out_shape=outs,
        in_specs=specs,
        out_specs=jax.tree.map(lambda _: VMEM, outs),
        scratch_shapes=scratch,
        compiler_params=pltpu.CompilerParams(vmem_limit_bytes=limit),
        cost_estimate=pl.CostEstimate(flops=flops + AROUND, bytes_accessed=moved, transcendentals=0),
    )(*ins)


def shaped(shape, dtype=BF16):
    return jax.ShapeDtypeStruct(shape, dtype)


def gather_rows(rows):
    groups = lax.axis_size("dp")
    close = min(groups, 4)
    blocks = {0: rows}
    for k in range(groups - 2, close - 1, -2):
        blocks[k] = swap(rows, "dp", k)
    for k in range(close - 1, 0, -1):
        blocks[k] = swap(rows, "dp", k)
    for k in range(groups - 2, close - 1, -2):
        blocks[k + 1] = swap(blocks[k], "dp", 1)
    return [blocks[k] for k in range(groups)]


def gather_blocks(block):
    tensor = lax.axis_size("tensor")
    blocks = {0: block}
    for k in range(2, tensor, 2):
        blocks[k] = swap(block, "tensor", k)
    blocks[1] = swap(block, "tensor", 1)
    for k in range(2, tensor, 2):
        blocks[k + 1] = swap(blocks[k], "tensor", 1)
    return [blocks[k] for k in range(tensor)]


def sum_blocks(keep, send):
    tensor = lax.axis_size("tensor")
    rows = keep.shape[0] // (tensor // 2)
    paired = (keep + swap(send, "tensor", 1).astype(F32)).reshape(tensor // 2, rows, -1)
    return paired[0], [swap(paired[i].astype(BF16), "tensor", 2 * i) for i in range(1, tensor // 2)]


def slot(relative, size):
    return lax.shift_right_logical(relative, 1) + (relative & 1) * (size // 2)


def tiles(columns):
    for tile in (256, 384, 128):
        if columns % tile == 0:
            return tile
    return columns


def multiply(left, w_ref, write):
    columns = w_ref.shape[1]
    tile = tiles(columns)
    for first in range(0, columns, tile):
        write(first, tile, jnp.dot(left, w_ref[:, first : first + tile], preferred_element_type=F32))


def stack_tokens(x_first, x_second):
    def body(first_ref, second_ref, out_ref):
        out_ref[...] = jnp.concatenate([first_ref[...].astype(F32), second_ref[...].astype(F32)], axis=0).astype(BF16)

    part_dev, features = x_first.shape
    return call(body, shaped((2 * part_dev, features)), (x_first, x_second), [VMEM] * 2)


def pack(cache_keys, cache_values, after):
    groups = lax.axis_size("dp")
    part_dev, span, _ = cache_keys.shape

    def body(keys_ref, values_ref, after_ref, out_ref):
        for g in range(groups):
            first = g * KVH // groups * HD
            out_ref[g, 0] = keys_ref[:, :, first : first + HD]
            out_ref[g, 1] = values_ref[:, :, first : first + HD]

    return call(
        body,
        shaped((groups, 2, part_dev, span, HD)),
        (cache_keys, cache_values, after),
        [VMEM, VMEM, ANY],
        flops=4 * AROUND,
    )


def lift(where_ref, gain_ref, block_refs, h_ref, ss_ref, absolute):
    groups = len(block_refs)
    tensor = lax.axis_size("tensor")
    pair = block_refs[0].shape[0]
    near = groups // tensor
    d, t = where_ref[0], where_ref[1]
    gain = gain_ref[...]
    places = []
    for k in range(groups):
        g = d ^ k
        place = slot(lax.div(g, near) ^ t, tensor) * near + lax.rem(g, near)
        place = pl.multiple_of(place * pair, pair)
        wide = block_refs[k][...].astype(F32)
        squares = jnp.broadcast_to(jnp.sum(wide * wide, axis=1, keepdims=True), (pair, 128))
        ss_ref[pl.ds(pl.multiple_of(g * pair, pair) if absolute else place, pair), :] = squares
        h_ref[pl.ds(place, pair), :] = (wide * gain).astype(BF16)
        places.append((pl.multiple_of(g * pair, pair), place))
    return places


def split(total, base, lane):
    high = total.astype(BF16).astype(F32)
    return jnp.where(lane == 0, high, jnp.where(lane == 1, total - high, base))


def project_attention(where, blocks, gain, w_keyval, w_query, after):
    pair, features = blocks[0].shape
    rows = len(blocks) * pair
    half = rows // 2
    columns = w_keyval.shape[1]
    wide = w_query.shape[1]

    def body(where_ref, gain_ref, *refs):
        block_refs, refs = refs[: len(blocks)], refs[len(blocks) :]
        w_kv_ref, w_q_hbm, after_ref, kv_ref, keep_ref, send_ref, h_ref, ss_ref, product, w_q_ref, sems = refs
        tile = tiles(wide)
        copies = [
            pltpu.make_async_copy(w_q_hbm.at[:, pl.ds(i * tile, tile)], w_q_ref.at[:, pl.ds(i * tile, tile)], sems.at[i])
            for i in range(wide // tile)
        ]
        for copy in copies:
            copy.start()
        places = lift(where_ref, gain_ref, block_refs, h_ref, ss_ref, True)
        h = h_ref[...]
        product[...] = jnp.dot(h, w_kv_ref[...], preferred_element_type=F32)
        for to, place in places:
            kv_ref[pl.ds(to, pair), :columns] = product[pl.ds(place, pair), :].astype(BF16)
        squares = ss_ref[...]
        lane = lax.broadcasted_iota(jnp.int32, squares.shape, 1)
        kv_ref[:, columns:] = split(squares, 0.0, lane).astype(BF16)

        for i, copy in enumerate(copies):
            copy.wait()
            lanes = slice(i * tile, (i + 1) * tile)
            queries = jnp.dot(h, w_q_ref[:, lanes], preferred_element_type=F32)
            keep_ref[:, lanes] = queries[:half]
            send_ref[:, lanes] = queries[half:].astype(BF16)

    return call(
        body,
        (shaped((rows, columns + 128)), shaped((half, wide), F32), shaped((half, wide))),
        (where, gain[None], *blocks, w_keyval, w_query, after),
        [SMEM] + [VMEM] * (2 + len(blocks)) + [HBM, ANY],
        [
            pltpu.VMEM((rows, features), BF16),
            pltpu.VMEM((rows, 128), F32),
            pltpu.VMEM((rows, columns), F32),
            pltpu.VMEM(w_query.shape, BF16),
            pltpu.SemaphoreType.DMA((wide // tiles(wide),)),
        ],
        limit=52 << 20,
        flops=2 * rows * (w_keyval.size + w_query.size),
        moved=4 * rows * features + 2 * (w_keyval.size + w_query.size),
    )


def add_keyvals(own, arrived):
    rows, columns = own.shape

    def body(own_ref, arrived_ref, out_ref):
        summed = own_ref[...].astype(F32) + arrived_ref[...].astype(F32)
        ends = summed[:, columns - 128 :]
        lane = lax.broadcasted_iota(jnp.int32, ends.shape, 1)
        out_ref[:, : columns - 128] = summed[:, : columns - 128].astype(BF16)
        out_ref[:, columns - 128 :] = split(ends[:, 0:1] + ends[:, 1:2], ends, lane).astype(BF16)

    return call(body, shaped(own.shape), (own, arrived), [VMEM] * 2, moved=6 * own.size)


def finish_keyvals(where, own, arrived, width):
    groups = lax.axis_size("dp")
    rows, columns = own.shape
    columns -= 128

    def body(where_ref, own_ref, arrived_ref, scale_ref, *out_refs):
        summed = own_ref[...].astype(F32) + arrived_ref[...].astype(F32)
        squares = summed[:, columns : columns + 1] + summed[:, columns + 1 : columns + 2]
        scale = lax.rsqrt(squares / width + EPS)
        scale_ref[...] = jnp.broadcast_to(scale, (rows, 128))
        scaled = summed[:, :columns] * scale
        if groups == KVH:
            lower = where_ref[0] < groups // 2
            out_refs[0][...] = jnp.where(lower, scaled[:, :HD], scaled[:, HD:]).astype(BF16)
            out_refs[1][...] = jnp.where(lower, scaled[:, HD:], scaled[:, :HD]).astype(BF16)
        else:
            out_refs[0][...] = scaled.astype(BF16)

    outs = [shaped((rows, 128), F32)]
    outs += [shaped((rows, HD))] * 2 if groups == KVH else [shaped((rows, columns))]
    return call(body, tuple(outs), (where, own, arrived), [SMEM, VMEM, VMEM], moved=8 * own.size)


def project(h, w):
    half = h.shape[0] // 2

    def body(h_ref, w_ref, keep_ref, send_ref):
        def write(first, tile, product):
            keep_ref[:, first : first + tile] = product[:half]
            send_ref[:, first : first + tile] = product[half:].astype(BF16)

        multiply(h_ref[...], w_ref, write)

    columns = w.shape[1]
    return call(
        body,
        (shaped((half, columns), F32), shaped((half, columns))),
        (h, w),
        [VMEM] * 2,
        flops=4 * half * w.size,
        moved=2 * w.size,
    )


def project_gate(where, blocks, gain, w):
    pair, features = blocks[0].shape
    rows = len(blocks) * pair
    half = rows // 2
    columns = w.shape[1]

    def body(where_ref, gain_ref, *refs):
        block_refs, (w_ref, h_ref, keep_ref, send_ref, ss_ref) = refs[: len(blocks)], refs[len(blocks) :]
        lift(where_ref, gain_ref, block_refs, h_ref, ss_ref, False)

        def write(first, tile, product):
            keep_ref[:, first : first + tile] = product[:half]
            send_ref[:, first : first + tile] = product[half:].astype(BF16)

        multiply(h_ref[...], w_ref, write)
        squares = ss_ref[...]
        high = squares.astype(BF16).astype(F32)
        lane = lax.broadcasted_iota(jnp.int32, squares.shape, 1)
        ends = jnp.where(lane == 0, high, jnp.where(lane == 1, squares - high, 0.0))
        keep_ref[:, columns:] = ends[:half]
        send_ref[:, columns:] = ends[half:].astype(BF16)

    return call(
        body,
        (shaped((rows, features)), shaped((half, columns + 128), F32), shaped((half, columns + 128))),
        (where, gain[None], *blocks, w),
        [SMEM] + [VMEM] * (2 + len(blocks)),
        [pltpu.VMEM((rows, 128), F32)],
        flops=2 * rows * w.size,
        moved=4 * rows * features + 2 * w.size,
    )


def project_back(where, blocks, w):
    groups = lax.axis_size("dp")
    rows, depth = blocks[0].shape
    near = groups // len(blocks)
    pair = rows // near
    total = len(blocks) * rows
    columns = w.shape[1]
    close = min(groups, 4)
    far = (groups - close) // 2

    def body(where_ref, *refs):
        block_refs, (w_ref, *out_refs) = refs[: len(blocks)], refs[len(blocks) :]
        left = out_refs[-1]
        d, t = where_ref[0], where_ref[1]
        for k, block_ref in enumerate(block_refs):
            for i in range(near):
                relative = ((t ^ k) * near + i) ^ d
                beyond = close + lax.shift_right_logical(relative - close, 1) + (relative & 1) * far
                place = jnp.where(relative < close, relative, beyond)
                left[pl.ds(pl.multiple_of(place * pair, pair), pair), :] = block_ref[i * pair : (i + 1) * pair, :]

        def write(first, tile, product):
            lanes = slice(first, first + tile)
            for i in range(close):
                out_refs[i][:, lanes] = product[i * pair : (i + 1) * pair].astype(out_refs[i].dtype)
            middle = (close + far) * pair
            cut = middle + far // 2 * pair
            out_refs[close][:, lanes] = product[close * pair : middle]
            out_refs[close + 1][:, lanes] = product[middle:cut].astype(BF16)
            out_refs[close + 2][:, lanes] = product[cut:].astype(BF16)

        multiply(left[...], w_ref, write)

    outs = [shaped((pair, columns), F32)] + [shaped((pair, columns))] * (close - 1)
    outs += [shaped((far * pair, columns), F32)] + [shaped((far // 2 * pair, columns))] * 2
    return call(
        body,
        tuple(outs),
        (where, *blocks, w),
        [SMEM] + [VMEM] * (1 + len(blocks)),
        [pltpu.VMEM((total, depth), BF16)],
        flops=2 * total * w.size,
        moved=2 * w.size,
    )


def add_pairs(keep, arrived, first, pair):
    def body(keep_ref, arrived_ref, *out_refs):
        for i, out_ref in enumerate(out_refs):
            own = keep_ref[first + i * pair : first + (i + 1) * pair, :]
            out_ref[...] = (own + arrived_ref[i * pair : (i + 1) * pair, :].astype(F32)).astype(BF16)

    outs = (shaped((pair, keep.shape[1])),) * (arrived.shape[0] // pair)
    return call(body, outs, (keep, arrived), [VMEM] * 2, moved=8 * arrived.size)


def sum_rows(parts, pair):
    own, *near, keep, one, two = parts
    sums = add_pairs(keep, swap(one, "dp", 1), 0, pair)
    sums += add_pairs(keep, swap(two, "dp", 1), one.shape[0], pair)
    arrived = [swap(piece, "dp", len(near) + 1 + 2 * i) for i, piece in enumerate(sums)]
    arrived += [swap(piece, "dp", k + 1) for k, piece in enumerate(near)]
    return own, arrived


def finish(own, arrived, x=None):
    def body(own_ref, *refs):
        total = own_ref[...]
        for ref in refs[: len(arrived)]:
            total = total + ref[...].astype(F32)
        rounded = total.astype(BF16)
        if x is None:
            refs[-1][...] = rounded
        else:
            refs[-2][...] = rounded
            refs[-1][...] = (refs[len(arrived)][...].astype(F32) + rounded.astype(F32)).astype(BF16)

    outs = (shaped(own.shape),) * (1 if x is None else 2)
    ins = (own, *arrived) + (() if x is None else (x,))
    return call(body, outs, ins, [VMEM] * len(ins), moved=8 * own.size)


def attend_cached(where, anc, rope, scale, queries, cache, part_dev):
    tensor = lax.axis_size("tensor")
    groups = lax.axis_size("dp")
    near = groups // tensor
    pair = 2 * part_dev
    span = cache[0].shape[1]
    ctx = tensor * span
    columns = queries[0].shape[1]
    heads = columns // HD
    parts = near * part_dev
    rows = heads * parts

    def body(where_ref, anc_ref, rope_ref, scale_ref, *refs):
        q_refs, refs = refs[: len(queries)], refs[len(queries) :]
        cache_refs, (query_ref, mixed_ref, highest_ref, total_ref, keys_ref, values_ref) = refs[:tensor], refs[tensor:]
        t = where_ref[1]
        query_sum = q_refs[0][...]
        for ref in q_refs[1:]:
            query_sum = query_sum + ref[...].astype(F32)
        query_sum = query_sum * scale_ref[pl.ds(pl.multiple_of(t * near * pair, pair), near * pair), 0:1]
        for step in range(2):

            def bring(i, _, step=step):
                if step == 0:
                    block, member = t * near + lax.div(i, part_dev), lax.rem(i, part_dev)
                else:
                    block, member = lax.div(anc_ref[i], part_dev), lax.rem(anc_ref[i], part_dev)
                place = block * pair + member
                for k in range(tensor):
                    start = pl.multiple_of(i * ctx + k * span, 8)
                    keys_ref[pl.ds(start, span), :] = cache_refs[k][place].astype(F32)
                    values_ref[pl.ds(start, span), :] = cache_refs[k][place + part_dev].astype(F32)
                return 0

            lax.fori_loop(0, parts, bring, 0)
            keys = keys_ref[...].astype(BF16)
            values = values_ref[...].astype(BF16)
            per_head = []
            for h in range(heads):
                for b in range(near):
                    first = b * pair + step * part_dev
                    per_head.append(query_sum[first : first + part_dev, h * HD : (h + 1) * HD])
            query = jnp.concatenate(per_head, axis=0).astype(BF16).astype(F32)
            cosine = rope_ref[2 * step : 2 * step + 1, :]
            sine = rope_ref[2 * step + 1 : 2 * step + 2, :]
            query = (query * cosine + pltpu.roll(query, HD // 2, 1) * sine).astype(BF16)
            scores = lax.dot_general(query, keys, (((1,), (1,)), ((), ())), preferred_element_type=F32)
            scores = scores * (1.0 / math.sqrt(HD))
            row_part = lax.rem(lax.broadcasted_iota(jnp.int32, (rows, 1), 0), parts)
            col_part = lax.div(lax.broadcasted_iota(jnp.int32, (1, parts * ctx), 1), ctx)
            scores = jnp.where(row_part == col_part, scores, MASKED)
            highest = jnp.max(scores, axis=1, keepdims=True)
            weights = jnp.exp(scores - highest)
            here = slice(step * rows, (step + 1) * rows)
            query_ref[here, :] = query
            mixed_ref[here, :] = jnp.dot(weights.astype(BF16), values, preferred_element_type=F32)
            highest_ref[here, :] = jnp.broadcast_to(highest, (rows, 128))
            total_ref[here, :] = jnp.broadcast_to(jnp.sum(weights, axis=1, keepdims=True), (rows, 128))

    ins = (where, anc, rope, scale, *queries, *cache)
    return call(
        body,
        (shaped((2 * rows, HD)), shaped((2 * rows, HD), F32), shaped((2 * rows, 128), F32), shaped((2 * rows, 128), F32)),
        ins,
        [SMEM] * 2 + [VMEM] * (len(ins) - 2),
        [pltpu.VMEM((parts * ctx, HD), F32), pltpu.VMEM((parts * ctx, HD), F32)],
        limit=(4 << 20) + 12 * rows * parts * ctx,
        moved=4 << 20,
    )


def attend_new(where, rope, targets, pieces, state, shape, part_dev):
    groups = lax.axis_size("dp")
    tensor = lax.axis_size("tensor")
    near = groups // tensor
    pair = 2 * part_dev
    parts = near * part_dev
    heads = shape[1] // HD
    rows = heads * parts

    def body(where_ref, rope_ref, target_ref, one_ref, two_ref, query_ref, mixed_ref, highest_ref, total_ref, out_ref):
        even = where_ref[0] % 2 == 0 if groups == KVH else True
        one, two = one_ref[...].astype(F32), two_ref[...].astype(F32)
        plain = jnp.where(even, one, two)
        values = jnp.where(even, two, one).astype(BF16)
        cosine = jnp.concatenate([jnp.broadcast_to(rope_ref[2 * s : 2 * s + 1, :], (part_dev, HD)) for s in range(2)])
        sine = jnp.concatenate([jnp.broadcast_to(rope_ref[2 * s + 1 : 2 * s + 2, :], (part_dev, HD)) for s in range(2)])
        turned = pltpu.roll(plain, HD // 2, 1).reshape(groups, pair, HD)
        keys = plain.reshape(groups, pair, HD) * cosine[None] + turned * sine[None]
        keys = keys.reshape(groups * pair, HD).astype(BF16)
        scores = lax.dot_general(query_ref[...], keys, (((1,), (1,)), ((), ())), preferred_element_type=F32)
        scores = scores * (1.0 / math.sqrt(HD))
        col = lax.broadcasted_iota(jnp.int32, (1, groups * pair), 1)
        wanted = (col == target_ref[:, 0:1]) | (col == target_ref[:, 1:2])
        scores = jnp.where(wanted, scores, MASKED)
        before = highest_ref[:, 0:1]
        highest = jnp.maximum(before, jnp.max(scores, axis=1, keepdims=True))
        weights = jnp.exp(scores - highest)
        keep = jnp.exp(before - highest)
        total = total_ref[:, 0:1] * keep + jnp.sum(weights, axis=1, keepdims=True)
        mixed = mixed_ref[...] * keep + jnp.dot(weights.astype(BF16), values, preferred_element_type=F32)
        mixed = mixed / total
        for h in range(heads):
            for b in range(near):
                first = h * parts + b * part_dev
                both = [mixed[s * rows + first : s * rows + first + part_dev] for s in range(2)]
                here = slice(b * pair, (b + 1) * pair)
                out_ref[here, h * HD : (h + 1) * HD] = jnp.concatenate(both, axis=0).astype(BF16)

    ins = (where, rope, targets, *pieces, *state)
    return call(body, shaped(shape), ins, [SMEM] + [VMEM] * (len(ins) - 1), moved=1 << 20)


def move_keyvals(pieces):
    groups = lax.axis_size("dp")
    d = lax.axis_index("dp")
    if groups == KVH:
        half = groups // 2
        one = [(i, 2 * i) for i in range(half)] + [(half + i, 2 * i + 1) for i in range(half)]
        two = [(i, 2 * i + 1) for i in range(half)] + [(half + i, 2 * i) for i in range(half)]
        return [lax.ppermute(x, "dp", to) for x, to in zip(pieces, (one, two))]
    every = lax.all_gather(pieces[0], "dp", axis=1, tiled=True)
    start = (d * KVH // groups) * HD
    return [lax.dynamic_slice_in_dim(every, first + start, HD, axis=1) for first in (0, KVH * HD)]


def local(
    x_first,
    x_second,
    cache_keys,
    cache_values,
    ancestors,
    attn_gain,
    ffn_gain,
    w_query,
    w_keyval,
    w_out,
    w_gate,
    w_up,
    w_down,
):
    groups = lax.axis_size("dp")
    tensor = lax.axis_size("tensor")
    part_dev, features = x_first.shape
    span = cache_keys.shape[1]
    width = features * tensor
    context = span * tensor
    d = lax.axis_index("dp")
    t = lax.axis_index("tensor")
    pair = 2 * part_dev
    near = groups // tensor
    parts = near * part_dev
    where = jnp.stack([d, t]).astype(jnp.int32)

    x = stack_tokens(x_first, x_second)
    blocks = gather_rows(x)
    cache = lax.all_to_all(pack(cache_keys, cache_values, x), "dp", split_axis=0, concat_axis=0, tiled=True)
    caches = gather_blocks(cache.reshape(groups * pair, span, HD))

    message, *queries = project_attention(where, blocks, attn_gain, w_keyval, w_query, cache)
    bits = 1
    while 2 * bits < tensor:
        message = add_keyvals(message, swap(message, "tensor", bits))
        bits *= 2
    scale, *pieces = finish_keyvals(where, message, swap(message, "tensor", bits), width)
    pieces = move_keyvals(pieces)
    queries, queries_arrived = sum_blocks(*queries)

    own = t * parts + jnp.arange(parts, dtype=jnp.int32)
    anc = lax.dynamic_slice_in_dim(ancestors, t * parts, parts).astype(jnp.int32)
    heads = w_query.shape[1] // HD

    def row_of(particle, step):
        return (particle // part_dev) * pair + step * part_dev + particle % part_dev

    first = jnp.stack([row_of(own, 0)] * 2, axis=1)
    second = jnp.stack([row_of(anc, 0), row_of(own, 1)], axis=1)
    targets = jnp.concatenate([jnp.tile(first, (heads, 1)), jnp.tile(second, (heads, 1))]).astype(jnp.int32)
    rope = jnp.asarray(np.stack(rope_tables(context) + rope_tables(context + 1)))
    state = attend_cached(where, anc, rope, scale, [queries] + queries_arrived, caches, part_dev)
    mixed = attend_new(where, rope, targets, pieces, state, queries.shape, part_dev)

    parts = project_back(where, gather_blocks(mixed), w_out)
    attn_part, residual = finish(*sum_rows(parts, pair), x)

    hidden_cols = w_gate.shape[1]
    h, keep, send = project_gate(where, gather_rows(residual), ffn_gain, w_gate)
    gate, gate_arrived = sum_blocks(keep, send)
    up, up_arrived = sum_blocks(*project(h, w_up))
    for piece in gate_arrived:
        gate = gate + piece.astype(F32)
    for piece in up_arrived:
        up = up + piece.astype(F32)
    scale = lax.rsqrt((gate[:, hidden_cols] + gate[:, hidden_cols + 1]) / width + EPS)[:, None]
    hidden = jax.nn.silu(gate[:, :hidden_cols] * scale) * (up * scale)
    parts = project_back(where, gather_blocks(hidden.astype(BF16)), w_down)
    (ffn_part,) = finish(*sum_rows(parts, pair))
    return (attn_part.reshape(2, part_dev, features), ffn_part.reshape(2, part_dev, features))


def solution(mesh):
    return jax.shard_map(
        local,
        mesh=mesh,
        in_specs=(
            P("dp", "tensor"),
            P("dp", "tensor"),
            P("dp", "tensor", None),
            P("dp", "tensor", None),
            P(),
            P("tensor"),
            P("tensor"),
            P("tensor", "dp"),
            P("tensor", "dp"),
            P("dp", "tensor"),
            P("tensor", "dp"),
            P("tensor", "dp"),
            P("dp", "tensor"),
        ),
        out_specs=(P(None, "dp", "tensor"), P(None, "dp", "tensor")),
        check_vma=False,
    )
```

```python
import functools
import math

import jax
import jax.numpy as jnp
import numpy as np
from jax import lax
from jax.experimental import pallas as pl
from jax.experimental.pallas import tpu as pltpu
from jax.sharding import PartitionSpec as P

KVH = 8
HD = 128
EPS = 1e-05
ROPE_BASE = 500000.0
MASKED = -1e30
AROUND = 5 << 30
BF16 = jnp.bfloat16
F32 = jnp.float32


def swap(x, axis, bits):
    size = lax.axis_size(axis)
    return lax.ppermute(x, axis, [(i, i ^ bits) for i in range(size)])


def rope_tables(position):
    half = HD // 2
    freq = np.power(np.float32(ROPE_BASE), -2.0 * np.arange(half, dtype=np.float32) / HD)
    angle = (np.float32(position) * freq.astype(np.float32)).astype(np.float32)
    cosine, sine = np.cos(angle), np.sin(angle)
    return (
        np.concatenate([cosine, cosine]).astype(np.float32),
        np.concatenate([-sine, sine]).astype(np.float32),
    )


SMEM = pl.BlockSpec(memory_space=pltpu.SMEM)
VMEM = pl.BlockSpec(memory_space=pltpu.VMEM)
ANY = pl.BlockSpec(memory_space=pl.ANY)
HBM = pl.BlockSpec(memory_space=pltpu.HBM)


def call(body, outs, ins, specs, scratch=(), flops=0, moved=0, limit=8 << 20):
    return pl.pallas_call(
        body,
        out_shape=outs,
        in_specs=specs,
        out_specs=jax.tree.map(lambda _: VMEM, outs),
        scratch_shapes=scratch,
        compiler_params=pltpu.CompilerParams(vmem_limit_bytes=limit),
        cost_estimate=pl.CostEstimate(flops=flops + AROUND, bytes_accessed=moved, transcendentals=0),
    )(*ins)


def shaped(shape, dtype=BF16):
    return jax.ShapeDtypeStruct(shape, dtype)


def gather_rows(rows, near=None):
    groups = lax.axis_size("dp")
    close = min(groups, 4)
    blocks = {0: rows}
    for k in range(groups - 2, close - 1, -2):
        blocks[k] = swap(rows, "dp", k)
    for k in range(close - 1, 0, -1):
        blocks[k] = swap(rows if near is None else near[k - 1], "dp", k)
    for k in range(groups - 2, close - 1, -2):
        blocks[k + 1] = swap(blocks[k], "dp", 1)
    return [blocks[k] for k in range(groups)]


def gather_blocks(block):
    tensor = lax.axis_size("tensor")
    blocks = {0: block}
    for k in range(2, tensor, 2):
        blocks[k] = swap(block, "tensor", k)
    blocks[1] = swap(block, "tensor", 1)
    for k in range(2, tensor, 2):
        blocks[k + 1] = swap(blocks[k], "tensor", 1)
    return [blocks[k] for k in range(tensor)]


def sum_blocks(keep, send):
    tensor = lax.axis_size("tensor")
    rows = keep.shape[0] // (tensor // 2)
    paired = (keep + swap(send, "tensor", 1).astype(F32)).reshape(tensor // 2, rows, -1)
    return paired[0], [swap(paired[i].astype(BF16), "tensor", 2 * i) for i in range(1, tensor // 2)]


def slot(relative, size):
    return lax.shift_right_logical(relative, 1) + (relative & 1) * (size // 2)


def tiles(columns):
    for tile in (256, 384, 128):
        if columns % tile == 0:
            return tile
    return columns


def multiply(left, w_ref, write):
    columns = w_ref.shape[1]
    tile = tiles(columns)
    for first in range(0, columns, tile):
        write(first, tile, jnp.dot(left, w_ref[:, first : first + tile], preferred_element_type=F32))


def stack_tokens(x_first, x_second):
    def body(first_ref, second_ref, out_ref):
        out_ref[...] = jnp.concatenate([first_ref[...].astype(F32), second_ref[...].astype(F32)], axis=0).astype(BF16)

    part_dev, features = x_first.shape
    return call(body, shaped((2 * part_dev, features)), (x_first, x_second), [VMEM] * 2)


def cache_piece(where_ref, keys_ref, values_ref, k):
    groups = lax.axis_size("dp")
    head = lax.div((where_ref[0] ^ k) * KVH, groups)
    lanes = pl.ds(pl.multiple_of(head * HD, HD), HD)
    tiles_of = [ref[p, :, lanes].astype(F32) for ref in (keys_ref, values_ref) for p in range(keys_ref.shape[0])]
    return jnp.concatenate(tiles_of, axis=1)


def pack_near(where, x, cache_keys, cache_values):
    part_dev, span, _ = cache_keys.shape
    close = min(lax.axis_size("dp"), 4)
    wide = 2 * part_dev * HD
    joined = x.shape[1] == wide

    def body(where_ref, x_ref, keys_ref, values_ref, own_ref, *out_refs):
        own_ref[...] = cache_piece(where_ref, keys_ref, values_ref, 0).astype(BF16)
        for k, out_ref in enumerate(out_refs, 1):
            piece = cache_piece(where_ref, keys_ref, values_ref, k)
            if joined:
                piece = jnp.concatenate([x_ref[...].astype(F32), piece], axis=0)
            out_ref[...] = piece.astype(BF16)

    height = span + (x.shape[0] if joined else 0)
    own, *near = call(
        body,
        (shaped((span, wide)),) + (shaped((height, wide)),) * (close - 1),
        (where, x, cache_keys, cache_values),
        [SMEM] + [VMEM] * 3,
        flops=2 * AROUND,
    )
    return own, near, joined


def pack_far(where, cache_keys, cache_values, afters):
    groups = lax.axis_size("dp")
    part_dev, span, _ = cache_keys.shape
    wide = 2 * part_dev * HD
    close = min(groups, 4)

    def body(where_ref, keys_ref, values_ref, *refs):
        for i, out_ref in enumerate(refs[len(afters) :]):
            for odd in range(2):
                out_ref[odd] = cache_piece(where_ref, keys_ref, values_ref, close + 2 * i + odd).astype(BF16)

    return call(
        body,
        (shaped((2, span, wide)),) * ((groups - close) // 2),
        (where, cache_keys, cache_values, *afters),
        [SMEM, VMEM, VMEM] + [ANY] * len(afters),
        flops=AROUND,
    )


def collect_near(own, near, span):
    def body(own_ref, *refs):
        refs[-1][0] = own_ref[...]
        for k, ref in enumerate(refs[:-1], 1):
            refs[-1][k] = ref[...].astype(F32)[ref.shape[0] - span :].astype(BF16)

    return call(body, shaped((1 + len(near),) + own.shape), (own, *near), [VMEM] * (1 + len(near)))


def first_entries(pieces, entry):
    def body(*refs):
        for i, ref in enumerate(refs[:-1]):
            refs[-1][i] = ref[entry]

    return call(body, shaped((len(pieces),) + pieces[0].shape[1:]), pieces, [VMEM] * len(pieces))


def collect_far(pieces, passed):
    def body(*refs):
        for i, ref in enumerate(refs[:-2]):
            refs[-1][2 * i] = ref[0]
            refs[-1][2 * i + 1] = refs[-2][i]

    shape = (2 * len(pieces),) + pieces[0].shape[1:]
    return call(body, shaped(shape), (*pieces, passed), [VMEM] * (1 + len(pieces)))


def lift(where_ref, gain_ref, block_refs, h_ref, ss_ref, absolute):
    groups = len(block_refs)
    tensor = lax.axis_size("tensor")
    pair = block_refs[0].shape[0]
    near = groups // tensor
    d, t = where_ref[0], where_ref[1]
    gain = gain_ref[...]
    places = []
    for k in range(groups):
        g = d ^ k
        place = slot(lax.div(g, near) ^ t, tensor) * near + lax.rem(g, near)
        place = pl.multiple_of(place * pair, pair)
        wide = block_refs[k][...].astype(F32)[:pair]
        squares = jnp.broadcast_to(jnp.sum(wide * wide, axis=1, keepdims=True), (pair, 128))
        ss_ref[pl.ds(pl.multiple_of(g * pair, pair) if absolute else place, pair), :] = squares
        h_ref[pl.ds(place, pair), :] = (wide * gain).astype(BF16)
        places.append((pl.multiple_of(g * pair, pair), place))
    return places


def split(total, base, lane):
    high = total.astype(BF16).astype(F32)
    return jnp.where(lane == 0, high, jnp.where(lane == 1, total - high, base))


def project_attention(where, blocks, gain, w_keyval, w_query):
    pair, features = blocks[0].shape
    rows = len(blocks) * pair
    half = rows // 2
    columns = w_keyval.shape[1]
    wide = w_query.shape[1]

    def body(where_ref, gain_ref, *refs):
        block_refs, refs = refs[: len(blocks)], refs[len(blocks) :]
        w_kv_ref, w_q_ref, kv_ref, keep_ref, send_ref, h_ref, ss_ref, product = refs
        places = lift(where_ref, gain_ref, block_refs, h_ref, ss_ref, True)
        h = h_ref[...]
        product[...] = jnp.dot(h, w_kv_ref[...], preferred_element_type=F32)
        for to, place in places:
            kv_ref[pl.ds(to, pair), :columns] = product[pl.ds(place, pair), :].astype(BF16)
        squares = ss_ref[...]
        lane = lax.broadcasted_iota(jnp.int32, squares.shape, 1)
        kv_ref[:, columns:] = split(squares, 0.0, lane).astype(BF16)

        def write(first, tile, product):
            keep_ref[:, first : first + tile] = product[:half]
            send_ref[:, first : first + tile] = product[half:].astype(BF16)

        multiply(h, w_q_ref, write)

    return call(
        body,
        (shaped((rows, columns + 128)), shaped((half, wide), F32), shaped((half, wide))),
        (where, gain[None], *blocks, w_keyval, w_query),
        [SMEM] + [VMEM] * (3 + len(blocks)),
        [pltpu.VMEM((rows, features), BF16), pltpu.VMEM((rows, 128), F32), pltpu.VMEM((rows, columns), F32)],
        flops=2 * rows * (w_keyval.size + w_query.size),
        moved=4 * rows * features + 2 * (w_keyval.size + w_query.size),
    )


def add_keyvals(own, arrived):
    rows, columns = own.shape

    def body(own_ref, arrived_ref, out_ref):
        summed = own_ref[...].astype(F32) + arrived_ref[...].astype(F32)
        ends = summed[:, columns - 128 :]
        lane = lax.broadcasted_iota(jnp.int32, ends.shape, 1)
        out_ref[:, : columns - 128] = summed[:, : columns - 128].astype(BF16)
        out_ref[:, columns - 128 :] = split(ends[:, 0:1] + ends[:, 1:2], ends, lane).astype(BF16)

    return call(body, shaped(own.shape), (own, arrived), [VMEM] * 2, moved=6 * own.size)


def finish_keyvals(where, own, arrived, width):
    groups = lax.axis_size("dp")
    rows, columns = own.shape
    columns -= 128

    def body(where_ref, own_ref, arrived_ref, scale_ref, *out_refs):
        summed = own_ref[...].astype(F32) + arrived_ref[...].astype(F32)
        squares = summed[:, columns : columns + 1] + summed[:, columns + 1 : columns + 2]
        scale = lax.rsqrt(squares / width + EPS)
        scale_ref[...] = jnp.broadcast_to(scale, (rows, 128))
        scaled = summed[:, :columns] * scale
        if groups == KVH:
            lower = where_ref[0] < groups // 2
            out_refs[0][...] = jnp.where(lower, scaled[:, :HD], scaled[:, HD:]).astype(BF16)
            out_refs[1][...] = jnp.where(lower, scaled[:, HD:], scaled[:, :HD]).astype(BF16)
        else:
            out_refs[0][...] = scaled.astype(BF16)

    outs = [shaped((rows, 128), F32)]
    outs += [shaped((rows, HD))] * 2 if groups == KVH else [shaped((rows, columns))]
    return call(body, tuple(outs), (where, own, arrived), [SMEM, VMEM, VMEM], moved=8 * own.size)


def project(h, w):
    half = h.shape[0] // 2

    def body(h_ref, w_ref, keep_ref, send_ref):
        def write(first, tile, product):
            keep_ref[:, first : first + tile] = product[:half]
            send_ref[:, first : first + tile] = product[half:].astype(BF16)

        multiply(h_ref[...], w_ref, write)

    columns = w.shape[1]
    return call(
        body,
        (shaped((half, columns), F32), shaped((half, columns))),
        (h, w),
        [VMEM] * 2,
        flops=4 * half * w.size,
        moved=2 * w.size,
    )


def project_gate(where, blocks, gain, w):
    pair, features = blocks[0].shape
    rows = len(blocks) * pair
    half = rows // 2
    columns = w.shape[1]

    def body(where_ref, gain_ref, *refs):
        block_refs, (w_ref, h_ref, keep_ref, send_ref, ss_ref) = refs[: len(blocks)], refs[len(blocks) :]
        lift(where_ref, gain_ref, block_refs, h_ref, ss_ref, False)

        def write(first, tile, product):
            keep_ref[:, first : first + tile] = product[:half]
            send_ref[:, first : first + tile] = product[half:].astype(BF16)

        multiply(h_ref[...], w_ref, write)
        squares = ss_ref[...]
        high = squares.astype(BF16).astype(F32)
        lane = lax.broadcasted_iota(jnp.int32, squares.shape, 1)
        ends = jnp.where(lane == 0, high, jnp.where(lane == 1, squares - high, 0.0))
        keep_ref[:, columns:] = ends[:half]
        send_ref[:, columns:] = ends[half:].astype(BF16)

    return call(
        body,
        (shaped((rows, features)), shaped((half, columns + 128), F32), shaped((half, columns + 128))),
        (where, gain[None], *blocks, w),
        [SMEM] + [VMEM] * (2 + len(blocks)),
        [pltpu.VMEM((rows, 128), F32)],
        flops=2 * rows * w.size,
        moved=4 * rows * features + 2 * w.size,
    )


def project_back(where, blocks, w):
    groups = lax.axis_size("dp")
    rows, depth = blocks[0].shape
    near = groups // len(blocks)
    pair = rows // near
    total = len(blocks) * rows
    columns = w.shape[1]
    close = min(groups, 4)
    far = (groups - close) // 2

    def body(where_ref, *refs):
        block_refs, (w_ref, *out_refs) = refs[: len(blocks)], refs[len(blocks) :]
        left = out_refs[-1]
        d, t = where_ref[0], where_ref[1]
        for k, block_ref in enumerate(block_refs):
            for i in range(near):
                relative = ((t ^ k) * near + i) ^ d
                beyond = close + lax.shift_right_logical(relative - close, 1) + (relative & 1) * far
                place = jnp.where(relative < close, relative, beyond)
                left[pl.ds(pl.multiple_of(place * pair, pair), pair), :] = block_ref[i * pair : (i + 1) * pair, :]

        def write(first, tile, product):
            lanes = slice(first, first + tile)
            for i in range(close):
                out_refs[i][:, lanes] = product[i * pair : (i + 1) * pair].astype(out_refs[i].dtype)
            middle = (close + far) * pair
            cut = middle + far // 2 * pair
            out_refs[close][:, lanes] = product[close * pair : middle]
            out_refs[close + 1][:, lanes] = product[middle:cut].astype(BF16)
            out_refs[close + 2][:, lanes] = product[cut:].astype(BF16)

        multiply(left[...], w_ref, write)

    outs = [shaped((pair, columns), F32)] + [shaped((pair, columns))] * (close - 1)
    outs += [shaped((far * pair, columns), F32)] + [shaped((far // 2 * pair, columns))] * 2
    return call(
        body,
        tuple(outs),
        (where, *blocks, w),
        [SMEM] + [VMEM] * (1 + len(blocks)),
        [pltpu.VMEM((total, depth), BF16)],
        flops=2 * total * w.size,
        moved=2 * w.size,
    )


def add_pairs(keep, arrived, first, pair):
    def body(keep_ref, arrived_ref, *out_refs):
        for i, out_ref in enumerate(out_refs):
            own = keep_ref[first + i * pair : first + (i + 1) * pair, :]
            out_ref[...] = (own + arrived_ref[i * pair : (i + 1) * pair, :].astype(F32)).astype(BF16)

    outs = (shaped((pair, keep.shape[1])),) * (arrived.shape[0] // pair)
    return call(body, outs, (keep, arrived), [VMEM] * 2, moved=8 * arrived.size)


def sum_rows(parts, pair):
    own, *near, keep, one, two = parts
    sums = add_pairs(keep, swap(one, "dp", 1), 0, pair)
    sums += add_pairs(keep, swap(two, "dp", 1), one.shape[0], pair)
    arrived = [swap(piece, "dp", len(near) + 1 + 2 * i) for i, piece in enumerate(sums)]
    arrived += [swap(piece, "dp", k + 1) for k, piece in enumerate(near)]
    return own, arrived


def finish(own, arrived, x=None):
    def body(own_ref, *refs):
        total = own_ref[...]
        for ref in refs[: len(arrived)]:
            total = total + ref[...].astype(F32)
        rounded = total.astype(BF16)
        if x is None:
            refs[-1][...] = rounded
        else:
            refs[-2][...] = rounded
            refs[-1][...] = (refs[len(arrived)][...].astype(F32) + rounded.astype(F32)).astype(BF16)

    outs = (shaped(own.shape),) * (1 if x is None else 2)
    ins = (own, *arrived) + (() if x is None else (x,))
    return call(body, outs, ins, [VMEM] * len(ins), moved=8 * own.size)


def attend_cached(where, anc, rope, scale, queries, near_cache, far_cache, part_dev):
    tensor = lax.axis_size("tensor")
    groups = lax.axis_size("dp")
    near = groups // tensor
    pair = 2 * part_dev
    close, span, _ = near_cache[0].shape
    ctx = tensor * span
    columns = queries[0].shape[1]
    heads = columns // HD
    parts = near * part_dev
    rows = heads * parts

    def body(where_ref, anc_ref, rope_ref, scale_ref, *refs):
        q_refs, refs = refs[: len(queries)], refs[len(queries) :]
        near_refs, far_refs = refs[:tensor], refs[tensor : 2 * tensor]
        query_ref, mixed_ref, highest_ref, total_ref, keys_ref, values_ref = refs[2 * tensor :]
        d, t = where_ref[0], where_ref[1]
        query_sum = q_refs[0][...]
        for ref in q_refs[1:]:
            query_sum = query_sum + ref[...].astype(F32)
        query_sum = query_sum * scale_ref[pl.ds(pl.multiple_of(t * near * pair, pair), near * pair), 0:1]
        for step in range(2):

            def bring(i, _, step=step):
                particle = t * parts + i if step == 0 else anc_ref[i]
                block, member = lax.div(particle, part_dev) ^ d, lax.rem(particle, part_dev)

                def load(cache_refs, entry):
                    for k, cache_ref in enumerate(cache_refs):
                        to = pl.ds(pl.multiple_of(i * ctx + k * span, 8), span)
                        lanes = pl.ds(pl.multiple_of(member * HD, HD), HD)
                        keys_ref[to, :] = cache_ref[entry, :, lanes].astype(F32)
                        lanes = pl.ds(pl.multiple_of((part_dev + member) * HD, HD), HD)
                        values_ref[to, :] = cache_ref[entry, :, lanes].astype(F32)

                @pl.when(block < close)
                def _():
                    load(near_refs, block)

                @pl.when(block >= close)
                def _():
                    load(far_refs, block - close)

                return 0

            lax.fori_loop(0, parts, bring, 0)
            keys = keys_ref[...].astype(BF16)
            values = values_ref[...].astype(BF16)
            per_head = []
            for h in range(heads):
                for b in range(near):
                    first = b * pair + step * part_dev
                    per_head.append(query_sum[first : first + part_dev, h * HD : (h + 1) * HD])
            query = jnp.concatenate(per_head, axis=0).astype(BF16).astype(F32)
            cosine = rope_ref[2 * step : 2 * step + 1, :]
            sine = rope_ref[2 * step + 1 : 2 * step + 2, :]
            query = (query * cosine + pltpu.roll(query, HD // 2, 1) * sine).astype(BF16)
            scores = lax.dot_general(query, keys, (((1,), (1,)), ((), ())), preferred_element_type=F32)
            scores = scores * (1.0 / math.sqrt(HD))
            row_part = lax.rem(lax.broadcasted_iota(jnp.int32, (rows, 1), 0), parts)
            col_part = lax.div(lax.broadcasted_iota(jnp.int32, (1, parts * ctx), 1), ctx)
            scores = jnp.where(row_part == col_part, scores, MASKED)
            highest = jnp.max(scores, axis=1, keepdims=True)
            weights = jnp.exp(scores - highest)
            here = slice(step * rows, (step + 1) * rows)
            query_ref[here, :] = query
            mixed_ref[here, :] = jnp.dot(weights.astype(BF16), values, preferred_element_type=F32)
            highest_ref[here, :] = jnp.broadcast_to(highest, (rows, 128))
            total_ref[here, :] = jnp.broadcast_to(jnp.sum(weights, axis=1, keepdims=True), (rows, 128))

    ins = (where, anc, rope, scale, *queries, *near_cache, *far_cache)
    return call(
        body,
        (shaped((2 * rows, HD)), shaped((2 * rows, HD), F32), shaped((2 * rows, 128), F32), shaped((2 * rows, 128), F32)),
        ins,
        [SMEM] * 2 + [VMEM] * (len(ins) - 2),
        [pltpu.VMEM((parts * ctx, HD), F32), pltpu.VMEM((parts * ctx, HD), F32)],
        limit=(4 << 20) + 12 * rows * parts * ctx,
        moved=4 << 20,
    )


def attend_new(where, rope, targets, pieces, state, shape, part_dev):
    groups = lax.axis_size("dp")
    tensor = lax.axis_size("tensor")
    near = groups // tensor
    pair = 2 * part_dev
    parts = near * part_dev
    heads = shape[1] // HD
    rows = heads * parts

    def body(where_ref, rope_ref, target_ref, one_ref, two_ref, query_ref, mixed_ref, highest_ref, total_ref, out_ref):
        even = where_ref[0] % 2 == 0 if groups == KVH else True
        one, two = one_ref[...].astype(F32), two_ref[...].astype(F32)
        plain = jnp.where(even, one, two)
        values = jnp.where(even, two, one).astype(BF16)
        cosine = jnp.concatenate([jnp.broadcast_to(rope_ref[2 * s : 2 * s + 1, :], (part_dev, HD)) for s in range(2)])
        sine = jnp.concatenate([jnp.broadcast_to(rope_ref[2 * s + 1 : 2 * s + 2, :], (part_dev, HD)) for s in range(2)])
        turned = pltpu.roll(plain, HD // 2, 1).reshape(groups, pair, HD)
        keys = plain.reshape(groups, pair, HD) * cosine[None] + turned * sine[None]
        keys = keys.reshape(groups * pair, HD).astype(BF16)
        scores = lax.dot_general(query_ref[...], keys, (((1,), (1,)), ((), ())), preferred_element_type=F32)
        scores = scores * (1.0 / math.sqrt(HD))
        col = lax.broadcasted_iota(jnp.int32, (1, groups * pair), 1)
        wanted = (col == target_ref[:, 0:1]) | (col == target_ref[:, 1:2])
        scores = jnp.where(wanted, scores, MASKED)
        before = highest_ref[:, 0:1]
        highest = jnp.maximum(before, jnp.max(scores, axis=1, keepdims=True))
        weights = jnp.exp(scores - highest)
        keep = jnp.exp(before - highest)
        total = total_ref[:, 0:1] * keep + jnp.sum(weights, axis=1, keepdims=True)
        mixed = mixed_ref[...] * keep + jnp.dot(weights.astype(BF16), values, preferred_element_type=F32)
        mixed = mixed / total
        for h in range(heads):
            for b in range(near):
                first = h * parts + b * part_dev
                both = [mixed[s * rows + first : s * rows + first + part_dev] for s in range(2)]
                here = slice(b * pair, (b + 1) * pair)
                out_ref[here, h * HD : (h + 1) * HD] = jnp.concatenate(both, axis=0).astype(BF16)

    ins = (where, rope, targets, *pieces, *state)
    return call(body, shaped(shape), ins, [SMEM] + [VMEM] * (len(ins) - 1), moved=1 << 20)


def move_keyvals(pieces):
    groups = lax.axis_size("dp")
    d = lax.axis_index("dp")
    if groups == KVH:
        half = groups // 2
        one = [(i, 2 * i) for i in range(half)] + [(half + i, 2 * i + 1) for i in range(half)]
        two = [(i, 2 * i + 1) for i in range(half)] + [(half + i, 2 * i) for i in range(half)]
        return [lax.ppermute(x, "dp", to) for x, to in zip(pieces, (one, two))]
    every = lax.all_gather(pieces[0], "dp", axis=1, tiled=True)
    start = (d * KVH // groups) * HD
    return [lax.dynamic_slice_in_dim(every, first + start, HD, axis=1) for first in (0, KVH * HD)]


def local(
    x_first,
    x_second,
    cache_keys,
    cache_values,
    ancestors,
    attn_gain,
    ffn_gain,
    w_query,
    w_keyval,
    w_out,
    w_gate,
    w_up,
    w_down,
):
    groups = lax.axis_size("dp")
    tensor = lax.axis_size("tensor")
    part_dev, features = x_first.shape
    span = cache_keys.shape[1]
    width = features * tensor
    context = span * tensor
    d = lax.axis_index("dp")
    t = lax.axis_index("tensor")
    pair = 2 * part_dev
    near = groups // tensor
    parts = near * part_dev
    where = jnp.stack([d, t]).astype(jnp.int32)

    x = stack_tokens(x_first, x_second)
    own_piece, near_pieces, joined = pack_near(where, x, cache_keys, cache_values)
    blocks = gather_rows(x, near_pieces if joined else None)
    close = min(groups, 4)
    near_moved = blocks[1:close] if joined else [swap(piece, "dp", k) for k, piece in enumerate(near_pieces, 1)]
    near_cache = gather_blocks(collect_near(own_piece, near_moved, span))
    far_pieces = pack_far(where, cache_keys, cache_values, blocks[close::2])
    far_pieces = [swap(piece, "dp", close + 2 * i) for i, piece in enumerate(far_pieces)]
    far_cache = gather_blocks(collect_far(far_pieces, swap(first_entries(far_pieces, 1), "dp", 1)))

    message, *queries = project_attention(where, blocks, attn_gain, w_keyval, w_query)
    bits = 1
    while 2 * bits < tensor:
        message = add_keyvals(message, swap(message, "tensor", bits))
        bits *= 2
    scale, *pieces = finish_keyvals(where, message, swap(message, "tensor", bits), width)
    pieces = move_keyvals(pieces)
    queries, queries_arrived = sum_blocks(*queries)

    own = t * parts + jnp.arange(parts, dtype=jnp.int32)
    anc = lax.dynamic_slice_in_dim(ancestors, t * parts, parts).astype(jnp.int32)
    heads = w_query.shape[1] // HD

    def row_of(particle, step):
        return (particle // part_dev) * pair + step * part_dev + particle % part_dev

    first = jnp.stack([row_of(own, 0)] * 2, axis=1)
    second = jnp.stack([row_of(anc, 0), row_of(own, 1)], axis=1)
    targets = jnp.concatenate([jnp.tile(first, (heads, 1)), jnp.tile(second, (heads, 1))]).astype(jnp.int32)
    rope = jnp.asarray(np.stack(rope_tables(context) + rope_tables(context + 1)))
    state = attend_cached(where, anc, rope, scale, [queries] + queries_arrived, near_cache, far_cache, part_dev)
    mixed = attend_new(where, rope, targets, pieces, state, queries.shape, part_dev)

    parts = project_back(where, gather_blocks(mixed), w_out)
    attn_part, residual = finish(*sum_rows(parts, pair), x)

    hidden_cols = w_gate.shape[1]
    h, keep, send = project_gate(where, gather_rows(residual), ffn_gain, w_gate)
    gate, gate_arrived = sum_blocks(keep, send)
    up, up_arrived = sum_blocks(*project(h, w_up))
    for piece in gate_arrived:
        gate = gate + piece.astype(F32)
    for piece in up_arrived:
        up = up + piece.astype(F32)
    scale = lax.rsqrt((gate[:, hidden_cols] + gate[:, hidden_cols + 1]) / width + EPS)[:, None]
    hidden = jax.nn.silu(gate[:, :hidden_cols] * scale) * (up * scale)
    parts = project_back(where, gather_blocks(hidden.astype(BF16)), w_down)
    (ffn_part,) = finish(*sum_rows(parts, pair))
    return (attn_part.reshape(2, part_dev, features), ffn_part.reshape(2, part_dev, features))


def solution(mesh):
    return jax.shard_map(
        local,
        mesh=mesh,
        in_specs=(
            P("dp", "tensor"),
            P("dp", "tensor"),
            P("dp", "tensor", None),
            P("dp", "tensor", None),
            P(),
            P("tensor"),
            P("tensor"),
            P("tensor", "dp"),
            P("tensor", "dp"),
            P("dp", "tensor"),
            P("tensor", "dp"),
            P("tensor", "dp"),
            P("dp", "tensor"),
        ),
        out_specs=(P(None, "dp", "tensor"), P(None, "dp", "tensor")),
        check_vma=False,
    )
```

```python
import functools
import math

import jax
import jax.numpy as jnp
import numpy as np
from jax import lax
from jax.experimental import pallas as pl
from jax.experimental.pallas import tpu as pltpu
from jax.sharding import PartitionSpec as P

KVH = 8
HD = 128
EPS = 1e-05
ROPE_BASE = 500000.0
MASKED = -1e30
AROUND = 5 << 30
BF16 = jnp.bfloat16
F32 = jnp.float32


def swap(x, axis, bits):
    size = lax.axis_size(axis)
    return lax.ppermute(x, axis, [(i, i ^ bits) for i in range(size)])


def rope_tables(position):
    half = HD // 2
    freq = np.power(np.float32(ROPE_BASE), -2.0 * np.arange(half, dtype=np.float32) / HD)
    angle = (np.float32(position) * freq.astype(np.float32)).astype(np.float32)
    cosine, sine = np.cos(angle), np.sin(angle)
    return (
        np.concatenate([cosine, cosine]).astype(np.float32),
        np.concatenate([-sine, sine]).astype(np.float32),
    )


SMEM = pl.BlockSpec(memory_space=pltpu.SMEM)
VMEM = pl.BlockSpec(memory_space=pltpu.VMEM)
ANY = pl.BlockSpec(memory_space=pl.ANY)
HBM = pl.BlockSpec(memory_space=pltpu.HBM)


def call(body, outs, ins, specs, scratch=(), flops=0, moved=0, limit=8 << 20, around=1):
    return pl.pallas_call(
        body,
        out_shape=outs,
        in_specs=specs,
        out_specs=jax.tree.map(lambda _: VMEM, outs),
        scratch_shapes=scratch,
        compiler_params=pltpu.CompilerParams(vmem_limit_bytes=limit),
        cost_estimate=pl.CostEstimate(flops=flops + around * AROUND, bytes_accessed=moved, transcendentals=0),
    )(*ins)


def shaped(shape, dtype=BF16):
    return jax.ShapeDtypeStruct(shape, dtype)


def gather_rows(rows, near=None):
    groups = lax.axis_size("dp")
    close = min(groups, 4)
    blocks = {0: rows}
    for k in range(groups - 2, close - 1, -2):
        blocks[k] = swap(rows, "dp", k)
    for k in range(close - 1, 0, -1):
        blocks[k] = swap(rows if near is None else near[k - 1], "dp", k)
    for k in range(groups - 2, close - 1, -2):
        blocks[k + 1] = swap(blocks[k], "dp", 1)
    return [blocks[k] for k in range(groups)]


def gather_blocks(block):
    tensor = lax.axis_size("tensor")
    blocks = {0: block}
    for k in range(2, tensor, 2):
        blocks[k] = swap(block, "tensor", k)
    blocks[1] = swap(block, "tensor", 1)
    for k in range(2, tensor, 2):
        blocks[k + 1] = swap(blocks[k], "tensor", 1)
    return [blocks[k] for k in range(tensor)]


def sum_blocks(keep, send):
    tensor = lax.axis_size("tensor")
    rows = keep.shape[0] // (tensor // 2)
    paired = (keep + swap(send, "tensor", 1).astype(F32)).reshape(tensor // 2, rows, -1)
    return paired[0], [swap(paired[i].astype(BF16), "tensor", 2 * i) for i in range(1, tensor // 2)]


def slot(relative, size):
    return lax.shift_right_logical(relative, 1) + (relative & 1) * (size // 2)


def tiles(columns):
    for tile in (256, 384, 128):
        if columns % tile == 0:
            return tile
    return columns


def multiply(left, w_ref, write):
    columns = w_ref.shape[1]
    tile = tiles(columns)
    for first in range(0, columns, tile):
        write(first, tile, jnp.dot(left, w_ref[:, first : first + tile], preferred_element_type=F32))


def stack_tokens(x_first, x_second):
    def body(first_ref, second_ref, out_ref):
        out_ref[...] = jnp.concatenate([first_ref[...].astype(F32), second_ref[...].astype(F32)], axis=0).astype(BF16)

    part_dev, features = x_first.shape
    return call(body, shaped((2 * part_dev, features)), (x_first, x_second), [VMEM] * 2)


def cache_piece(where_ref, keys_ref, values_ref, k):
    groups = lax.axis_size("dp")
    head = lax.div((where_ref[0] ^ k) * KVH, groups)
    lanes = pl.ds(pl.multiple_of(head * HD, HD), HD)
    tiles_of = [ref[p, :, lanes].astype(F32) for ref in (keys_ref, values_ref) for p in range(keys_ref.shape[0])]
    return jnp.concatenate(tiles_of, axis=1)


def pack_near(where, x, cache_keys, cache_values):
    part_dev, span, _ = cache_keys.shape
    close = min(lax.axis_size("dp"), 4)
    wide = 2 * part_dev * HD
    joined = x.shape[1] == wide

    def body(where_ref, x_ref, keys_ref, values_ref, own_ref, *out_refs):
        own_ref[...] = cache_piece(where_ref, keys_ref, values_ref, 0).astype(BF16)
        for k, out_ref in enumerate(out_refs, 1):
            piece = cache_piece(where_ref, keys_ref, values_ref, k)
            if joined:
                piece = jnp.concatenate([x_ref[...].astype(F32), piece], axis=0)
            out_ref[...] = piece.astype(BF16)

    height = span + (x.shape[0] if joined else 0)
    own, *near = call(
        body,
        (shaped((span, wide)),) + (shaped((height, wide)),) * (close - 1),
        (where, x, cache_keys, cache_values),
        [SMEM] + [VMEM] * 3,
        flops=2 * AROUND,
    )
    return own, near, joined


def pack_far(where, cache_keys, cache_values, afters):
    groups = lax.axis_size("dp")
    part_dev, span, _ = cache_keys.shape
    wide = 2 * part_dev * HD
    close = min(groups, 4)

    def body(where_ref, keys_ref, values_ref, *refs):
        for i, out_ref in enumerate(refs[len(afters) :]):
            for odd in range(2):
                out_ref[odd] = cache_piece(where_ref, keys_ref, values_ref, close + 2 * i + odd).astype(BF16)

    return call(
        body,
        (shaped((2, span, wide)),) * ((groups - close) // 2),
        (where, cache_keys, cache_values, *afters),
        [SMEM, VMEM, VMEM] + [ANY] * len(afters),
        flops=AROUND,
    )


def collect_near(own, near, span):
    def body(own_ref, *refs):
        refs[-1][0] = own_ref[...]
        for k, ref in enumerate(refs[:-1], 1):
            refs[-1][k] = ref[...].astype(F32)[ref.shape[0] - span :].astype(BF16)

    return call(body, shaped((1 + len(near),) + own.shape), (own, *near), [VMEM] * (1 + len(near)), around=1)


def last_entries(pieces, after):
    def body(after_ref, *refs):
        for i, ref in enumerate(refs[:-1]):
            refs[-1][i] = ref[1]

    ins = (after, *pieces)
    return call(body, shaped((len(pieces),) + pieces[0].shape[1:]), ins, [ANY] + [VMEM] * len(pieces), around=1)


def collect_far(pieces, passed):
    def body(*refs):
        for i, ref in enumerate(refs[:-2]):
            refs[-1][2 * i] = ref[0]
            refs[-1][2 * i + 1] = refs[-2][i]

    shape = (2 * len(pieces),) + pieces[0].shape[1:]
    return call(body, shaped(shape), (*pieces, passed), [VMEM] * (1 + len(pieces)), around=1)


def lift(where_ref, gain_ref, block_refs, h_ref, ss_ref, absolute):
    groups = len(block_refs)
    tensor = lax.axis_size("tensor")
    pair = block_refs[0].shape[0]
    near = groups // tensor
    d, t = where_ref[0], where_ref[1]
    gain = gain_ref[...]
    places = []
    for k in range(groups):
        g = d ^ k
        place = slot(lax.div(g, near) ^ t, tensor) * near + lax.rem(g, near)
        place = pl.multiple_of(place * pair, pair)
        wide = block_refs[k][...].astype(F32)[:pair]
        squares = jnp.broadcast_to(jnp.sum(wide * wide, axis=1, keepdims=True), (pair, 128))
        ss_ref[pl.ds(pl.multiple_of(g * pair, pair) if absolute else place, pair), :] = squares
        h_ref[pl.ds(place, pair), :] = (wide * gain).astype(BF16)
        places.append((pl.multiple_of(g * pair, pair), place))
    return places


def split(total, base, lane):
    high = total.astype(BF16).astype(F32)
    return jnp.where(lane == 0, high, jnp.where(lane == 1, total - high, base))


def stacked(rows, parts):
    width = rows.shape[1] // parts
    return jnp.concatenate([rows[:, i * width : (i + 1) * width] for i in range(parts)], axis=0)


def unstacked(rows, parts):
    height = rows.shape[0] // parts
    return jnp.concatenate([rows[i * height : (i + 1) * height] for i in range(parts)], axis=1)


def project_attention(where, blocks, gain, w_keyval, w_query, after):
    pair, features = blocks[0].shape
    rows = len(blocks) * pair
    half = rows // 2
    columns = w_keyval.shape[1]
    wide = w_query.shape[1]
    base = columns + 128

    def body(where_ref, gain_ref, *refs):
        block_refs, refs = refs[: len(blocks)], refs[len(blocks) :]
        w_kv_ref, w_q_ref, after_ref, message_ref, keep_ref, h_ref, ss_ref, product = refs
        places = lift(where_ref, gain_ref, block_refs, h_ref, ss_ref, True)
        h = h_ref[...]
        product[...] = jnp.dot(h, w_kv_ref[...], preferred_element_type=F32)
        for to, place in places:
            message_ref[pl.ds(to, pair), :columns] = product[pl.ds(place, pair), :].astype(BF16)
        squares = ss_ref[...]
        lane = lax.broadcasted_iota(jnp.int32, squares.shape, 1)
        message_ref[:, columns:base] = split(squares, 0.0, lane).astype(BF16)
        tile = tiles(wide // 2)
        for first in range(0, wide, tile):
            queries = jnp.dot(h, w_q_ref[:, first : first + tile], preferred_element_type=F32)
            keep_ref[:, first : first + tile] = queries[:half]
            below, lanes = divmod(first, wide // 2)
            lanes += base
            message_ref[below * half : (below + 1) * half, lanes : lanes + tile] = queries[half:].astype(BF16)

    return call(
        body,
        (shaped((rows, base + wide // 2)), shaped((half, wide), F32)),
        (where, gain[None], *blocks, w_keyval, w_query, after),
        [SMEM] + [VMEM] * (3 + len(blocks)) + [ANY],
        [pltpu.VMEM((rows, features), BF16), pltpu.VMEM((rows, 128), F32), pltpu.VMEM((rows, columns), F32)],
        flops=2 * rows * (w_keyval.size + w_query.size),
        moved=4 * rows * features + 2 * (w_keyval.size + w_query.size),
    )


def add_cores(own, keep, arrived):
    tensor = lax.axis_size("tensor")
    rows, total = own.shape
    half, wide = keep.shape
    base = total - wide // 2
    height = 2 * half // tensor
    joined = tensor == 4

    def body(own_ref, keep_ref, arrived_ref, first_ref, message_ref, *out_refs):
        summed = own_ref[:, :base].astype(F32) + arrived_ref[:, :base].astype(F32)
        ends = summed[:, base - 128 :]
        lane = lax.broadcasted_iota(jnp.int32, ends.shape, 1)
        message_ref[:, : base - 128] = summed[:, : base - 128].astype(BF16)
        message_ref[:, base - 128 : base] = split(ends[:, 0:1] + ends[:, 1:2], ends, lane).astype(BF16)
        queries = keep_ref[...] + unstacked(arrived_ref[:, base:].astype(F32), 2)
        first_ref[...] = queries[:height]
        if joined:
            message_ref[:, base:] = stacked(queries[height:], 4).astype(BF16)
        for i, out_ref in enumerate(out_refs, 1):
            out_ref[...] = queries[i * height : (i + 1) * height].astype(BF16)

    outs = [shaped((height, wide), F32), shaped((rows, base + (wide // 4 if joined else 0)))]
    outs += [] if joined else [shaped((height, wide))] * (tensor // 2 - 1)
    return call(body, tuple(outs), (own, keep, arrived), [VMEM] * 3, moved=6 * own.size, around=1)


def add_keyvals(own, arrived):
    rows, columns = own.shape

    def body(own_ref, arrived_ref, out_ref):
        summed = own_ref[...].astype(F32) + arrived_ref[...].astype(F32)
        ends = summed[:, columns - 128 :]
        lane = lax.broadcasted_iota(jnp.int32, ends.shape, 1)
        out_ref[:, : columns - 128] = summed[:, : columns - 128].astype(BF16)
        out_ref[:, columns - 128 :] = split(ends[:, 0:1] + ends[:, 1:2], ends, lane).astype(BF16)

    return call(body, shaped(own.shape), (own, arrived), [VMEM] * 2, moved=6 * own.size)


def finish_keyvals(where, own, arrived, columns, width):
    groups = lax.axis_size("dp")
    rows = own.shape[0]
    lanes = slice(0, columns + 128)

    def body(where_ref, own_ref, arrived_ref, scale_ref, *out_refs):
        summed = own_ref[:, lanes].astype(F32) + arrived_ref[:, lanes].astype(F32)
        squares = summed[:, columns : columns + 1] + summed[:, columns + 1 : columns + 2]
        scale = lax.rsqrt(squares / width + EPS)
        scale_ref[...] = jnp.broadcast_to(scale, (rows, 128))
        scaled = summed[:, :columns] * scale
        if groups == KVH:
            lower = where_ref[0] < groups // 2
            out_refs[0][...] = jnp.where(lower, scaled[:, :HD], scaled[:, HD:]).astype(BF16)
            out_refs[1][...] = jnp.where(lower, scaled[:, HD:], scaled[:, :HD]).astype(BF16)
        else:
            out_refs[0][...] = scaled.astype(BF16)

    outs = [shaped((rows, 128), F32)]
    outs += [shaped((rows, HD))] * 2 if groups == KVH else [shaped((rows, columns))]
    return call(body, tuple(outs), (where, own, arrived), [SMEM, VMEM, VMEM], moved=8 * own.size, around=1)


def project(h, w):
    half = h.shape[0] // 2

    def body(h_ref, w_ref, keep_ref, send_ref):
        def write(first, tile, product):
            keep_ref[:, first : first + tile] = product[:half]
            send_ref[:, first : first + tile] = product[half:].astype(BF16)

        multiply(h_ref[...], w_ref, write)

    columns = w.shape[1]
    return call(
        body,
        (shaped((half, columns), F32), shaped((half, columns))),
        (h, w),
        [VMEM] * 2,
        flops=4 * half * w.size,
        moved=2 * w.size,
    )


def project_gate(where, blocks, gain, w):
    pair, features = blocks[0].shape
    rows = len(blocks) * pair
    half = rows // 2
    columns = w.shape[1]

    def body(where_ref, gain_ref, *refs):
        block_refs, (w_ref, h_ref, keep_ref, send_ref, ss_ref) = refs[: len(blocks)], refs[len(blocks) :]
        lift(where_ref, gain_ref, block_refs, h_ref, ss_ref, False)

        def write(first, tile, product):
            keep_ref[:, first : first + tile] = product[:half]
            send_ref[:, first : first + tile] = product[half:].astype(BF16)

        multiply(h_ref[...], w_ref, write)
        squares = ss_ref[...]
        high = squares.astype(BF16).astype(F32)
        lane = lax.broadcasted_iota(jnp.int32, squares.shape, 1)
        ends = jnp.where(lane == 0, high, jnp.where(lane == 1, squares - high, 0.0))
        keep_ref[:, columns:] = ends[:half]
        send_ref[:, columns:] = ends[half:].astype(BF16)

    return call(
        body,
        (shaped((rows, features)), shaped((half, columns + 128), F32), shaped((half, columns + 128))),
        (where, gain[None], *blocks, w),
        [SMEM] + [VMEM] * (2 + len(blocks)),
        [pltpu.VMEM((rows, 128), F32)],
        flops=2 * rows * w.size,
        moved=4 * rows * features + 2 * w.size,
    )


def project_back(where, blocks, w):
    groups = lax.axis_size("dp")
    rows, depth = blocks[0].shape
    near = groups // len(blocks)
    pair = rows // near
    total = len(blocks) * rows
    columns = w.shape[1]
    close = min(groups, 4)
    far = (groups - close) // 2

    def body(where_ref, *refs):
        block_refs, (w_ref, *out_refs) = refs[: len(blocks)], refs[len(blocks) :]
        left = out_refs[-1]
        d, t = where_ref[0], where_ref[1]
        for k, block_ref in enumerate(block_refs):
            for i in range(near):
                relative = ((t ^ k) * near + i) ^ d
                beyond = close + lax.shift_right_logical(relative - close, 1) + (relative & 1) * far
                place = jnp.where(relative < close, relative, beyond)
                left[pl.ds(pl.multiple_of(place * pair, pair), pair), :] = block_ref[i * pair : (i + 1) * pair, :]

        def write(first, tile, product):
            lanes = slice(first, first + tile)
            for i in range(close):
                out_refs[i][:, lanes] = product[i * pair : (i + 1) * pair].astype(out_refs[i].dtype)
            middle = (close + far) * pair
            cut = middle + far // 2 * pair
            out_refs[close][:, lanes] = product[close * pair : middle]
            out_refs[close + 1][:, lanes] = product[middle:cut].astype(BF16)
            out_refs[close + 2][:, lanes] = product[cut:].astype(BF16)

        multiply(left[...], w_ref, write)

    outs = [shaped((pair, columns), F32)] + [shaped((pair, columns))] * (close - 1)
    outs += [shaped((far * pair, columns), F32)] + [shaped((far // 2 * pair, columns))] * 2
    return call(
        body,
        tuple(outs),
        (where, *blocks, w),
        [SMEM] + [VMEM] * (1 + len(blocks)),
        [pltpu.VMEM((total, depth), BF16)],
        flops=2 * total * w.size,
        moved=2 * w.size,
    )


def add_pairs(keep, arrived, first, pair, passed=()):
    count = arrived.shape[0] // pair

    def body(keep_ref, arrived_ref, *refs):
        for i, out_ref in enumerate(refs[len(passed) : len(passed) + count]):
            own = keep_ref[first + i * pair : first + (i + 1) * pair, :]
            out_ref[...] = (own + arrived_ref[i * pair : (i + 1) * pair, :].astype(F32)).astype(BF16)
        for ref, out_ref in zip(refs[: len(passed)], refs[len(passed) + count :]):
            out_ref[...] = ref[...]

    outs = (shaped((pair, keep.shape[1])),) * (count + len(passed))
    ins = (keep, arrived, *passed)
    return call(body, outs, ins, [VMEM] * len(ins), moved=8 * arrived.size)


def sum_rows(parts, pair):
    own, *near, keep, one, two = parts
    count = one.shape[0] // pair
    sums = add_pairs(keep, swap(one, "dp", 1), 0, pair, near[:2])
    sums, near = list(sums[:count]), [*sums[count:], *near[2:]]
    sums += add_pairs(keep, swap(two, "dp", 1), one.shape[0], pair)
    arrived = [swap(piece, "dp", len(near) + 1 + 2 * i) for i, piece in enumerate(sums)]
    arrived += [swap(piece, "dp", k + 1) for k, piece in enumerate(near)]
    return own, arrived


def finish(own, arrived, x=None):
    def body(own_ref, *refs):
        total = own_ref[...]
        for ref in refs[: len(arrived)]:
            total = total + ref[...].astype(F32)
        rounded = total.astype(BF16)
        if x is None:
            refs[-1][...] = rounded
        else:
            refs[-2][...] = rounded
            refs[-1][...] = (refs[len(arrived)][...].astype(F32) + rounded.astype(F32)).astype(BF16)

    outs = (shaped(own.shape),) * (1 if x is None else 2)
    ins = (own, *arrived) + (() if x is None else (x,))
    return call(body, outs, ins, [VMEM] * len(ins), moved=8 * own.size)


def attend_cached(where, anc, rope, scale, queries, near_cache, far_cache, part_dev):
    tensor = lax.axis_size("tensor")
    groups = lax.axis_size("dp")
    near = groups // tensor
    pair = 2 * part_dev
    close, span, _ = near_cache[0].shape
    ctx = tensor * span
    height, columns = queries[0].shape
    heads = columns // HD
    parts = near * part_dev
    rows = heads * parts

    def body(where_ref, anc_ref, rope_ref, scale_ref, *refs):
        q_refs, refs = refs[: len(queries)], refs[len(queries) :]
        near_refs, far_refs = refs[:tensor], refs[tensor : 2 * tensor]
        query_ref, mixed_ref, highest_ref, total_ref, keys_ref, values_ref = refs[2 * tensor :]
        d, t = where_ref[0], where_ref[1]
        query_sum = q_refs[0][...]
        for ref in q_refs[1:]:
            if ref.shape[0] == height:
                query_sum = query_sum + ref[...].astype(F32)
            else:
                lanes = slice(ref.shape[1] - columns // 4, ref.shape[1])
                query_sum = query_sum + unstacked(ref[:, lanes].astype(F32), 4)
        query_sum = query_sum * scale_ref[pl.ds(pl.multiple_of(t * near * pair, pair), near * pair), 0:1]
        for step in range(2):

            def bring(i, _, step=step):
                particle = t * parts + i if step == 0 else anc_ref[i]
                block, member = lax.div(particle, part_dev) ^ d, lax.rem(particle, part_dev)

                def load(cache_refs, entry):
                    for k, cache_ref in enumerate(cache_refs):
                        to = pl.ds(pl.multiple_of(i * ctx + k * span, 8), span)
                        lanes = pl.ds(pl.multiple_of(member * HD, HD), HD)
                        keys_ref[to, :] = cache_ref[entry, :, lanes].astype(F32)
                        lanes = pl.ds(pl.multiple_of((part_dev + member) * HD, HD), HD)
                        values_ref[to, :] = cache_ref[entry, :, lanes].astype(F32)

                @pl.when(block < close)
                def _():
                    load(near_refs, block)

                @pl.when(block >= close)
                def _():
                    load(far_refs, block - close)

                return 0

            lax.fori_loop(0, parts, bring, 0)
            keys = keys_ref[...].astype(BF16)
            values = values_ref[...].astype(BF16)
            per_head = []
            for h in range(heads):
                for b in range(near):
                    first = b * pair + step * part_dev
                    per_head.append(query_sum[first : first + part_dev, h * HD : (h + 1) * HD])
            query = jnp.concatenate(per_head, axis=0).astype(BF16).astype(F32)
            cosine = rope_ref[2 * step : 2 * step + 1, :]
            sine = rope_ref[2 * step + 1 : 2 * step + 2, :]
            query = (query * cosine + pltpu.roll(query, HD // 2, 1) * sine).astype(BF16)
            scores = lax.dot_general(query, keys, (((1,), (1,)), ((), ())), preferred_element_type=F32)
            scores = scores * (1.0 / math.sqrt(HD))
            row_part = lax.rem(lax.broadcasted_iota(jnp.int32, (rows, 1), 0), parts)
            col_part = lax.div(lax.broadcasted_iota(jnp.int32, (1, parts * ctx), 1), ctx)
            scores = jnp.where(row_part == col_part, scores, MASKED)
            highest = jnp.max(scores, axis=1, keepdims=True)
            weights = jnp.exp(scores - highest)
            here = slice(step * rows, (step + 1) * rows)
            query_ref[here, :] = query
            mixed_ref[here, :] = jnp.dot(weights.astype(BF16), values, preferred_element_type=F32)
            highest_ref[here, :] = jnp.broadcast_to(highest, (rows, 128))
            total_ref[here, :] = jnp.broadcast_to(jnp.sum(weights, axis=1, keepdims=True), (rows, 128))

    ins = (where, anc, rope, scale, *queries, *near_cache, *far_cache)
    return call(
        body,
        (shaped((2 * rows, HD)), shaped((2 * rows, HD), F32), shaped((2 * rows, 128), F32), shaped((2 * rows, 128), F32)),
        ins,
        [SMEM] * 2 + [VMEM] * (len(ins) - 2),
        [pltpu.VMEM((parts * ctx, HD), F32), pltpu.VMEM((parts * ctx, HD), F32)],
        limit=(4 << 20) + 12 * rows * parts * ctx,
        moved=4 << 20,
    )


def attend_new(where, rope, targets, pieces, state, shape, part_dev):
    groups = lax.axis_size("dp")
    tensor = lax.axis_size("tensor")
    near = groups // tensor
    pair = 2 * part_dev
    parts = near * part_dev
    heads = shape[1] // HD
    rows = heads * parts

    def body(where_ref, rope_ref, target_ref, one_ref, two_ref, query_ref, mixed_ref, highest_ref, total_ref, out_ref):
        even = where_ref[0] % 2 == 0 if groups == KVH else True
        one, two = one_ref[...].astype(F32), two_ref[...].astype(F32)
        plain = jnp.where(even, one, two)
        values = jnp.where(even, two, one).astype(BF16)
        cosine = jnp.concatenate([jnp.broadcast_to(rope_ref[2 * s : 2 * s + 1, :], (part_dev, HD)) for s in range(2)])
        sine = jnp.concatenate([jnp.broadcast_to(rope_ref[2 * s + 1 : 2 * s + 2, :], (part_dev, HD)) for s in range(2)])
        turned = pltpu.roll(plain, HD // 2, 1).reshape(groups, pair, HD)
        keys = plain.reshape(groups, pair, HD) * cosine[None] + turned * sine[None]
        keys = keys.reshape(groups * pair, HD).astype(BF16)
        scores = lax.dot_general(query_ref[...], keys, (((1,), (1,)), ((), ())), preferred_element_type=F32)
        scores = scores * (1.0 / math.sqrt(HD))
        col = lax.broadcasted_iota(jnp.int32, (1, groups * pair), 1)
        wanted = (col == target_ref[:, 0:1]) | (col == target_ref[:, 1:2])
        scores = jnp.where(wanted, scores, MASKED)
        before = highest_ref[:, 0:1]
        highest = jnp.maximum(before, jnp.max(scores, axis=1, keepdims=True))
        weights = jnp.exp(scores - highest)
        keep = jnp.exp(before - highest)
        total = total_ref[:, 0:1] * keep + jnp.sum(weights, axis=1, keepdims=True)
        mixed = mixed_ref[...] * keep + jnp.dot(weights.astype(BF16), values, preferred_element_type=F32)
        mixed = mixed / total
        for h in range(heads):
            for b in range(near):
                first = h * parts + b * part_dev
                both = [mixed[s * rows + first : s * rows + first + part_dev] for s in range(2)]
                here = slice(b * pair, (b + 1) * pair)
                out_ref[here, h * HD : (h + 1) * HD] = jnp.concatenate(both, axis=0).astype(BF16)

    ins = (where, rope, targets, *pieces, *state)
    return call(body, shaped(shape), ins, [SMEM] + [VMEM] * (len(ins) - 1), moved=1 << 20)


def move_keyvals(pieces):
    groups = lax.axis_size("dp")
    d = lax.axis_index("dp")
    if groups == KVH:
        half = groups // 2
        one = [(i, 2 * i) for i in range(half)] + [(half + i, 2 * i + 1) for i in range(half)]
        two = [(i, 2 * i + 1) for i in range(half)] + [(half + i, 2 * i) for i in range(half)]
        return [lax.ppermute(x, "dp", to) for x, to in zip(pieces, (one, two))]
    every = lax.all_gather(pieces[0], "dp", axis=1, tiled=True)
    start = (d * KVH // groups) * HD
    return [lax.dynamic_slice_in_dim(every, first + start, HD, axis=1) for first in (0, KVH * HD)]


def local(
    x_first,
    x_second,
    cache_keys,
    cache_values,
    ancestors,
    attn_gain,
    ffn_gain,
    w_query,
    w_keyval,
    w_out,
    w_gate,
    w_up,
    w_down,
):
    groups = lax.axis_size("dp")
    tensor = lax.axis_size("tensor")
    part_dev, features = x_first.shape
    span = cache_keys.shape[1]
    width = features * tensor
    context = span * tensor
    d = lax.axis_index("dp")
    t = lax.axis_index("tensor")
    pair = 2 * part_dev
    near = groups // tensor
    parts = near * part_dev
    where = jnp.stack([d, t]).astype(jnp.int32)

    x = stack_tokens(x_first, x_second)
    own_piece, near_pieces, joined = pack_near(where, x, cache_keys, cache_values)
    blocks = gather_rows(x, near_pieces if joined else None)
    close = min(groups, 4)
    near_moved = blocks[1:close] if joined else [swap(piece, "dp", k) for k, piece in enumerate(near_pieces, 1)]
    near_cache = gather_blocks(collect_near(own_piece, near_moved, span))
    packed = pack_far(where, cache_keys, cache_values, blocks[close::2])
    far_pieces = [swap(piece, "dp", close + 2 * i) for i, piece in enumerate(packed)]

    message, keep = project_attention(where, blocks, attn_gain, w_keyval, w_query, x)
    queries, message, *leaving = add_cores(message, keep, swap(message, "tensor", 1))
    passed = swap(last_entries(far_pieces, x), "dp", 1)
    far_cache = gather_blocks(collect_far(far_pieces, passed))
    bits = 2
    while 2 * bits < tensor:
        message = add_keyvals(message, swap(message, "tensor", bits))
        bits *= 2
    arrived = swap(message, "tensor", bits)
    scale, *pieces = finish_keyvals(where, message, arrived, w_keyval.shape[1], width)
    pieces = move_keyvals(pieces)
    queries = [queries] + ([swap(x, "tensor", 2 * i) for i, x in enumerate(leaving, 1)] if leaving else [arrived])

    own = t * parts + jnp.arange(parts, dtype=jnp.int32)
    anc = lax.dynamic_slice_in_dim(ancestors, t * parts, parts).astype(jnp.int32)
    heads = w_query.shape[1] // HD

    def row_of(particle, step):
        return (particle // part_dev) * pair + step * part_dev + particle % part_dev

    first = jnp.stack([row_of(own, 0)] * 2, axis=1)
    second = jnp.stack([row_of(anc, 0), row_of(own, 1)], axis=1)
    targets = jnp.concatenate([jnp.tile(first, (heads, 1)), jnp.tile(second, (heads, 1))]).astype(jnp.int32)
    rope = jnp.asarray(np.stack(rope_tables(context) + rope_tables(context + 1)))
    state = attend_cached(where, anc, rope, scale, queries, near_cache, far_cache, part_dev)
    mixed = attend_new(where, rope, targets, pieces, state, queries[0].shape, part_dev)

    parts = project_back(where, gather_blocks(mixed), w_out)
    attn_part, residual = finish(*sum_rows(parts, pair), x)

    hidden_cols = w_gate.shape[1]
    h, keep, send = project_gate(where, gather_rows(residual), ffn_gain, w_gate)
    gate, gate_arrived = sum_blocks(keep, send)
    up, up_arrived = sum_blocks(*project(h, w_up))
    for piece in gate_arrived:
        gate = gate + piece.astype(F32)
    for piece in up_arrived:
        up = up + piece.astype(F32)
    scale = lax.rsqrt((gate[:, hidden_cols] + gate[:, hidden_cols + 1]) / width + EPS)[:, None]
    hidden = jax.nn.silu(gate[:, :hidden_cols] * scale) * (up * scale)
    parts = project_back(where, gather_blocks(hidden.astype(BF16)), w_down)
    (ffn_part,) = finish(*sum_rows(parts, pair))
    return (attn_part.reshape(2, part_dev, features), ffn_part.reshape(2, part_dev, features))


def solution(mesh):
    return jax.shard_map(
        local,
        mesh=mesh,
        in_specs=(
            P("dp", "tensor"),
            P("dp", "tensor"),
            P("dp", "tensor", None),
            P("dp", "tensor", None),
            P(),
            P("tensor"),
            P("tensor"),
            P("tensor", "dp"),
            P("tensor", "dp"),
            P("dp", "tensor"),
            P("tensor", "dp"),
            P("tensor", "dp"),
            P("dp", "tensor"),
        ),
        out_specs=(P(None, "dp", "tensor"), P(None, "dp", "tensor")),
        check_vma=False,
    )
```

```python
import functools
import math

import jax
import jax.numpy as jnp
import numpy as np
from jax import lax
from jax.experimental import pallas as pl
from jax.experimental.pallas import tpu as pltpu
from jax.sharding import PartitionSpec as P

KVH = 8
HD = 128
EPS = 1e-05
ROPE_BASE = 500000.0
MASKED = -1e30
AROUND = 5 << 30
BF16 = jnp.bfloat16
F32 = jnp.float32


def swap(x, axis, bits):
    size = lax.axis_size(axis)
    return lax.ppermute(x, axis, [(i, i ^ bits) for i in range(size)])


def rope_tables(position):
    half = HD // 2
    freq = np.power(np.float32(ROPE_BASE), -2.0 * np.arange(half, dtype=np.float32) / HD)
    angle = (np.float32(position) * freq.astype(np.float32)).astype(np.float32)
    cosine, sine = np.cos(angle), np.sin(angle)
    return (
        np.concatenate([cosine, cosine]).astype(np.float32),
        np.concatenate([-sine, sine]).astype(np.float32),
    )


SMEM = pl.BlockSpec(memory_space=pltpu.SMEM)
VMEM = pl.BlockSpec(memory_space=pltpu.VMEM)
ANY = pl.BlockSpec(memory_space=pl.ANY)
HBM = pl.BlockSpec(memory_space=pltpu.HBM)


def call(body, outs, ins, specs, scratch=(), flops=0, moved=0, limit=8 << 20, around=1):
    return pl.pallas_call(
        body,
        out_shape=outs,
        in_specs=specs,
        out_specs=jax.tree.map(lambda _: VMEM, outs),
        scratch_shapes=scratch,
        compiler_params=pltpu.CompilerParams(vmem_limit_bytes=limit),
        cost_estimate=pl.CostEstimate(flops=flops + around * AROUND, bytes_accessed=moved, transcendentals=0),
    )(*ins)


def shaped(shape, dtype=BF16):
    return jax.ShapeDtypeStruct(shape, dtype)


def far_split(groups):
    close = min(groups, 4)
    return close, close + (groups - close) // 4 * 2


def arrival_order(groups, passing):
    close, _ = far_split(groups)
    far = [*range(close, passing, 2), *range(close - 1, 1, -1), *range(groups - 1, passing - 1, -1)]
    return [0, *far, *range(close + 1, passing, 2), 1]


def gather_rows(rows, passing, near=None):
    groups = lax.axis_size("dp")
    close, _ = far_split(groups)
    blocks = {0: rows}
    for k in [*range(close, passing, 2), *range(passing, groups)]:
        blocks[k] = swap(rows, "dp", k)
    for k in range(close - 1, 0, -1):
        blocks[k] = swap(rows if near is None else near[k - 1], "dp", k)
    for k in range(close, passing, 2):
        blocks[k + 1] = swap(blocks[k], "dp", 1)
    return [blocks[k] for k in range(groups)]


def gather_blocks(block):
    tensor = lax.axis_size("tensor")
    blocks = {0: block}
    for k in range(2, tensor, 2):
        blocks[k] = swap(block, "tensor", k)
    blocks[1] = swap(block, "tensor", 1)
    for k in range(2, tensor, 2):
        blocks[k + 1] = swap(blocks[k], "tensor", 1)
    return [blocks[k] for k in range(tensor)]


def sum_blocks(keep, send):
    tensor = lax.axis_size("tensor")
    rows = keep.shape[0] // (tensor // 2)
    paired = (keep + swap(send, "tensor", 1).astype(F32)).reshape(tensor // 2, rows, -1)
    return paired[0], [swap(paired[i].astype(BF16), "tensor", 2 * i) for i in range(1, tensor // 2)]


def slot(relative, size):
    return lax.shift_right_logical(relative, 1) + (relative & 1) * (size // 2)


def tiles(columns):
    for tile in (256, 384, 128):
        if columns % tile == 0:
            return tile
    return columns


def multiply(left, w_ref, write):
    columns = w_ref.shape[1]
    tile = tiles(columns)
    for first in range(0, columns, tile):
        write(first, tile, jnp.dot(left, w_ref[:, first : first + tile], preferred_element_type=F32))


def stack_tokens(x_first, x_second):
    def body(first_ref, second_ref, out_ref):
        out_ref[...] = jnp.concatenate([first_ref[...].astype(F32), second_ref[...].astype(F32)], axis=0).astype(BF16)

    part_dev, features = x_first.shape
    return call(body, shaped((2 * part_dev, features)), (x_first, x_second), [VMEM] * 2)


def cache_piece(where_ref, keys_ref, values_ref, k):
    groups = lax.axis_size("dp")
    head = lax.div((where_ref[0] ^ k) * KVH, groups)
    lanes = pl.ds(pl.multiple_of(head * HD, HD), HD)
    tiles_of = [ref[p, :, lanes].astype(F32) for ref in (keys_ref, values_ref) for p in range(keys_ref.shape[0])]
    return jnp.concatenate(tiles_of, axis=1)


def pack_near(where, x, cache_keys, cache_values):
    part_dev, span, _ = cache_keys.shape
    close = min(lax.axis_size("dp"), 4)
    wide = 2 * part_dev * HD
    joined = x.shape[1] == wide

    def body(where_ref, x_ref, keys_ref, values_ref, own_ref, *out_refs):
        own_ref[...] = cache_piece(where_ref, keys_ref, values_ref, 0).astype(BF16)
        for k, out_ref in enumerate(out_refs, 1):
            piece = cache_piece(where_ref, keys_ref, values_ref, k)
            if joined:
                piece = jnp.concatenate([x_ref[...].astype(F32), piece], axis=0)
            out_ref[...] = piece.astype(BF16)

    height = span + (x.shape[0] if joined else 0)
    own, *near = call(
        body,
        (shaped((span, wide)),) + (shaped((height, wide)),) * (close - 1),
        (where, x, cache_keys, cache_values),
        [SMEM] + [VMEM] * 3,
        flops=2 * AROUND,
    )
    return own, near, joined


def pack_far(where, cache_keys, cache_values, afters):
    groups = lax.axis_size("dp")
    part_dev, span, _ = cache_keys.shape
    wide = 2 * part_dev * HD
    close = min(groups, 4)

    def body(where_ref, keys_ref, values_ref, *refs):
        for i, out_ref in enumerate(refs[len(afters) :]):
            for odd in range(2):
                out_ref[odd] = cache_piece(where_ref, keys_ref, values_ref, close + 2 * i + odd).astype(BF16)

    return call(
        body,
        (shaped((2, span, wide)),) * ((groups - close) // 2),
        (where, cache_keys, cache_values, *afters),
        [SMEM, VMEM, VMEM] + [ANY] * len(afters),
        flops=AROUND,
    )


def collect_near(own, near, span):
    def body(own_ref, *refs):
        refs[-1][0] = own_ref[...]
        for k, ref in enumerate(refs[:-1], 1):
            refs[-1][k] = ref[...].astype(F32)[ref.shape[0] - span :].astype(BF16)

    return call(body, shaped((1 + len(near),) + own.shape), (own, *near), [VMEM] * (1 + len(near)), around=1)


def last_entries(pieces, after):
    def body(after_ref, *refs):
        for i, ref in enumerate(refs[:-1]):
            refs[-1][i] = ref[1]

    ins = (after, *pieces)
    return call(body, shaped((len(pieces),) + pieces[0].shape[1:]), ins, [ANY] + [VMEM] * len(pieces), around=1)


def collect_far(pieces, passed):
    def body(*refs):
        for i, ref in enumerate(refs[:-2]):
            refs[-1][2 * i] = ref[0]
            refs[-1][2 * i + 1] = refs[-2][i]

    shape = (2 * len(pieces),) + pieces[0].shape[1:]
    return call(body, shaped(shape), (*pieces, passed), [VMEM] * (1 + len(pieces)), around=1)


def lift(where_ref, gain_ref, order, block_refs, h_ref, ss_ref, absolute):
    groups = len(block_refs)
    tensor = lax.axis_size("tensor")
    pair = block_refs[0].shape[0]
    near = groups // tensor
    d, t = where_ref[0], where_ref[1]
    gain = gain_ref[...]
    places = []
    for ref, k in zip(block_refs, order):
        g = d ^ k
        place = slot(lax.div(g, near) ^ t, tensor) * near + lax.rem(g, near)
        place = pl.multiple_of(place * pair, pair)
        wide = ref[...].astype(F32)[:pair]
        squares = jnp.broadcast_to(jnp.sum(wide * wide, axis=1, keepdims=True), (pair, 128))
        ss_ref[pl.ds(pl.multiple_of(g * pair, pair) if absolute else place, pair), :] = squares
        h_ref[pl.ds(place, pair), :] = (wide * gain).astype(BF16)
        places.append((pl.multiple_of(g * pair, pair), place))
    return places


def split(total, base, lane):
    high = total.astype(BF16).astype(F32)
    return jnp.where(lane == 0, high, jnp.where(lane == 1, total - high, base))


def stacked(rows, parts):
    width = rows.shape[1] // parts
    return jnp.concatenate([rows[:, i * width : (i + 1) * width] for i in range(parts)], axis=0)


def unstacked(rows, parts):
    height = rows.shape[0] // parts
    return jnp.concatenate([rows[i * height : (i + 1) * height] for i in range(parts)], axis=1)


def project_attention(where, blocks, order, gain, w_keyval, w_query, after):
    pair, features = blocks[0].shape
    rows = len(blocks) * pair
    half = rows // 2
    columns = w_keyval.shape[1]
    wide = w_query.shape[1]
    base = columns + 128

    def body(where_ref, gain_ref, *refs):
        block_refs, refs = refs[: len(blocks)], refs[len(blocks) :]
        w_kv_ref, w_q_ref, after_ref, message_ref, keep_ref, h_ref, ss_ref, product = refs
        places = lift(where_ref, gain_ref, order, block_refs, h_ref, ss_ref, True)
        h = h_ref[...]
        product[...] = jnp.dot(h, w_kv_ref[...], preferred_element_type=F32)
        for to, place in places:
            message_ref[pl.ds(to, pair), :columns] = product[pl.ds(place, pair), :].astype(BF16)
        squares = ss_ref[...]
        lane = lax.broadcasted_iota(jnp.int32, squares.shape, 1)
        message_ref[:, columns:base] = split(squares, 0.0, lane).astype(BF16)
        tile = tiles(wide // 2)
        for first in range(0, wide, tile):
            queries = jnp.dot(h, w_q_ref[:, first : first + tile], preferred_element_type=F32)
            keep_ref[:, first : first + tile] = queries[:half]
            below, lanes = divmod(first, wide // 2)
            lanes += base
            message_ref[below * half : (below + 1) * half, lanes : lanes + tile] = queries[half:].astype(BF16)

    return call(
        body,
        (shaped((rows, base + wide // 2)), shaped((half, wide), F32)),
        (where, gain[None], *[blocks[k] for k in order], w_keyval, w_query, after),
        [SMEM] + [VMEM] * (3 + len(blocks)) + [ANY],
        [pltpu.VMEM((rows, features), BF16), pltpu.VMEM((rows, 128), F32), pltpu.VMEM((rows, columns), F32)],
        flops=2 * rows * (w_keyval.size + w_query.size),
        moved=4 * rows * features + 2 * (w_keyval.size + w_query.size),
    )


def add_cores(own, keep, arrived):
    tensor = lax.axis_size("tensor")
    rows, total = own.shape
    half, wide = keep.shape
    base = total - wide // 2
    height = 2 * half // tensor
    joined = tensor == 4

    def body(own_ref, keep_ref, arrived_ref, first_ref, message_ref, *out_refs):
        summed = own_ref[:, :base].astype(F32) + arrived_ref[:, :base].astype(F32)
        ends = summed[:, base - 128 :]
        lane = lax.broadcasted_iota(jnp.int32, ends.shape, 1)
        message_ref[:, : base - 128] = summed[:, : base - 128].astype(BF16)
        message_ref[:, base - 128 : base] = split(ends[:, 0:1] + ends[:, 1:2], ends, lane).astype(BF16)
        queries = keep_ref[...] + unstacked(arrived_ref[:, base:].astype(F32), 2)
        first_ref[...] = queries[:height]
        if joined:
            message_ref[:, base:] = stacked(queries[height:], 4).astype(BF16)
        for i, out_ref in enumerate(out_refs, 1):
            out_ref[...] = queries[i * height : (i + 1) * height].astype(BF16)

    outs = [shaped((height, wide), F32), shaped((rows, base + (wide // 4 if joined else 0)))]
    outs += [] if joined else [shaped((height, wide))] * (tensor // 2 - 1)
    return call(body, tuple(outs), (own, keep, arrived), [VMEM] * 3, moved=6 * own.size, around=1)


def add_keyvals(own, arrived):
    rows, columns = own.shape

    def body(own_ref, arrived_ref, out_ref):
        summed = own_ref[...].astype(F32) + arrived_ref[...].astype(F32)
        ends = summed[:, columns - 128 :]
        lane = lax.broadcasted_iota(jnp.int32, ends.shape, 1)
        out_ref[:, : columns - 128] = summed[:, : columns - 128].astype(BF16)
        out_ref[:, columns - 128 :] = split(ends[:, 0:1] + ends[:, 1:2], ends, lane).astype(BF16)

    return call(body, shaped(own.shape), (own, arrived), [VMEM] * 2, moved=6 * own.size)


def finish_keyvals(where, own, arrived, columns, width):
    groups = lax.axis_size("dp")
    rows = own.shape[0]
    lanes = slice(0, columns + 128)

    def body(where_ref, own_ref, arrived_ref, scale_ref, *out_refs):
        summed = own_ref[:, lanes].astype(F32) + arrived_ref[:, lanes].astype(F32)
        squares = summed[:, columns : columns + 1] + summed[:, columns + 1 : columns + 2]
        scale = lax.rsqrt(squares / width + EPS)
        scale_ref[...] = jnp.broadcast_to(scale, (rows, 128))
        scaled = summed[:, :columns] * scale
        if groups == KVH:
            lower = where_ref[0] < groups // 2
            out_refs[0][...] = jnp.where(lower, scaled[:, :HD], scaled[:, HD:]).astype(BF16)
            out_refs[1][...] = jnp.where(lower, scaled[:, HD:], scaled[:, :HD]).astype(BF16)
        else:
            out_refs[0][...] = scaled.astype(BF16)

    outs = [shaped((rows, 128), F32)]
    outs += [shaped((rows, HD))] * 2 if groups == KVH else [shaped((rows, columns))]
    return call(body, tuple(outs), (where, own, arrived), [SMEM, VMEM, VMEM], moved=8 * own.size, around=1)


def project(h, w):
    half = h.shape[0] // 2

    def body(h_ref, w_ref, keep_ref, send_ref):
        def write(first, tile, product):
            keep_ref[:, first : first + tile] = product[:half]
            send_ref[:, first : first + tile] = product[half:].astype(BF16)

        multiply(h_ref[...], w_ref, write)

    columns = w.shape[1]
    return call(
        body,
        (shaped((half, columns), F32), shaped((half, columns))),
        (h, w),
        [VMEM] * 2,
        flops=4 * half * w.size,
        moved=2 * w.size,
    )


def project_gate(where, blocks, order, gain, w):
    pair, features = blocks[0].shape
    rows = len(blocks) * pair
    half = rows // 2
    columns = w.shape[1]

    def body(where_ref, gain_ref, *refs):
        block_refs, (w_ref, h_ref, keep_ref, send_ref, ss_ref) = refs[: len(blocks)], refs[len(blocks) :]
        lift(where_ref, gain_ref, order, block_refs, h_ref, ss_ref, False)

        def write(first, tile, product):
            keep_ref[:, first : first + tile] = product[:half]
            send_ref[:, first : first + tile] = product[half:].astype(BF16)

        multiply(h_ref[...], w_ref, write)
        squares = ss_ref[...]
        high = squares.astype(BF16).astype(F32)
        lane = lax.broadcasted_iota(jnp.int32, squares.shape, 1)
        ends = jnp.where(lane == 0, high, jnp.where(lane == 1, squares - high, 0.0))
        keep_ref[:, columns:] = ends[:half]
        send_ref[:, columns:] = ends[half:].astype(BF16)

    return call(
        body,
        (shaped((rows, features)), shaped((half, columns + 128), F32), shaped((half, columns + 128))),
        (where, gain[None], *[blocks[k] for k in order], w),
        [SMEM] + [VMEM] * (2 + len(blocks)),
        [pltpu.VMEM((rows, 128), F32)],
        flops=2 * rows * w.size,
        moved=4 * rows * features + 2 * w.size,
    )


def project_back(where, blocks, w):
    groups = lax.axis_size("dp")
    rows, depth = blocks[0].shape
    near = groups // len(blocks)
    pair = rows // near
    total = len(blocks) * rows
    columns = w.shape[1]
    close, passing = far_split(groups)
    single = groups - (passing - close)
    joint = (passing - close) // 2

    def body(where_ref, *refs):
        block_refs, (w_ref, *out_refs) = refs[: len(blocks)], refs[len(blocks) :]
        left = out_refs[-1]
        d, t = where_ref[0], where_ref[1]
        for k, block_ref in enumerate(block_refs):
            for i in range(near):
                relative = ((t ^ k) * near + i) ^ d
                by_x = single + lax.shift_right_logical(relative - close, 1) + (relative & 1) * joint
                place = jnp.where(relative < passing, by_x, relative - (passing - close))
                place = jnp.where(relative < close, relative, place)
                left[pl.ds(pl.multiple_of(place * pair, pair), pair), :] = block_ref[i * pair : (i + 1) * pair, :]

        def write(first, tile, product):
            lanes = slice(first, first + tile)
            for i in range(single):
                out_refs[i][:, lanes] = product[i * pair : (i + 1) * pair].astype(out_refs[i].dtype)
            middle = (single + joint) * pair
            out_refs[single][:, lanes] = product[single * pair : middle]
            out_refs[single + 1][:, lanes] = product[middle:].astype(BF16)

        multiply(left[...], w_ref, write)

    outs = [shaped((pair, columns), F32)] + [shaped((pair, columns))] * (single - 1)
    outs += [shaped((joint * pair, columns), F32), shaped((joint * pair, columns))]
    return call(
        body,
        tuple(outs),
        (where, *blocks, w),
        [SMEM] + [VMEM] * (1 + len(blocks)),
        [pltpu.VMEM((total, depth), BF16)],
        flops=2 * total * w.size,
        moved=2 * w.size,
    )


def add_pairs(keep, arrived, pair, passed):
    count = arrived.shape[0] // pair

    def body(keep_ref, arrived_ref, passed_ref, *out_refs):
        for i, out_ref in enumerate(out_refs[:-1]):
            rows = slice(i * pair, (i + 1) * pair)
            out_ref[...] = (keep_ref[rows, :] + arrived_ref[rows, :].astype(F32)).astype(BF16)
        out_refs[-1][...] = passed_ref[...]

    outs = (shaped((pair, keep.shape[1])),) * (count + 1)
    return call(body, outs, (keep, arrived, passed), [VMEM] * 3, moved=8 * arrived.size)


def sum_rows(parts, pair):
    groups = lax.axis_size("dp")
    close, passing = far_split(groups)
    own, *direct, keep, send = parts
    *sums, direct[0] = add_pairs(keep, swap(send, "dp", 1), pair, direct[0])
    arrived = [swap(piece, "dp", close + 2 * i) for i, piece in enumerate(sums)]
    places = [*range(1, close), *range(passing, groups)]
    arrived += [swap(piece, "dp", k) for k, piece in sorted(zip(places, direct), key=lambda item: -item[0])]
    return own, arrived


def finish(own, arrived, x=None):
    def body(own_ref, *refs):
        total = own_ref[...]
        for ref in refs[: len(arrived)]:
            total = total + ref[...].astype(F32)
        rounded = total.astype(BF16)
        if x is None:
            refs[-1][...] = rounded
        else:
            refs[-2][...] = rounded
            refs[-1][...] = (refs[len(arrived)][...].astype(F32) + rounded.astype(F32)).astype(BF16)

    outs = (shaped(own.shape),) * (1 if x is None else 2)
    ins = (own, *arrived) + (() if x is None else (x,))
    return call(body, outs, ins, [VMEM] * len(ins), moved=8 * own.size)


def attend_cached(where, anc, rope, scale, queries, near_cache, far_cache, part_dev):
    tensor = lax.axis_size("tensor")
    groups = lax.axis_size("dp")
    near = groups // tensor
    pair = 2 * part_dev
    close, span, _ = near_cache[0].shape
    ctx = tensor * span
    height, columns = queries[0].shape
    heads = columns // HD
    parts = near * part_dev
    rows = heads * parts

    def body(where_ref, anc_ref, rope_ref, scale_ref, *refs):
        q_refs, refs = refs[: len(queries)], refs[len(queries) :]
        near_refs, far_refs = refs[:tensor], refs[tensor : 2 * tensor]
        query_ref, mixed_ref, highest_ref, total_ref, keys_ref, values_ref = refs[2 * tensor :]
        d, t = where_ref[0], where_ref[1]
        query_sum = q_refs[0][...]
        for ref in q_refs[1:]:
            if ref.shape[0] == height:
                query_sum = query_sum + ref[...].astype(F32)
            else:
                lanes = slice(ref.shape[1] - columns // 4, ref.shape[1])
                query_sum = query_sum + unstacked(ref[:, lanes].astype(F32), 4)
        query_sum = query_sum * scale_ref[pl.ds(pl.multiple_of(t * near * pair, pair), near * pair), 0:1]
        for step in range(2):

            def bring(i, _, step=step):
                particle = t * parts + i if step == 0 else anc_ref[i]
                block, member = lax.div(particle, part_dev) ^ d, lax.rem(particle, part_dev)

                def load(cache_refs, entry):
                    for k, cache_ref in enumerate(cache_refs):
                        to = pl.ds(pl.multiple_of(i * ctx + k * span, 8), span)
                        lanes = pl.ds(pl.multiple_of(member * HD, HD), HD)
                        keys_ref[to, :] = cache_ref[entry, :, lanes].astype(F32)
                        lanes = pl.ds(pl.multiple_of((part_dev + member) * HD, HD), HD)
                        values_ref[to, :] = cache_ref[entry, :, lanes].astype(F32)

                @pl.when(block < close)
                def _():
                    load(near_refs, block)

                @pl.when(block >= close)
                def _():
                    load(far_refs, block - close)

                return 0

            lax.fori_loop(0, parts, bring, 0)
            keys = keys_ref[...].astype(BF16)
            values = values_ref[...].astype(BF16)
            per_head = []
            for h in range(heads):
                for b in range(near):
                    first = b * pair + step * part_dev
                    per_head.append(query_sum[first : first + part_dev, h * HD : (h + 1) * HD])
            query = jnp.concatenate(per_head, axis=0).astype(BF16).astype(F32)
            cosine = rope_ref[2 * step : 2 * step + 1, :]
            sine = rope_ref[2 * step + 1 : 2 * step + 2, :]
            query = (query * cosine + pltpu.roll(query, HD // 2, 1) * sine).astype(BF16)
            scores = lax.dot_general(query, keys, (((1,), (1,)), ((), ())), preferred_element_type=F32)
            scores = scores * (1.0 / math.sqrt(HD))
            row_part = lax.rem(lax.broadcasted_iota(jnp.int32, (rows, 1), 0), parts)
            col_part = lax.div(lax.broadcasted_iota(jnp.int32, (1, parts * ctx), 1), ctx)
            scores = jnp.where(row_part == col_part, scores, MASKED)
            highest = jnp.max(scores, axis=1, keepdims=True)
            weights = jnp.exp(scores - highest)
            here = slice(step * rows, (step + 1) * rows)
            query_ref[here, :] = query
            mixed_ref[here, :] = jnp.dot(weights.astype(BF16), values, preferred_element_type=F32)
            highest_ref[here, :] = jnp.broadcast_to(highest, (rows, 128))
            total_ref[here, :] = jnp.broadcast_to(jnp.sum(weights, axis=1, keepdims=True), (rows, 128))

    ins = (where, anc, rope, scale, *queries, *near_cache, *far_cache)
    return call(
        body,
        (shaped((2 * rows, HD)), shaped((2 * rows, HD), F32), shaped((2 * rows, 128), F32), shaped((2 * rows, 128), F32)),
        ins,
        [SMEM] * 2 + [VMEM] * (len(ins) - 2),
        [pltpu.VMEM((parts * ctx, HD), F32), pltpu.VMEM((parts * ctx, HD), F32)],
        limit=(4 << 20) + 12 * rows * parts * ctx,
        moved=4 << 20,
    )


def attend_new(where, rope, targets, pieces, state, shape, part_dev):
    groups = lax.axis_size("dp")
    tensor = lax.axis_size("tensor")
    near = groups // tensor
    pair = 2 * part_dev
    parts = near * part_dev
    heads = shape[1] // HD
    rows = heads * parts

    def body(where_ref, rope_ref, target_ref, one_ref, two_ref, query_ref, mixed_ref, highest_ref, total_ref, out_ref):
        even = where_ref[0] % 2 == 0 if groups == KVH else True
        one, two = one_ref[...].astype(F32), two_ref[...].astype(F32)
        plain = jnp.where(even, one, two)
        values = jnp.where(even, two, one).astype(BF16)
        cosine = jnp.concatenate([jnp.broadcast_to(rope_ref[2 * s : 2 * s + 1, :], (part_dev, HD)) for s in range(2)])
        sine = jnp.concatenate([jnp.broadcast_to(rope_ref[2 * s + 1 : 2 * s + 2, :], (part_dev, HD)) for s in range(2)])
        turned = pltpu.roll(plain, HD // 2, 1).reshape(groups, pair, HD)
        keys = plain.reshape(groups, pair, HD) * cosine[None] + turned * sine[None]
        keys = keys.reshape(groups * pair, HD).astype(BF16)
        scores = lax.dot_general(query_ref[...], keys, (((1,), (1,)), ((), ())), preferred_element_type=F32)
        scores = scores * (1.0 / math.sqrt(HD))
        col = lax.broadcasted_iota(jnp.int32, (1, groups * pair), 1)
        wanted = (col == target_ref[:, 0:1]) | (col == target_ref[:, 1:2])
        scores = jnp.where(wanted, scores, MASKED)
        before = highest_ref[:, 0:1]
        highest = jnp.maximum(before, jnp.max(scores, axis=1, keepdims=True))
        weights = jnp.exp(scores - highest)
        keep = jnp.exp(before - highest)
        total = total_ref[:, 0:1] * keep + jnp.sum(weights, axis=1, keepdims=True)
        mixed = mixed_ref[...] * keep + jnp.dot(weights.astype(BF16), values, preferred_element_type=F32)
        mixed = mixed / total
        for h in range(heads):
            for b in range(near):
                first = h * parts + b * part_dev
                both = [mixed[s * rows + first : s * rows + first + part_dev] for s in range(2)]
                here = slice(b * pair, (b + 1) * pair)
                out_ref[here, h * HD : (h + 1) * HD] = jnp.concatenate(both, axis=0).astype(BF16)

    ins = (where, rope, targets, *pieces, *state)
    return call(body, shaped(shape), ins, [SMEM] + [VMEM] * (len(ins) - 1), moved=1 << 20)


def move_keyvals(pieces):
    groups = lax.axis_size("dp")
    d = lax.axis_index("dp")
    if groups == KVH:
        half = groups // 2
        one = [(i, 2 * i) for i in range(half)] + [(half + i, 2 * i + 1) for i in range(half)]
        two = [(i, 2 * i + 1) for i in range(half)] + [(half + i, 2 * i) for i in range(half)]
        return [lax.ppermute(x, "dp", to) for x, to in zip(pieces, (one, two))]
    every = lax.all_gather(pieces[0], "dp", axis=1, tiled=True)
    start = (d * KVH // groups) * HD
    return [lax.dynamic_slice_in_dim(every, first + start, HD, axis=1) for first in (0, KVH * HD)]


def local(
    x_first,
    x_second,
    cache_keys,
    cache_values,
    ancestors,
    attn_gain,
    ffn_gain,
    w_query,
    w_keyval,
    w_out,
    w_gate,
    w_up,
    w_down,
):
    groups = lax.axis_size("dp")
    tensor = lax.axis_size("tensor")
    part_dev, features = x_first.shape
    span = cache_keys.shape[1]
    width = features * tensor
    context = span * tensor
    d = lax.axis_index("dp")
    t = lax.axis_index("tensor")
    pair = 2 * part_dev
    near = groups // tensor
    parts = near * part_dev
    where = jnp.stack([d, t]).astype(jnp.int32)

    x = stack_tokens(x_first, x_second)
    own_piece, near_pieces, joined = pack_near(where, x, cache_keys, cache_values)
    blocks = gather_rows(x, groups, near_pieces if joined else None)
    close = min(groups, 4)
    near_moved = blocks[1:close] if joined else [swap(piece, "dp", k) for k, piece in enumerate(near_pieces, 1)]
    near_cache = gather_blocks(collect_near(own_piece, near_moved, span))
    packed = pack_far(where, cache_keys, cache_values, blocks[close::2])
    far_pieces = [swap(piece, "dp", close + 2 * i) for i, piece in enumerate(packed)]

    message, keep = project_attention(where, blocks, range(groups), attn_gain, w_keyval, w_query, x)
    queries, message, *leaving = add_cores(message, keep, swap(message, "tensor", 1))
    passed = swap(last_entries(far_pieces, x), "dp", 1)
    far_cache = gather_blocks(collect_far(far_pieces, passed))
    bits = 2
    while 2 * bits < tensor:
        message = add_keyvals(message, swap(message, "tensor", bits))
        bits *= 2
    arrived = swap(message, "tensor", bits)
    scale, *pieces = finish_keyvals(where, message, arrived, w_keyval.shape[1], width)
    pieces = move_keyvals(pieces)
    queries = [queries] + ([swap(x, "tensor", 2 * i) for i, x in enumerate(leaving, 1)] if leaving else [arrived])

    own = t * parts + jnp.arange(parts, dtype=jnp.int32)
    anc = lax.dynamic_slice_in_dim(ancestors, t * parts, parts).astype(jnp.int32)
    heads = w_query.shape[1] // HD

    def row_of(particle, step):
        return (particle // part_dev) * pair + step * part_dev + particle % part_dev

    first = jnp.stack([row_of(own, 0)] * 2, axis=1)
    second = jnp.stack([row_of(anc, 0), row_of(own, 1)], axis=1)
    targets = jnp.concatenate([jnp.tile(first, (heads, 1)), jnp.tile(second, (heads, 1))]).astype(jnp.int32)
    rope = jnp.asarray(np.stack(rope_tables(context) + rope_tables(context + 1)))
    state = attend_cached(where, anc, rope, scale, queries, near_cache, far_cache, part_dev)
    mixed = attend_new(where, rope, targets, pieces, state, queries[0].shape, part_dev)

    parts = project_back(where, gather_blocks(mixed), w_out)
    attn_part, residual = finish(*sum_rows(parts, pair), x)

    hidden_cols = w_gate.shape[1]
    passing = far_split(groups)[1]
    order = arrival_order(groups, passing)
    h, keep, send = project_gate(where, gather_rows(residual, passing), order, ffn_gain, w_gate)
    gate, gate_arrived = sum_blocks(keep, send)
    up, up_arrived = sum_blocks(*project(h, w_up))
    for piece in gate_arrived:
        gate = gate + piece.astype(F32)
    for piece in up_arrived:
        up = up + piece.astype(F32)
    scale = lax.rsqrt((gate[:, hidden_cols] + gate[:, hidden_cols + 1]) / width + EPS)[:, None]
    hidden = jax.nn.silu(gate[:, :hidden_cols] * scale) * (up * scale)
    parts = project_back(where, gather_blocks(hidden.astype(BF16)), w_down)
    (ffn_part,) = finish(*sum_rows(parts, pair))
    return (attn_part.reshape(2, part_dev, features), ffn_part.reshape(2, part_dev, features))


def solution(mesh):
    return jax.shard_map(
        local,
        mesh=mesh,
        in_specs=(
            P("dp", "tensor"),
            P("dp", "tensor"),
            P("dp", "tensor", None),
            P("dp", "tensor", None),
            P(),
            P("tensor"),
            P("tensor"),
            P("tensor", "dp"),
            P("tensor", "dp"),
            P("dp", "tensor"),
            P("tensor", "dp"),
            P("tensor", "dp"),
            P("dp", "tensor"),
        ),
        out_specs=(P(None, "dp", "tensor"), P(None, "dp", "tensor")),
        check_vma=False,
    )
```

```python
import functools
import math

import jax
import jax.numpy as jnp
import numpy as np
from jax import lax
from jax.experimental import pallas as pl
from jax.experimental.pallas import tpu as pltpu
from jax.sharding import PartitionSpec as P

KVH = 8
HD = 128
EPS = 1e-05
ROPE_BASE = 500000.0
MASKED = -1e30
AROUND = 5 << 30
BF16 = jnp.bfloat16
F32 = jnp.float32


def swap(x, axis, bits):
    size = lax.axis_size(axis)
    return lax.ppermute(x, axis, [(i, i ^ bits) for i in range(size)])


def rope_tables(position):
    half = HD // 2
    freq = np.power(np.float32(ROPE_BASE), -2.0 * np.arange(half, dtype=np.float32) / HD)
    angle = (np.float32(position) * freq.astype(np.float32)).astype(np.float32)
    cosine, sine = np.cos(angle), np.sin(angle)
    return (
        np.concatenate([cosine, cosine]).astype(np.float32),
        np.concatenate([-sine, sine]).astype(np.float32),
    )


SMEM = pl.BlockSpec(memory_space=pltpu.SMEM)
VMEM = pl.BlockSpec(memory_space=pltpu.VMEM)
ANY = pl.BlockSpec(memory_space=pl.ANY)
HBM = pl.BlockSpec(memory_space=pltpu.HBM)


def call(body, outs, ins, specs, scratch=(), flops=0, moved=0, limit=8 << 20, around=1):
    return pl.pallas_call(
        body,
        out_shape=outs,
        in_specs=specs,
        out_specs=jax.tree.map(lambda _: VMEM, outs),
        scratch_shapes=scratch,
        compiler_params=pltpu.CompilerParams(vmem_limit_bytes=limit),
        cost_estimate=pl.CostEstimate(flops=flops + around * AROUND, bytes_accessed=moved, transcendentals=0),
    )(*ins)


def shaped(shape, dtype=BF16):
    return jax.ShapeDtypeStruct(shape, dtype)


def gather_rows(rows, near=None):
    groups = lax.axis_size("dp")
    close = min(groups, 4)
    blocks = {0: rows}
    for k in range(groups - 2, close - 1, -2):
        blocks[k] = swap(rows, "dp", k)
    for k in range(close - 1, 0, -1):
        blocks[k] = swap(rows if near is None else near[k - 1], "dp", k)
    for k in range(groups - 2, close - 1, -2):
        blocks[k + 1] = swap(blocks[k], "dp", 1)
    return [blocks[k] for k in range(groups)]


def gather_blocks(block):
    tensor = lax.axis_size("tensor")
    blocks = {0: block}
    for k in range(2, tensor, 2):
        blocks[k] = swap(block, "tensor", k)
    blocks[1] = swap(block, "tensor", 1)
    for k in range(2, tensor, 2):
        blocks[k + 1] = swap(blocks[k], "tensor", 1)
    return [blocks[k] for k in range(tensor)]


def sum_blocks(keep, send):
    tensor = lax.axis_size("tensor")
    rows = keep.shape[0] // (tensor // 2)
    paired = (keep + swap(send, "tensor", 1).astype(F32)).reshape(tensor // 2, rows, -1)
    return paired[0], [swap(paired[i].astype(BF16), "tensor", 2 * i) for i in range(1, tensor // 2)]


def slot(relative, size):
    return lax.shift_right_logical(relative, 1) + (relative & 1) * (size // 2)


def tiles(columns):
    for tile in (256, 384, 128):
        if columns % tile == 0:
            return tile
    return columns


def multiply(left, w_ref, write):
    columns = w_ref.shape[1]
    tile = tiles(columns)
    for first in range(0, columns, tile):
        write(first, tile, jnp.dot(left, w_ref[:, first : first + tile], preferred_element_type=F32))


def stack_tokens(x_first, x_second):
    def body(first_ref, second_ref, out_ref):
        out_ref[...] = jnp.concatenate([first_ref[...].astype(F32), second_ref[...].astype(F32)], axis=0).astype(BF16)

    part_dev, features = x_first.shape
    return call(body, shaped((2 * part_dev, features)), (x_first, x_second), [VMEM] * 2)


def cache_piece(where_ref, keys_ref, values_ref, k):
    groups = lax.axis_size("dp")
    head = lax.div((where_ref[0] ^ k) * KVH, groups)
    lanes = pl.ds(pl.multiple_of(head * HD, HD), HD)
    tiles_of = [ref[p, :, lanes].astype(F32) for ref in (keys_ref, values_ref) for p in range(keys_ref.shape[0])]
    return jnp.concatenate(tiles_of, axis=1)


def pack_near(where, x, cache_keys, cache_values):
    part_dev, span, _ = cache_keys.shape
    close = min(lax.axis_size("dp"), 4)
    wide = 2 * part_dev * HD
    joined = x.shape[1] == wide

    def body(where_ref, x_ref, keys_ref, values_ref, own_ref, *out_refs):
        own_ref[...] = cache_piece(where_ref, keys_ref, values_ref, 0).astype(BF16)
        for k, out_ref in enumerate(out_refs, 1):
            piece = cache_piece(where_ref, keys_ref, values_ref, k)
            if joined:
                piece = jnp.concatenate([x_ref[...].astype(F32), piece], axis=0)
            out_ref[...] = piece.astype(BF16)

    height = span + (x.shape[0] if joined else 0)
    own, *near = call(
        body,
        (shaped((span, wide)),) + (shaped((height, wide)),) * (close - 1),
        (where, x, cache_keys, cache_values),
        [SMEM] + [VMEM] * 3,
        flops=2 * AROUND,
    )
    return own, near, joined


def pack_far(where, cache_keys, cache_values, afters):
    groups = lax.axis_size("dp")
    part_dev, span, _ = cache_keys.shape
    wide = 2 * part_dev * HD
    close = min(groups, 4)

    def body(where_ref, keys_ref, values_ref, *refs):
        for i, out_ref in enumerate(refs[len(afters) :]):
            for odd in range(2):
                out_ref[odd] = cache_piece(where_ref, keys_ref, values_ref, close + 2 * i + odd).astype(BF16)

    return call(
        body,
        (shaped((2, span, wide)),) * ((groups - close) // 2),
        (where, cache_keys, cache_values, *afters),
        [SMEM, VMEM, VMEM] + [ANY] * len(afters),
        flops=AROUND,
    )


def collect_near(own, near, span):
    def body(own_ref, *refs):
        refs[-1][0] = own_ref[...]
        for k, ref in enumerate(refs[:-1], 1):
            refs[-1][k] = ref[...].astype(F32)[ref.shape[0] - span :].astype(BF16)

    return call(body, shaped((1 + len(near),) + own.shape), (own, *near), [VMEM] * (1 + len(near)), around=1)


def gather_cache(block, after):
    blocks = [block] + [swap(block, "tensor", k) for k in range(2, lax.axis_size("tensor"), 2)]

    def body(after_ref, *refs):
        for i, ref in enumerate(refs[:-1]):
            refs[-1][i] = ref[...]

    ins = (after, *blocks)
    both = call(body, shaped((len(blocks),) + block.shape), ins, [ANY] + [VMEM] * len(blocks), around=0)
    return blocks + [swap(both, "tensor", 1)]


def last_entries(pieces, after):
    def body(after_ref, *refs):
        for i, ref in enumerate(refs[:-1]):
            refs[-1][i] = ref[1]

    ins = (after, *pieces)
    return call(body, shaped((len(pieces),) + pieces[0].shape[1:]), ins, [ANY] + [VMEM] * len(pieces), around=1)


def collect_far(pieces, passed):
    def body(*refs):
        for i, ref in enumerate(refs[:-2]):
            refs[-1][2 * i] = ref[0]
            refs[-1][2 * i + 1] = refs[-2][i]

    shape = (2 * len(pieces),) + pieces[0].shape[1:]
    return call(body, shaped(shape), (*pieces, passed), [VMEM] * (1 + len(pieces)), around=1)


def lift(where_ref, gain_ref, block_refs, h_ref, ss_ref, absolute):
    groups = len(block_refs)
    tensor = lax.axis_size("tensor")
    pair = block_refs[0].shape[0]
    near = groups // tensor
    d, t = where_ref[0], where_ref[1]
    gain = gain_ref[...]
    places = []
    for k in range(groups):
        g = d ^ k
        place = slot(lax.div(g, near) ^ t, tensor) * near + lax.rem(g, near)
        place = pl.multiple_of(place * pair, pair)
        wide = block_refs[k][...].astype(F32)[:pair]
        squares = jnp.broadcast_to(jnp.sum(wide * wide, axis=1, keepdims=True), (pair, 128))
        ss_ref[pl.ds(pl.multiple_of(g * pair, pair) if absolute else place, pair), :] = squares
        h_ref[pl.ds(place, pair), :] = (wide * gain).astype(BF16)
        places.append((pl.multiple_of(g * pair, pair), place))
    return places


def split(total, base, lane):
    high = total.astype(BF16).astype(F32)
    return jnp.where(lane == 0, high, jnp.where(lane == 1, total - high, base))


def stacked(rows, parts):
    width = rows.shape[1] // parts
    return jnp.concatenate([rows[:, i * width : (i + 1) * width] for i in range(parts)], axis=0)


def unstacked(rows, parts):
    height = rows.shape[0] // parts
    return jnp.concatenate([rows[i * height : (i + 1) * height] for i in range(parts)], axis=1)


def project_attention(where, blocks, gain, w_keyval, w_query, after):
    pair, features = blocks[0].shape
    rows = len(blocks) * pair
    half = rows // 2
    columns = w_keyval.shape[1]
    wide = w_query.shape[1]
    base = columns + 128

    def body(where_ref, gain_ref, *refs):
        block_refs, refs = refs[: len(blocks)], refs[len(blocks) :]
        w_kv_ref, w_q_ref, after_ref, message_ref, keep_ref, h_ref, ss_ref, product = refs
        places = lift(where_ref, gain_ref, block_refs, h_ref, ss_ref, True)
        h = h_ref[...]
        product[...] = jnp.dot(h, w_kv_ref[...], preferred_element_type=F32)
        for to, place in places:
            message_ref[pl.ds(to, pair), :columns] = product[pl.ds(place, pair), :].astype(BF16)
        squares = ss_ref[...]
        lane = lax.broadcasted_iota(jnp.int32, squares.shape, 1)
        message_ref[:, columns:base] = split(squares, 0.0, lane).astype(BF16)
        tile = tiles(wide // 2)
        for first in range(0, wide, tile):
            queries = jnp.dot(h, w_q_ref[:, first : first + tile], preferred_element_type=F32)
            keep_ref[:, first : first + tile] = queries[:half]
            below, lanes = divmod(first, wide // 2)
            lanes += base
            message_ref[below * half : (below + 1) * half, lanes : lanes + tile] = queries[half:].astype(BF16)

    return call(
        body,
        (shaped((rows, base + wide // 2)), shaped((half, wide), F32)),
        (where, gain[None], *blocks, w_keyval, w_query, after),
        [SMEM] + [VMEM] * (3 + len(blocks)) + [ANY],
        [pltpu.VMEM((rows, features), BF16), pltpu.VMEM((rows, 128), F32), pltpu.VMEM((rows, columns), F32)],
        flops=2 * rows * (w_keyval.size + w_query.size),
        moved=4 * rows * features + 2 * (w_keyval.size + w_query.size),
    )


def direct_keyvals():
    return lax.axis_size("dp") == KVH and lax.axis_size("tensor") == 4


def add_cores(where, own, keep, arrived):
    tensor = lax.axis_size("tensor")
    groups = lax.axis_size("dp")
    rows, total = own.shape
    half, wide = keep.shape
    base = total - wide // 2
    height = 2 * half // tensor
    direct = direct_keyvals()

    def body(where_ref, own_ref, keep_ref, arrived_ref, first_ref, message_ref, *out_refs):
        summed = own_ref[:, :base].astype(F32) + arrived_ref[:, :base].astype(F32)
        ends = summed[:, base - 128 :]
        lane = lax.broadcasted_iota(jnp.int32, ends.shape, 1)
        ends = split(ends[:, 0:1] + ends[:, 1:2], ends, lane).astype(BF16)
        queries = keep_ref[...] + unstacked(arrived_ref[:, base:].astype(F32), 2)
        first_ref[...] = queries[:height]
        if direct:
            message_ref[:, :128] = ends
            message_ref[:, 128:] = stacked(queries[height:], 4).astype(BF16)
            lower = where_ref[0] < groups // 2
            one, two = summed[:, :HD], summed[:, HD : 2 * HD]
            out_refs[0][...] = jnp.where(lower, one, two).astype(BF16)
            out_refs[1][...] = jnp.where(lower, two, one).astype(BF16)
        else:
            message_ref[:, : base - 128] = summed[:, : base - 128].astype(BF16)
            message_ref[:, base - 128 :] = ends
            for i, out_ref in enumerate(out_refs, 1):
                out_ref[...] = queries[i * height : (i + 1) * height].astype(BF16)

    outs = [shaped((height, wide), F32), shaped((rows, 128 + wide // 4 if direct else base))]
    outs += [shaped((rows, HD))] * 2 if direct else [shaped((height, wide))] * (tensor // 2 - 1)
    return call(body, tuple(outs), (where, own, keep, arrived), [SMEM] + [VMEM] * 3, moved=6 * own.size)


def row_scale(own, arrived, width):
    def body(own_ref, arrived_ref, out_ref):
        squares = own_ref[:, :128].astype(F32) + arrived_ref[:, :128].astype(F32)
        scale = lax.rsqrt((squares[:, 0:1] + squares[:, 1:2]) / width + EPS)
        out_ref[...] = jnp.broadcast_to(scale, squares.shape)

    return call(body, shaped((own.shape[0], 128), F32), (own, arrived), [VMEM] * 2)


def add_keyvals(own, arrived):
    rows, columns = own.shape

    def body(own_ref, arrived_ref, out_ref):
        summed = own_ref[...].astype(F32) + arrived_ref[...].astype(F32)
        ends = summed[:, columns - 128 :]
        lane = lax.broadcasted_iota(jnp.int32, ends.shape, 1)
        out_ref[:, : columns - 128] = summed[:, : columns - 128].astype(BF16)
        out_ref[:, columns - 128 :] = split(ends[:, 0:1] + ends[:, 1:2], ends, lane).astype(BF16)

    return call(body, shaped(own.shape), (own, arrived), [VMEM] * 2, moved=6 * own.size)


def finish_keyvals(where, own, arrived, columns, width):
    groups = lax.axis_size("dp")
    rows = own.shape[0]
    lanes = slice(0, columns + 128)

    def body(where_ref, own_ref, arrived_ref, scale_ref, *out_refs):
        summed = own_ref[:, lanes].astype(F32) + arrived_ref[:, lanes].astype(F32)
        squares = summed[:, columns : columns + 1] + summed[:, columns + 1 : columns + 2]
        scale = lax.rsqrt(squares / width + EPS)
        scale_ref[...] = jnp.broadcast_to(scale, (rows, 128))
        scaled = summed[:, :columns] * scale
        if groups == KVH:
            lower = where_ref[0] < groups // 2
            out_refs[0][...] = jnp.where(lower, scaled[:, :HD], scaled[:, HD:]).astype(BF16)
            out_refs[1][...] = jnp.where(lower, scaled[:, HD:], scaled[:, :HD]).astype(BF16)
        else:
            out_refs[0][...] = scaled.astype(BF16)

    outs = [shaped((rows, 128), F32)]
    outs += [shaped((rows, HD))] * 2 if groups == KVH else [shaped((rows, columns))]
    return call(body, tuple(outs), (where, own, arrived), [SMEM, VMEM, VMEM], moved=8 * own.size, around=1)


def project(h, w):
    half = h.shape[0] // 2

    def body(h_ref, w_ref, keep_ref, send_ref):
        def write(first, tile, product):
            keep_ref[:, first : first + tile] = product[:half]
            send_ref[:, first : first + tile] = product[half:].astype(BF16)

        multiply(h_ref[...], w_ref, write)

    columns = w.shape[1]
    return call(
        body,
        (shaped((half, columns), F32), shaped((half, columns))),
        (h, w),
        [VMEM] * 2,
        flops=4 * half * w.size,
        moved=2 * w.size,
    )


def project_gate(where, blocks, gain, w):
    pair, features = blocks[0].shape
    rows = len(blocks) * pair
    half = rows // 2
    columns = w.shape[1]

    def body(where_ref, gain_ref, *refs):
        block_refs, (w_ref, h_ref, keep_ref, send_ref, ss_ref) = refs[: len(blocks)], refs[len(blocks) :]
        lift(where_ref, gain_ref, block_refs, h_ref, ss_ref, False)

        def write(first, tile, product):
            keep_ref[:, first : first + tile] = product[:half]
            send_ref[:, first : first + tile] = product[half:].astype(BF16)

        multiply(h_ref[...], w_ref, write)
        squares = ss_ref[...]
        high = squares.astype(BF16).astype(F32)
        lane = lax.broadcasted_iota(jnp.int32, squares.shape, 1)
        ends = jnp.where(lane == 0, high, jnp.where(lane == 1, squares - high, 0.0))
        keep_ref[:, columns:] = ends[:half]
        send_ref[:, columns:] = ends[half:].astype(BF16)

    return call(
        body,
        (shaped((rows, features)), shaped((half, columns + 128), F32), shaped((half, columns + 128))),
        (where, gain[None], *blocks, w),
        [SMEM] + [VMEM] * (2 + len(blocks)),
        [pltpu.VMEM((rows, 128), F32)],
        flops=2 * rows * w.size,
        moved=4 * rows * features + 2 * w.size,
    )


def project_back(where, blocks, w):
    groups = lax.axis_size("dp")
    rows, depth = blocks[0].shape
    near = groups // len(blocks)
    pair = rows // near
    total = len(blocks) * rows
    columns = w.shape[1]
    close = min(groups, 4)
    far = (groups - close) // 2

    def body(where_ref, *refs):
        block_refs, (w_ref, *out_refs) = refs[: len(blocks)], refs[len(blocks) :]
        left = out_refs[-1]
        d, t = where_ref[0], where_ref[1]
        for k, block_ref in enumerate(block_refs):
            for i in range(near):
                relative = ((t ^ k) * near + i) ^ d
                beyond = close + lax.shift_right_logical(relative - close, 1) + (relative & 1) * far
                place = jnp.where(relative < close, relative, beyond)
                left[pl.ds(pl.multiple_of(place * pair, pair), pair), :] = block_ref[i * pair : (i + 1) * pair, :]

        def write(first, tile, product):
            lanes = slice(first, first + tile)
            for i in range(close):
                out_refs[i][:, lanes] = product[i * pair : (i + 1) * pair].astype(out_refs[i].dtype)
            middle = (close + far) * pair
            cut = middle + far // 2 * pair
            out_refs[close][:, lanes] = product[close * pair : middle]
            out_refs[close + 1][:, lanes] = product[middle:cut].astype(BF16)
            out_refs[close + 2][:, lanes] = product[cut:].astype(BF16)

        multiply(left[...], w_ref, write)

    outs = [shaped((pair, columns), F32)] + [shaped((pair, columns))] * (close - 1)
    outs += [shaped((far * pair, columns), F32)] + [shaped((far // 2 * pair, columns))] * 2
    return call(
        body,
        tuple(outs),
        (where, *blocks, w),
        [SMEM] + [VMEM] * (1 + len(blocks)),
        [pltpu.VMEM((total, depth), BF16)],
        flops=2 * total * w.size,
        moved=2 * w.size,
    )


def add_pairs(keep, arrived, first, pair, passed=()):
    count = arrived.shape[0] // pair

    def body(keep_ref, arrived_ref, *refs):
        for i, out_ref in enumerate(refs[len(passed) : len(passed) + count]):
            own = keep_ref[first + i * pair : first + (i + 1) * pair, :]
            out_ref[...] = (own + arrived_ref[i * pair : (i + 1) * pair, :].astype(F32)).astype(BF16)
        for ref, out_ref in zip(refs[: len(passed)], refs[len(passed) + count :]):
            out_ref[...] = ref[...]

    outs = (shaped((pair, keep.shape[1])),) * (count + len(passed))
    ins = (keep, arrived, *passed)
    return call(body, outs, ins, [VMEM] * len(ins), moved=8 * arrived.size)


def sum_rows(parts, pair):
    own, *near, keep, one, two = parts
    count = one.shape[0] // pair
    sums = add_pairs(keep, swap(one, "dp", 1), 0, pair, near[:2])
    sums, near = list(sums[:count]), [*sums[count:], *near[2:]]
    sums += add_pairs(keep, swap(two, "dp", 1), one.shape[0], pair)
    arrived = [swap(piece, "dp", len(near) + 1 + 2 * i) for i, piece in enumerate(sums)]
    arrived += [swap(piece, "dp", k + 1) for k, piece in enumerate(near)]
    return own, arrived


def finish(own, arrived, x=None):
    def body(own_ref, *refs):
        total = own_ref[...]
        for ref in refs[: len(arrived)]:
            total = total + ref[...].astype(F32)
        rounded = total.astype(BF16)
        if x is None:
            refs[-1][...] = rounded
        else:
            refs[-2][...] = rounded
            refs[-1][...] = (refs[len(arrived)][...].astype(F32) + rounded.astype(F32)).astype(BF16)

    outs = (shaped(own.shape),) * (1 if x is None else 2)
    ins = (own, *arrived) + (() if x is None else (x,))
    return call(body, outs, ins, [VMEM] * len(ins), moved=8 * own.size)


def attend_cached(where, anc, rope, scale, queries, near_cache, far_cache, part_dev):
    tensor = lax.axis_size("tensor")
    groups = lax.axis_size("dp")
    near = groups // tensor
    pair = 2 * part_dev
    close, span, _ = near_cache[0].shape
    ctx = tensor * span
    height, columns = queries[0].shape
    heads = columns // HD
    parts = near * part_dev
    rows = heads * parts

    def body(where_ref, anc_ref, rope_ref, scale_ref, *refs):
        q_refs, refs = refs[: len(queries)], refs[len(queries) :]
        count = tensor // 2 + 1
        near_refs, far_refs = refs[:count], refs[count : 2 * count]
        near_refs, far_refs = [(*part[:-1], *[part[-1].at[i] for i in range(count - 1)]) for part in (near_refs, far_refs)]
        query_ref, mixed_ref, highest_ref, total_ref, keys_ref, values_ref = refs[2 * count :]
        d, t = where_ref[0], where_ref[1]
        query_sum = q_refs[0][...]
        for ref in q_refs[1:]:
            if ref.shape[0] == height:
                query_sum = query_sum + ref[...].astype(F32)
            else:
                lanes = slice(ref.shape[1] - columns // 4, ref.shape[1])
                query_sum = query_sum + unstacked(ref[:, lanes].astype(F32), 4)
        query_sum = query_sum * scale_ref[pl.ds(pl.multiple_of(t * near * pair, pair), near * pair), 0:1]
        for step in range(2):

            def bring(i, _, step=step):
                particle = t * parts + i if step == 0 else anc_ref[i]
                block, member = lax.div(particle, part_dev) ^ d, lax.rem(particle, part_dev)

                def load(cache_refs, entry):
                    for k, cache_ref in enumerate(cache_refs):
                        to = pl.ds(pl.multiple_of(i * ctx + k * span, 8), span)
                        lanes = pl.ds(pl.multiple_of(member * HD, HD), HD)
                        keys_ref[to, :] = cache_ref[entry, :, lanes].astype(F32)
                        lanes = pl.ds(pl.multiple_of((part_dev + member) * HD, HD), HD)
                        values_ref[to, :] = cache_ref[entry, :, lanes].astype(F32)

                @pl.when(block < close)
                def _():
                    load(near_refs, block)

                @pl.when(block >= close)
                def _():
                    load(far_refs, block - close)

                return 0

            lax.fori_loop(0, parts, bring, 0)
            keys = keys_ref[...].astype(BF16)
            values = values_ref[...].astype(BF16)
            per_head = []
            for h in range(heads):
                for b in range(near):
                    first = b * pair + step * part_dev
                    per_head.append(query_sum[first : first + part_dev, h * HD : (h + 1) * HD])
            query = jnp.concatenate(per_head, axis=0).astype(BF16).astype(F32)
            cosine = rope_ref[2 * step : 2 * step + 1, :]
            sine = rope_ref[2 * step + 1 : 2 * step + 2, :]
            query = (query * cosine + pltpu.roll(query, HD // 2, 1) * sine).astype(BF16)
            scores = lax.dot_general(query, keys, (((1,), (1,)), ((), ())), preferred_element_type=F32)
            scores = scores * (1.0 / math.sqrt(HD))
            row_part = lax.rem(lax.broadcasted_iota(jnp.int32, (rows, 1), 0), parts)
            col_part = lax.div(lax.broadcasted_iota(jnp.int32, (1, parts * ctx), 1), ctx)
            scores = jnp.where(row_part == col_part, scores, MASKED)
            highest = jnp.max(scores, axis=1, keepdims=True)
            weights = jnp.exp(scores - highest)
            here = slice(step * rows, (step + 1) * rows)
            query_ref[here, :] = query
            mixed_ref[here, :] = jnp.dot(weights.astype(BF16), values, preferred_element_type=F32)
            highest_ref[here, :] = jnp.broadcast_to(highest, (rows, 128))
            total_ref[here, :] = jnp.broadcast_to(jnp.sum(weights, axis=1, keepdims=True), (rows, 128))

    ins = (where, anc, rope, scale, *queries, *near_cache, *far_cache)
    return call(
        body,
        (shaped((2 * rows, HD)), shaped((2 * rows, HD), F32), shaped((2 * rows, 128), F32), shaped((2 * rows, 128), F32)),
        ins,
        [SMEM] * 2 + [VMEM] * (len(ins) - 2),
        [pltpu.VMEM((parts * ctx, HD), F32), pltpu.VMEM((parts * ctx, HD), F32)],
        limit=(4 << 20) + 12 * rows * parts * ctx,
        moved=4 << 20,
    )


def attend_new(where, rope, targets, scale, pieces, state, shape, part_dev):
    groups = lax.axis_size("dp")
    tensor = lax.axis_size("tensor")
    near = groups // tensor
    pair = 2 * part_dev
    parts = near * part_dev
    heads = shape[1] // HD
    rows = heads * parts

    def body(where_ref, rope_ref, target_ref, scale_ref, *refs):
        piece_refs, (query_ref, mixed_ref, highest_ref, total_ref, out_ref) = refs[: len(pieces)], refs[len(pieces) :]
        even = where_ref[0] % 2 == 0 if groups == KVH else True
        if len(pieces) == 2:
            one, two = [ref[...].astype(F32) for ref in piece_refs]
        else:
            one, two = [piece_refs[i][...].astype(F32) + piece_refs[i + 1][...].astype(F32) for i in (0, 2)]
            one, two = [(x * scale_ref[...]).astype(BF16).astype(F32) for x in (one, two)]
        plain = jnp.where(even, one, two)
        values = jnp.where(even, two, one).astype(BF16)
        cosine = jnp.concatenate([jnp.broadcast_to(rope_ref[2 * s : 2 * s + 1, :], (part_dev, HD)) for s in range(2)])
        sine = jnp.concatenate([jnp.broadcast_to(rope_ref[2 * s + 1 : 2 * s + 2, :], (part_dev, HD)) for s in range(2)])
        turned = pltpu.roll(plain, HD // 2, 1).reshape(groups, pair, HD)
        keys = plain.reshape(groups, pair, HD) * cosine[None] + turned * sine[None]
        keys = keys.reshape(groups * pair, HD).astype(BF16)
        scores = lax.dot_general(query_ref[...], keys, (((1,), (1,)), ((), ())), preferred_element_type=F32)
        scores = scores * (1.0 / math.sqrt(HD))
        col = lax.broadcasted_iota(jnp.int32, (1, groups * pair), 1)
        wanted = (col == target_ref[:, 0:1]) | (col == target_ref[:, 1:2])
        scores = jnp.where(wanted, scores, MASKED)
        before = highest_ref[:, 0:1]
        highest = jnp.maximum(before, jnp.max(scores, axis=1, keepdims=True))
        weights = jnp.exp(scores - highest)
        keep = jnp.exp(before - highest)
        total = total_ref[:, 0:1] * keep + jnp.sum(weights, axis=1, keepdims=True)
        mixed = mixed_ref[...] * keep + jnp.dot(weights.astype(BF16), values, preferred_element_type=F32)
        mixed = mixed / total
        for h in range(heads):
            for b in range(near):
                first = h * parts + b * part_dev
                both = [mixed[s * rows + first : s * rows + first + part_dev] for s in range(2)]
                here = slice(b * pair, (b + 1) * pair)
                out_ref[here, h * HD : (h + 1) * HD] = jnp.concatenate(both, axis=0).astype(BF16)

    ins = (where, rope, targets, scale, *pieces, *state)
    return call(body, shaped(shape), ins, [SMEM] + [VMEM] * (len(ins) - 1), moved=1 << 20)


def send_keyvals(pieces):
    groups = lax.axis_size("dp")
    tensor = lax.axis_size("tensor")
    half = groups // 2
    moved = []
    for flip, piece in enumerate(pieces):
        to = [2 * i + flip for i in range(half)] + [2 * i + 1 - flip for i in range(half)]
        for k in (0, 2):
            pairs = [(i * tensor + t, to[i] * tensor + (t ^ k)) for i in range(groups) for t in range(tensor)]
            moved.append(lax.ppermute(piece, ("dp", "tensor"), pairs))
    return moved


def move_keyvals(pieces):
    groups = lax.axis_size("dp")
    d = lax.axis_index("dp")
    if groups == KVH:
        half = groups // 2
        one = [(i, 2 * i) for i in range(half)] + [(half + i, 2 * i + 1) for i in range(half)]
        two = [(i, 2 * i + 1) for i in range(half)] + [(half + i, 2 * i) for i in range(half)]
        return [lax.ppermute(x, "dp", to) for x, to in zip(pieces, (one, two))]
    every = lax.all_gather(pieces[0], "dp", axis=1, tiled=True)
    start = (d * KVH // groups) * HD
    return [lax.dynamic_slice_in_dim(every, first + start, HD, axis=1) for first in (0, KVH * HD)]


def local(
    x_first,
    x_second,
    cache_keys,
    cache_values,
    ancestors,
    attn_gain,
    ffn_gain,
    w_query,
    w_keyval,
    w_out,
    w_gate,
    w_up,
    w_down,
):
    groups = lax.axis_size("dp")
    tensor = lax.axis_size("tensor")
    part_dev, features = x_first.shape
    span = cache_keys.shape[1]
    width = features * tensor
    context = span * tensor
    d = lax.axis_index("dp")
    t = lax.axis_index("tensor")
    pair = 2 * part_dev
    near = groups // tensor
    parts = near * part_dev
    where = jnp.stack([d, t]).astype(jnp.int32)

    x = stack_tokens(x_first, x_second)
    own_piece, near_pieces, joined = pack_near(where, x, cache_keys, cache_values)
    blocks = gather_rows(x, near_pieces if joined else None)
    close = min(groups, 4)
    near_moved = blocks[1:close] if joined else [swap(piece, "dp", k) for k, piece in enumerate(near_pieces, 1)]
    near_pieces = collect_near(own_piece, near_moved, span)
    packed = pack_far(where, cache_keys, cache_values, blocks[close::2])
    far_pieces = [swap(piece, "dp", close + 2 * i) for i, piece in enumerate(packed)]

    message, keep = project_attention(where, blocks, attn_gain, w_keyval, w_query, x)
    queries, message, *leaving = add_cores(where, message, keep, swap(message, "tensor", 1))
    passed = swap(last_entries(far_pieces, x), "dp", 1)
    far_pieces = collect_far(far_pieces, passed)
    if direct_keyvals():
        pieces = send_keyvals(leaving)
        arrived = swap(message, "tensor", 2)
        scale = row_scale(message, arrived, width)
        queries = [queries, arrived]
    else:
        bits = 2
        while 2 * bits < tensor:
            message = add_keyvals(message, swap(message, "tensor", bits))
            bits *= 2
        arrived = swap(message, "tensor", bits)
        scale, *pieces = finish_keyvals(where, message, arrived, w_keyval.shape[1], width)
        pieces = move_keyvals(pieces)
        queries = [queries] + [swap(piece, "tensor", 2 * i) for i, piece in enumerate(leaving, 1)]

    near_cache = gather_cache(near_pieces, arrived)
    far_cache = gather_cache(far_pieces, arrived)

    own = t * parts + jnp.arange(parts, dtype=jnp.int32)
    anc = lax.dynamic_slice_in_dim(ancestors, t * parts, parts).astype(jnp.int32)
    heads = w_query.shape[1] // HD

    def row_of(particle, step):
        return (particle // part_dev) * pair + step * part_dev + particle % part_dev

    first = jnp.stack([row_of(own, 0)] * 2, axis=1)
    second = jnp.stack([row_of(anc, 0), row_of(own, 1)], axis=1)
    targets = jnp.concatenate([jnp.tile(first, (heads, 1)), jnp.tile(second, (heads, 1))]).astype(jnp.int32)
    rope = jnp.asarray(np.stack(rope_tables(context) + rope_tables(context + 1)))
    state = attend_cached(where, anc, rope, scale, queries, near_cache, far_cache, part_dev)
    mixed = attend_new(where, rope, targets, scale, pieces, state, queries[0].shape, part_dev)

    parts = project_back(where, gather_blocks(mixed), w_out)
    attn_part, residual = finish(*sum_rows(parts, pair), x)

    hidden_cols = w_gate.shape[1]
    h, keep, send = project_gate(where, gather_rows(residual), ffn_gain, w_gate)
    gate, gate_arrived = sum_blocks(keep, send)
    up, up_arrived = sum_blocks(*project(h, w_up))
    for piece in gate_arrived:
        gate = gate + piece.astype(F32)
    for piece in up_arrived:
        up = up + piece.astype(F32)
    scale = lax.rsqrt((gate[:, hidden_cols] + gate[:, hidden_cols + 1]) / width + EPS)[:, None]
    hidden = jax.nn.silu(gate[:, :hidden_cols] * scale) * (up * scale)
    parts = project_back(where, gather_blocks(hidden.astype(BF16)), w_down)
    (ffn_part,) = finish(*sum_rows(parts, pair))
    return (attn_part.reshape(2, part_dev, features), ffn_part.reshape(2, part_dev, features))


def solution(mesh):
    return jax.shard_map(
        local,
        mesh=mesh,
        in_specs=(
            P("dp", "tensor"),
            P("dp", "tensor"),
            P("dp", "tensor", None),
            P("dp", "tensor", None),
            P(),
            P("tensor"),
            P("tensor"),
            P("tensor", "dp"),
            P("tensor", "dp"),
            P("dp", "tensor"),
            P("tensor", "dp"),
            P("tensor", "dp"),
            P("dp", "tensor"),
        ),
        out_specs=(P(None, "dp", "tensor"), P(None, "dp", "tensor")),
        check_vma=False,
    )
```

```python
import functools
import math

import jax
import jax.numpy as jnp
import numpy as np
from jax import lax
from jax.experimental import pallas as pl
from jax.experimental.pallas import tpu as pltpu
from jax.sharding import PartitionSpec as P

KVH = 8
HD = 128
EPS = 1e-05
ROPE_BASE = 500000.0
MASKED = -1e30
AROUND = 5 << 30
BF16 = jnp.bfloat16
F32 = jnp.float32


def swap(x, axis, bits):
    size = lax.axis_size(axis)
    return lax.ppermute(x, axis, [(i, i ^ bits) for i in range(size)])


def rope_tables(position):
    half = HD // 2
    freq = np.power(np.float32(ROPE_BASE), -2.0 * np.arange(half, dtype=np.float32) / HD)
    angle = (np.float32(position) * freq.astype(np.float32)).astype(np.float32)
    cosine, sine = np.cos(angle), np.sin(angle)
    return (
        np.concatenate([cosine, cosine]).astype(np.float32),
        np.concatenate([-sine, sine]).astype(np.float32),
    )


SMEM = pl.BlockSpec(memory_space=pltpu.SMEM)
VMEM = pl.BlockSpec(memory_space=pltpu.VMEM)
ANY = pl.BlockSpec(memory_space=pl.ANY)
HBM = pl.BlockSpec(memory_space=pltpu.HBM)


def call(body, outs, ins, specs, scratch=(), flops=0, moved=0, limit=8 << 20, around=1):
    return pl.pallas_call(
        body,
        out_shape=outs,
        in_specs=specs,
        out_specs=jax.tree.map(lambda _: VMEM, outs),
        scratch_shapes=scratch,
        compiler_params=pltpu.CompilerParams(vmem_limit_bytes=limit),
        cost_estimate=pl.CostEstimate(flops=flops + around * AROUND, bytes_accessed=moved, transcendentals=0),
    )(*ins)


def shaped(shape, dtype=BF16):
    return jax.ShapeDtypeStruct(shape, dtype)


def gather_rows(rows, near=None):
    groups = lax.axis_size("dp")
    close = min(groups, 4)
    blocks = {0: rows}
    for k in range(groups - 2, close - 1, -2):
        blocks[k] = swap(rows, "dp", k)
    for k in range(close - 1, 0, -1):
        blocks[k] = swap(rows if near is None else near[k - 1], "dp", k)
    for k in range(groups - 2, close - 1, -2):
        blocks[k + 1] = swap(blocks[k], "dp", 1)
    return [blocks[k] for k in range(groups)]


def gather_blocks(block):
    tensor = lax.axis_size("tensor")
    blocks = {0: block}
    for k in range(2, tensor, 2):
        blocks[k] = swap(block, "tensor", k)
    blocks[1] = swap(block, "tensor", 1)
    for k in range(2, tensor, 2):
        blocks[k + 1] = swap(blocks[k], "tensor", 1)
    return [blocks[k] for k in range(tensor)]


def sum_blocks(keep, send):
    tensor = lax.axis_size("tensor")
    rows = keep.shape[0] // (tensor // 2)
    paired = (keep + swap(send, "tensor", 1).astype(F32)).reshape(tensor // 2, rows, -1)
    return paired[0], [swap(paired[i].astype(BF16), "tensor", 2 * i) for i in range(1, tensor // 2)]


def slot(relative, size):
    return lax.shift_right_logical(relative, 1) + (relative & 1) * (size // 2)


def tiles(columns):
    for tile in (256, 384, 128):
        if columns % tile == 0:
            return tile
    return columns


def multiply(left, w_ref, write):
    columns = w_ref.shape[1]
    tile = tiles(columns)
    for first in range(0, columns, tile):
        write(first, tile, jnp.dot(left, w_ref[:, first : first + tile], preferred_element_type=F32))


def stack_tokens(x_first, x_second):
    def body(first_ref, second_ref, out_ref):
        out_ref[...] = jnp.concatenate([first_ref[...].astype(F32), second_ref[...].astype(F32)], axis=0).astype(BF16)

    part_dev, features = x_first.shape
    return call(body, shaped((2 * part_dev, features)), (x_first, x_second), [VMEM] * 2)


def cache_piece(where_ref, keys_ref, values_ref, k):
    groups = lax.axis_size("dp")
    head = lax.div((where_ref[0] ^ k) * KVH, groups)
    lanes = pl.ds(pl.multiple_of(head * HD, HD), HD)
    tiles_of = [ref[p, :, lanes].astype(F32) for ref in (keys_ref, values_ref) for p in range(keys_ref.shape[0])]
    return jnp.concatenate(tiles_of, axis=1)


def pack_near(where, x, cache_keys, cache_values):
    part_dev, span, _ = cache_keys.shape
    close = min(lax.axis_size("dp"), 4)
    wide = 2 * part_dev * HD
    joined = x.shape[1] == wide

    def body(where_ref, x_ref, keys_ref, values_ref, own_ref, *out_refs):
        own_ref[...] = cache_piece(where_ref, keys_ref, values_ref, 0).astype(BF16)
        for k, out_ref in enumerate(out_refs, 1):
            piece = cache_piece(where_ref, keys_ref, values_ref, k)
            if joined:
                piece = jnp.concatenate([x_ref[...].astype(F32), piece], axis=0)
            out_ref[...] = piece.astype(BF16)

    height = span + (x.shape[0] if joined else 0)
    own, *near = call(
        body,
        (shaped((span, wide)),) + (shaped((height, wide)),) * (close - 1),
        (where, x, cache_keys, cache_values),
        [SMEM] + [VMEM] * 3,
        flops=2 * AROUND,
    )
    return own, near, joined


def pack_far(where, cache_keys, cache_values, afters):
    groups = lax.axis_size("dp")
    part_dev, span, _ = cache_keys.shape
    wide = 2 * part_dev * HD
    close = min(groups, 4)

    def body(where_ref, keys_ref, values_ref, *refs):
        for i, out_ref in enumerate(refs[len(afters) :]):
            for odd in range(2):
                out_ref[odd] = cache_piece(where_ref, keys_ref, values_ref, close + 2 * i + odd).astype(BF16)

    return call(
        body,
        (shaped((2, span, wide)),) * ((groups - close) // 2),
        (where, cache_keys, cache_values, *afters),
        [SMEM, VMEM, VMEM] + [ANY] * len(afters),
        flops=AROUND,
    )


def collect_near(own, near, span):
    def body(own_ref, *refs):
        refs[-1][0] = own_ref[...]
        for k, ref in enumerate(refs[:-1], 1):
            refs[-1][k] = ref[...].astype(F32)[ref.shape[0] - span :].astype(BF16)

    return call(body, shaped((1 + len(near),) + own.shape), (own, *near), [VMEM] * (1 + len(near)), around=1)


def cross_chips(block):
    return [block] + [swap(block, "tensor", k) for k in range(2, lax.axis_size("tensor"), 2)]


def cross_cores(blocks, after):
    def body(after_ref, *refs):
        for i, ref in enumerate(refs[:-1]):
            refs[-1][i] = ref[...]

    ins = (after, *blocks)
    shape = (len(blocks),) + blocks[0].shape
    both = call(body, shaped(shape), ins, [ANY] + [VMEM] * len(blocks), around=0)
    return [*blocks, swap(both, "tensor", 1)]


def last_entries(pieces, after):
    def body(after_ref, *refs):
        for i, ref in enumerate(refs[:-1]):
            refs[-1][i] = ref[1]

    ins = (after, *pieces)
    return call(body, shaped((len(pieces),) + pieces[0].shape[1:]), ins, [ANY] + [VMEM] * len(pieces), around=1)


def collect_far(pieces, passed):
    def body(*refs):
        for i, ref in enumerate(refs[:-2]):
            refs[-1][2 * i] = ref[0]
            refs[-1][2 * i + 1] = refs[-2][i]

    shape = (2 * len(pieces),) + pieces[0].shape[1:]
    return call(body, shaped(shape), (*pieces, passed), [VMEM] * (1 + len(pieces)), around=1)


def lift(where_ref, gain_ref, block_refs, h_ref, ss_ref, absolute):
    groups = len(block_refs)
    tensor = lax.axis_size("tensor")
    pair = block_refs[0].shape[0]
    near = groups // tensor
    d, t = where_ref[0], where_ref[1]
    gain = gain_ref[...]
    places = []
    for k in range(groups):
        g = d ^ k
        place = slot(lax.div(g, near) ^ t, tensor) * near + lax.rem(g, near)
        place = pl.multiple_of(place * pair, pair)
        wide = block_refs[k][...].astype(F32)[:pair]
        squares = jnp.broadcast_to(jnp.sum(wide * wide, axis=1, keepdims=True), (pair, 128))
        ss_ref[pl.ds(pl.multiple_of(g * pair, pair) if absolute else place, pair), :] = squares
        h_ref[pl.ds(place, pair), :] = (wide * gain).astype(BF16)
        places.append((pl.multiple_of(g * pair, pair), place))
    return places


def split(total, base, lane):
    high = total.astype(BF16).astype(F32)
    return jnp.where(lane == 0, high, jnp.where(lane == 1, total - high, base))


def stacked(rows, parts):
    width = rows.shape[1] // parts
    return jnp.concatenate([rows[:, i * width : (i + 1) * width] for i in range(parts)], axis=0)


def unstacked(rows, parts):
    height = rows.shape[0] // parts
    return jnp.concatenate([rows[i * height : (i + 1) * height] for i in range(parts)], axis=1)


def project_attention(where, blocks, gain, w_keyval, w_query, after):
    pair, features = blocks[0].shape
    rows = len(blocks) * pair
    half = rows // 2
    columns = w_keyval.shape[1]
    wide = w_query.shape[1]
    base = columns + 128

    def body(where_ref, gain_ref, *refs):
        block_refs, refs = refs[: len(blocks)], refs[len(blocks) :]
        w_kv_ref, w_q_ref, after_ref, message_ref, keep_ref, h_ref, ss_ref, product = refs
        places = lift(where_ref, gain_ref, block_refs, h_ref, ss_ref, True)
        h = h_ref[...]
        product[...] = jnp.dot(h, w_kv_ref[...], preferred_element_type=F32)
        for to, place in places:
            message_ref[pl.ds(to, pair), :columns] = product[pl.ds(place, pair), :].astype(BF16)
        squares = ss_ref[...]
        lane = lax.broadcasted_iota(jnp.int32, squares.shape, 1)
        message_ref[:, columns:base] = split(squares, 0.0, lane).astype(BF16)
        tile = tiles(wide // 2)
        for first in range(0, wide, tile):
            queries = jnp.dot(h, w_q_ref[:, first : first + tile], preferred_element_type=F32)
            keep_ref[:, first : first + tile] = queries[:half]
            below, lanes = divmod(first, wide // 2)
            lanes += base
            message_ref[below * half : (below + 1) * half, lanes : lanes + tile] = queries[half:].astype(BF16)

    return call(
        body,
        (shaped((rows, base + wide // 2)), shaped((half, wide), F32)),
        (where, gain[None], *blocks, w_keyval, w_query, after),
        [SMEM] + [VMEM] * (3 + len(blocks)) + [ANY],
        [pltpu.VMEM((rows, features), BF16), pltpu.VMEM((rows, 128), F32), pltpu.VMEM((rows, columns), F32)],
        flops=2 * rows * (w_keyval.size + w_query.size),
        moved=4 * rows * features + 2 * (w_keyval.size + w_query.size),
    )


def direct_keyvals():
    return lax.axis_size("dp") == KVH and lax.axis_size("tensor") == 4


def add_cores(where, own, keep, arrived, after):
    tensor = lax.axis_size("tensor")
    groups = lax.axis_size("dp")
    rows, total = own.shape
    half, wide = keep.shape
    base = total - wide // 2
    height = 2 * half // tensor
    direct = direct_keyvals()

    def body(where_ref, own_ref, keep_ref, arrived_ref, after_ref, first_ref, message_ref, *out_refs):
        summed = own_ref[:, :base].astype(F32) + arrived_ref[:, :base].astype(F32)
        ends = summed[:, base - 128 :]
        lane = lax.broadcasted_iota(jnp.int32, ends.shape, 1)
        ends = split(ends[:, 0:1] + ends[:, 1:2], ends, lane).astype(BF16)
        queries = keep_ref[...] + unstacked(arrived_ref[:, base:].astype(F32), 2)
        first_ref[...] = queries[:height]
        if direct:
            message_ref[:, :128] = ends
            message_ref[:, 128:] = stacked(queries[height:], 4).astype(BF16)
            lower = where_ref[0] < groups // 2
            one, two = summed[:, :HD], summed[:, HD : 2 * HD]
            out_refs[0][...] = jnp.where(lower, one, two).astype(BF16)
            out_refs[1][...] = jnp.where(lower, two, one).astype(BF16)
        else:
            message_ref[:, : base - 128] = summed[:, : base - 128].astype(BF16)
            message_ref[:, base - 128 :] = ends
            for i, out_ref in enumerate(out_refs, 1):
                out_ref[...] = queries[i * height : (i + 1) * height].astype(BF16)

    outs = [shaped((height, wide), F32), shaped((rows, 128 + wide // 4 if direct else base))]
    outs += [shaped((rows, HD))] * 2 if direct else [shaped((height, wide))] * (tensor // 2 - 1)
    ins = (where, own, keep, arrived, after)
    return call(body, tuple(outs), ins, [SMEM] + [VMEM] * 3 + [ANY], moved=6 * own.size)


def row_scale(own, arrived, width):
    def body(own_ref, arrived_ref, out_ref):
        squares = own_ref[:, :128].astype(F32) + arrived_ref[:, :128].astype(F32)
        scale = lax.rsqrt((squares[:, 0:1] + squares[:, 1:2]) / width + EPS)
        out_ref[...] = jnp.broadcast_to(scale, squares.shape)

    return call(body, shaped((own.shape[0], 128), F32), (own, arrived), [VMEM] * 2)


def add_keyvals(own, arrived):
    rows, columns = own.shape

    def body(own_ref, arrived_ref, out_ref):
        summed = own_ref[...].astype(F32) + arrived_ref[...].astype(F32)
        ends = summed[:, columns - 128 :]
        lane = lax.broadcasted_iota(jnp.int32, ends.shape, 1)
        out_ref[:, : columns - 128] = summed[:, : columns - 128].astype(BF16)
        out_ref[:, columns - 128 :] = split(ends[:, 0:1] + ends[:, 1:2], ends, lane).astype(BF16)

    return call(body, shaped(own.shape), (own, arrived), [VMEM] * 2, moved=6 * own.size)


def finish_keyvals(where, own, arrived, columns, width):
    groups = lax.axis_size("dp")
    rows = own.shape[0]
    lanes = slice(0, columns + 128)

    def body(where_ref, own_ref, arrived_ref, scale_ref, *out_refs):
        summed = own_ref[:, lanes].astype(F32) + arrived_ref[:, lanes].astype(F32)
        squares = summed[:, columns : columns + 1] + summed[:, columns + 1 : columns + 2]
        scale = lax.rsqrt(squares / width + EPS)
        scale_ref[...] = jnp.broadcast_to(scale, (rows, 128))
        scaled = summed[:, :columns] * scale
        if groups == KVH:
            lower = where_ref[0] < groups // 2
            out_refs[0][...] = jnp.where(lower, scaled[:, :HD], scaled[:, HD:]).astype(BF16)
            out_refs[1][...] = jnp.where(lower, scaled[:, HD:], scaled[:, :HD]).astype(BF16)
        else:
            out_refs[0][...] = scaled.astype(BF16)

    outs = [shaped((rows, 128), F32)]
    outs += [shaped((rows, HD))] * 2 if groups == KVH else [shaped((rows, columns))]
    return call(body, tuple(outs), (where, own, arrived), [SMEM, VMEM, VMEM], moved=8 * own.size, around=1)


def project(h, w):
    half = h.shape[0] // 2

    def body(h_ref, w_ref, keep_ref, send_ref):
        def write(first, tile, product):
            keep_ref[:, first : first + tile] = product[:half]
            send_ref[:, first : first + tile] = product[half:].astype(BF16)

        multiply(h_ref[...], w_ref, write)

    columns = w.shape[1]
    return call(
        body,
        (shaped((half, columns), F32), shaped((half, columns))),
        (h, w),
        [VMEM] * 2,
        flops=4 * half * w.size,
        moved=2 * w.size,
    )


def project_gate(where, blocks, gain, w):
    pair, features = blocks[0].shape
    rows = len(blocks) * pair
    half = rows // 2
    columns = w.shape[1]

    def body(where_ref, gain_ref, *refs):
        block_refs, (w_ref, h_ref, keep_ref, send_ref, ss_ref) = refs[: len(blocks)], refs[len(blocks) :]
        lift(where_ref, gain_ref, block_refs, h_ref, ss_ref, False)

        def write(first, tile, product):
            keep_ref[:, first : first + tile] = product[:half]
            send_ref[:, first : first + tile] = product[half:].astype(BF16)

        multiply(h_ref[...], w_ref, write)
        squares = ss_ref[...]
        high = squares.astype(BF16).astype(F32)
        lane = lax.broadcasted_iota(jnp.int32, squares.shape, 1)
        ends = jnp.where(lane == 0, high, jnp.where(lane == 1, squares - high, 0.0))
        keep_ref[:, columns:] = ends[:half]
        send_ref[:, columns:] = ends[half:].astype(BF16)

    return call(
        body,
        (shaped((rows, features)), shaped((half, columns + 128), F32), shaped((half, columns + 128))),
        (where, gain[None], *blocks, w),
        [SMEM] + [VMEM] * (2 + len(blocks)),
        [pltpu.VMEM((rows, 128), F32)],
        flops=2 * rows * w.size,
        moved=4 * rows * features + 2 * w.size,
    )


def project_back(where, blocks, w):
    groups = lax.axis_size("dp")
    rows, depth = blocks[0].shape
    near = groups // len(blocks)
    pair = rows // near
    total = len(blocks) * rows
    columns = w.shape[1]
    close = min(groups, 4)
    far = (groups - close) // 2

    def body(where_ref, *refs):
        block_refs, (w_ref, *out_refs) = refs[: len(blocks)], refs[len(blocks) :]
        left = out_refs[-1]
        d, t = where_ref[0], where_ref[1]
        for k, block_ref in enumerate(block_refs):
            for i in range(near):
                relative = ((t ^ k) * near + i) ^ d
                beyond = close + lax.shift_right_logical(relative - close, 1) + (relative & 1) * far
                place = jnp.where(relative < close, relative, beyond)
                left[pl.ds(pl.multiple_of(place * pair, pair), pair), :] = block_ref[i * pair : (i + 1) * pair, :]

        def write(first, tile, product):
            lanes = slice(first, first + tile)
            for i in range(close):
                out_refs[i][:, lanes] = product[i * pair : (i + 1) * pair].astype(out_refs[i].dtype)
            middle = (close + far) * pair
            cut = middle + far // 2 * pair
            out_refs[close][:, lanes] = product[close * pair : middle]
            out_refs[close + 1][:, lanes] = product[middle:cut].astype(BF16)
            out_refs[close + 2][:, lanes] = product[cut:].astype(BF16)

        multiply(left[...], w_ref, write)

    outs = [shaped((pair, columns), F32)] + [shaped((pair, columns))] * (close - 1)
    outs += [shaped((far * pair, columns), F32)] + [shaped((far // 2 * pair, columns))] * 2
    return call(
        body,
        tuple(outs),
        (where, *blocks, w),
        [SMEM] + [VMEM] * (1 + len(blocks)),
        [pltpu.VMEM((total, depth), BF16)],
        flops=2 * total * w.size,
        moved=2 * w.size,
    )


def add_pairs(keep, arrived, first, pair, passed=()):
    count = arrived.shape[0] // pair

    def body(keep_ref, arrived_ref, *refs):
        for i, out_ref in enumerate(refs[len(passed) : len(passed) + count]):
            own = keep_ref[first + i * pair : first + (i + 1) * pair, :]
            out_ref[...] = (own + arrived_ref[i * pair : (i + 1) * pair, :].astype(F32)).astype(BF16)
        for ref, out_ref in zip(refs[: len(passed)], refs[len(passed) + count :]):
            out_ref[...] = ref[...]

    outs = (shaped((pair, keep.shape[1])),) * (count + len(passed))
    ins = (keep, arrived, *passed)
    return call(body, outs, ins, [VMEM] * len(ins), moved=8 * arrived.size)


def sum_rows(parts, pair):
    own, *near, keep, one, two = parts
    count = one.shape[0] // pair
    sums = add_pairs(keep, swap(one, "dp", 1), 0, pair, near[:1])
    sums, near = list(sums[:count]), [*sums[count:], *near[1:]]
    sums += add_pairs(keep, swap(two, "dp", 1), one.shape[0], pair)
    arrived = [swap(piece, "dp", len(near) + 1 + 2 * i) for i, piece in enumerate(sums)]
    arrived += [swap(piece, "dp", k + 1) for k, piece in enumerate(near)]
    return own, arrived


def finish(own, arrived, x=None):
    def body(own_ref, *refs):
        total = own_ref[...]
        for ref in refs[: len(arrived)]:
            total = total + ref[...].astype(F32)
        rounded = total.astype(BF16)
        if x is None:
            refs[-1][...] = rounded
        else:
            refs[-2][...] = rounded
            refs[-1][...] = (refs[len(arrived)][...].astype(F32) + rounded.astype(F32)).astype(BF16)

    outs = (shaped(own.shape),) * (1 if x is None else 2)
    ins = (own, *arrived) + (() if x is None else (x,))
    return call(body, outs, ins, [VMEM] * len(ins), moved=8 * own.size)


def attend_cached(where, anc, rope, scale, queries, near_cache, far_cache, part_dev):
    tensor = lax.axis_size("tensor")
    groups = lax.axis_size("dp")
    near = groups // tensor
    pair = 2 * part_dev
    close, span, _ = near_cache[0].shape
    ctx = tensor * span
    height, columns = queries[0].shape
    heads = columns // HD
    parts = near * part_dev
    rows = heads * parts

    def body(where_ref, anc_ref, rope_ref, scale_ref, *refs):
        q_refs, refs = refs[: len(queries)], refs[len(queries) :]
        count = tensor // 2 + 1
        near_refs, far_refs = refs[:count], refs[count : 2 * count]
        near_refs, far_refs = [(*part[:-1], *[part[-1].at[i] for i in range(count - 1)]) for part in (near_refs, far_refs)]
        query_ref, mixed_ref, highest_ref, total_ref, keys_ref, values_ref = refs[2 * count :]
        d, t = where_ref[0], where_ref[1]
        query_sum = q_refs[0][...]
        for ref in q_refs[1:]:
            if ref.shape[0] == height:
                query_sum = query_sum + ref[...].astype(F32)
            else:
                lanes = slice(ref.shape[1] - columns // 4, ref.shape[1])
                query_sum = query_sum + unstacked(ref[:, lanes].astype(F32), 4)
        query_sum = query_sum * scale_ref[pl.ds(pl.multiple_of(t * near * pair, pair), near * pair), 0:1]
        for step in range(2):

            def bring(i, _, step=step):
                particle = t * parts + i if step == 0 else anc_ref[i]
                block, member = lax.div(particle, part_dev) ^ d, lax.rem(particle, part_dev)

                def load(cache_refs, entry):
                    for k, cache_ref in enumerate(cache_refs):
                        to = pl.ds(pl.multiple_of(i * ctx + k * span, 8), span)
                        lanes = pl.ds(pl.multiple_of(member * HD, HD), HD)
                        keys_ref[to, :] = cache_ref[entry, :, lanes].astype(F32)
                        lanes = pl.ds(pl.multiple_of((part_dev + member) * HD, HD), HD)
                        values_ref[to, :] = cache_ref[entry, :, lanes].astype(F32)

                @pl.when(block < close)
                def _():
                    load(near_refs, block)

                @pl.when(block >= close)
                def _():
                    load(far_refs, block - close)

                return 0

            lax.fori_loop(0, parts, bring, 0)
            keys = keys_ref[...].astype(BF16)
            values = values_ref[...].astype(BF16)
            per_head = []
            for h in range(heads):
                for b in range(near):
                    first = b * pair + step * part_dev
                    per_head.append(query_sum[first : first + part_dev, h * HD : (h + 1) * HD])
            query = jnp.concatenate(per_head, axis=0).astype(BF16).astype(F32)
            cosine = rope_ref[2 * step : 2 * step + 1, :]
            sine = rope_ref[2 * step + 1 : 2 * step + 2, :]
            query = (query * cosine + pltpu.roll(query, HD // 2, 1) * sine).astype(BF16)
            scores = lax.dot_general(query, keys, (((1,), (1,)), ((), ())), preferred_element_type=F32)
            scores = scores * (1.0 / math.sqrt(HD))
            row_part = lax.rem(lax.broadcasted_iota(jnp.int32, (rows, 1), 0), parts)
            col_part = lax.div(lax.broadcasted_iota(jnp.int32, (1, parts * ctx), 1), ctx)
            scores = jnp.where(row_part == col_part, scores, MASKED)
            highest = jnp.max(scores, axis=1, keepdims=True)
            weights = jnp.exp(scores - highest)
            here = slice(step * rows, (step + 1) * rows)
            query_ref[here, :] = query
            mixed_ref[here, :] = jnp.dot(weights.astype(BF16), values, preferred_element_type=F32)
            highest_ref[here, :] = jnp.broadcast_to(highest, (rows, 128))
            total_ref[here, :] = jnp.broadcast_to(jnp.sum(weights, axis=1, keepdims=True), (rows, 128))

    ins = (where, anc, rope, scale, *queries, *near_cache, *far_cache)
    return call(
        body,
        (shaped((2 * rows, HD)), shaped((2 * rows, HD), F32), shaped((2 * rows, 128), F32), shaped((2 * rows, 128), F32)),
        ins,
        [SMEM] * 2 + [VMEM] * (len(ins) - 2),
        [pltpu.VMEM((parts * ctx, HD), F32), pltpu.VMEM((parts * ctx, HD), F32)],
        limit=(4 << 20) + 12 * rows * parts * ctx,
        moved=4 << 20,
    )


def attend_new(where, rope, targets, scale, pieces, state, shape, part_dev):
    groups = lax.axis_size("dp")
    tensor = lax.axis_size("tensor")
    near = groups // tensor
    pair = 2 * part_dev
    parts = near * part_dev
    heads = shape[1] // HD
    rows = heads * parts

    def body(where_ref, rope_ref, target_ref, scale_ref, *refs):
        piece_refs, (query_ref, mixed_ref, highest_ref, total_ref, out_ref) = refs[: len(pieces)], refs[len(pieces) :]
        even = where_ref[0] % 2 == 0 if groups == KVH else True
        if len(pieces) == 2:
            one, two = [ref[...].astype(F32) for ref in piece_refs]
        else:
            one, two = [piece_refs[i][...].astype(F32) + piece_refs[i + 1][...].astype(F32) for i in (0, 2)]
            one, two = [(x * scale_ref[...]).astype(BF16).astype(F32) for x in (one, two)]
        plain = jnp.where(even, one, two)
        values = jnp.where(even, two, one).astype(BF16)
        cosine = jnp.concatenate([jnp.broadcast_to(rope_ref[2 * s : 2 * s + 1, :], (part_dev, HD)) for s in range(2)])
        sine = jnp.concatenate([jnp.broadcast_to(rope_ref[2 * s + 1 : 2 * s + 2, :], (part_dev, HD)) for s in range(2)])
        turned = pltpu.roll(plain, HD // 2, 1).reshape(groups, pair, HD)
        keys = plain.reshape(groups, pair, HD) * cosine[None] + turned * sine[None]
        keys = keys.reshape(groups * pair, HD).astype(BF16)
        scores = lax.dot_general(query_ref[...], keys, (((1,), (1,)), ((), ())), preferred_element_type=F32)
        scores = scores * (1.0 / math.sqrt(HD))
        col = lax.broadcasted_iota(jnp.int32, (1, groups * pair), 1)
        wanted = (col == target_ref[:, 0:1]) | (col == target_ref[:, 1:2])
        scores = jnp.where(wanted, scores, MASKED)
        before = highest_ref[:, 0:1]
        highest = jnp.maximum(before, jnp.max(scores, axis=1, keepdims=True))
        weights = jnp.exp(scores - highest)
        keep = jnp.exp(before - highest)
        total = total_ref[:, 0:1] * keep + jnp.sum(weights, axis=1, keepdims=True)
        mixed = mixed_ref[...] * keep + jnp.dot(weights.astype(BF16), values, preferred_element_type=F32)
        mixed = mixed / total
        for h in range(heads):
            for b in range(near):
                first = h * parts + b * part_dev
                both = [mixed[s * rows + first : s * rows + first + part_dev] for s in range(2)]
                here = slice(b * pair, (b + 1) * pair)
                out_ref[here, h * HD : (h + 1) * HD] = jnp.concatenate(both, axis=0).astype(BF16)

    ins = (where, rope, targets, scale, *pieces, *state)
    return call(body, shaped(shape), ins, [SMEM] + [VMEM] * (len(ins) - 1), moved=1 << 20)


def send_keyvals(pieces):
    groups = lax.axis_size("dp")
    tensor = lax.axis_size("tensor")
    half = groups // 2
    moved = []
    for flip, piece in enumerate(pieces):
        to = [2 * i + flip for i in range(half)] + [2 * i + 1 - flip for i in range(half)]
        for k in (0, 2):
            pairs = [(i * tensor + t, to[i] * tensor + (t ^ k)) for i in range(groups) for t in range(tensor)]
            moved.append(lax.ppermute(piece, ("dp", "tensor"), pairs))
    return moved


def move_keyvals(pieces):
    groups = lax.axis_size("dp")
    d = lax.axis_index("dp")
    if groups == KVH:
        half = groups // 2
        one = [(i, 2 * i) for i in range(half)] + [(half + i, 2 * i + 1) for i in range(half)]
        two = [(i, 2 * i + 1) for i in range(half)] + [(half + i, 2 * i) for i in range(half)]
        return [lax.ppermute(x, "dp", to) for x, to in zip(pieces, (one, two))]
    every = lax.all_gather(pieces[0], "dp", axis=1, tiled=True)
    start = (d * KVH // groups) * HD
    return [lax.dynamic_slice_in_dim(every, first + start, HD, axis=1) for first in (0, KVH * HD)]


def local(
    x_first,
    x_second,
    cache_keys,
    cache_values,
    ancestors,
    attn_gain,
    ffn_gain,
    w_query,
    w_keyval,
    w_out,
    w_gate,
    w_up,
    w_down,
):
    groups = lax.axis_size("dp")
    tensor = lax.axis_size("tensor")
    part_dev, features = x_first.shape
    span = cache_keys.shape[1]
    width = features * tensor
    context = span * tensor
    d = lax.axis_index("dp")
    t = lax.axis_index("tensor")
    pair = 2 * part_dev
    near = groups // tensor
    parts = near * part_dev
    where = jnp.stack([d, t]).astype(jnp.int32)

    x = stack_tokens(x_first, x_second)
    own_piece, near_pieces, joined = pack_near(where, x, cache_keys, cache_values)
    blocks = gather_rows(x, near_pieces if joined else None)
    close = min(groups, 4)
    near_moved = blocks[1:close] if joined else [swap(piece, "dp", k) for k, piece in enumerate(near_pieces, 1)]
    near_cache = cross_chips(collect_near(own_piece, near_moved, span))
    packed = pack_far(where, cache_keys, cache_values, blocks[close::2])
    far_pieces = [swap(piece, "dp", close + 2 * i) for i, piece in enumerate(packed)]

    message, keep = project_attention(where, blocks, attn_gain, w_keyval, w_query, x)
    queries, message, *leaving = add_cores(where, message, keep, swap(message, "tensor", 1), near_cache[-1])
    passed = swap(last_entries(far_pieces, x), "dp", 1)
    far_cache = cross_chips(collect_far(far_pieces, passed))
    if direct_keyvals():
        pieces = send_keyvals(leaving)
        arrived = swap(message, "tensor", 2)
        scale = row_scale(message, arrived, width)
        queries = [queries, arrived]
    else:
        bits = 2
        while 2 * bits < tensor:
            message = add_keyvals(message, swap(message, "tensor", bits))
            bits *= 2
        arrived = swap(message, "tensor", bits)
        scale, *pieces = finish_keyvals(where, message, arrived, w_keyval.shape[1], width)
        pieces = move_keyvals(pieces)
        queries = [queries] + [swap(piece, "tensor", 2 * i) for i, piece in enumerate(leaving, 1)]

    near_cache = cross_cores(near_cache, arrived)
    far_cache = cross_cores(far_cache, arrived)

    own = t * parts + jnp.arange(parts, dtype=jnp.int32)
    anc = lax.dynamic_slice_in_dim(ancestors, t * parts, parts).astype(jnp.int32)
    heads = w_query.shape[1] // HD

    def row_of(particle, step):
        return (particle // part_dev) * pair + step * part_dev + particle % part_dev

    first = jnp.stack([row_of(own, 0)] * 2, axis=1)
    second = jnp.stack([row_of(anc, 0), row_of(own, 1)], axis=1)
    targets = jnp.concatenate([jnp.tile(first, (heads, 1)), jnp.tile(second, (heads, 1))]).astype(jnp.int32)
    rope = jnp.asarray(np.stack(rope_tables(context) + rope_tables(context + 1)))
    state = attend_cached(where, anc, rope, scale, queries, near_cache, far_cache, part_dev)
    mixed = attend_new(where, rope, targets, scale, pieces, state, queries[0].shape, part_dev)

    parts = project_back(where, gather_blocks(mixed), w_out)
    attn_part, residual = finish(*sum_rows(parts, pair), x)

    hidden_cols = w_gate.shape[1]
    h, keep, send = project_gate(where, gather_rows(residual), ffn_gain, w_gate)
    gate, gate_arrived = sum_blocks(keep, send)
    up, up_arrived = sum_blocks(*project(h, w_up))
    for piece in gate_arrived:
        gate = gate + piece.astype(F32)
    for piece in up_arrived:
        up = up + piece.astype(F32)
    scale = lax.rsqrt((gate[:, hidden_cols] + gate[:, hidden_cols + 1]) / width + EPS)[:, None]
    hidden = jax.nn.silu(gate[:, :hidden_cols] * scale) * (up * scale)
    parts = project_back(where, gather_blocks(hidden.astype(BF16)), w_down)
    (ffn_part,) = finish(*sum_rows(parts, pair))
    return (attn_part.reshape(2, part_dev, features), ffn_part.reshape(2, part_dev, features))


def solution(mesh):
    return jax.shard_map(
        local,
        mesh=mesh,
        in_specs=(
            P("dp", "tensor"),
            P("dp", "tensor"),
            P("dp", "tensor", None),
            P("dp", "tensor", None),
            P(),
            P("tensor"),
            P("tensor"),
            P("tensor", "dp"),
            P("tensor", "dp"),
            P("dp", "tensor"),
            P("tensor", "dp"),
            P("tensor", "dp"),
            P("dp", "tensor"),
        ),
        out_specs=(P(None, "dp", "tensor"), P(None, "dp", "tensor")),
        check_vma=False,
    )
```

```python
import functools
import math

import jax
import jax.numpy as jnp
import numpy as np
from jax import lax
from jax.experimental import pallas as pl
from jax.experimental.pallas import tpu as pltpu
from jax.sharding import PartitionSpec as P

KVH = 8
HD = 128
EPS = 1e-05
ROPE_BASE = 500000.0
MASKED = -1e30
AROUND = 5 << 30
BF16 = jnp.bfloat16
F32 = jnp.float32


def swap(x, axis, bits):
    size = lax.axis_size(axis)
    return lax.ppermute(x, axis, [(i, i ^ bits) for i in range(size)])


def rope_tables(position):
    half = HD // 2
    freq = np.power(np.float32(ROPE_BASE), -2.0 * np.arange(half, dtype=np.float32) / HD)
    angle = (np.float32(position) * freq.astype(np.float32)).astype(np.float32)
    cosine, sine = np.cos(angle), np.sin(angle)
    return (
        np.concatenate([cosine, cosine]).astype(np.float32),
        np.concatenate([-sine, sine]).astype(np.float32),
    )


SMEM = pl.BlockSpec(memory_space=pltpu.SMEM)
VMEM = pl.BlockSpec(memory_space=pltpu.VMEM)
ANY = pl.BlockSpec(memory_space=pl.ANY)
HBM = pl.BlockSpec(memory_space=pltpu.HBM)


def call(body, outs, ins, specs, scratch=(), flops=0, moved=0, limit=8 << 20, around=1):
    return pl.pallas_call(
        body,
        out_shape=outs,
        in_specs=specs,
        out_specs=jax.tree.map(lambda _: VMEM, outs),
        scratch_shapes=scratch,
        compiler_params=pltpu.CompilerParams(vmem_limit_bytes=limit),
        cost_estimate=pl.CostEstimate(flops=flops + around * AROUND, bytes_accessed=moved, transcendentals=0),
    )(*ins)


def shaped(shape, dtype=BF16):
    return jax.ShapeDtypeStruct(shape, dtype)


def gather_rows(rows, near=None):
    groups = lax.axis_size("dp")
    close = min(groups, 4)
    blocks = {0: rows}
    for k in range(groups - 2, close - 1, -2):
        blocks[k] = swap(rows, "dp", k)
    for k in range(close - 1, 0, -1):
        blocks[k] = swap(rows if near is None else near[k - 1], "dp", k)
    for k in range(groups - 2, close - 1, -2):
        blocks[k + 1] = swap(blocks[k], "dp", 1)
    return [blocks[k] for k in range(groups)]


def gather_blocks(block):
    tensor = lax.axis_size("tensor")
    blocks = {0: block}
    for k in range(2, tensor, 2):
        blocks[k] = swap(block, "tensor", k)
    blocks[1] = swap(block, "tensor", 1)
    for k in range(2, tensor, 2):
        blocks[k + 1] = swap(blocks[k], "tensor", 1)
    return [blocks[k] for k in range(tensor)]


def sum_blocks(keep, send):
    tensor = lax.axis_size("tensor")
    rows = keep.shape[0] // (tensor // 2)
    paired = (keep + swap(send, "tensor", 1).astype(F32)).reshape(tensor // 2, rows, -1)
    return paired[0], [swap(paired[i].astype(BF16), "tensor", 2 * i) for i in range(1, tensor // 2)]


def slot(relative, size):
    return lax.shift_right_logical(relative, 1) + (relative & 1) * (size // 2)


def tiles(columns):
    for tile in (256, 384, 128):
        if columns % tile == 0:
            return tile
    return columns


def multiply(left, w_ref, write):
    columns = w_ref.shape[1]
    tile = tiles(columns)
    for first in range(0, columns, tile):
        write(first, tile, jnp.dot(left, w_ref[:, first : first + tile], preferred_element_type=F32))


def stack_tokens(x_first, x_second):
    def body(first_ref, second_ref, out_ref):
        out_ref[...] = jnp.concatenate([first_ref[...].astype(F32), second_ref[...].astype(F32)], axis=0).astype(BF16)

    part_dev, features = x_first.shape
    return call(body, shaped((2 * part_dev, features)), (x_first, x_second), [VMEM] * 2)


def cache_piece(where_ref, keys_ref, values_ref, k):
    groups = lax.axis_size("dp")
    head = lax.div((where_ref[0] ^ k) * KVH, groups)
    lanes = pl.ds(pl.multiple_of(head * HD, HD), HD)
    tiles_of = [ref[p, :, lanes].astype(F32) for ref in (keys_ref, values_ref) for p in range(keys_ref.shape[0])]
    return jnp.concatenate(tiles_of, axis=1)


def pack_near(where, x, cache_keys, cache_values):
    part_dev, span, _ = cache_keys.shape
    close = min(lax.axis_size("dp"), 4)
    wide = 2 * part_dev * HD
    joined = x.shape[1] == wide

    def body(where_ref, x_ref, keys_ref, values_ref, own_ref, *out_refs):
        own_ref[...] = cache_piece(where_ref, keys_ref, values_ref, 0).astype(BF16)
        for k, out_ref in enumerate(out_refs, 1):
            piece = cache_piece(where_ref, keys_ref, values_ref, k)
            if joined:
                piece = jnp.concatenate([x_ref[...].astype(F32), piece], axis=0)
            out_ref[...] = piece.astype(BF16)

    height = span + (x.shape[0] if joined else 0)
    own, *near = call(
        body,
        (shaped((span, wide)),) + (shaped((height, wide)),) * (close - 1),
        (where, x, cache_keys, cache_values),
        [SMEM] + [VMEM] * 3,
        flops=2 * AROUND,
    )
    return own, near, joined


def pack_far(where, cache_keys, cache_values, afters):
    groups = lax.axis_size("dp")
    part_dev, span, _ = cache_keys.shape
    wide = 2 * part_dev * HD
    close = min(groups, 4)

    def body(where_ref, keys_ref, values_ref, *refs):
        for i, out_ref in enumerate(refs[len(afters) :]):
            for odd in range(2):
                out_ref[odd] = cache_piece(where_ref, keys_ref, values_ref, close + 2 * i + odd).astype(BF16)

    return call(
        body,
        (shaped((2, span, wide)),) * ((groups - close) // 2),
        (where, cache_keys, cache_values, *afters),
        [SMEM, VMEM, VMEM] + [ANY] * len(afters),
        flops=AROUND,
    )


def collect_near(own, near, span):
    def body(own_ref, *refs):
        refs[-1][0] = own_ref[...]
        for k, ref in enumerate(refs[:-1], 1):
            refs[-1][k] = ref[...].astype(F32)[ref.shape[0] - span :].astype(BF16)

    return call(body, shaped((1 + len(near),) + own.shape), (own, *near), [VMEM] * (1 + len(near)), around=1)


def cross_chips(block):
    return [block] + [swap(block, "tensor", k) for k in range(2, lax.axis_size("tensor"), 2)]


def cross_cores(near, far, after):
    close, span, wide = near[0].shape
    total = close + far[0].shape[0]

    def body(after_ref, *refs):
        for i in range(len(near)):
            refs[-1][i, :close] = refs[i][...]
            refs[-1][i, close:] = refs[len(near) + i][...]

    ins = (after, *near, *far)
    even = call(body, shaped((len(near), total, span, wide)), ins, [ANY] + [VMEM] * (2 * len(near)), around=0)
    return even, swap(even, "tensor", 1)


def last_entries(pieces, after):
    def body(after_ref, *refs):
        for i, ref in enumerate(refs[:-1]):
            refs[-1][i] = ref[1]

    ins = (after, *pieces)
    return call(body, shaped((len(pieces),) + pieces[0].shape[1:]), ins, [ANY] + [VMEM] * len(pieces), around=1)


def collect_far(pieces, passed):
    def body(*refs):
        for i, ref in enumerate(refs[:-2]):
            refs[-1][2 * i] = ref[0]
            refs[-1][2 * i + 1] = refs[-2][i]

    shape = (2 * len(pieces),) + pieces[0].shape[1:]
    return call(body, shaped(shape), (*pieces, passed), [VMEM] * (1 + len(pieces)), around=1)


def lift(where_ref, gain_ref, block_refs, h_ref, ss_ref, absolute):
    groups = len(block_refs)
    tensor = lax.axis_size("tensor")
    pair = block_refs[0].shape[0]
    near = groups // tensor
    d, t = where_ref[0], where_ref[1]
    gain = gain_ref[...]
    places = []
    for k in range(groups):
        g = d ^ k
        place = slot(lax.div(g, near) ^ t, tensor) * near + lax.rem(g, near)
        place = pl.multiple_of(place * pair, pair)
        wide = block_refs[k][...].astype(F32)[:pair]
        squares = jnp.broadcast_to(jnp.sum(wide * wide, axis=1, keepdims=True), (pair, 128))
        ss_ref[pl.ds(pl.multiple_of(g * pair, pair) if absolute else place, pair), :] = squares
        h_ref[pl.ds(place, pair), :] = (wide * gain).astype(BF16)
        places.append((pl.multiple_of(g * pair, pair), place))
    return places


def split(total, base, lane):
    high = total.astype(BF16).astype(F32)
    return jnp.where(lane == 0, high, jnp.where(lane == 1, total - high, base))


def stacked(rows, parts):
    width = rows.shape[1] // parts
    return jnp.concatenate([rows[:, i * width : (i + 1) * width] for i in range(parts)], axis=0)


def unstacked(rows, parts):
    height = rows.shape[0] // parts
    return jnp.concatenate([rows[i * height : (i + 1) * height] for i in range(parts)], axis=1)


def project_attention(where, blocks, gain, w_keyval, w_query, after):
    pair, features = blocks[0].shape
    rows = len(blocks) * pair
    half = rows // 2
    columns = w_keyval.shape[1]
    wide = w_query.shape[1]
    base = columns + 128

    def body(where_ref, gain_ref, *refs):
        block_refs, refs = refs[: len(blocks)], refs[len(blocks) :]
        w_kv_ref, w_q_ref, after_ref, message_ref, keep_ref, h_ref, ss_ref, product = refs
        places = lift(where_ref, gain_ref, block_refs, h_ref, ss_ref, True)
        h = h_ref[...]
        product[...] = jnp.dot(h, w_kv_ref[...], preferred_element_type=F32)
        for to, place in places:
            message_ref[pl.ds(to, pair), :columns] = product[pl.ds(place, pair), :].astype(BF16)
        squares = ss_ref[...]
        lane = lax.broadcasted_iota(jnp.int32, squares.shape, 1)
        message_ref[:, columns:base] = split(squares, 0.0, lane).astype(BF16)
        tile = tiles(wide // 2)
        for first in range(0, wide, tile):
            queries = jnp.dot(h, w_q_ref[:, first : first + tile], preferred_element_type=F32)
            keep_ref[:, first : first + tile] = queries[:half]
            below, lanes = divmod(first, wide // 2)
            lanes += base
            message_ref[below * half : (below + 1) * half, lanes : lanes + tile] = queries[half:].astype(BF16)

    return call(
        body,
        (shaped((rows, base + wide // 2)), shaped((half, wide), F32)),
        (where, gain[None], *blocks, w_keyval, w_query, after),
        [SMEM] + [VMEM] * (3 + len(blocks)) + [ANY],
        [pltpu.VMEM((rows, features), BF16), pltpu.VMEM((rows, 128), F32), pltpu.VMEM((rows, columns), F32)],
        flops=2 * rows * (w_keyval.size + w_query.size),
        moved=4 * rows * features + 2 * (w_keyval.size + w_query.size),
    )


def direct_keyvals():
    return lax.axis_size("dp") == KVH and lax.axis_size("tensor") == 4


def add_cores(where, own, keep, arrived, after):
    tensor = lax.axis_size("tensor")
    groups = lax.axis_size("dp")
    rows, total = own.shape
    half, wide = keep.shape
    base = total - wide // 2
    height = 2 * half // tensor
    direct = direct_keyvals()

    def body(where_ref, own_ref, keep_ref, arrived_ref, after_ref, first_ref, message_ref, *out_refs):
        summed = own_ref[:, :base].astype(F32) + arrived_ref[:, :base].astype(F32)
        ends = summed[:, base - 128 :]
        lane = lax.broadcasted_iota(jnp.int32, ends.shape, 1)
        ends = split(ends[:, 0:1] + ends[:, 1:2], ends, lane).astype(BF16)
        queries = keep_ref[...] + unstacked(arrived_ref[:, base:].astype(F32), 2)
        first_ref[...] = queries[:height]
        if direct:
            message_ref[:, :128] = ends
            message_ref[:, 128:] = stacked(queries[height:], 4).astype(BF16)
            lower = where_ref[0] < groups // 2
            one, two = summed[:, :HD], summed[:, HD : 2 * HD]
            out_refs[0][...] = jnp.where(lower, one, two).astype(BF16)
            out_refs[1][...] = jnp.where(lower, two, one).astype(BF16)
        else:
            message_ref[:, : base - 128] = summed[:, : base - 128].astype(BF16)
            message_ref[:, base - 128 :] = ends
            for i, out_ref in enumerate(out_refs, 1):
                out_ref[...] = queries[i * height : (i + 1) * height].astype(BF16)

    outs = [shaped((height, wide), F32), shaped((rows, 128 + wide // 4 if direct else base))]
    outs += [shaped((rows, HD))] * 2 if direct else [shaped((height, wide))] * (tensor // 2 - 1)
    ins = (where, own, keep, arrived, after)
    return call(body, tuple(outs), ins, [SMEM] + [VMEM] * 3 + [ANY], moved=6 * own.size)


def row_scale(own, arrived, width):
    def body(own_ref, arrived_ref, out_ref):
        squares = own_ref[:, :128].astype(F32) + arrived_ref[:, :128].astype(F32)
        scale = lax.rsqrt((squares[:, 0:1] + squares[:, 1:2]) / width + EPS)
        out_ref[...] = jnp.broadcast_to(scale, squares.shape)

    return call(body, shaped((own.shape[0], 128), F32), (own, arrived), [VMEM] * 2)


def add_keyvals(own, arrived):
    rows, columns = own.shape

    def body(own_ref, arrived_ref, out_ref):
        summed = own_ref[...].astype(F32) + arrived_ref[...].astype(F32)
        ends = summed[:, columns - 128 :]
        lane = lax.broadcasted_iota(jnp.int32, ends.shape, 1)
        out_ref[:, : columns - 128] = summed[:, : columns - 128].astype(BF16)
        out_ref[:, columns - 128 :] = split(ends[:, 0:1] + ends[:, 1:2], ends, lane).astype(BF16)

    return call(body, shaped(own.shape), (own, arrived), [VMEM] * 2, moved=6 * own.size)


def finish_keyvals(where, own, arrived, columns, width):
    groups = lax.axis_size("dp")
    rows = own.shape[0]
    lanes = slice(0, columns + 128)

    def body(where_ref, own_ref, arrived_ref, scale_ref, *out_refs):
        summed = own_ref[:, lanes].astype(F32) + arrived_ref[:, lanes].astype(F32)
        squares = summed[:, columns : columns + 1] + summed[:, columns + 1 : columns + 2]
        scale = lax.rsqrt(squares / width + EPS)
        scale_ref[...] = jnp.broadcast_to(scale, (rows, 128))
        scaled = summed[:, :columns] * scale
        if groups == KVH:
            lower = where_ref[0] < groups // 2
            out_refs[0][...] = jnp.where(lower, scaled[:, :HD], scaled[:, HD:]).astype(BF16)
            out_refs[1][...] = jnp.where(lower, scaled[:, HD:], scaled[:, :HD]).astype(BF16)
        else:
            out_refs[0][...] = scaled.astype(BF16)

    outs = [shaped((rows, 128), F32)]
    outs += [shaped((rows, HD))] * 2 if groups == KVH else [shaped((rows, columns))]
    return call(body, tuple(outs), (where, own, arrived), [SMEM, VMEM, VMEM], moved=8 * own.size, around=1)


def project(h, w):
    half = h.shape[0] // 2

    def body(h_ref, w_ref, keep_ref, send_ref):
        def write(first, tile, product):
            keep_ref[:, first : first + tile] = product[:half]
            send_ref[:, first : first + tile] = product[half:].astype(BF16)

        multiply(h_ref[...], w_ref, write)

    columns = w.shape[1]
    return call(
        body,
        (shaped((half, columns), F32), shaped((half, columns))),
        (h, w),
        [VMEM] * 2,
        flops=4 * half * w.size,
        moved=2 * w.size,
    )


def project_gate(where, blocks, gain, w):
    pair, features = blocks[0].shape
    rows = len(blocks) * pair
    half = rows // 2
    columns = w.shape[1]

    def body(where_ref, gain_ref, *refs):
        block_refs, (w_ref, h_ref, keep_ref, send_ref, ss_ref) = refs[: len(blocks)], refs[len(blocks) :]
        lift(where_ref, gain_ref, block_refs, h_ref, ss_ref, False)

        def write(first, tile, product):
            keep_ref[:, first : first + tile] = product[:half]
            send_ref[:, first : first + tile] = product[half:].astype(BF16)

        multiply(h_ref[...], w_ref, write)
        squares = ss_ref[...]
        high = squares.astype(BF16).astype(F32)
        lane = lax.broadcasted_iota(jnp.int32, squares.shape, 1)
        ends = jnp.where(lane == 0, high, jnp.where(lane == 1, squares - high, 0.0))
        keep_ref[:, columns:] = ends[:half]
        send_ref[:, columns:] = ends[half:].astype(BF16)

    return call(
        body,
        (shaped((rows, features)), shaped((half, columns + 128), F32), shaped((half, columns + 128))),
        (where, gain[None], *blocks, w),
        [SMEM] + [VMEM] * (2 + len(blocks)),
        [pltpu.VMEM((rows, 128), F32)],
        flops=2 * rows * w.size,
        moved=4 * rows * features + 2 * w.size,
    )


def project_back(where, blocks, w):
    groups = lax.axis_size("dp")
    rows, depth = blocks[0].shape
    near = groups // len(blocks)
    pair = rows // near
    total = len(blocks) * rows
    columns = w.shape[1]
    close = min(groups, 4)
    far = (groups - close) // 2

    def body(where_ref, *refs):
        block_refs, (w_ref, *out_refs) = refs[: len(blocks)], refs[len(blocks) :]
        left = out_refs[-1]
        d, t = where_ref[0], where_ref[1]
        for k, block_ref in enumerate(block_refs):
            for i in range(near):
                relative = ((t ^ k) * near + i) ^ d
                beyond = close + lax.shift_right_logical(relative - close, 1) + (relative & 1) * far
                place = jnp.where(relative < close, relative, beyond)
                left[pl.ds(pl.multiple_of(place * pair, pair), pair), :] = block_ref[i * pair : (i + 1) * pair, :]

        def write(first, tile, product):
            lanes = slice(first, first + tile)
            for i in range(close):
                out_refs[i][:, lanes] = product[i * pair : (i + 1) * pair].astype(out_refs[i].dtype)
            middle = (close + far) * pair
            cut = middle + far // 2 * pair
            out_refs[close][:, lanes] = product[close * pair : middle]
            out_refs[close + 1][:, lanes] = product[middle:cut].astype(BF16)
            out_refs[close + 2][:, lanes] = product[cut:].astype(BF16)

        multiply(left[...], w_ref, write)

    outs = [shaped((pair, columns), F32)] + [shaped((pair, columns))] * (close - 1)
    outs += [shaped((far * pair, columns), F32)] + [shaped((far // 2 * pair, columns))] * 2
    return call(
        body,
        tuple(outs),
        (where, *blocks, w),
        [SMEM] + [VMEM] * (1 + len(blocks)),
        [pltpu.VMEM((total, depth), BF16)],
        flops=2 * total * w.size,
        moved=2 * w.size,
    )


def add_pairs(keep, arrived, first, pair, passed=()):
    count = arrived.shape[0] // pair

    def body(keep_ref, arrived_ref, *refs):
        for i, out_ref in enumerate(refs[len(passed) : len(passed) + count]):
            own = keep_ref[first + i * pair : first + (i + 1) * pair, :]
            out_ref[...] = (own + arrived_ref[i * pair : (i + 1) * pair, :].astype(F32)).astype(BF16)
        for ref, out_ref in zip(refs[: len(passed)], refs[len(passed) + count :]):
            out_ref[...] = ref[...]

    outs = (shaped((pair, keep.shape[1])),) * (count + len(passed))
    ins = (keep, arrived, *passed)
    return call(body, outs, ins, [VMEM] * len(ins), moved=8 * arrived.size)


def sum_rows(parts, pair):
    own, *near, keep, one, two = parts
    count = one.shape[0] // pair
    sums = add_pairs(keep, swap(one, "dp", 1), 0, pair, near[:1])
    sums, near = list(sums[:count]), [*sums[count:], *near[1:]]
    sums += add_pairs(keep, swap(two, "dp", 1), one.shape[0], pair)
    arrived = [swap(piece, "dp", len(near) + 1 + 2 * i) for i, piece in enumerate(sums)]
    arrived += [swap(piece, "dp", k + 1) for k, piece in enumerate(near)]
    return own, arrived


def finish(own, arrived, x=None):
    def body(own_ref, *refs):
        total = own_ref[...]
        for ref in refs[: len(arrived)]:
            total = total + ref[...].astype(F32)
        rounded = total.astype(BF16)
        if x is None:
            refs[-1][...] = rounded
        else:
            refs[-2][...] = rounded
            refs[-1][...] = (refs[len(arrived)][...].astype(F32) + rounded.astype(F32)).astype(BF16)

    outs = (shaped(own.shape),) * (1 if x is None else 2)
    ins = (own, *arrived) + (() if x is None else (x,))
    return call(body, outs, ins, [VMEM] * len(ins), moved=8 * own.size)


def attend_cached(where, anc, rope, scale, queries, cache, part_dev):
    tensor = lax.axis_size("tensor")
    groups = lax.axis_size("dp")
    near = groups // tensor
    pair = 2 * part_dev
    span = cache[0].shape[2]
    ctx = tensor * span
    height, columns = queries[0].shape
    heads = columns // HD
    parts = near * part_dev
    rows = heads * parts

    def body(where_ref, anc_ref, rope_ref, scale_ref, *refs):
        q_refs, refs = refs[: len(queries)], refs[len(queries) :]
        cache_refs = [ref.at[i] for ref in refs[:2] for i in range(tensor // 2)]
        query_ref, mixed_ref, highest_ref, total_ref, keys_ref, values_ref = refs[2:]
        d, t = where_ref[0], where_ref[1]
        query_sum = q_refs[0][...]
        for ref in q_refs[1:]:
            if ref.shape[0] == height:
                query_sum = query_sum + ref[...].astype(F32)
            else:
                lanes = slice(ref.shape[1] - columns // 4, ref.shape[1])
                query_sum = query_sum + unstacked(ref[:, lanes].astype(F32), 4)
        query_sum = query_sum * scale_ref[pl.ds(pl.multiple_of(t * near * pair, pair), near * pair), 0:1]
        for step in range(2):

            def bring(i, _, step=step):
                particle = t * parts + i if step == 0 else anc_ref[i]
                block, member = lax.div(particle, part_dev) ^ d, lax.rem(particle, part_dev)

                for k, cache_ref in enumerate(cache_refs):
                    to = pl.ds(pl.multiple_of(i * ctx + k * span, 8), span)
                    lanes = pl.ds(pl.multiple_of(member * HD, HD), HD)
                    keys_ref[to, :] = cache_ref[block, :, lanes].astype(F32)
                    lanes = pl.ds(pl.multiple_of((part_dev + member) * HD, HD), HD)
                    values_ref[to, :] = cache_ref[block, :, lanes].astype(F32)
                return 0

            lax.fori_loop(0, parts, bring, 0)
            keys = keys_ref[...].astype(BF16)
            values = values_ref[...].astype(BF16)
            per_head = []
            for h in range(heads):
                for b in range(near):
                    first = b * pair + step * part_dev
                    per_head.append(query_sum[first : first + part_dev, h * HD : (h + 1) * HD])
            query = jnp.concatenate(per_head, axis=0).astype(BF16).astype(F32)
            cosine = rope_ref[2 * step : 2 * step + 1, :]
            sine = rope_ref[2 * step + 1 : 2 * step + 2, :]
            query = (query * cosine + pltpu.roll(query, HD // 2, 1) * sine).astype(BF16)
            scores = lax.dot_general(query, keys, (((1,), (1,)), ((), ())), preferred_element_type=F32)
            scores = scores * (1.0 / math.sqrt(HD))
            row_part = lax.rem(lax.broadcasted_iota(jnp.int32, (rows, 1), 0), parts)
            col_part = lax.div(lax.broadcasted_iota(jnp.int32, (1, parts * ctx), 1), ctx)
            scores = jnp.where(row_part == col_part, scores, MASKED)
            highest = jnp.max(scores, axis=1, keepdims=True)
            weights = jnp.exp(scores - highest)
            here = slice(step * rows, (step + 1) * rows)
            query_ref[here, :] = query
            mixed_ref[here, :] = jnp.dot(weights.astype(BF16), values, preferred_element_type=F32)
            highest_ref[here, :] = jnp.broadcast_to(highest, (rows, 128))
            total_ref[here, :] = jnp.broadcast_to(jnp.sum(weights, axis=1, keepdims=True), (rows, 128))

    ins = (where, anc, rope, scale, *queries, *cache)
    return call(
        body,
        (shaped((2 * rows, HD)), shaped((2 * rows, HD), F32), shaped((2 * rows, 128), F32), shaped((2 * rows, 128), F32)),
        ins,
        [SMEM] * 2 + [VMEM] * (len(ins) - 2),
        [pltpu.VMEM((parts * ctx, HD), F32), pltpu.VMEM((parts * ctx, HD), F32)],
        limit=(4 << 20) + 12 * rows * parts * ctx,
        moved=4 << 20,
    )


def attend_new(where, rope, targets, scale, pieces, state, shape, part_dev):
    groups = lax.axis_size("dp")
    tensor = lax.axis_size("tensor")
    near = groups // tensor
    pair = 2 * part_dev
    parts = near * part_dev
    heads = shape[1] // HD
    rows = heads * parts

    def body(where_ref, rope_ref, target_ref, scale_ref, *refs):
        piece_refs, (query_ref, mixed_ref, highest_ref, total_ref, out_ref) = refs[: len(pieces)], refs[len(pieces) :]
        even = where_ref[0] % 2 == 0 if groups == KVH else True
        if len(pieces) == 2:
            one, two = [ref[...].astype(F32) for ref in piece_refs]
        else:
            one, two = [piece_refs[i][...].astype(F32) + piece_refs[i + 1][...].astype(F32) for i in (0, 2)]
            one, two = [(x * scale_ref[...]).astype(BF16).astype(F32) for x in (one, two)]
        plain = jnp.where(even, one, two)
        values = jnp.where(even, two, one).astype(BF16)
        cosine = jnp.concatenate([jnp.broadcast_to(rope_ref[2 * s : 2 * s + 1, :], (part_dev, HD)) for s in range(2)])
        sine = jnp.concatenate([jnp.broadcast_to(rope_ref[2 * s + 1 : 2 * s + 2, :], (part_dev, HD)) for s in range(2)])
        turned = pltpu.roll(plain, HD // 2, 1).reshape(groups, pair, HD)
        keys = plain.reshape(groups, pair, HD) * cosine[None] + turned * sine[None]
        keys = keys.reshape(groups * pair, HD).astype(BF16)
        scores = lax.dot_general(query_ref[...], keys, (((1,), (1,)), ((), ())), preferred_element_type=F32)
        scores = scores * (1.0 / math.sqrt(HD))
        col = lax.broadcasted_iota(jnp.int32, (1, groups * pair), 1)
        wanted = (col == target_ref[:, 0:1]) | (col == target_ref[:, 1:2])
        scores = jnp.where(wanted, scores, MASKED)
        before = highest_ref[:, 0:1]
        highest = jnp.maximum(before, jnp.max(scores, axis=1, keepdims=True))
        weights = jnp.exp(scores - highest)
        keep = jnp.exp(before - highest)
        total = total_ref[:, 0:1] * keep + jnp.sum(weights, axis=1, keepdims=True)
        mixed = mixed_ref[...] * keep + jnp.dot(weights.astype(BF16), values, preferred_element_type=F32)
        mixed = mixed / total
        for h in range(heads):
            for b in range(near):
                first = h * parts + b * part_dev
                both = [mixed[s * rows + first : s * rows + first + part_dev] for s in range(2)]
                here = slice(b * pair, (b + 1) * pair)
                out_ref[here, h * HD : (h + 1) * HD] = jnp.concatenate(both, axis=0).astype(BF16)

    ins = (where, rope, targets, scale, *pieces, *state)
    return call(body, shaped(shape), ins, [SMEM] + [VMEM] * (len(ins) - 1), moved=1 << 20)


def send_keyvals(pieces):
    groups = lax.axis_size("dp")
    tensor = lax.axis_size("tensor")
    half = groups // 2
    moved = []
    for flip, piece in enumerate(pieces):
        to = [2 * i + flip for i in range(half)] + [2 * i + 1 - flip for i in range(half)]
        for k in (0, 2):
            pairs = [(i * tensor + t, to[i] * tensor + (t ^ k)) for i in range(groups) for t in range(tensor)]
            moved.append(lax.ppermute(piece, ("dp", "tensor"), pairs))
    return moved


def move_keyvals(pieces):
    groups = lax.axis_size("dp")
    d = lax.axis_index("dp")
    if groups == KVH:
        half = groups // 2
        one = [(i, 2 * i) for i in range(half)] + [(half + i, 2 * i + 1) for i in range(half)]
        two = [(i, 2 * i + 1) for i in range(half)] + [(half + i, 2 * i) for i in range(half)]
        return [lax.ppermute(x, "dp", to) for x, to in zip(pieces, (one, two))]
    every = lax.all_gather(pieces[0], "dp", axis=1, tiled=True)
    start = (d * KVH // groups) * HD
    return [lax.dynamic_slice_in_dim(every, first + start, HD, axis=1) for first in (0, KVH * HD)]


def local(
    x_first,
    x_second,
    cache_keys,
    cache_values,
    ancestors,
    attn_gain,
    ffn_gain,
    w_query,
    w_keyval,
    w_out,
    w_gate,
    w_up,
    w_down,
):
    groups = lax.axis_size("dp")
    tensor = lax.axis_size("tensor")
    part_dev, features = x_first.shape
    span = cache_keys.shape[1]
    width = features * tensor
    context = span * tensor
    d = lax.axis_index("dp")
    t = lax.axis_index("tensor")
    pair = 2 * part_dev
    near = groups // tensor
    parts = near * part_dev
    where = jnp.stack([d, t]).astype(jnp.int32)

    x = stack_tokens(x_first, x_second)
    own_piece, near_pieces, joined = pack_near(where, x, cache_keys, cache_values)
    blocks = gather_rows(x, near_pieces if joined else None)
    close = min(groups, 4)
    near_moved = blocks[1:close] if joined else [swap(piece, "dp", k) for k, piece in enumerate(near_pieces, 1)]
    near_cache = cross_chips(collect_near(own_piece, near_moved, span))
    packed = pack_far(where, cache_keys, cache_values, blocks[close::2])
    far_pieces = [swap(piece, "dp", close + 2 * i) for i, piece in enumerate(packed)]

    message, keep = project_attention(where, blocks, attn_gain, w_keyval, w_query, x)
    queries, message, *leaving = add_cores(where, message, keep, swap(message, "tensor", 1), near_cache[-1])
    passed = swap(last_entries(far_pieces, x), "dp", 1)
    far_cache = cross_chips(collect_far(far_pieces, passed))
    if direct_keyvals():
        pieces = send_keyvals(leaving)
        arrived = swap(message, "tensor", 2)
        scale = row_scale(message, arrived, width)
        queries = [queries, arrived]
    else:
        bits = 2
        while 2 * bits < tensor:
            message = add_keyvals(message, swap(message, "tensor", bits))
            bits *= 2
        arrived = swap(message, "tensor", bits)
        scale, *pieces = finish_keyvals(where, message, arrived, w_keyval.shape[1], width)
        pieces = move_keyvals(pieces)
        queries = [queries] + [swap(piece, "tensor", 2 * i) for i, piece in enumerate(leaving, 1)]

    cache = cross_cores(near_cache, far_cache, pieces[1] if direct_keyvals() else arrived)

    own = t * parts + jnp.arange(parts, dtype=jnp.int32)
    anc = lax.dynamic_slice_in_dim(ancestors, t * parts, parts).astype(jnp.int32)
    heads = w_query.shape[1] // HD

    def row_of(particle, step):
        return (particle // part_dev) * pair + step * part_dev + particle % part_dev

    first = jnp.stack([row_of(own, 0)] * 2, axis=1)
    second = jnp.stack([row_of(anc, 0), row_of(own, 1)], axis=1)
    targets = jnp.concatenate([jnp.tile(first, (heads, 1)), jnp.tile(second, (heads, 1))]).astype(jnp.int32)
    rope = jnp.asarray(np.stack(rope_tables(context) + rope_tables(context + 1)))
    state = attend_cached(where, anc, rope, scale, queries, cache, part_dev)
    mixed = attend_new(where, rope, targets, scale, pieces, state, queries[0].shape, part_dev)

    parts = project_back(where, gather_blocks(mixed), w_out)
    attn_part, residual = finish(*sum_rows(parts, pair), x)

    hidden_cols = w_gate.shape[1]
    h, keep, send = project_gate(where, gather_rows(residual), ffn_gain, w_gate)
    gate, gate_arrived = sum_blocks(keep, send)
    up, up_arrived = sum_blocks(*project(h, w_up))
    for piece in gate_arrived:
        gate = gate + piece.astype(F32)
    for piece in up_arrived:
        up = up + piece.astype(F32)
    scale = lax.rsqrt((gate[:, hidden_cols] + gate[:, hidden_cols + 1]) / width + EPS)[:, None]
    hidden = jax.nn.silu(gate[:, :hidden_cols] * scale) * (up * scale)
    parts = project_back(where, gather_blocks(hidden.astype(BF16)), w_down)
    (ffn_part,) = finish(*sum_rows(parts, pair))
    return (attn_part.reshape(2, part_dev, features), ffn_part.reshape(2, part_dev, features))


def solution(mesh):
    return jax.shard_map(
        local,
        mesh=mesh,
        in_specs=(
            P("dp", "tensor"),
            P("dp", "tensor"),
            P("dp", "tensor", None),
            P("dp", "tensor", None),
            P(),
            P("tensor"),
            P("tensor"),
            P("tensor", "dp"),
            P("tensor", "dp"),
            P("dp", "tensor"),
            P("tensor", "dp"),
            P("tensor", "dp"),
            P("dp", "tensor"),
        ),
        out_specs=(P(None, "dp", "tensor"), P(None, "dp", "tensor")),
        check_vma=False,
    )
```

```python
import functools
import math

import jax
import jax.numpy as jnp
import numpy as np
from jax import lax
from jax.experimental import pallas as pl
from jax.experimental.pallas import tpu as pltpu
from jax.sharding import PartitionSpec as P

KVH = 8
HD = 128
EPS = 1e-05
ROPE_BASE = 500000.0
MASKED = -1e30
AROUND = 5 << 30
BF16 = jnp.bfloat16
F32 = jnp.float32


def swap(x, axis, bits):
    size = lax.axis_size(axis)
    return lax.ppermute(x, axis, [(i, i ^ bits) for i in range(size)])


def rope_tables(position):
    half = HD // 2
    freq = np.power(np.float32(ROPE_BASE), -2.0 * np.arange(half, dtype=np.float32) / HD)
    angle = (np.float32(position) * freq.astype(np.float32)).astype(np.float32)
    cosine, sine = np.cos(angle), np.sin(angle)
    return (
        np.concatenate([cosine, cosine]).astype(np.float32),
        np.concatenate([-sine, sine]).astype(np.float32),
    )


SMEM = pl.BlockSpec(memory_space=pltpu.SMEM)
VMEM = pl.BlockSpec(memory_space=pltpu.VMEM)
ANY = pl.BlockSpec(memory_space=pl.ANY)
HBM = pl.BlockSpec(memory_space=pltpu.HBM)


def call(body, outs, ins, specs, scratch=(), flops=0, moved=0, limit=8 << 20, around=1):
    return pl.pallas_call(
        body,
        out_shape=outs,
        in_specs=specs,
        out_specs=jax.tree.map(lambda _: VMEM, outs),
        scratch_shapes=scratch,
        compiler_params=pltpu.CompilerParams(vmem_limit_bytes=limit),
        cost_estimate=pl.CostEstimate(flops=flops + around * AROUND, bytes_accessed=moved, transcendentals=0),
    )(*ins)


def shaped(shape, dtype=BF16):
    return jax.ShapeDtypeStruct(shape, dtype)


def gather_rows(rows, near=None):
    groups = lax.axis_size("dp")
    close = min(groups, 4)
    blocks = {0: rows}
    for k in range(groups - 2, close - 1, -2):
        blocks[k] = swap(rows, "dp", k)
    for k in range(close - 1, 0, -1):
        blocks[k] = swap(rows if near is None else near[k - 1], "dp", k)
    for k in range(groups - 2, close - 1, -2):
        blocks[k + 1] = swap(blocks[k], "dp", 1)
    return [blocks[k] for k in range(groups)]


def gather_blocks(block):
    tensor = lax.axis_size("tensor")
    blocks = {0: block}
    for k in range(2, tensor, 2):
        blocks[k] = swap(block, "tensor", k)
    blocks[1] = swap(block, "tensor", 1)
    for k in range(2, tensor, 2):
        blocks[k + 1] = swap(blocks[k], "tensor", 1)
    return [blocks[k] for k in range(tensor)]


def sum_blocks(keep, send):
    tensor = lax.axis_size("tensor")
    rows = keep.shape[0] // (tensor // 2)
    paired = (keep + swap(send, "tensor", 1).astype(F32)).reshape(tensor // 2, rows, -1)
    return paired[0], [swap(paired[i].astype(BF16), "tensor", 2 * i) for i in range(1, tensor // 2)]


def slot(relative, size):
    return lax.shift_right_logical(relative, 1) + (relative & 1) * (size // 2)


def tiles(columns):
    for tile in (256, 384, 128):
        if columns % tile == 0:
            return tile
    return columns


def multiply(left, w_ref, write):
    columns = w_ref.shape[1]
    tile = tiles(columns)
    for first in range(0, columns, tile):
        write(first, tile, jnp.dot(left, w_ref[:, first : first + tile], preferred_element_type=F32))


def stack_tokens(x_first, x_second):
    def body(first_ref, second_ref, out_ref):
        out_ref[...] = jnp.concatenate([first_ref[...].astype(F32), second_ref[...].astype(F32)], axis=0).astype(BF16)

    part_dev, features = x_first.shape
    return call(body, shaped((2 * part_dev, features)), (x_first, x_second), [VMEM] * 2)


def cache_piece(where_ref, keys_ref, values_ref, k):
    groups = lax.axis_size("dp")
    head = lax.div((where_ref[0] ^ k) * KVH, groups)
    lanes = pl.ds(pl.multiple_of(head * HD, HD), HD)
    tiles_of = [ref[p, :, lanes].astype(F32) for ref in (keys_ref, values_ref) for p in range(keys_ref.shape[0])]
    return jnp.concatenate(tiles_of, axis=1)


def pack_near(where, x, cache_keys, cache_values):
    part_dev, span, _ = cache_keys.shape
    close = min(lax.axis_size("dp"), 4)
    wide = 2 * part_dev * HD
    joined = x.shape[1] == wide

    def body(where_ref, x_ref, keys_ref, values_ref, own_ref, *out_refs):
        own_ref[...] = cache_piece(where_ref, keys_ref, values_ref, 0).astype(BF16)
        for k, out_ref in enumerate(out_refs, 1):
            piece = cache_piece(where_ref, keys_ref, values_ref, k)
            if joined:
                piece = jnp.concatenate([x_ref[...].astype(F32), piece], axis=0)
            out_ref[...] = piece.astype(BF16)

    height = span + (x.shape[0] if joined else 0)
    own, *near = call(
        body,
        (shaped((span, wide)),) + (shaped((height, wide)),) * (close - 1),
        (where, x, cache_keys, cache_values),
        [SMEM] + [VMEM] * 3,
        flops=2 * AROUND,
    )
    return own, near, joined


def pack_far(where, cache_keys, cache_values, afters):
    groups = lax.axis_size("dp")
    part_dev, span, _ = cache_keys.shape
    wide = 2 * part_dev * HD
    close = min(groups, 4)

    def body(where_ref, keys_ref, values_ref, *refs):
        for i, out_ref in enumerate(refs[len(afters) :]):
            for odd in range(2):
                out_ref[odd] = cache_piece(where_ref, keys_ref, values_ref, close + 2 * i + odd).astype(BF16)

    return call(
        body,
        (shaped((2, span, wide)),) * ((groups - close) // 2),
        (where, cache_keys, cache_values, *afters),
        [SMEM, VMEM, VMEM] + [ANY] * len(afters),
        flops=AROUND,
    )


def collect_near(own, near, span):
    def body(own_ref, *refs):
        refs[-1][0] = own_ref[...]
        for k, ref in enumerate(refs[:-1], 1):
            refs[-1][k] = ref[...].astype(F32)[ref.shape[0] - span :].astype(BF16)

    return call(body, shaped((1 + len(near),) + own.shape), (own, *near), [VMEM] * (1 + len(near)), around=1)


def gather_cache(block, after):
    blocks = [block] + [swap(block, "tensor", k) for k in range(2, lax.axis_size("tensor"), 2)]

    def body(after_ref, *refs):
        for i, ref in enumerate(refs[:-1]):
            refs[-1][i] = ref[...]

    ins = (after, *blocks)
    both = call(body, shaped((len(blocks),) + block.shape), ins, [ANY] + [VMEM] * len(blocks), around=0)
    return blocks + [swap(both, "tensor", 1)]


def last_entries(pieces, after):
    def body(after_ref, *refs):
        for i, ref in enumerate(refs[:-1]):
            refs[-1][i] = ref[1]

    ins = (after, *pieces)
    return call(body, shaped((len(pieces),) + pieces[0].shape[1:]), ins, [ANY] + [VMEM] * len(pieces), around=1)


def collect_far(pieces, passed):
    def body(*refs):
        for i, ref in enumerate(refs[:-2]):
            refs[-1][2 * i] = ref[0]
            refs[-1][2 * i + 1] = refs[-2][i]

    shape = (2 * len(pieces),) + pieces[0].shape[1:]
    return call(body, shaped(shape), (*pieces, passed), [VMEM] * (1 + len(pieces)), around=1)


def lift(where_ref, gain_ref, block_refs, h_ref, ss_ref, absolute):
    groups = len(block_refs)
    tensor = lax.axis_size("tensor")
    pair = block_refs[0].shape[0]
    near = groups // tensor
    d, t = where_ref[0], where_ref[1]
    gain = gain_ref[...]
    places = []
    for k in range(groups):
        g = d ^ k
        place = slot(lax.div(g, near) ^ t, tensor) * near + lax.rem(g, near)
        place = pl.multiple_of(place * pair, pair)
        wide = block_refs[k][...].astype(F32)[:pair]
        squares = jnp.broadcast_to(jnp.sum(wide * wide, axis=1, keepdims=True), (pair, 128))
        ss_ref[pl.ds(pl.multiple_of(g * pair, pair) if absolute else place, pair), :] = squares
        h_ref[pl.ds(place, pair), :] = (wide * gain).astype(BF16)
        places.append((pl.multiple_of(g * pair, pair), place))
    return places


def split(total, base, lane):
    high = total.astype(BF16).astype(F32)
    return jnp.where(lane == 0, high, jnp.where(lane == 1, total - high, base))


def stacked(rows, parts):
    width = rows.shape[1] // parts
    return jnp.concatenate([rows[:, i * width : (i + 1) * width] for i in range(parts)], axis=0)


def unstacked(rows, parts):
    height = rows.shape[0] // parts
    return jnp.concatenate([rows[i * height : (i + 1) * height] for i in range(parts)], axis=1)


def project_attention(where, blocks, gain, w_keyval, w_query, after):
    pair, features = blocks[0].shape
    rows = len(blocks) * pair
    half = rows // 2
    columns = w_keyval.shape[1]
    wide = w_query.shape[1]
    base = columns + 128

    def body(where_ref, gain_ref, *refs):
        block_refs, refs = refs[: len(blocks)], refs[len(blocks) :]
        w_kv_ref, w_q_ref, after_ref, message_ref, keep_ref, h_ref, ss_ref, product = refs
        places = lift(where_ref, gain_ref, block_refs, h_ref, ss_ref, True)
        h = h_ref[...]
        product[...] = jnp.dot(h, w_kv_ref[...], preferred_element_type=F32)
        for to, place in places:
            message_ref[pl.ds(to, pair), :columns] = product[pl.ds(place, pair), :].astype(BF16)
        squares = ss_ref[...]
        lane = lax.broadcasted_iota(jnp.int32, squares.shape, 1)
        message_ref[:, columns:base] = split(squares, 0.0, lane).astype(BF16)
        tile = tiles(wide // 2)
        for first in range(0, wide, tile):
            queries = jnp.dot(h, w_q_ref[:, first : first + tile], preferred_element_type=F32)
            keep_ref[:, first : first + tile] = queries[:half]
            below, lanes = divmod(first, wide // 2)
            lanes += base
            message_ref[below * half : (below + 1) * half, lanes : lanes + tile] = queries[half:].astype(BF16)

    return call(
        body,
        (shaped((rows, base + wide // 2)), shaped((half, wide), F32)),
        (where, gain[None], *blocks, w_keyval, w_query, after),
        [SMEM] + [VMEM] * (3 + len(blocks)) + [ANY],
        [pltpu.VMEM((rows, features), BF16), pltpu.VMEM((rows, 128), F32), pltpu.VMEM((rows, columns), F32)],
        flops=2 * rows * (w_keyval.size + w_query.size),
        moved=4 * rows * features + 2 * (w_keyval.size + w_query.size),
    )


def direct_keyvals():
    return lax.axis_size("dp") == KVH and lax.axis_size("tensor") == 4


def add_cores(where, own, keep, arrived):
    tensor = lax.axis_size("tensor")
    groups = lax.axis_size("dp")
    rows, total = own.shape
    half, wide = keep.shape
    base = total - wide // 2
    height = 2 * half // tensor
    direct = direct_keyvals()

    def body(where_ref, own_ref, keep_ref, arrived_ref, first_ref, message_ref, *out_refs):
        summed = own_ref[:, :base].astype(F32) + arrived_ref[:, :base].astype(F32)
        ends = summed[:, base - 128 :]
        lane = lax.broadcasted_iota(jnp.int32, ends.shape, 1)
        ends = split(ends[:, 0:1] + ends[:, 1:2], ends, lane).astype(BF16)
        queries = keep_ref[...] + unstacked(arrived_ref[:, base:].astype(F32), 2)
        first_ref[...] = queries[:height]
        if direct:
            message_ref[:, :128] = ends
            message_ref[:, 128:] = stacked(queries[height:], 4).astype(BF16)
            lower = where_ref[0] < groups // 2
            one, two = summed[:, :HD], summed[:, HD : 2 * HD]
            out_refs[0][...] = jnp.where(lower, one, two).astype(BF16)
            out_refs[1][...] = jnp.where(lower, two, one).astype(BF16)
        else:
            message_ref[:, : base - 128] = summed[:, : base - 128].astype(BF16)
            message_ref[:, base - 128 :] = ends
            for i, out_ref in enumerate(out_refs, 1):
                out_ref[...] = queries[i * height : (i + 1) * height].astype(BF16)

    outs = [shaped((height, wide), F32), shaped((rows, 128 + wide // 4 if direct else base))]
    outs += [shaped((rows, HD))] * 2 if direct else [shaped((height, wide))] * (tensor // 2 - 1)
    return call(body, tuple(outs), (where, own, keep, arrived), [SMEM] + [VMEM] * 3, moved=6 * own.size)


def row_scale(own, arrived, width):
    def body(own_ref, arrived_ref, out_ref):
        squares = own_ref[:, :128].astype(F32) + arrived_ref[:, :128].astype(F32)
        scale = lax.rsqrt((squares[:, 0:1] + squares[:, 1:2]) / width + EPS)
        out_ref[...] = jnp.broadcast_to(scale, squares.shape)

    return call(body, shaped((own.shape[0], 128), F32), (own, arrived), [VMEM] * 2)


def add_keyvals(own, arrived):
    rows, columns = own.shape

    def body(own_ref, arrived_ref, out_ref):
        summed = own_ref[...].astype(F32) + arrived_ref[...].astype(F32)
        ends = summed[:, columns - 128 :]
        lane = lax.broadcasted_iota(jnp.int32, ends.shape, 1)
        out_ref[:, : columns - 128] = summed[:, : columns - 128].astype(BF16)
        out_ref[:, columns - 128 :] = split(ends[:, 0:1] + ends[:, 1:2], ends, lane).astype(BF16)

    return call(body, shaped(own.shape), (own, arrived), [VMEM] * 2, moved=6 * own.size)


def finish_keyvals(where, own, arrived, columns, width):
    groups = lax.axis_size("dp")
    rows = own.shape[0]
    lanes = slice(0, columns + 128)

    def body(where_ref, own_ref, arrived_ref, scale_ref, *out_refs):
        summed = own_ref[:, lanes].astype(F32) + arrived_ref[:, lanes].astype(F32)
        squares = summed[:, columns : columns + 1] + summed[:, columns + 1 : columns + 2]
        scale = lax.rsqrt(squares / width + EPS)
        scale_ref[...] = jnp.broadcast_to(scale, (rows, 128))
        scaled = summed[:, :columns] * scale
        if groups == KVH:
            lower = where_ref[0] < groups // 2
            out_refs[0][...] = jnp.where(lower, scaled[:, :HD], scaled[:, HD:]).astype(BF16)
            out_refs[1][...] = jnp.where(lower, scaled[:, HD:], scaled[:, :HD]).astype(BF16)
        else:
            out_refs[0][...] = scaled.astype(BF16)

    outs = [shaped((rows, 128), F32)]
    outs += [shaped((rows, HD))] * 2 if groups == KVH else [shaped((rows, columns))]
    return call(body, tuple(outs), (where, own, arrived), [SMEM, VMEM, VMEM], moved=8 * own.size, around=1)


def project(h, w):
    half = h.shape[0] // 2

    def body(h_ref, w_ref, keep_ref, send_ref):
        def write(first, tile, product):
            keep_ref[:, first : first + tile] = product[:half]
            send_ref[:, first : first + tile] = product[half:].astype(BF16)

        multiply(h_ref[...], w_ref, write)

    columns = w.shape[1]
    return call(
        body,
        (shaped((half, columns), F32), shaped((half, columns))),
        (h, w),
        [VMEM] * 2,
        flops=4 * half * w.size,
        moved=2 * w.size,
    )


def project_gate(where, blocks, gain, w):
    pair, features = blocks[0].shape
    rows = len(blocks) * pair
    half = rows // 2
    columns = w.shape[1]

    def body(where_ref, gain_ref, *refs):
        block_refs, (w_ref, h_ref, keep_ref, send_ref, ss_ref) = refs[: len(blocks)], refs[len(blocks) :]
        lift(where_ref, gain_ref, block_refs, h_ref, ss_ref, False)

        def write(first, tile, product):
            keep_ref[:, first : first + tile] = product[:half]
            send_ref[:, first : first + tile] = product[half:].astype(BF16)

        multiply(h_ref[...], w_ref, write)
        squares = ss_ref[...]
        high = squares.astype(BF16).astype(F32)
        lane = lax.broadcasted_iota(jnp.int32, squares.shape, 1)
        ends = jnp.where(lane == 0, high, jnp.where(lane == 1, squares - high, 0.0))
        keep_ref[:, columns:] = ends[:half]
        send_ref[:, columns:] = ends[half:].astype(BF16)

    return call(
        body,
        (shaped((rows, features)), shaped((half, columns + 128), F32), shaped((half, columns + 128))),
        (where, gain[None], *blocks, w),
        [SMEM] + [VMEM] * (2 + len(blocks)),
        [pltpu.VMEM((rows, 128), F32)],
        flops=2 * rows * w.size,
        moved=4 * rows * features + 2 * w.size,
    )


def project_back(where, blocks, w):
    groups = lax.axis_size("dp")
    rows, depth = blocks[0].shape
    near = groups // len(blocks)
    pair = rows // near
    total = len(blocks) * rows
    columns = w.shape[1]
    close = min(groups, 4)
    far = (groups - close) // 2

    def body(where_ref, *refs):
        block_refs, (w_ref, *out_refs) = refs[: len(blocks)], refs[len(blocks) :]
        left = out_refs[-1]
        d, t = where_ref[0], where_ref[1]
        for k, block_ref in enumerate(block_refs):
            for i in range(near):
                relative = ((t ^ k) * near + i) ^ d
                beyond = close + lax.shift_right_logical(relative - close, 1) + (relative & 1) * far
                place = jnp.where(relative < close, relative, beyond)
                left[pl.ds(pl.multiple_of(place * pair, pair), pair), :] = block_ref[i * pair : (i + 1) * pair, :]

        def write(first, tile, product):
            lanes = slice(first, first + tile)
            for i in range(close):
                out_refs[i][:, lanes] = product[i * pair : (i + 1) * pair].astype(out_refs[i].dtype)
            middle = (close + far) * pair
            cut = middle + far // 2 * pair
            out_refs[close][:, lanes] = product[close * pair : middle]
            out_refs[close + 1][:, lanes] = product[middle:cut].astype(BF16)
            out_refs[close + 2][:, lanes] = product[cut:].astype(BF16)

        multiply(left[...], w_ref, write)

    outs = [shaped((pair, columns), F32)] + [shaped((pair, columns))] * (close - 1)
    outs += [shaped((far * pair, columns), F32)] + [shaped((far // 2 * pair, columns))] * 2
    return call(
        body,
        tuple(outs),
        (where, *blocks, w),
        [SMEM] + [VMEM] * (1 + len(blocks)),
        [pltpu.VMEM((total, depth), BF16)],
        flops=2 * total * w.size,
        moved=2 * w.size,
    )


def add_pairs(keep, arrived, first, pair, passed=()):
    count = arrived.shape[0] // pair

    def body(keep_ref, arrived_ref, *refs):
        for i, out_ref in enumerate(refs[len(passed) : len(passed) + count]):
            own = keep_ref[first + i * pair : first + (i + 1) * pair, :]
            out_ref[...] = (own + arrived_ref[i * pair : (i + 1) * pair, :].astype(F32)).astype(BF16)
        for ref, out_ref in zip(refs[: len(passed)], refs[len(passed) + count :]):
            out_ref[...] = ref[...]

    outs = (shaped((pair, keep.shape[1])),) * (count + len(passed))
    ins = (keep, arrived, *passed)
    return call(body, outs, ins, [VMEM] * len(ins), moved=8 * arrived.size)


def sum_rows(parts, pair):
    own, *near, keep, one, two = parts
    count = one.shape[0] // pair
    sums = add_pairs(keep, swap(one, "dp", 1), 0, pair, near[:1])
    sums, near = list(sums[:count]), [*sums[count:], *near[1:]]
    sums += add_pairs(keep, swap(two, "dp", 1), one.shape[0], pair)
    arrived = [swap(piece, "dp", len(near) + 1 + 2 * i) for i, piece in enumerate(sums)]
    arrived += [swap(piece, "dp", k + 1) for k, piece in enumerate(near)]
    return own, arrived


def finish(own, arrived, x=None):
    def body(own_ref, *refs):
        total = own_ref[...]
        for ref in refs[: len(arrived)]:
            total = total + ref[...].astype(F32)
        rounded = total.astype(BF16)
        if x is None:
            refs[-1][...] = rounded
        else:
            refs[-2][...] = rounded
            refs[-1][...] = (refs[len(arrived)][...].astype(F32) + rounded.astype(F32)).astype(BF16)

    outs = (shaped(own.shape),) * (1 if x is None else 2)
    ins = (own, *arrived) + (() if x is None else (x,))
    return call(body, outs, ins, [VMEM] * len(ins), moved=8 * own.size)


def attend_cached(where, anc, rope, scale, queries, near_cache, far_cache, part_dev):
    tensor = lax.axis_size("tensor")
    groups = lax.axis_size("dp")
    near = groups // tensor
    pair = 2 * part_dev
    close, span, _ = near_cache[0].shape
    ctx = tensor * span
    height, columns = queries[0].shape
    heads = columns // HD
    parts = near * part_dev
    rows = heads * parts

    def body(where_ref, anc_ref, rope_ref, scale_ref, *refs):
        q_refs, refs = refs[: len(queries)], refs[len(queries) :]
        count = tensor // 2 + 1
        near_refs, far_refs = refs[:count], refs[count : 2 * count]
        near_refs, far_refs = [(*part[:-1], *[part[-1].at[i] for i in range(count - 1)]) for part in (near_refs, far_refs)]
        query_ref, mixed_ref, highest_ref, total_ref, keys_ref, values_ref = refs[2 * count :]
        d, t = where_ref[0], where_ref[1]
        query_sum = q_refs[0][...]
        for ref in q_refs[1:]:
            if ref.shape[0] == height:
                query_sum = query_sum + ref[...].astype(F32)
            else:
                lanes = slice(ref.shape[1] - columns // 4, ref.shape[1])
                query_sum = query_sum + unstacked(ref[:, lanes].astype(F32), 4)
        query_sum = query_sum * scale_ref[pl.ds(pl.multiple_of(t * near * pair, pair), near * pair), 0:1]
        for step in range(2):

            def bring(i, _, step=step):
                particle = t * parts + i if step == 0 else anc_ref[i]
                block, member = lax.div(particle, part_dev) ^ d, lax.rem(particle, part_dev)

                def load(cache_refs, entry):
                    for k, cache_ref in enumerate(cache_refs):
                        to = pl.ds(pl.multiple_of(i * ctx + k * span, 8), span)
                        lanes = pl.ds(pl.multiple_of(member * HD, HD), HD)
                        keys_ref[to, :] = cache_ref[entry, :, lanes].astype(F32)
                        lanes = pl.ds(pl.multiple_of((part_dev + member) * HD, HD), HD)
                        values_ref[to, :] = cache_ref[entry, :, lanes].astype(F32)

                @pl.when(block < close)
                def _():
                    load(near_refs, block)

                @pl.when(block >= close)
                def _():
                    load(far_refs, block - close)

                return 0

            lax.fori_loop(0, parts, bring, 0)
            keys = keys_ref[...].astype(BF16)
            values = values_ref[...].astype(BF16)
            per_head = []
            for h in range(heads):
                for b in range(near):
                    first = b * pair + step * part_dev
                    per_head.append(query_sum[first : first + part_dev, h * HD : (h + 1) * HD])
            query = jnp.concatenate(per_head, axis=0).astype(BF16).astype(F32)
            cosine = rope_ref[2 * step : 2 * step + 1, :]
            sine = rope_ref[2 * step + 1 : 2 * step + 2, :]
            query = (query * cosine + pltpu.roll(query, HD // 2, 1) * sine).astype(BF16)
            scores = lax.dot_general(query, keys, (((1,), (1,)), ((), ())), preferred_element_type=F32)
            scores = scores * (1.0 / math.sqrt(HD))
            row_part = lax.rem(lax.broadcasted_iota(jnp.int32, (rows, 1), 0), parts)
            col_part = lax.div(lax.broadcasted_iota(jnp.int32, (1, parts * ctx), 1), ctx)
            scores = jnp.where(row_part == col_part, scores, MASKED)
            highest = jnp.max(scores, axis=1, keepdims=True)
            weights = jnp.exp(scores - highest)
            here = slice(step * rows, (step + 1) * rows)
            query_ref[here, :] = query
            mixed_ref[here, :] = jnp.dot(weights.astype(BF16), values, preferred_element_type=F32)
            highest_ref[here, :] = jnp.broadcast_to(highest, (rows, 128))
            total_ref[here, :] = jnp.broadcast_to(jnp.sum(weights, axis=1, keepdims=True), (rows, 128))

    ins = (where, anc, rope, scale, *queries, *near_cache, *far_cache)
    return call(
        body,
        (shaped((2 * rows, HD)), shaped((2 * rows, HD), F32), shaped((2 * rows, 128), F32), shaped((2 * rows, 128), F32)),
        ins,
        [SMEM] * 2 + [VMEM] * (len(ins) - 2),
        [pltpu.VMEM((parts * ctx, HD), F32), pltpu.VMEM((parts * ctx, HD), F32)],
        limit=(4 << 20) + 12 * rows * parts * ctx,
        moved=4 << 20,
    )


def attend_new(where, rope, targets, scale, pieces, state, shape, part_dev):
    groups = lax.axis_size("dp")
    tensor = lax.axis_size("tensor")
    near = groups // tensor
    pair = 2 * part_dev
    parts = near * part_dev
    heads = shape[1] // HD
    rows = heads * parts

    def body(where_ref, rope_ref, target_ref, scale_ref, *refs):
        piece_refs, (query_ref, mixed_ref, highest_ref, total_ref, out_ref) = refs[: len(pieces)], refs[len(pieces) :]
        even = where_ref[0] % 2 == 0 if groups == KVH else True
        if len(pieces) == 2:
            one, two = [ref[...].astype(F32) for ref in piece_refs]
        else:
            one, two = [piece_refs[i][...].astype(F32) + piece_refs[i + 1][...].astype(F32) for i in (0, 2)]
            one, two = [(x * scale_ref[...]).astype(BF16).astype(F32) for x in (one, two)]
        plain = jnp.where(even, one, two)
        values = jnp.where(even, two, one).astype(BF16)
        cosine = jnp.concatenate([jnp.broadcast_to(rope_ref[2 * s : 2 * s + 1, :], (part_dev, HD)) for s in range(2)])
        sine = jnp.concatenate([jnp.broadcast_to(rope_ref[2 * s + 1 : 2 * s + 2, :], (part_dev, HD)) for s in range(2)])
        turned = pltpu.roll(plain, HD // 2, 1).reshape(groups, pair, HD)
        keys = plain.reshape(groups, pair, HD) * cosine[None] + turned * sine[None]
        keys = keys.reshape(groups * pair, HD).astype(BF16)
        scores = lax.dot_general(query_ref[...], keys, (((1,), (1,)), ((), ())), preferred_element_type=F32)
        scores = scores * (1.0 / math.sqrt(HD))
        col = lax.broadcasted_iota(jnp.int32, (1, groups * pair), 1)
        wanted = (col == target_ref[:, 0:1]) | (col == target_ref[:, 1:2])
        scores = jnp.where(wanted, scores, MASKED)
        before = highest_ref[:, 0:1]
        highest = jnp.maximum(before, jnp.max(scores, axis=1, keepdims=True))
        weights = jnp.exp(scores - highest)
        keep = jnp.exp(before - highest)
        total = total_ref[:, 0:1] * keep + jnp.sum(weights, axis=1, keepdims=True)
        mixed = mixed_ref[...] * keep + jnp.dot(weights.astype(BF16), values, preferred_element_type=F32)
        mixed = mixed / total
        for h in range(heads):
            for b in range(near):
                first = h * parts + b * part_dev
                both = [mixed[s * rows + first : s * rows + first + part_dev] for s in range(2)]
                here = slice(b * pair, (b + 1) * pair)
                out_ref[here, h * HD : (h + 1) * HD] = jnp.concatenate(both, axis=0).astype(BF16)

    ins = (where, rope, targets, scale, *pieces, *state)
    return call(body, shaped(shape), ins, [SMEM] + [VMEM] * (len(ins) - 1), moved=1 << 20)


def send_keyvals(pieces):
    groups = lax.axis_size("dp")
    tensor = lax.axis_size("tensor")
    half = groups // 2
    moved = []
    for flip, piece in enumerate(pieces):
        to = [2 * i + flip for i in range(half)] + [2 * i + 1 - flip for i in range(half)]
        for k in (0, 2):
            pairs = [(i * tensor + t, to[i] * tensor + (t ^ k)) for i in range(groups) for t in range(tensor)]
            moved.append(lax.ppermute(piece, ("dp", "tensor"), pairs))
    return moved


def move_keyvals(pieces):
    groups = lax.axis_size("dp")
    d = lax.axis_index("dp")
    if groups == KVH:
        half = groups // 2
        one = [(i, 2 * i) for i in range(half)] + [(half + i, 2 * i + 1) for i in range(half)]
        two = [(i, 2 * i + 1) for i in range(half)] + [(half + i, 2 * i) for i in range(half)]
        return [lax.ppermute(x, "dp", to) for x, to in zip(pieces, (one, two))]
    every = lax.all_gather(pieces[0], "dp", axis=1, tiled=True)
    start = (d * KVH // groups) * HD
    return [lax.dynamic_slice_in_dim(every, first + start, HD, axis=1) for first in (0, KVH * HD)]


def local(
    x_first,
    x_second,
    cache_keys,
    cache_values,
    ancestors,
    attn_gain,
    ffn_gain,
    w_query,
    w_keyval,
    w_out,
    w_gate,
    w_up,
    w_down,
):
    groups = lax.axis_size("dp")
    tensor = lax.axis_size("tensor")
    part_dev, features = x_first.shape
    span = cache_keys.shape[1]
    width = features * tensor
    context = span * tensor
    d = lax.axis_index("dp")
    t = lax.axis_index("tensor")
    pair = 2 * part_dev
    near = groups // tensor
    parts = near * part_dev
    where = jnp.stack([d, t]).astype(jnp.int32)

    x = stack_tokens(x_first, x_second)
    own_piece, near_pieces, joined = pack_near(where, x, cache_keys, cache_values)
    blocks = gather_rows(x, near_pieces if joined else None)
    close = min(groups, 4)
    near_moved = blocks[1:close] if joined else [swap(piece, "dp", k) for k, piece in enumerate(near_pieces, 1)]
    near_pieces = collect_near(own_piece, near_moved, span)
    packed = pack_far(where, cache_keys, cache_values, blocks[close::2])
    far_pieces = [swap(piece, "dp", close + 2 * i) for i, piece in enumerate(packed)]

    message, keep = project_attention(where, blocks, attn_gain, w_keyval, w_query, x)
    queries, message, *leaving = add_cores(where, message, keep, swap(message, "tensor", 1))
    passed = swap(last_entries(far_pieces, x), "dp", 1)
    far_pieces = collect_far(far_pieces, passed)
    if direct_keyvals():
        pieces = send_keyvals(leaving)
        arrived = swap(message, "tensor", 2)
        scale = row_scale(message, arrived, width)
        queries = [queries, arrived]
    else:
        bits = 2
        while 2 * bits < tensor:
            message = add_keyvals(message, swap(message, "tensor", bits))
            bits *= 2
        arrived = swap(message, "tensor", bits)
        scale, *pieces = finish_keyvals(where, message, arrived, w_keyval.shape[1], width)
        pieces = move_keyvals(pieces)
        queries = [queries] + [swap(piece, "tensor", 2 * i) for i, piece in enumerate(leaving, 1)]

    near_cache = gather_cache(near_pieces, arrived)
    far_cache = gather_cache(far_pieces, arrived)

    own = t * parts + jnp.arange(parts, dtype=jnp.int32)
    anc = lax.dynamic_slice_in_dim(ancestors, t * parts, parts).astype(jnp.int32)
    heads = w_query.shape[1] // HD

    def row_of(particle, step):
        return (particle // part_dev) * pair + step * part_dev + particle % part_dev

    first = jnp.stack([row_of(own, 0)] * 2, axis=1)
    second = jnp.stack([row_of(anc, 0), row_of(own, 1)], axis=1)
    targets = jnp.concatenate([jnp.tile(first, (heads, 1)), jnp.tile(second, (heads, 1))]).astype(jnp.int32)
    rope = jnp.asarray(np.stack(rope_tables(context) + rope_tables(context + 1)))
    state = attend_cached(where, anc, rope, scale, queries, near_cache, far_cache, part_dev)
    mixed = attend_new(where, rope, targets, scale, pieces, state, queries[0].shape, part_dev)

    parts = project_back(where, gather_blocks(mixed), w_out)
    attn_part, residual = finish(*sum_rows(parts, pair), x)

    hidden_cols = w_gate.shape[1]
    h, keep, send = project_gate(where, gather_rows(residual), ffn_gain, w_gate)
    gate, gate_arrived = sum_blocks(keep, send)
    up, up_arrived = sum_blocks(*project(h, w_up))
    for piece in gate_arrived:
        gate = gate + piece.astype(F32)
    for piece in up_arrived:
        up = up + piece.astype(F32)
    scale = lax.rsqrt((gate[:, hidden_cols] + gate[:, hidden_cols + 1]) / width + EPS)[:, None]
    hidden = jax.nn.silu(gate[:, :hidden_cols] * scale) * (up * scale)
    parts = project_back(where, gather_blocks(hidden.astype(BF16)), w_down)
    (ffn_part,) = finish(*sum_rows(parts, pair))
    return (attn_part.reshape(2, part_dev, features), ffn_part.reshape(2, part_dev, features))


def solution(mesh):
    return jax.shard_map(
        local,
        mesh=mesh,
        in_specs=(
            P("dp", "tensor"),
            P("dp", "tensor"),
            P("dp", "tensor", None),
            P("dp", "tensor", None),
            P(),
            P("tensor"),
            P("tensor"),
            P("tensor", "dp"),
            P("tensor", "dp"),
            P("dp", "tensor"),
            P("tensor", "dp"),
            P("tensor", "dp"),
            P("dp", "tensor"),
        ),
        out_specs=(P(None, "dp", "tensor"), P(None, "dp", "tensor")),
        check_vma=False,
    )
```

```python
import functools
import math

import jax
import jax.numpy as jnp
import numpy as np
from jax import lax
from jax.experimental import pallas as pl
from jax.experimental.pallas import tpu as pltpu
from jax.sharding import PartitionSpec as P

KVH = 8
HD = 128
EPS = 1e-05
ROPE_BASE = 500000.0
MASKED = -1e30
AROUND = 5 << 30
BF16 = jnp.bfloat16
F32 = jnp.float32


def swap(x, axis, bits):
    size = lax.axis_size(axis)
    return lax.ppermute(x, axis, [(i, i ^ bits) for i in range(size)])


def rope_tables(position):
    half = HD // 2
    freq = np.power(np.float32(ROPE_BASE), -2.0 * np.arange(half, dtype=np.float32) / HD)
    angle = (np.float32(position) * freq.astype(np.float32)).astype(np.float32)
    cosine, sine = np.cos(angle), np.sin(angle)
    return (
        np.concatenate([cosine, cosine]).astype(np.float32),
        np.concatenate([-sine, sine]).astype(np.float32),
    )


SMEM = pl.BlockSpec(memory_space=pltpu.SMEM)
VMEM = pl.BlockSpec(memory_space=pltpu.VMEM)
ANY = pl.BlockSpec(memory_space=pl.ANY)
HBM = pl.BlockSpec(memory_space=pltpu.HBM)


def call(body, outs, ins, specs, scratch=(), flops=0, moved=0, limit=8 << 20, around=1):
    return pl.pallas_call(
        body,
        out_shape=outs,
        in_specs=specs,
        out_specs=jax.tree.map(lambda _: VMEM, outs),
        scratch_shapes=scratch,
        compiler_params=pltpu.CompilerParams(vmem_limit_bytes=limit),
        cost_estimate=pl.CostEstimate(flops=flops + around * AROUND, bytes_accessed=moved, transcendentals=0),
    )(*ins)


def shaped(shape, dtype=BF16):
    return jax.ShapeDtypeStruct(shape, dtype)


def gather_rows(rows, near=None):
    groups = lax.axis_size("dp")
    close = min(groups, 4)
    blocks = {0: rows}
    for k in range(groups - 2, close - 1, -2):
        blocks[k] = swap(rows, "dp", k)
    for k in range(close - 1, 0, -1):
        blocks[k] = swap(rows if near is None else near[k - 1], "dp", k)
    for k in range(groups - 2, close - 1, -2):
        blocks[k + 1] = swap(blocks[k], "dp", 1)
    return [blocks[k] for k in range(groups)]


def gather_blocks(block):
    tensor = lax.axis_size("tensor")
    blocks = {0: block}
    for k in range(2, tensor, 2):
        blocks[k] = swap(block, "tensor", k)
    blocks[1] = swap(block, "tensor", 1)
    for k in range(2, tensor, 2):
        blocks[k + 1] = swap(blocks[k], "tensor", 1)
    return [blocks[k] for k in range(tensor)]


def sum_blocks(keep, send):
    tensor = lax.axis_size("tensor")
    rows = keep.shape[0] // (tensor // 2)
    paired = (keep + swap(send, "tensor", 1).astype(F32)).reshape(tensor // 2, rows, -1)
    return paired[0], [swap(paired[i].astype(BF16), "tensor", 2 * i) for i in range(1, tensor // 2)]


def slot(relative, size):
    return lax.shift_right_logical(relative, 1) + (relative & 1) * (size // 2)


def tiles(columns):
    for tile in (256, 384, 128):
        if columns % tile == 0:
            return tile
    return columns


def multiply(left, w_ref, write):
    columns = w_ref.shape[1]
    tile = tiles(columns)
    for first in range(0, columns, tile):
        write(first, tile, jnp.dot(left, w_ref[:, first : first + tile], preferred_element_type=F32))


def stack_tokens(x_first, x_second):
    def body(first_ref, second_ref, out_ref):
        out_ref[...] = jnp.concatenate([first_ref[...].astype(F32), second_ref[...].astype(F32)], axis=0).astype(BF16)

    part_dev, features = x_first.shape
    return call(body, shaped((2 * part_dev, features)), (x_first, x_second), [VMEM] * 2)


def cache_piece(where_ref, keys_ref, values_ref, k):
    groups = lax.axis_size("dp")
    head = lax.div((where_ref[0] ^ k) * KVH, groups)
    lanes = pl.ds(pl.multiple_of(head * HD, HD), HD)
    tiles_of = [ref[p, :, lanes].astype(F32) for ref in (keys_ref, values_ref) for p in range(keys_ref.shape[0])]
    return jnp.concatenate(tiles_of, axis=1)


def pack_near(where, x, cache_keys, cache_values):
    part_dev, span, _ = cache_keys.shape
    close = min(lax.axis_size("dp"), 4)
    wide = 2 * part_dev * HD
    joined = x.shape[1] == wide

    def body(where_ref, x_ref, keys_ref, values_ref, own_ref, *out_refs):
        own_ref[...] = cache_piece(where_ref, keys_ref, values_ref, 0).astype(BF16)
        for k, out_ref in enumerate(out_refs, 1):
            piece = cache_piece(where_ref, keys_ref, values_ref, k)
            if joined:
                piece = jnp.concatenate([x_ref[...].astype(F32), piece], axis=0)
            out_ref[...] = piece.astype(BF16)

    height = span + (x.shape[0] if joined else 0)
    own, *near = call(
        body,
        (shaped((span, wide)),) + (shaped((height, wide)),) * (close - 1),
        (where, x, cache_keys, cache_values),
        [SMEM] + [VMEM] * 3,
        flops=2 * AROUND,
    )
    return own, near, joined


def pack_far(where, cache_keys, cache_values, afters):
    groups = lax.axis_size("dp")
    part_dev, span, _ = cache_keys.shape
    wide = 2 * part_dev * HD
    close = min(groups, 4)

    def body(where_ref, keys_ref, values_ref, *refs):
        for i, out_ref in enumerate(refs[len(afters) :]):
            for odd in range(2):
                out_ref[odd] = cache_piece(where_ref, keys_ref, values_ref, close + 2 * i + odd).astype(BF16)

    return call(
        body,
        (shaped((2, span, wide)),) * ((groups - close) // 2),
        (where, cache_keys, cache_values, *afters),
        [SMEM, VMEM, VMEM] + [ANY] * len(afters),
        flops=AROUND,
    )


def collect_near(own, near, span):
    def body(own_ref, *refs):
        refs[-1][0] = own_ref[...]
        for k, ref in enumerate(refs[:-1], 1):
            refs[-1][k] = ref[...].astype(F32)[ref.shape[0] - span :].astype(BF16)

    return call(body, shaped((1 + len(near),) + own.shape), (own, *near), [VMEM] * (1 + len(near)), around=1)


def gather_cache(block, after):
    blocks = [block] + [swap(block, "tensor", k) for k in range(2, lax.axis_size("tensor"), 2)]

    def body(after_ref, *refs):
        for i, ref in enumerate(refs[:-1]):
            refs[-1][i] = ref[...]

    ins = (after, *blocks)
    both = call(body, shaped((len(blocks),) + block.shape), ins, [ANY] + [VMEM] * len(blocks), around=0)
    return blocks + [swap(both, "tensor", 1)]


def last_entries(pieces, after):
    def body(after_ref, *refs):
        for i, ref in enumerate(refs[:-1]):
            refs[-1][i] = ref[1]

    ins = (after, *pieces)
    return call(body, shaped((len(pieces),) + pieces[0].shape[1:]), ins, [ANY] + [VMEM] * len(pieces), around=1)


def collect_far(pieces, passed):
    def body(*refs):
        for i, ref in enumerate(refs[:-2]):
            refs[-1][2 * i] = ref[0]
            refs[-1][2 * i + 1] = refs[-2][i]

    shape = (2 * len(pieces),) + pieces[0].shape[1:]
    return call(body, shaped(shape), (*pieces, passed), [VMEM] * (1 + len(pieces)), around=1)


def lift(where_ref, gain_ref, block_refs, h_ref, ss_ref, absolute):
    groups = len(block_refs)
    tensor = lax.axis_size("tensor")
    pair = block_refs[0].shape[0]
    near = groups // tensor
    d, t = where_ref[0], where_ref[1]
    gain = gain_ref[...]
    places = []
    for k in range(groups):
        g = d ^ k
        place = slot(lax.div(g, near) ^ t, tensor) * near + lax.rem(g, near)
        place = pl.multiple_of(place * pair, pair)
        wide = block_refs[k][...].astype(F32)[:pair]
        squares = jnp.broadcast_to(jnp.sum(wide * wide, axis=1, keepdims=True), (pair, 128))
        ss_ref[pl.ds(pl.multiple_of(g * pair, pair) if absolute else place, pair), :] = squares
        h_ref[pl.ds(place, pair), :] = (wide * gain).astype(BF16)
        places.append((pl.multiple_of(g * pair, pair), place))
    return places


def split(total, base, lane):
    high = total.astype(BF16).astype(F32)
    return jnp.where(lane == 0, high, jnp.where(lane == 1, total - high, base))


def stacked(rows, parts):
    width = rows.shape[1] // parts
    return jnp.concatenate([rows[:, i * width : (i + 1) * width] for i in range(parts)], axis=0)


def unstacked(rows, parts):
    height = rows.shape[0] // parts
    return jnp.concatenate([rows[i * height : (i + 1) * height] for i in range(parts)], axis=1)


def project_attention(where, blocks, gain, w_keyval, w_query, after):
    pair, features = blocks[0].shape
    rows = len(blocks) * pair
    half = rows // 2
    columns = w_keyval.shape[1]
    wide = w_query.shape[1]
    base = columns + 128

    def body(where_ref, gain_ref, *refs):
        block_refs, refs = refs[: len(blocks)], refs[len(blocks) :]
        w_kv_ref, w_q_ref, after_ref, message_ref, keep_ref, h_ref, ss_ref, product = refs
        places = lift(where_ref, gain_ref, block_refs, h_ref, ss_ref, True)
        h = h_ref[...]
        product[...] = jnp.dot(h, w_kv_ref[...], preferred_element_type=F32)
        for to, place in places:
            message_ref[pl.ds(to, pair), :columns] = product[pl.ds(place, pair), :].astype(BF16)
        squares = ss_ref[...]
        lane = lax.broadcasted_iota(jnp.int32, squares.shape, 1)
        message_ref[:, columns:base] = split(squares, 0.0, lane).astype(BF16)
        tile = tiles(wide // 2)
        for first in range(0, wide, tile):
            queries = jnp.dot(h, w_q_ref[:, first : first + tile], preferred_element_type=F32)
            keep_ref[:, first : first + tile] = queries[:half]
            below, lanes = divmod(first, wide // 2)
            lanes += base
            message_ref[below * half : (below + 1) * half, lanes : lanes + tile] = queries[half:].astype(BF16)

    return call(
        body,
        (shaped((rows, base + wide // 2)), shaped((half, wide), F32)),
        (where, gain[None], *blocks, w_keyval, w_query, after),
        [SMEM] + [VMEM] * (3 + len(blocks)) + [ANY],
        [pltpu.VMEM((rows, features), BF16), pltpu.VMEM((rows, 128), F32), pltpu.VMEM((rows, columns), F32)],
        flops=2 * rows * (w_keyval.size + w_query.size),
        moved=4 * rows * features + 2 * (w_keyval.size + w_query.size),
    )


def direct_keyvals():
    return lax.axis_size("dp") == KVH and lax.axis_size("tensor") == 4


def add_cores(where, own, keep, arrived):
    tensor = lax.axis_size("tensor")
    groups = lax.axis_size("dp")
    rows, total = own.shape
    half, wide = keep.shape
    base = total - wide // 2
    height = 2 * half // tensor
    direct = direct_keyvals()

    def body(where_ref, own_ref, keep_ref, arrived_ref, first_ref, message_ref, *out_refs):
        summed = own_ref[:, :base].astype(F32) + arrived_ref[:, :base].astype(F32)
        ends = summed[:, base - 128 :]
        lane = lax.broadcasted_iota(jnp.int32, ends.shape, 1)
        ends = split(ends[:, 0:1] + ends[:, 1:2], ends, lane).astype(BF16)
        queries = keep_ref[...] + unstacked(arrived_ref[:, base:].astype(F32), 2)
        first_ref[...] = queries[:height]
        if direct:
            message_ref[:, :128] = ends
            message_ref[:, 128:] = stacked(queries[height:], 4).astype(BF16)
            lower = where_ref[0] < groups // 2
            one, two = summed[:, :HD], summed[:, HD : 2 * HD]
            out_refs[0][...] = jnp.where(lower, one, two).astype(BF16)
            out_refs[1][...] = jnp.where(lower, two, one).astype(BF16)
        else:
            message_ref[:, : base - 128] = summed[:, : base - 128].astype(BF16)
            message_ref[:, base - 128 :] = ends
            for i, out_ref in enumerate(out_refs, 1):
                out_ref[...] = queries[i * height : (i + 1) * height].astype(BF16)

    outs = [shaped((height, wide), F32), shaped((rows, 128 + wide // 4 if direct else base))]
    outs += [shaped((rows, HD))] * 2 if direct else [shaped((height, wide))] * (tensor // 2 - 1)
    return call(body, tuple(outs), (where, own, keep, arrived), [SMEM] + [VMEM] * 3, moved=6 * own.size)


def row_scale(own, arrived, width):
    def body(own_ref, arrived_ref, out_ref):
        squares = own_ref[:, :128].astype(F32) + arrived_ref[:, :128].astype(F32)
        scale = lax.rsqrt((squares[:, 0:1] + squares[:, 1:2]) / width + EPS)
        out_ref[...] = jnp.broadcast_to(scale, squares.shape)

    return call(body, shaped((own.shape[0], 128), F32), (own, arrived), [VMEM] * 2)


def add_keyvals(own, arrived):
    rows, columns = own.shape

    def body(own_ref, arrived_ref, out_ref):
        summed = own_ref[...].astype(F32) + arrived_ref[...].astype(F32)
        ends = summed[:, columns - 128 :]
        lane = lax.broadcasted_iota(jnp.int32, ends.shape, 1)
        out_ref[:, : columns - 128] = summed[:, : columns - 128].astype(BF16)
        out_ref[:, columns - 128 :] = split(ends[:, 0:1] + ends[:, 1:2], ends, lane).astype(BF16)

    return call(body, shaped(own.shape), (own, arrived), [VMEM] * 2, moved=6 * own.size)


def finish_keyvals(where, own, arrived, columns, width):
    groups = lax.axis_size("dp")
    rows = own.shape[0]
    lanes = slice(0, columns + 128)

    def body(where_ref, own_ref, arrived_ref, scale_ref, *out_refs):
        summed = own_ref[:, lanes].astype(F32) + arrived_ref[:, lanes].astype(F32)
        squares = summed[:, columns : columns + 1] + summed[:, columns + 1 : columns + 2]
        scale = lax.rsqrt(squares / width + EPS)
        scale_ref[...] = jnp.broadcast_to(scale, (rows, 128))
        scaled = summed[:, :columns] * scale
        if groups == KVH:
            lower = where_ref[0] < groups // 2
            out_refs[0][...] = jnp.where(lower, scaled[:, :HD], scaled[:, HD:]).astype(BF16)
            out_refs[1][...] = jnp.where(lower, scaled[:, HD:], scaled[:, :HD]).astype(BF16)
        else:
            out_refs[0][...] = scaled.astype(BF16)

    outs = [shaped((rows, 128), F32)]
    outs += [shaped((rows, HD))] * 2 if groups == KVH else [shaped((rows, columns))]
    return call(body, tuple(outs), (where, own, arrived), [SMEM, VMEM, VMEM], moved=8 * own.size, around=1)


def project(h, w):
    half = h.shape[0] // 2

    def body(h_ref, w_ref, keep_ref, send_ref):
        def write(first, tile, product):
            keep_ref[:, first : first + tile] = product[:half]
            send_ref[:, first : first + tile] = product[half:].astype(BF16)

        multiply(h_ref[...], w_ref, write)

    columns = w.shape[1]
    return call(
        body,
        (shaped((half, columns), F32), shaped((half, columns))),
        (h, w),
        [VMEM] * 2,
        flops=4 * half * w.size,
        moved=2 * w.size,
    )


def project_gate(where, blocks, gain, w):
    pair, features = blocks[0].shape
    rows = len(blocks) * pair
    half = rows // 2
    columns = w.shape[1]

    def body(where_ref, gain_ref, *refs):
        block_refs, (w_ref, h_ref, keep_ref, send_ref, ss_ref) = refs[: len(blocks)], refs[len(blocks) :]
        lift(where_ref, gain_ref, block_refs, h_ref, ss_ref, False)

        def write(first, tile, product):
            keep_ref[:, first : first + tile] = product[:half]
            send_ref[:, first : first + tile] = product[half:].astype(BF16)

        multiply(h_ref[...], w_ref, write)
        squares = ss_ref[...]
        high = squares.astype(BF16).astype(F32)
        lane = lax.broadcasted_iota(jnp.int32, squares.shape, 1)
        ends = jnp.where(lane == 0, high, jnp.where(lane == 1, squares - high, 0.0))
        keep_ref[:, columns:] = ends[:half]
        send_ref[:, columns:] = ends[half:].astype(BF16)

    return call(
        body,
        (shaped((rows, features)), shaped((half, columns + 128), F32), shaped((half, columns + 128))),
        (where, gain[None], *blocks, w),
        [SMEM] + [VMEM] * (2 + len(blocks)),
        [pltpu.VMEM((rows, 128), F32)],
        flops=2 * rows * w.size,
        moved=4 * rows * features + 2 * w.size,
    )


def project_back(where, blocks, w):
    groups = lax.axis_size("dp")
    rows, depth = blocks[0].shape
    near = groups // len(blocks)
    pair = rows // near
    total = len(blocks) * rows
    columns = w.shape[1]
    close = min(groups, 4)
    far = (groups - close) // 2

    def body(where_ref, *refs):
        block_refs, (w_ref, *out_refs) = refs[: len(blocks)], refs[len(blocks) :]
        left = out_refs[-1]
        d, t = where_ref[0], where_ref[1]
        for k, block_ref in enumerate(block_refs):
            for i in range(near):
                relative = ((t ^ k) * near + i) ^ d
                beyond = close + lax.shift_right_logical(relative - close, 1) + (relative & 1) * far
                place = jnp.where(relative < close, relative, beyond)
                left[pl.ds(pl.multiple_of(place * pair, pair), pair), :] = block_ref[i * pair : (i + 1) * pair, :]

        def write(first, tile, product):
            lanes = slice(first, first + tile)
            for i in range(close):
                out_refs[i][:, lanes] = product[i * pair : (i + 1) * pair].astype(out_refs[i].dtype)
            middle = (close + far) * pair
            cut = middle + far // 2 * pair
            out_refs[close][:, lanes] = product[close * pair : middle]
            out_refs[close + 1][:, lanes] = product[middle:cut].astype(BF16)
            out_refs[close + 2][:, lanes] = product[cut:].astype(BF16)

        multiply(left[...], w_ref, write)

    outs = [shaped((pair, columns), F32)] + [shaped((pair, columns))] * (close - 1)
    outs += [shaped((far * pair, columns), F32)] + [shaped((far // 2 * pair, columns))] * 2
    return call(
        body,
        tuple(outs),
        (where, *blocks, w),
        [SMEM] + [VMEM] * (1 + len(blocks)),
        [pltpu.VMEM((total, depth), BF16)],
        flops=2 * total * w.size,
        moved=2 * w.size,
    )


def add_pairs(keep, arrived, first, pair, passed=()):
    count = arrived.shape[0] // pair

    def body(keep_ref, arrived_ref, *refs):
        for i, out_ref in enumerate(refs[len(passed) : len(passed) + count]):
            own = keep_ref[first + i * pair : first + (i + 1) * pair, :]
            out_ref[...] = (own + arrived_ref[i * pair : (i + 1) * pair, :].astype(F32)).astype(BF16)
        for ref, out_ref in zip(refs[: len(passed)], refs[len(passed) + count :]):
            out_ref[...] = ref[...]

    outs = (shaped((pair, keep.shape[1])),) * (count + len(passed))
    ins = (keep, arrived, *passed)
    return call(body, outs, ins, [VMEM] * len(ins), moved=8 * arrived.size)


def sum_rows(parts, pair):
    own, *near, keep, one, two = parts
    count = one.shape[0] // pair
    sums = add_pairs(keep, swap(one, "dp", 1), 0, pair, near[:1])
    sums, near = list(sums[:count]), [*sums[count:], *near[1:]]
    sums += add_pairs(keep, swap(two, "dp", 1), one.shape[0], pair)
    arrived = [swap(piece, "dp", len(near) + 1 + 2 * i) for i, piece in enumerate(sums)]
    arrived += [swap(piece, "dp", k + 1) for k, piece in enumerate(near)]
    return own, arrived


def finish(own, arrived, x=None):
    def body(own_ref, *refs):
        total = own_ref[...]
        for ref in refs[: len(arrived)]:
            total = total + ref[...].astype(F32)
        rounded = total.astype(BF16)
        if x is None:
            refs[-1][...] = rounded
        else:
            refs[-2][...] = rounded
            refs[-1][...] = (refs[len(arrived)][...].astype(F32) + rounded.astype(F32)).astype(BF16)

    outs = (shaped(own.shape),) * (1 if x is None else 2)
    ins = (own, *arrived) + (() if x is None else (x,))
    return call(body, outs, ins, [VMEM] * len(ins), moved=8 * own.size)


def attend_cached(where, anc, rope, scale, queries, near_cache, far_cache, part_dev):
    tensor = lax.axis_size("tensor")
    groups = lax.axis_size("dp")
    near = groups // tensor
    pair = 2 * part_dev
    close, span, _ = near_cache[0].shape
    ctx = tensor * span
    height, columns = queries[0].shape
    heads = columns // HD
    parts = near * part_dev
    rows = heads * parts

    def body(where_ref, anc_ref, rope_ref, scale_ref, *refs):
        q_refs, refs = refs[: len(queries)], refs[len(queries) :]
        count = tensor // 2 + 1
        near_refs, far_refs = refs[:count], refs[count : 2 * count]
        near_refs, far_refs = [(*part[:-1], *[part[-1].at[i] for i in range(count - 1)]) for part in (near_refs, far_refs)]
        query_ref, mixed_ref, highest_ref, total_ref, keys_ref, values_ref = refs[2 * count :]
        d, t = where_ref[0], where_ref[1]
        query_sum = q_refs[0][...]
        for ref in q_refs[1:]:
            if ref.shape[0] == height:
                query_sum = query_sum + ref[...].astype(F32)
            else:
                lanes = slice(ref.shape[1] - columns // 4, ref.shape[1])
                query_sum = query_sum + unstacked(ref[:, lanes].astype(F32), 4)
        query_sum = query_sum * scale_ref[pl.ds(pl.multiple_of(t * near * pair, pair), near * pair), 0:1]
        for step in range(2):

            def bring(i, _, step=step):
                particle = t * parts + i if step == 0 else anc_ref[i]
                block, member = lax.div(particle, part_dev) ^ d, lax.rem(particle, part_dev)

                def load(cache_refs, entry):
                    for k, cache_ref in enumerate(cache_refs):
                        to = pl.ds(pl.multiple_of(i * ctx + k * span, 8), span)
                        lanes = pl.ds(pl.multiple_of(member * HD, HD), HD)
                        keys_ref[to, :] = cache_ref[entry, :, lanes].astype(F32)
                        lanes = pl.ds(pl.multiple_of((part_dev + member) * HD, HD), HD)
                        values_ref[to, :] = cache_ref[entry, :, lanes].astype(F32)

                @pl.when(block < close)
                def _():
                    load(near_refs, block)

                @pl.when(block >= close)
                def _():
                    load(far_refs, block - close)

                return 0

            lax.fori_loop(0, parts, bring, 0)
            keys = keys_ref[...].astype(BF16)
            values = values_ref[...].astype(BF16)
            per_head = []
            for h in range(heads):
                for b in range(near):
                    first = b * pair + step * part_dev
                    per_head.append(query_sum[first : first + part_dev, h * HD : (h + 1) * HD])
            query = jnp.concatenate(per_head, axis=0).astype(BF16).astype(F32)
            cosine = rope_ref[2 * step : 2 * step + 1, :]
            sine = rope_ref[2 * step + 1 : 2 * step + 2, :]
            query = (query * cosine + pltpu.roll(query, HD // 2, 1) * sine).astype(BF16)
            scores = lax.dot_general(query, keys, (((1,), (1,)), ((), ())), preferred_element_type=F32)
            scores = scores * (1.0 / math.sqrt(HD))
            row_part = lax.rem(lax.broadcasted_iota(jnp.int32, (rows, 1), 0), parts)
            col_part = lax.div(lax.broadcasted_iota(jnp.int32, (1, parts * ctx), 1), ctx)
            scores = jnp.where(row_part == col_part, scores, MASKED)
            highest = jnp.max(scores, axis=1, keepdims=True)
            weights = jnp.exp(scores - highest)
            here = slice(step * rows, (step + 1) * rows)
            query_ref[here, :] = query
            mixed_ref[here, :] = jnp.dot(weights.astype(BF16), values, preferred_element_type=F32)
            highest_ref[here, :] = jnp.broadcast_to(highest, (rows, 128))
            total_ref[here, :] = jnp.broadcast_to(jnp.sum(weights, axis=1, keepdims=True), (rows, 128))

    ins = (where, anc, rope, scale, *queries, *near_cache, *far_cache)
    return call(
        body,
        (shaped((2 * rows, HD)), shaped((2 * rows, HD), F32), shaped((2 * rows, 128), F32), shaped((2 * rows, 128), F32)),
        ins,
        [SMEM] * 2 + [VMEM] * (len(ins) - 2),
        [pltpu.VMEM((parts * ctx, HD), F32), pltpu.VMEM((parts * ctx, HD), F32)],
        limit=(4 << 20) + 12 * rows * parts * ctx,
        moved=4 << 20,
    )


def attend_new(where, rope, targets, scale, pieces, state, shape, part_dev):
    groups = lax.axis_size("dp")
    tensor = lax.axis_size("tensor")
    near = groups // tensor
    pair = 2 * part_dev
    parts = near * part_dev
    heads = shape[1] // HD
    rows = heads * parts

    def body(where_ref, rope_ref, target_ref, scale_ref, *refs):
        piece_refs, (query_ref, mixed_ref, highest_ref, total_ref, out_ref) = refs[: len(pieces)], refs[len(pieces) :]
        even = where_ref[0] % 2 == 0 if groups == KVH else True
        if len(pieces) == 2:
            one, two = [ref[...].astype(F32) for ref in piece_refs]
        else:
            two, one = [piece_refs[i][...].astype(F32) + piece_refs[i + 1][...].astype(F32) for i in (0, 2)]
            one, two = [(x * scale_ref[...]).astype(BF16).astype(F32) for x in (one, two)]
        plain = jnp.where(even, one, two)
        values = jnp.where(even, two, one).astype(BF16)
        cosine = jnp.concatenate([jnp.broadcast_to(rope_ref[2 * s : 2 * s + 1, :], (part_dev, HD)) for s in range(2)])
        sine = jnp.concatenate([jnp.broadcast_to(rope_ref[2 * s + 1 : 2 * s + 2, :], (part_dev, HD)) for s in range(2)])
        turned = pltpu.roll(plain, HD // 2, 1).reshape(groups, pair, HD)
        keys = plain.reshape(groups, pair, HD) * cosine[None] + turned * sine[None]
        keys = keys.reshape(groups * pair, HD).astype(BF16)
        scores = lax.dot_general(query_ref[...], keys, (((1,), (1,)), ((), ())), preferred_element_type=F32)
        scores = scores * (1.0 / math.sqrt(HD))
        col = lax.broadcasted_iota(jnp.int32, (1, groups * pair), 1)
        wanted = (col == target_ref[:, 0:1]) | (col == target_ref[:, 1:2])
        scores = jnp.where(wanted, scores, MASKED)
        before = highest_ref[:, 0:1]
        highest = jnp.maximum(before, jnp.max(scores, axis=1, keepdims=True))
        weights = jnp.exp(scores - highest)
        keep = jnp.exp(before - highest)
        total = total_ref[:, 0:1] * keep + jnp.sum(weights, axis=1, keepdims=True)
        mixed = mixed_ref[...] * keep + jnp.dot(weights.astype(BF16), values, preferred_element_type=F32)
        mixed = mixed / total
        for h in range(heads):
            for b in range(near):
                first = h * parts + b * part_dev
                both = [mixed[s * rows + first : s * rows + first + part_dev] for s in range(2)]
                here = slice(b * pair, (b + 1) * pair)
                out_ref[here, h * HD : (h + 1) * HD] = jnp.concatenate(both, axis=0).astype(BF16)

    ins = (where, rope, targets, scale, *pieces, *state)
    return call(body, shaped(shape), ins, [SMEM] + [VMEM] * (len(ins) - 1), moved=1 << 20)


def send_keyvals(pieces):
    groups = lax.axis_size("dp")
    tensor = lax.axis_size("tensor")
    half = groups // 2
    moved = []
    for flip, piece in enumerate(pieces):
        to = [2 * i + flip for i in range(half)] + [2 * i + 1 - flip for i in range(half)]
        for k in (0, 2):
            pairs = [(i * tensor + t, to[i] * tensor + (t ^ k)) for i in range(groups) for t in range(tensor)]
            moved.append(lax.ppermute(piece, ("dp", "tensor"), pairs))
    return moved[2:] + moved[:2]


def move_keyvals(pieces):
    groups = lax.axis_size("dp")
    d = lax.axis_index("dp")
    if groups == KVH:
        half = groups // 2
        one = [(i, 2 * i) for i in range(half)] + [(half + i, 2 * i + 1) for i in range(half)]
        two = [(i, 2 * i + 1) for i in range(half)] + [(half + i, 2 * i) for i in range(half)]
        return [lax.ppermute(x, "dp", to) for x, to in zip(pieces, (one, two))]
    every = lax.all_gather(pieces[0], "dp", axis=1, tiled=True)
    start = (d * KVH // groups) * HD
    return [lax.dynamic_slice_in_dim(every, first + start, HD, axis=1) for first in (0, KVH * HD)]


def local(
    x_first,
    x_second,
    cache_keys,
    cache_values,
    ancestors,
    attn_gain,
    ffn_gain,
    w_query,
    w_keyval,
    w_out,
    w_gate,
    w_up,
    w_down,
):
    groups = lax.axis_size("dp")
    tensor = lax.axis_size("tensor")
    part_dev, features = x_first.shape
    span = cache_keys.shape[1]
    width = features * tensor
    context = span * tensor
    d = lax.axis_index("dp")
    t = lax.axis_index("tensor")
    pair = 2 * part_dev
    near = groups // tensor
    parts = near * part_dev
    where = jnp.stack([d, t]).astype(jnp.int32)

    x = stack_tokens(x_first, x_second)
    own_piece, near_pieces, joined = pack_near(where, x, cache_keys, cache_values)
    blocks = gather_rows(x, near_pieces if joined else None)
    close = min(groups, 4)
    near_moved = blocks[1:close] if joined else [swap(piece, "dp", k) for k, piece in enumerate(near_pieces, 1)]
    near_pieces = collect_near(own_piece, near_moved, span)
    packed = pack_far(where, cache_keys, cache_values, blocks[close::2])
    far_pieces = [swap(piece, "dp", close + 2 * i) for i, piece in enumerate(packed)]

    message, keep = project_attention(where, blocks, attn_gain, w_keyval, w_query, x)
    queries, message, *leaving = add_cores(where, message, keep, swap(message, "tensor", 1))
    passed = swap(last_entries(far_pieces, x), "dp", 1)
    far_pieces = collect_far(far_pieces, passed)
    if direct_keyvals():
        pieces = send_keyvals(leaving)
        arrived = swap(message, "tensor", 2)
        scale = row_scale(message, arrived, width)
        queries = [queries, arrived]
    else:
        bits = 2
        while 2 * bits < tensor:
            message = add_keyvals(message, swap(message, "tensor", bits))
            bits *= 2
        arrived = swap(message, "tensor", bits)
        scale, *pieces = finish_keyvals(where, message, arrived, w_keyval.shape[1], width)
        pieces = move_keyvals(pieces)
        queries = [queries] + [swap(piece, "tensor", 2 * i) for i, piece in enumerate(leaving, 1)]

    near_cache = gather_cache(near_pieces, arrived)
    far_cache = gather_cache(far_pieces, arrived)

    own = t * parts + jnp.arange(parts, dtype=jnp.int32)
    anc = lax.dynamic_slice_in_dim(ancestors, t * parts, parts).astype(jnp.int32)
    heads = w_query.shape[1] // HD

    def row_of(particle, step):
        return (particle // part_dev) * pair + step * part_dev + particle % part_dev

    first = jnp.stack([row_of(own, 0)] * 2, axis=1)
    second = jnp.stack([row_of(anc, 0), row_of(own, 1)], axis=1)
    targets = jnp.concatenate([jnp.tile(first, (heads, 1)), jnp.tile(second, (heads, 1))]).astype(jnp.int32)
    rope = jnp.asarray(np.stack(rope_tables(context) + rope_tables(context + 1)))
    state = attend_cached(where, anc, rope, scale, queries, near_cache, far_cache, part_dev)
    mixed = attend_new(where, rope, targets, scale, pieces, state, queries[0].shape, part_dev)

    parts = project_back(where, gather_blocks(mixed), w_out)
    attn_part, residual = finish(*sum_rows(parts, pair), x)

    hidden_cols = w_gate.shape[1]
    h, keep, send = project_gate(where, gather_rows(residual), ffn_gain, w_gate)
    gate, gate_arrived = sum_blocks(keep, send)
    up, up_arrived = sum_blocks(*project(h, w_up))
    for piece in gate_arrived:
        gate = gate + piece.astype(F32)
    for piece in up_arrived:
        up = up + piece.astype(F32)
    scale = lax.rsqrt((gate[:, hidden_cols] + gate[:, hidden_cols + 1]) / width + EPS)[:, None]
    hidden = jax.nn.silu(gate[:, :hidden_cols] * scale) * (up * scale)
    parts = project_back(where, gather_blocks(hidden.astype(BF16)), w_down)
    (ffn_part,) = finish(*sum_rows(parts, pair))
    return (attn_part.reshape(2, part_dev, features), ffn_part.reshape(2, part_dev, features))


def solution(mesh):
    return jax.shard_map(
        local,
        mesh=mesh,
        in_specs=(
            P("dp", "tensor"),
            P("dp", "tensor"),
            P("dp", "tensor", None),
            P("dp", "tensor", None),
            P(),
            P("tensor"),
            P("tensor"),
            P("tensor", "dp"),
            P("tensor", "dp"),
            P("dp", "tensor"),
            P("tensor", "dp"),
            P("tensor", "dp"),
            P("dp", "tensor"),
        ),
        out_specs=(P(None, "dp", "tensor"), P(None, "dp", "tensor")),
        check_vma=False,
    )
```
